32 devices in a mesh: dp: 8 (over y, x, core), expert: 4 (over z).
Axes of the slice: x: 2, y: 2, z: 4, core: 2. Of those that a mesh axis runs over, the one named last changes fastest.
Arguments:
- hidden_in: bfloat16 [8192, 1536], P(('dp', 'expert')), may hold values from -6 to 6
- cotangent: bfloat16 [8192, 1536], P(('dp', 'expert')), may hold values from -6 to 6
- routes: int32 [8192, 6], P(('dp', 'expert')), may hold values from 0 to 23, all different within a row; in each aligned block of 256 rows (0 to 255, 256 to 511, ...) at most 80 rows name the same one
- route_weights: float32 [8192, 6], P(('dp', 'expert')), may hold values from 0.15 to 0.5
- dense_weights: float32 [1536, 7168], P(('dp', 'expert')), may hold values from -4 to 4
- dense_momentum: float32 [1536, 7168], P(('dp', 'expert')), may hold values from -160 to 160
- expert_weights: float32 [24, 3, 1536, 512], P('expert', None, 'dp'), may hold values from -0.25 to 0.25
- expert_momentum: float32 [24, 3, 1536, 512], P('expert', None, 'dp'), may hold values from -80 to 80
- norm_gains: float32 [2, 1536], P(None, ('dp', 'expert')), may hold values from 0.5 to 1.5
- gain_first: float32 [2, 1536], P(None, ('dp', 'expert')), may hold values from -448 to 448
- gain_second: float32 [2, 1536], P(None, ('dp', 'expert')), may hold values from 24576 to 98304
Outputs:
- block_out: bfloat16 [8192, 1536], P(('dp', 'expert'))
- input_grad: float32 [8192, 1536], P(('dp', 'expert'))
- dense_grad: float32 [1536, 7168], P(('dp', 'expert'))
- dense_moment: float32 [1536, 7168], P(('dp', 'expert'))
- dense_new: float32 [1536, 7168], P(('dp', 'expert'))
- expert_grad: float32 [24, 3, 1536, 512], P('expert', None, 'dp')
- expert_moment: float32 [24, 3, 1536, 512], P('expert', None, 'dp')
- expert_new: float32 [24, 3, 1536, 512], P('expert', None, 'dp')
- gain_grad: float32 [2, 1536], P(None, ('dp', 'expert'))
- gain_first_new: float32 [2, 1536], P(None, ('dp', 'expert'))
- gain_second_new: float32 [2, 1536], P(None, ('dp', 'expert'))
- gain_new: float32 [2, 1536], P(None, ('dp', 'expert'))
The draws below stay inside these ranges and needn't reach their ends.
Inputs may be any that keep to these rules, and one draw needn't show every extreme that they name: `routes`: each row names 6 different experts; in each aligned block of 256 rows, the rows of one device, no expert is named by more than 80 rows, and that bound is reached.
All inputs are finite; a program needn't handle non-finite values.
Results may differ from the reference program's by a relative error of at most 0.025.
Values may be sent and summed in bfloat16 or wider, within the bound.
A program may use at most 384 MiB of HBM per device.

```python
import math
import jax
import jax.numpy as jnp
import numpy as np
from jax import lax

D = 1536
HEADS = 12
HD = 128
KVH = 4
FFE = 512
FFS = 1024
TOPK = 6
TOK_DEV = 256
NS_STEPS = 5
STEP = 10
EXPERTS = 24
CAP = 80
TOKENS = 8192
DW = 7168


def draw_dense_weights(key, part):
    key = jax.random.fold_in(key, 11)
    query_width = HEADS * HD
    kv_width = KVH * HD
    noise = jnp.clip(jax.random.normal(key, (D, 2 * query_width + 2 * kv_width + 3 * FFS), jnp.float32), -6.0, 6.0)
    column_scale = jnp.concatenate([jnp.full((query_width,), 1.3 * D ** (-0.5), jnp.float32), jnp.full((kv_width,), 1.3 * D ** (-0.5), jnp.float32), jnp.full((kv_width,), D ** (-0.5), jnp.float32), jnp.full((query_width,), 6.0 * query_width ** (-0.5), jnp.float32), jnp.full((2 * FFS,), D ** (-0.5), jnp.float32), jnp.full((FFS,), FFS ** (-0.5), jnp.float32)])
    return noise * column_scale[None, :]


def block_scale(own_key, shape, split, low, high):
    gain, own = 1.0, jax.random.fold_in(own_key, 6)
    for position, shards_of in split:
        heights = jnp.exp(jax.random.uniform(jax.random.fold_in(own, position), (shards_of,), jnp.float32, low / len(split), high / len(split)))
        gain = gain * jnp.repeat(heights, shape[position] // shards_of).reshape([-1 if axis == position else 1 for axis in range(len(shape))])
    return gain


def deal_out(stream_key, own, number, rows, amount, top, most, skew):
    sequence = jax.random.permutation(stream_key, amount)
    crowded, ordinary = load_shares(amount, rows * top, most, skew, True), load_shares(amount, rows * top, most, skew, False)
    places = jnp.arange(amount)

    def named(sizes, offset_by):
        used = int((sizes > 0).sum())
        fixed = max(1, used // 4)
        passed = fixed + (places - fixed + offset_by * (used - fixed)) % max(1, amount - fixed)
        return jnp.zeros((amount,), jnp.int32).at[sequence[jnp.where(places < fixed, places, passed)]].set(jnp.asarray(sizes, jnp.int32))

    sizes = jnp.where(number % 4 == 0, named(crowded, number // 4), named(ordinary, number - number // 4 - 1))
    mixed = jax.random.permutation(jax.random.fold_in(own, 3), amount)
    giver, taker = mixed[0:amount // 2 * 2:2], mixed[1:amount // 2 * 2:2]
    slack = jnp.minimum(sizes[giver] - 1, most - sizes[taker]) // 2
    slack = jnp.where((giver == sequence[0]) | (taker == sequence[0]) | (sizes[taker] == 0), 0, jnp.maximum(slack, 0))
    passed = jax.random.randint(jax.random.fold_in(own, 4), (amount // 2,), 0, 1 << 20) % (slack + 1)
    sizes = sizes.at[giver].add(-passed).at[taker].add(passed)
    members = jnp.searchsorted(jnp.cumsum(sizes), jnp.arange(rows * top), side="right").astype(jnp.int32)
    table = members.reshape(top, rows).T
    table = table[jax.random.permutation(jax.random.fold_in(own, 1), rows)]
    offset_by = jax.random.randint(jax.random.fold_in(own, 2), (rows, 1), 0, top)
    return jnp.take_along_axis(table, (jnp.arange(top)[None, :] + offset_by) % top, axis=1)


def load_shares(count, total, limit, skew, full):
    loads = [(1 << 20) // math.isqrt(rank ** skew) + 1 for rank in range(1, count + 1)]
    largest = limit if full else min(limit, max(-(-total // count), total * loads[0] // sum(loads)))
    least = 1 if total - largest >= count - 1 else 0
    given, spare = [largest] + [least] * (count - 1), total - largest - least * (count - 1)
    while spare > 0:
        free = [i for i in range(1, count) if given[i] < largest] or [i for i in range(1, count) if given[i] < limit]
        mass, left = sum([loads[i] for i in free]), spare
        for i in free:
            extra = min(limit - given[i], max(1, left * loads[i] // mass), spare)
            given[i] = given[i] + extra
            spare = spare - extra
    return np.array(given)


def gaussian(own_key, extent, spread, limit, cuts=(), held_as=jnp.bfloat16):
    values = spread * jax.random.normal(own_key, extent, jnp.float32)
    if cuts:
        values = values * block_scale(own_key, extent, cuts, -0.22, 0.18)
    return jnp.clip(values, -limit, limit).astype(held_as)


def setup_inputs(seed: int = 0) -> dict:
    arg_keys = jax.random.split(jax.random.key(seed), 12)
    hidden_in = gaussian(arg_keys[0], (TOKENS, D), 1.0, 6.0, ((0, 32),))
    cotangent = gaussian(arg_keys[1], (TOKENS, D), 1.0, 6.0, ((0, 32),))
    routes_keys = jax.random.split(jax.random.fold_in(arg_keys[2], 1), TOKENS // TOK_DEV)
    routes_turns = jax.random.permutation(jax.random.fold_in(arg_keys[2], 3), TOKENS // TOK_DEV)
    routes = jax.vmap(lambda own, number: deal_out(jax.random.fold_in(arg_keys[2], 2), own, number, TOK_DEV, EXPERTS, TOPK, CAP, 2))(routes_keys, routes_turns).reshape((TOKENS, TOPK))
    route_weights = jnp.clip(jnp.exp(math.log(0.5) - 1.2039728 * jax.random.uniform(arg_keys[3], (TOKENS, TOPK), jnp.float32) ** block_scale(arg_keys[3], (TOKENS, TOPK), ((0, 32),), -0.2, 0.2)), 0.15, 0.5)
    dense_weights = draw_dense_weights(jax.random.fold_in(arg_keys[11], 71), 0)
    dense_momentum = gaussian(arg_keys[5], (D, DW), (0.3 * TOKENS ** 0.5), 160.0, ((0, 32),), jnp.float32)
    expert_weights = gaussian(arg_keys[6], (EXPERTS, 3, D, FFE), FFE ** -0.5, 0.25, ((0, 4), (2, 8)), jnp.float32)
    expert_momentum = gaussian(arg_keys[7], (EXPERTS, 3, D, FFE), (0.3 * (TOKENS * TOPK // EXPERTS) ** 0.5), 80.0, ((0, 4), (2, 8)), jnp.float32)
    norm_gains = jnp.clip(1.0 + 0.1 * jax.random.normal(arg_keys[8], (2, D), jnp.float32), 0.5, 1.5)
    gain_first = gaussian(arg_keys[9], (2, D), (0.8 * TOKENS ** 0.5), 448.0, ((1, 32),), jnp.float32)
    gain_second = jnp.clip(jnp.exp(math.log(98304.0) - 1.3862944 * jax.random.uniform(arg_keys[10], (2, D), jnp.float32) ** block_scale(arg_keys[10], (2, D), ((1, 32),), -0.2, 0.2)), 24576.0, 98304.0)
    return dict(hidden_in=hidden_in, cotangent=cotangent, routes=routes, route_weights=route_weights, dense_weights=dense_weights, dense_momentum=dense_momentum, expert_weights=expert_weights, expert_momentum=expert_momentum, norm_gains=norm_gains, gain_first=gain_first, gain_second=gain_second)


PRECISE = lax.Precision.HIGHEST
POLY_FIRST = 3.4445
POLY_SECOND = -4.775
POLY_THIRD = 2.0315
MOMENTUM_DECAY = 0.95
LEARN_RATE = 0.6
WEIGHT_DECAY = 0.1
GAIN_RATE = 0.8
FIRST_DECAY = 0.9
SECOND_DECAY = 0.95

@jax.custom_vjp
def low(v):
    return lax.optimization_barrier(v.astype(jnp.bfloat16)).astype(jnp.float32)

@jax.custom_vjp
def low_back(v):
    return v

def low_keep(v):
    return (low(v), None)

def low_pass(kept, grad):
    return (grad,)

def back_keep(v):
    return (v, None)

def back_low(kept, grad):
    return (low(grad),)
low.defvjp(low_keep, low_pass)
low_back.defvjp(back_keep, back_low)

def product(pattern, left_side, right_side):
    return jnp.einsum(pattern, left_side, right_side, precision=PRECISE, preferred_element_type=jnp.float32)

def norm_rows(values, gain_row):
    return values * lax.rsqrt(lax.optimization_barrier(jnp.mean(values * values, axis=-1, keepdims=True)) + 1e-06) * gain_row

def slot_table(route_rows, expert_count, capacity):
    flat_routes = route_rows.reshape(-1)
    choices_hot = (flat_routes[:, None] == jnp.arange(expert_count, dtype=jnp.int32)[None, :]).astype(jnp.int32)
    earlier = jnp.cumsum(choices_hot, axis=0) - choices_hot
    return flat_routes * capacity + lax.optimization_barrier(jnp.sum(earlier * choices_hot, axis=1))

def attention(query, key_rows, value_rows):
    length = query.shape[0]
    query_heads = query.reshape(length, KVH, HEADS // KVH, HD)
    key_heads = key_rows.reshape(length, KVH, HD)
    value_heads = value_rows.reshape(length, KVH, HD)
    scores = low_back(product('qgrd,kgd->grqk', query_heads, key_heads) * HD ** (-0.5))
    allowed = jnp.arange(length)[None, :] <= jnp.arange(length)[:, None]
    scores = jnp.where(allowed, scores, -1e+30)
    highest = lax.optimization_barrier(jnp.max(scores, axis=-1, keepdims=True))
    raised = jnp.exp(scores - highest)
    weights = raised / lax.optimization_barrier(jnp.sum(raised, axis=-1, keepdims=True))
    attended = product('grqk,kgd->qgrd', low(weights), value_heads)
    return attended.reshape(length, HEADS * HD)

def one_sequence(residual_in, route_rows, route_gates, dense_used, expert_used, gain_used):
    query_width = HEADS * HD
    kv_width = KVH * HD
    qkv_end = query_width + 2 * kv_width
    shared_base = 2 * query_width + 2 * kv_width
    normed_attend = low(norm_rows(residual_in, gain_used[0]))
    query = low(low_back(product('sd,dc->sc', normed_attend, dense_used[:, :query_width])))
    key_rows = low(low_back(product('sd,dc->sc', normed_attend, dense_used[:, query_width:query_width + kv_width])))
    value_rows = low(low_back(product('sd,dc->sc', normed_attend, dense_used[:, query_width + kv_width:qkv_end])))
    attended = low(low_back(attention(query, key_rows, value_rows)))
    attn_out = low_back(product('sq,dq->sd', attended, dense_used[:, qkv_end:shared_base]))
    residual = residual_in + attn_out
    normed_mixer = low(norm_rows(residual, gain_used[1]))
    shared_gate = low_back(product('sd,df->sf', normed_mixer, dense_used[:, shared_base:shared_base + FFS]))
    shared_up = low_back(product('sd,df->sf', normed_mixer, dense_used[:, shared_base + FFS:shared_base + 2 * FFS]))
    shared_act = low(jax.nn.silu(shared_gate) * shared_up)
    shared_out = low_back(product('sf,df->sd', shared_act, dense_used[:, shared_base + 2 * FFS:]))
    slots = slot_table(route_rows, EXPERTS, CAP)
    pair_count = route_rows.shape[0] * TOPK
    owner = jnp.zeros((EXPERTS * CAP,), jnp.int32).at[slots].set(jnp.arange(pair_count, dtype=jnp.int32) // TOPK)
    filled = jnp.zeros((EXPERTS * CAP,), jnp.float32).at[slots].set(1.0)
    buffer = low_back(normed_mixer[owner] * filled[:, None]).reshape(EXPERTS, CAP, D)
    expert_gate = low_back(product('ecd,edf->ecf', buffer, expert_used[:, 0]))
    expert_up = low_back(product('ecd,edf->ecf', buffer, expert_used[:, 1]))
    expert_act = low(jax.nn.silu(expert_gate) * expert_up)
    expert_out = low(low_back(product('ecf,edf->ecd', expert_act, expert_used[:, 2]))).reshape(EXPERTS * CAP, D)
    routed = lax.optimization_barrier(jnp.sum(expert_out[slots].reshape(-1, TOPK, D) * route_gates[:, :, None], axis=1))
    return residual + shared_out + routed

def forward(inputs, dense_master, expert_master, gain_master, routes, route_weights):
    dense_used = low(dense_master)
    expert_used = low(expert_master)
    gain_used = low(gain_master)
    count = TOKENS // TOK_DEV

    def sequence_step(pieces):
        return one_sequence(pieces[0], pieces[1], pieces[2], dense_used, expert_used, gain_used)
    outputs = lax.map(jax.checkpoint(sequence_step), (inputs.reshape(count, TOK_DEV, D), routes.reshape(count, TOK_DEV, TOPK), route_weights.reshape(count, TOK_DEV, TOPK)))
    return outputs.reshape(TOKENS, D)

def orthogonalize(moment):
    current = moment / (jnp.sqrt(jnp.sum(moment * moment)) + 1e-07)
    for iteration in range(NS_STEPS):
        rounded = low(current)
        gram_matrix = product('rf,rg->fg', rounded, rounded)
        gram_low = low(gram_matrix)
        polynomial = POLY_SECOND * gram_matrix + POLY_THIRD * product('fg,gh->fh', gram_low, gram_low)
        current = POLY_FIRST * current + product('rf,fg->rg', rounded, low(polynomial))
    return current

def reference(hidden_in, cotangent, routes, route_weights, dense_weights, dense_momentum, expert_weights, expert_momentum, norm_gains, gain_first, gain_second):
    inputs = hidden_in.astype(jnp.float32)

    def wrapped(tokens_in, dense_master, expert_master, gain_master):
        return forward(tokens_in, dense_master, expert_master, gain_master, routes, route_weights)
    outputs, pullback = jax.vjp(wrapped, inputs, dense_weights, expert_weights, norm_gains)
    input_grad, dense_grad, expert_grad, gain_grad = pullback(cotangent.astype(jnp.float32))
    block_out = outputs.astype(jnp.bfloat16)
    dense_moment = MOMENTUM_DECAY * dense_momentum + dense_grad
    expert_moment = MOMENTUM_DECAY * expert_momentum + expert_grad
    units = jnp.concatenate([expert_moment.reshape(-1, D, FFE), dense_moment.reshape(D, -1, FFE).transpose(1, 0, 2)], 0)
    orthogonal = lax.map(orthogonalize, units)
    expert_units = EXPERTS * 3
    orth_expert = orthogonal[:expert_units].reshape(expert_weights.shape)
    orth_dense = orthogonal[expert_units:].transpose(1, 0, 2).reshape(D, DW)
    keep_factor = 1.0 - LEARN_RATE * WEIGHT_DECAY
    dense_new = keep_factor * dense_weights - LEARN_RATE * orth_dense
    expert_new = keep_factor * expert_weights - LEARN_RATE * orth_expert
    first_new = FIRST_DECAY * gain_first + (1.0 - FIRST_DECAY) * gain_grad
    second_new = SECOND_DECAY * gain_second + (1.0 - SECOND_DECAY) * gain_grad * gain_grad
    step_ratio = first_new / (1.0 - FIRST_DECAY ** STEP) / (jnp.sqrt(second_new / (1.0 - SECOND_DECAY ** STEP)) + 1e-08)
    gain_new = norm_gains - GAIN_RATE * step_ratio
    return (block_out, input_grad, dense_grad, dense_moment, dense_new, expert_grad, expert_moment, expert_new, gain_grad, first_new, second_new, gain_new)
```

```python
import functools

import jax
import jax.numpy as jnp
from jax import lax
from jax.experimental import pallas as pl
from jax.experimental.pallas import tpu as pltpu
from jax.sharding import PartitionSpec as P

HEADS = 12
HD = 128
KVH = 4
FFE = 512
FFS = 1024
NS_STEPS = 5
STEP = 10


POLY_FIRST = 3.4445
POLY_SECOND = -4.775
POLY_THIRD = 2.0315
MOMENTUM_DECAY = 0.95
LEARN_RATE = 0.6
WEIGHT_DECAY = 0.1
GAIN_RATE = 0.8
FIRST_DECAY = 0.9
SECOND_DECAY = 0.95


def norm_scale(values):
    return lax.rsqrt(jnp.mean(values * values, axis=-1, keepdims=True) + 1e-06)


def block_scores(query_block, key_block, first_row, block_rows, last_row):
    score_scale = HD ** (-0.5)
    scores = (
        jnp.einsum("qgrd,kgd->grqk", query_block, key_block, preferred_element_type=jnp.float32)
        * score_scale
    )
    allowed = jnp.arange(last_row)[None, :] <= (first_row + jnp.arange(block_rows))[:, None]
    return jnp.where(allowed, scores, -1e30)


def attend_forward(query, key_rows, value_rows, block_rows):
    length = query.shape[0]
    query_heads = query.reshape(length, KVH, HEADS // KVH, HD)
    key_heads = key_rows.reshape(length, KVH, HD)
    value_heads = value_rows.reshape(length, KVH, HD)
    scores = block_scores(query_heads, key_heads, 0, block_rows, block_rows)
    highest = jnp.max(scores, axis=-1, keepdims=True)
    raised = jnp.exp(scores - highest)
    totals = jnp.sum(raised, axis=-1, keepdims=True)
    weights = (raised / totals).astype(jnp.bfloat16)
    outputs = jnp.einsum("grqk,kgd->qgrd", weights, value_heads, preferred_element_type=jnp.float32)
    saved_stats = [(highest, totals)]
    attended = outputs.reshape(length, HEADS * HD)
    return (attended.astype(jnp.bfloat16), saved_stats)


def attend_backward(query, key_rows, value_rows, grad_attended, saved_stats, block_rows):
    length = query.shape[0]
    score_scale = HD ** (-0.5)
    query_heads = query.reshape(length, KVH, HEADS // KVH, HD)
    grad_heads = grad_attended.reshape(length, KVH, HEADS // KVH, HD)
    key_heads = key_rows.reshape(length, KVH, HD)
    value_heads = value_rows.reshape(length, KVH, HD)
    grad_key = jnp.zeros((length, KVH, HD), jnp.float32)
    grad_value = jnp.zeros((length, KVH, HD), jnp.float32)
    query_parts = []
    for block_index, first_row in enumerate(range(0, length, block_rows)):
        last_row = first_row + block_rows
        scores = block_scores(query_heads, key_heads, first_row, block_rows, last_row)
        highest, totals = saved_stats[block_index]
        weights = jnp.exp(scores - highest) / totals
        grad_weights = jnp.einsum(
            "qgrd,kgd->grqk", grad_heads, value_heads, preferred_element_type=jnp.float32
        )
        inner_sum = jnp.sum(weights * grad_weights, axis=-1, keepdims=True)
        grad_scores = (weights * (grad_weights - inner_sum)).astype(jnp.bfloat16)
        query_parts.append(
            jnp.einsum("grqk,kgd->qgrd", grad_scores, key_heads, preferred_element_type=jnp.float32)
            * score_scale
        )
        grad_key = grad_key.at[:last_row].add(
            jnp.einsum(
                "grqk,qgrd->kgd", grad_scores, query_heads, preferred_element_type=jnp.float32
            )
            * score_scale
        )
        grad_value = grad_value.at[:last_row].add(
            jnp.einsum(
                "grqk,qgrd->kgd",
                weights.astype(jnp.bfloat16),
                grad_heads,
                preferred_element_type=jnp.float32,
            )
        )
    grad_query = query_parts[0].reshape(length, HEADS * HD)
    return (
        grad_query.astype(jnp.bfloat16),
        grad_key.reshape(length, KVH * HD).astype(jnp.bfloat16),
        grad_value.reshape(length, KVH * HD).astype(jnp.bfloat16),
    )


MIB = 2**20
GRAD_STEP = 11
SLOTS = 8
MESH = pl.DeviceIdType.MESH


def matmul(left, right):
    return jnp.dot(left, right, preferred_element_type=jnp.float32)


def matmul_nt(left, right):
    return lax.dot_general(left, right, (((1,), (1,)), ((), ())), preferred_element_type=jnp.float32)


def matmul_tn(left, right):
    return lax.dot_general(left, right, (((0,), (0,)), ((), ())), preferred_element_type=jnp.float32)


def newton_schulz_unit(moment_ref, orthogonal_ref, current, low, identity):
    columns, rows = current.shape
    step = 256
    parts = [pl.ds(index * step, step) for index in range(rows // step)]
    identity[...] = jnp.where(
        lax.broadcasted_iota(jnp.int32, identity.shape, 0)
        == lax.broadcasted_iota(jnp.int32, identity.shape, 1),
        1.0,
        0.0,
    ).astype(jnp.bfloat16)
    squares = jnp.zeros((1, columns), jnp.float32)
    for part in parts:
        values = moment_ref[part, :].astype(jnp.float32)
        squares = squares + jnp.sum(values * values, axis=0, keepdims=True)
    scale = 1.0 / (jnp.sqrt(jnp.sum(squares, axis=1, keepdims=True)) + 1e-07)
    for part in parts:
        scaled = matmul_nt(identity[...], moment_ref[part, :]) * scale
        current[:, part] = scaled
        low[:, part] = scaled.astype(jnp.bfloat16)

    def polynomial():
        gram = matmul_nt(low[...], low[...])
        gram_low = gram.astype(jnp.bfloat16)
        return (POLY_SECOND * gram + POLY_THIRD * matmul(gram_low, gram_low)).astype(jnp.bfloat16)

    @pl.loop(0, NS_STEPS - 1)
    def _(index):
        weights = polynomial()
        for part in parts:
            updated = POLY_FIRST * current[:, part] + matmul(weights, low[:, part])
            current[:, part] = updated
            low[:, part] = updated.astype(jnp.bfloat16)

    weights = polynomial()
    for part in parts:
        updated = POLY_FIRST * current[:, part] + matmul(weights, low[:, part])
        orthogonal_ref[part, :] = updated.T.astype(jnp.bfloat16)


def newton_schulz_kernel(moment_ref, orthogonal_ref, current, low, identity):
    newton_schulz_unit(moment_ref.at[0], orthogonal_ref.at[0], current, low, identity)


def newton_schulz(units):
    count, rows, columns = units.shape
    return pl.pallas_call(
        newton_schulz_kernel,
        grid=(count,),
        in_specs=[pl.BlockSpec((1, rows, columns), lambda unit: (unit, 0, 0))],
        out_specs=pl.BlockSpec((1, rows, columns), lambda unit: (unit, 0, 0)),
        out_shape=jax.ShapeDtypeStruct(units.shape, jnp.bfloat16),
        scratch_shapes=[
            pltpu.VMEM((columns, rows), jnp.float32),
            pltpu.VMEM((columns, rows), jnp.bfloat16),
            pltpu.VMEM((columns, columns), jnp.bfloat16),
        ],
        compiler_params=pltpu.CompilerParams(vmem_limit_bytes=48 * MIB),
        cost_estimate=pl.CostEstimate(
            flops=count * NS_STEPS * 2 * columns * columns * (2 * rows + columns),
            bytes_accessed=count * rows * columns * 4,
            transcendentals=0,
        ),
        name="newton_schulz",
    )(units)


def experts_kernel(
    tokens_ref,
    cotangent_ref,
    place_ref,
    gate_ref,
    weights_ref,
    routed_ref,
    grad_tokens_ref,
    received,
    grad_returned,
    act_ref,
    grad_gate_ref,
    grad_up_ref,
    routed_sum,
    grad_sum,
    chosen,
    weighted,
    grad_received,
):
    expert = pl.program_id(0)
    sequences, slots, length = chosen.shape

    @pl.when(expert == 0)
    def _():
        routed_sum[...] = jnp.zeros_like(routed_sum)
        grad_sum[...] = jnp.zeros_like(grad_sum)

    slot_weights = []
    for sequence in range(sequences):
        rows = pl.ds(sequence * length, length)
        spots = pl.ds(sequence * slots, slots)
        place = place_ref[0, sequence : sequence + 1, :]
        gate = gate_ref[0, sequence : sequence + 1, :]
        hot = lax.broadcasted_iota(jnp.int32, (slots, length), 0) == place
        slot_weight = jnp.sum(jnp.where(hot, gate, 0.0), axis=1, keepdims=True)
        slot_weights.append(slot_weight)
        hot_low = jnp.where(hot, 1.0, 0.0).astype(jnp.bfloat16)
        chosen[sequence] = hot_low
        received[0, spots, :] = matmul(hot_low, tokens_ref[rows, :]).astype(jnp.bfloat16)
        grad_returned[0, spots, :] = (
            matmul(hot_low, cotangent_ref[rows, :]) * slot_weight
        ).astype(jnp.bfloat16)
    tokens = received[0]
    grad_out = grad_returned[0]
    gate_pre = matmul(tokens, weights_ref[0, 0])
    up_pre = matmul(tokens, weights_ref[0, 1])
    gate_sig = jax.nn.sigmoid(gate_pre)
    gate_act = gate_pre * gate_sig
    act = (gate_act * up_pre).astype(jnp.bfloat16)
    act_ref[0] = act
    out = matmul_nt(act, weights_ref[0, 2]).astype(jnp.bfloat16).astype(jnp.float32)
    for sequence in range(sequences):
        spots = slice(sequence * slots, (sequence + 1) * slots)
        weighted[spots, :] = (out[spots] * slot_weights[sequence]).astype(jnp.bfloat16)
    grad_act = matmul(grad_out, weights_ref[0, 2])
    grad_gate = (grad_act * up_pre * gate_sig * (1.0 + gate_pre * (1.0 - gate_sig))).astype(
        jnp.bfloat16
    )
    grad_up = (grad_act * gate_act).astype(jnp.bfloat16)
    grad_gate_ref[0] = grad_gate
    grad_up_ref[0] = grad_up
    grad_received[...] = (
        matmul_nt(grad_gate, weights_ref[0, 0]) + matmul_nt(grad_up, weights_ref[0, 1])
    ).astype(jnp.bfloat16)
    for sequence in range(sequences):
        rows = pl.ds(sequence * length, length)
        spots = pl.ds(sequence * slots, slots)
        routed_sum[rows, :] += matmul_tn(chosen[sequence], weighted[spots, :])
        grad_sum[rows, :] += matmul_tn(chosen[sequence], grad_received[spots, :])

    @pl.when(expert == pl.num_programs(0) - 1)
    def _():
        routed_ref[...] = routed_sum[...].astype(jnp.bfloat16)
        grad_tokens_ref[...] = grad_sum[...].astype(jnp.bfloat16)


def run_experts(tokens, cotangents, place, gates, weights, capacity):
    experts, sequences, length = place.shape
    total, width = tokens.shape
    hidden = weights.shape[-1]
    slots = -(-capacity // 16) * 16
    spots = sequences * slots
    whole = pl.BlockSpec((total, width), lambda expert: (0, 0))
    table = pl.BlockSpec((1, sequences, length), lambda expert: (expert, 0, 0))
    matrices = pl.BlockSpec((1, 3, width, hidden), lambda expert: (expert, 0, 0, 0))
    wide = pl.BlockSpec((1, spots, width), lambda expert: (expert, 0, 0))
    narrow = pl.BlockSpec((1, spots, hidden), lambda expert: (expert, 0, 0))
    return pl.pallas_call(
        experts_kernel,
        grid=(experts,),
        in_specs=[whole, whole, table, table, matrices],
        out_specs=[whole, whole, wide, wide, narrow, narrow, narrow],
        out_shape=[
            *[jax.ShapeDtypeStruct((total, width), jnp.bfloat16)] * 2,
            *[jax.ShapeDtypeStruct((experts, spots, width), jnp.bfloat16)] * 2,
            *[jax.ShapeDtypeStruct((experts, spots, hidden), jnp.bfloat16)] * 3,
        ],
        scratch_shapes=[
            pltpu.VMEM((total, width), jnp.float32),
            pltpu.VMEM((total, width), jnp.float32),
            pltpu.VMEM((sequences, slots, length), jnp.bfloat16),
            pltpu.VMEM((spots, width), jnp.bfloat16),
            pltpu.VMEM((spots, width), jnp.bfloat16),
        ],
        compiler_params=pltpu.CompilerParams(vmem_limit_bytes=63 * MIB),
        cost_estimate=pl.CostEstimate(
            flops=experts * (12 * spots * width * hidden + 8 * spots * length * width),
            bytes_accessed=2 * weights.size + 16 * tokens.size,
            transcendentals=experts * spots * hidden,
        ),
        name="experts",
    )(tokens, cotangents, place, gates, weights)


def expert_grads_kernel(
    received_ref, grad_returned_ref, act_ref, grad_gate_ref, grad_up_ref, grad_weights_ref
):
    received, grad_returned = received_ref[0], grad_returned_ref[0]
    grad_weights_ref[0, 0] = matmul_tn(received, grad_gate_ref[0]).astype(jnp.bfloat16)
    grad_weights_ref[0, 1] = matmul_tn(received, grad_up_ref[0]).astype(jnp.bfloat16)
    grad_weights_ref[0, 2] = matmul_tn(grad_returned, act_ref[0]).astype(jnp.bfloat16)


def expert_grads(received, grad_returned, act, grad_gate, grad_up):
    experts, spots, width = received.shape
    hidden = act.shape[-1]
    wide = pl.BlockSpec((1, spots, width), lambda expert: (expert, 0, 0))
    narrow = pl.BlockSpec((1, spots, hidden), lambda expert: (expert, 0, 0))
    return pl.pallas_call(
        expert_grads_kernel,
        grid=(experts,),
        in_specs=[wide, wide, narrow, narrow, narrow],
        out_specs=pl.BlockSpec((1, 3, width, hidden), lambda expert: (expert, 0, 0, 0)),
        out_shape=jax.ShapeDtypeStruct((experts, 3, width, hidden), jnp.bfloat16),
        compiler_params=pltpu.CompilerParams(vmem_limit_bytes=48 * MIB),
        name="expert_grads",
    )(received, grad_returned, act, grad_gate, grad_up)


def grouped_experts(tokens, cotangents, place, gates, weights, capacity):
    experts, sequences, length = place.shape
    group = min(4, sequences)
    routed, grad_tokens, saved = [], [], []
    for first in range(0, sequences, group):
        rows = slice(first * length, (first + group) * length)
        part = slice(first, first + group)
        routed_part, grad_part, *kept = run_experts(
            tokens[rows], cotangents[rows], place[:, part], gates[:, part], weights, capacity
        )
        routed.append(routed_part)
        grad_tokens.append(grad_part)
        saved.append(kept)

    def joined(parts):
        return parts[0] if len(parts) == 1 else jnp.concatenate(parts, 0)

    return joined(routed), joined(grad_tokens), saved


def flipped(index, bit):
    unit = 2**bit
    return index + unit * (1 - 2 * ((index // unit) % 2))


class Links:
    def __init__(self, semaphores):
        self.semaphores = semaphores
        self.taken = 0
        self.dp = lax.axis_index("dp")
        self.z = lax.axis_index("expert")
        self.upper = self.z // 2
        self.position = self.z * (1 - 2 * self.upper) + 3 * self.upper
        self.step = 1 - 2 * self.upper
        self.core = (flipped(self.dp, 0), self.z)
        self.along_x = (flipped(self.dp, 1), self.z)
        self.along_y = (flipped(self.dp, 2), self.z)
        self.inward = (self.dp, self.z + self.step)
        self.outward = (self.dp, self.z - self.step)
        self.further = (self.dp, self.z + 2 * self.step)
        self.pending = []

    def order(self, index):
        near = (self.position + index) % 2 if index < 2 else index
        return near * self.step + 3 * self.upper

    def take(self, count=1):
        first = self.taken
        self.taken += count
        return first

    def barrier(self):
        barrier = pltpu.get_barrier_semaphore()
        for device in (self.core, self.along_x, self.along_y, self.inward, self.further):
            pl.semaphore_signal(barrier, inc=1, device_id=device, device_id_type=MESH)

        @pl.when(self.position == 1)
        def _():
            pl.semaphore_signal(barrier, inc=1, device_id=self.outward, device_id_type=MESH)

        pl.semaphore_wait(barrier, 5 + self.position)

    def copy_with(self, source, target, send, receive, device):
        return pltpu.make_async_remote_copy(
            src_ref=source,
            dst_ref=target,
            send_sem=send,
            recv_sem=receive,
            device_id=device,
            device_id_type=MESH,
        )

    def copy(self, source, target, send, receive, device):
        return self.copy_with(
            source, target, self.semaphores.at[send], self.semaphores.at[receive], device
        )

    def send(self, source, target, receive, device, position=None):
        copy = self.copy(source, target, self.take(), receive, device)
        if position is None:
            copy.start()
        else:
            pl.when(self.position == position)(copy.start)
        self.pending.append((copy, position))

    def arrived(self, region, receive):
        self.copy(region, region, receive, receive, self.core).wait_recv()

    def finish(self):
        for copy, position in self.pending:
            if position is None:
                copy.wait_send()
            else:
                pl.when(self.position == position)(copy.wait_send)


class LineGather:
    def __init__(self, links, region, own=None):
        self.links, self.region = links, region
        self.receives = links.take(4)
        self.own = region(links.z) if own is None else own

    def start(self):
        links = self.links
        target, receive = self.region(links.z), self.receives + links.z
        links.send(self.own, target, receive, links.further)
        links.send(self.own, target, receive, links.inward)
        links.send(self.own, target, receive, links.outward, 1)

    def relay(self):
        links = self.links
        source = links.order(3)
        block = self.region(source)

        @pl.when(links.position == 1)
        def _():
            links.arrived(block, self.receives + source)

        links.send(block, block, self.receives + source, links.outward, 1)

    def arrive(self, index):
        links = self.links
        source = links.order(index)

        def wait():
            links.arrived(self.region(source), self.receives + source)

        if index < 3:
            wait()
        else:
            pl.when(links.position == 0)(wait)


class PlaneGather:
    def __init__(self, links, region, parity, own=None):
        self.links, self.region, self.parity = links, region, parity
        self.receives = links.take(7)
        self.own = region(links.dp) if own is None else own

    def start(self):
        links, first = self.links, self.receives
        target = self.region(links.dp)
        links.send(self.own, target, first, links.along_x)
        links.send(self.own, target, first + 1, links.along_y)
        links.send(self.own, target, first + 2, links.core)

    def forward(self):
        links, first = self.links, self.receives
        across = self.region(flipped(links.dp, 1))
        links.arrived(across, first)
        if self.parity == 0:
            links.send(across, across, first + 3, links.along_y)
        links.send(across, across, first + 4, links.core)
        along = self.region(flipped(links.dp, 2))
        links.arrived(along, first + 1)
        if self.parity == 1:
            links.send(along, along, first + 3, links.along_x)
        links.send(along, along, first + 5, links.core)

    def last(self):
        links, first = self.links, self.receives
        corner = self.region(flipped(flipped(links.dp, 1), 2))
        links.arrived(corner, first + 3)
        links.send(corner, corner, first + 6, links.core)

    def complete(self):
        links, first = self.links, self.receives
        other = flipped(links.dp, 0)
        links.arrived(self.region(other), first + 2)
        links.arrived(self.region(flipped(other, 1)), first + 4)
        links.arrived(self.region(flipped(other, 2)), first + 5)
        links.arrived(self.region(flipped(flipped(other, 1), 2)), first + 6)


ANY = pl.BlockSpec(memory_space=pl.ANY)


def front_kernel(
    stripe_ref,
    gates_ref,
    masters_ref,
    hidden_ref,
    cotangent_ref,
    dense_ref,
    weights_ref,
    cotangents_ref,
    tokens_ref,
    routed_parts_ref,
    grad_parts_ref,
    received_ref,
    grad_returned_ref,
    act_ref,
    grad_gate_ref,
    grad_up_ref,
    normed_attend_ref,
    projected_ref,
    attended_ref,
    residual_ref,
    scale_ref,
    normed_mixer_ref,
    shared_act_ref,
    grad_shared_pre_ref,
    grad_shared_ref,
    base_ref,
    gains_ref,
    matrices,
    extra,
    all_gates,
    places,
    my_gates,
    chosen,
    slot_gates,
    forward_slots,
    backward_slots,
    narrow,
    masters,
    rounded,
    semaphores,
    shard_out,
    shard_in,
    local,
    load_sems,
    expert_sems,
):
    links = Links(semaphores)
    stripe, columns = stripe_ref.shape
    length, width = hidden_ref.shape
    panels, rows, hidden = masters_ref.shape
    experts = panels // 3
    slots = chosen.shape[1] // experts
    first_panels = 8
    middle = first_panels * hidden + extra.shape[1]
    halves = ((0, middle), (middle, columns - middle))
    query_width = HEADS * HD
    kv_width = KVH * HD
    ahead = 4

    def dense_region(dp, z, half):
        first, count = halves[half]
        row = pl.multiple_of((dp * 4 + z) * stripe, stripe)
        return dense_ref.at[pl.ds(row, stripe), pl.ds(first, count)]

    def own(half):
        first, count = halves[half]
        return stripe_ref.at[:, pl.ds(first, count)]

    def sequence(ref, z):
        return ref.at[pl.ds(pl.multiple_of(z * length, length), length), :]

    def shard_region(dp, panel):
        return weights_ref.at[panel, pl.ds(pl.multiple_of(dp * rows, rows), rows), :]

    lines = [
        LineGather(links, functools.partial(dense_region, links.dp, half=half), own(half))
        for half in range(2)
    ]
    cotangents = LineGather(links, functools.partial(sequence, cotangents_ref), cotangent_ref)
    tokens = LineGather(links, functools.partial(sequence, tokens_ref), normed_mixer_ref)
    gates = LineGather(links, lambda z: all_gates.at[z], gates_ref)
    planes = [
        [
            PlaneGather(
                links,
                functools.partial(dense_region, z=links.order(index), half=half),
                index % 2,
                own(half) if index == 0 else None,
            )
            for index in range(4)
        ]
        for half in range(2)
    ]

    def shard_copy(kind, panel, source_dp, device):
        block = shard_region(source_dp, panel)
        return links.copy_with(
            block, block, shard_out.at[kind, panel], shard_in.at[kind, panel], device
        )

    dp = links.dp
    dp_core, dp_x, dp_y = flipped(dp, 0), flipped(dp, 1), flipped(dp, 2)
    dp_corner = flipped(dp_x, 2)

    def hop(kind, panel):
        source, device = (
            (dp, links.along_x),
            (dp, links.along_y),
            (dp, links.core),
            None,
            (dp_x, links.core),
            (dp_y, links.core),
            (dp_corner, links.core),
        )[kind]
        return shard_copy(kind, panel, source, device)

    def corner_copy(panel, parity):
        if parity == 0:
            return shard_copy(3, panel, dp_x, links.along_y)
        return shard_copy(3, panel, dp_y, links.along_x)

    def shard_arrived(kind, panel, source_dp):
        shard_copy(kind, panel, source_dp, links.core).wait_recv()

    def shard_start(panel):
        for kind in range(3):
            hop(kind, panel).start()

    def shard_forward(panel):
        shard_arrived(0, panel, dp_x)
        pl.when(panel % 2 == 0)(corner_copy(panel, 0).start)
        hop(4, panel).start()
        shard_arrived(1, panel, dp_y)
        pl.when(panel % 2 == 1)(corner_copy(panel, 1).start)
        hop(5, panel).start()

    def shard_last(panel):
        shard_arrived(3, panel, dp_corner)
        hop(6, panel).start()

    def shard_complete(panel):
        shard_arrived(2, panel, dp_core)
        shard_arrived(4, panel, flipped(dp_core, 1))
        shard_arrived(5, panel, flipped(dp_core, 2))
        shard_arrived(6, panel, flipped(flipped(dp_core, 1), 2))

    def shard_finish(panel):
        for kind in (0, 1, 2, 4, 5, 6):
            hop(kind, panel).wait_send()
        corner_copy(panel, 0).wait_send()

    def exchange(panel):
        shard_forward(panel)
        if panel + ahead < panels:
            shard_start(panel + ahead)
        if panel >= 2:
            shard_last(panel - 2)

    local_copies = [
        pltpu.make_async_copy(source, target, local.at[index])
        for index, (source, target) in enumerate(
            (
                (
                    stripe_ref,
                    dense_ref.at[
                        pl.ds(pl.multiple_of((links.dp * 4 + links.z) * stripe, stripe), stripe), :
                    ],
                ),
                (gates_ref, all_gates.at[links.z]),
                (cotangent_ref, sequence(cotangents_ref, links.z)),
            )
        )
    ]
    token_copy = pltpu.make_async_copy(
        normed_mixer_ref, sequence(tokens_ref, links.z), local.at[3]
    )

    def dense_column(panel):
        return panel * hidden + (0 if panel < first_panels else extra.shape[1])

    loads = [
        pltpu.make_async_copy(
            dense_ref.at[:, pl.ds(dense_column(panel), hidden)],
            matrices.at[panel],
            load_sems.at[panel],
        )
        for panel in range(14)
    ]
    extra_load = pltpu.make_async_copy(
        dense_ref.at[:, pl.ds(first_panels * hidden, extra.shape[1])], extra, load_sems.at[14]
    )

    def master_load(panel):
        return pltpu.make_async_copy(
            masters_ref.at[panel], masters.at[panel % 2], expert_sems.at[0, panel % 2]
        )

    def master_store(panel):
        return pltpu.make_async_copy(
            rounded.at[panel % 2], shard_region(dp, panel), expert_sems.at[1, panel % 2]
        )

    master_load(0).start()
    links.barrier()
    lines[0].start()
    planes[0][0].start()
    lines[1].start()
    gates.start()
    for copy in local_copies:
        copy.start()

    def round_masters(first, last):
        @pl.loop(first, last)
        def _(panel):
            master_load(panel).wait()

            @pl.when(panel + 1 < panels)
            def _():
                master_load(panel + 1).start()

            @pl.when(panel >= 2)
            def _():
                master_store(panel - 2).wait()

            rounded[panel % 2] = masters[panel % 2].astype(jnp.bfloat16)
            master_store(panel).start()

    lines[0].arrive(1)
    planes[0][1].start()
    lines[0].arrive(2)
    planes[0][2].start()
    round_masters(0, panels // 2)
    planes[0][0].forward()
    lines[0].relay()
    lines[0].arrive(3)
    planes[0][3].start()
    planes[0][1].forward()
    lines[1].relay()
    round_masters(panels // 2, panels)
    for panel in (panels - 2, panels - 1):
        master_store(panel).wait()
    planes[1][0].start()
    planes[0][2].forward()
    lines[1].arrive(1)
    planes[1][1].start()
    planes[0][3].forward()
    cotangents.start()
    gates.relay()
    lines[1].arrive(2)
    planes[1][2].start()
    for plane in planes[0]:
        plane.last()
    planes[1][0].forward()
    for plane in planes[0]:
        plane.complete()
    local_copies[0].wait()
    extra_load.start()
    for copy in loads[:first_panels]:
        copy.start()

    rows_step = 32

    def norm_rows(source, gain, scale_out, target):
        @pl.loop(0, length // rows_step)
        def _(index):
            part = pl.ds(index * rows_step, rows_step)
            values = source[part, :].astype(jnp.float32)
            scale = lax.rsqrt(jnp.mean(values * values, axis=-1, keepdims=True) + 1e-06)
            if scale_out is not None:
                scale_out[part, :] = scale
            target[part, :] = (values * scale * gains_ref[gain : gain + 1, :]).astype(jnp.bfloat16)

    def project():
        extra_load.wait()
        gains_ref[...] = extra[...].astype(jnp.float32).T[:8, :]
        norm_rows(hidden_ref, 0, None, normed_attend_ref)
        for panel in range(5):
            loads[panel].wait()
            projected_ref[:, panel * hidden : (panel + 1) * hidden] = matmul(
                normed_attend_ref[...], matrices[panel]
            ).astype(jnp.bfloat16)

    def attend(group):
        key_rows = projected_ref[:, query_width + group * HD : query_width + (group + 1) * HD]
        value_first = query_width + kv_width + group * HD
        value_rows = projected_ref[:, value_first : value_first + HD]
        row = lax.broadcasted_iota(jnp.int32, (length, length), 0)
        column = lax.broadcasted_iota(jnp.int32, (length, length), 1)
        per_group = HEADS // KVH
        for head in range(group * per_group, (group + 1) * per_group):
            spot = slice(head * HD, (head + 1) * HD)
            scores = matmul_nt(projected_ref[:, spot], key_rows) * HD ** (-0.5)
            scores = jnp.where(column <= row, scores, -1e30)
            raised = jnp.exp(scores - jnp.max(scores, axis=-1, keepdims=True))
            shares = (raised / jnp.sum(raised, axis=-1, keepdims=True)).astype(jnp.bfloat16)
            attended_ref[:, spot] = matmul(shares, value_rows).astype(jnp.bfloat16)

    def join():
        for part in range(3):
            loads[5 + part].wait()
            update = matmul_nt(
                attended_ref[:, part * hidden : (part + 1) * hidden], matrices[5 + part]
            )
            if part == 0:
                residual_ref[...] = hidden_ref[...].astype(jnp.float32) + update
            else:
                residual_ref[...] += update
        norm_rows(residual_ref, 1, scale_ref, normed_mixer_ref)
        tokens.start()
        token_copy.start()

    def shared(part):
        spot = slice(part * hidden, (part + 1) * hidden)
        for panel in (8, 10, 12):
            loads[panel + part].wait()
        gate = matmul(normed_mixer_ref[...], matrices[8 + part])
        up = matmul(normed_mixer_ref[...], matrices[10 + part])
        sig = jax.nn.sigmoid(gate)
        gate_act = gate * sig
        shared_act_ref[:, spot] = (gate_act * up).astype(jnp.bfloat16)
        grad_act = matmul(cotangent_ref[...], matrices[12 + part])
        grad_shared_pre_ref[:, spot] = (
            grad_act * up * sig * (1.0 + gate * (1.0 - sig))
        ).astype(jnp.bfloat16)
        up_spot = slice((2 + part) * hidden, (3 + part) * hidden)
        grad_shared_pre_ref[:, up_spot] = (grad_act * gate_act).astype(jnp.bfloat16)

    def shared_back(part):
        spot = slice(part * hidden, (part + 1) * hidden)
        up_spot = slice((2 + part) * hidden, (3 + part) * hidden)
        grad = matmul_nt(grad_shared_pre_ref[:, spot], matrices[8 + part]) + matmul_nt(
            grad_shared_pre_ref[:, up_spot], matrices[10 + part]
        )
        out = matmul_nt(shared_act_ref[:, spot], matrices[12 + part])
        if part == 0:
            grad_shared_ref[...] = grad
            base_ref[...] = residual_ref[...] + out
        else:
            grad_shared_ref[...] += grad
            base_ref[...] += out

    def place_slots():
        local_copies[1].wait()
        before = (
            lax.broadcasted_iota(jnp.int32, (length, length), 0)
            < lax.broadcasted_iota(jnp.int32, (length, length), 1)
        )
        earlier_mask = jnp.where(before, 1.0, 0.0).astype(jnp.bfloat16)
        for source in range(4):
            gate = all_gates[source, links.z]
            hot = gate > 0.0
            earlier = matmul(jnp.where(hot, 1.0, 0.0).astype(jnp.bfloat16), earlier_mask)
            place = jnp.where(hot, earlier, -1.0).astype(jnp.int32)
            for expert in range(experts):
                places[expert, source : source + 1, :] = place[expert : expert + 1, :]
                my_gates[expert, source : source + 1, :] = gate[expert : expert + 1, :]

    project()
    lines[1].arrive(3)
    planes[1][3].start()
    planes[1][1].forward()
    attend(0)
    attend(1)
    planes[1][2].forward()
    for panel in range(2):
        shard_start(panel)
    attend(2)
    attend(3)
    planes[1][3].forward()
    cotangents.relay()
    join()
    for panel in range(2, ahead):
        shard_start(panel)
    for plane in planes[1]:
        plane.last()
    for index in range(1, 4):
        gates.arrive(index)
    place_slots()
    for plane in planes[1]:
        plane.complete()
    for copy in loads[first_panels:]:
        copy.start()
    exchange(0)
    shared(0)
    exchange(1)
    shared(1)
    exchange(2)
    shared_back(0)
    exchange(3)
    shared_back(1)
    exchange(4)
    tokens.relay()
    for panel in range(5, 11):
        exchange(panel)
    for index in range(1, 4):
        cotangents.arrive(index)
        tokens.arrive(index)
    local_copies[2].wait()
    token_copy.wait()
    token_loads = [
        pltpu.make_async_copy(
            source.at[:, pl.ds(part * hidden, hidden)],
            matrices.at[first + part, pl.ds(0, 4 * length)],
            load_sems.at[first + part],
        )
        for first, source in ((6, tokens_ref), (9, cotangents_ref))
        for part in range(3)
    ]
    for copy in token_loads:
        copy.start()
    slot_iota = lax.broadcasted_iota(jnp.int32, (slots, length), 0)
    for source in range(4):
        for expert in range(experts):
            hot = slot_iota == places[expert, source : source + 1, :]
            chosen[source, expert * slots : (expert + 1) * slots, :] = jnp.where(
                hot, 1.0, 0.0
            ).astype(jnp.bfloat16)
            slot_gates[expert, source * slots : (source + 1) * slots, :] = jnp.sum(
                jnp.where(hot, my_gates[expert, source : source + 1, :], 0.0),
                axis=1,
                keepdims=True,
            )
    exchange(11)
    for copy in token_loads:
        copy.wait()

    @pl.loop(0, 4)
    def _(source):
        part = pl.ds(source * length, length)
        spots = pl.ds(pl.multiple_of(source * slots, slots), slots)
        for block in range(3):
            spot = pl.ds(block * hidden, hidden)
            token_slots = matmul(chosen[source], matrices[6 + block, part, :])
            grad_slots = matmul(chosen[source], matrices[9 + block, part, :])
            for expert in range(experts):
                rows_of = slice(expert * slots, (expert + 1) * slots)
                forward_slots[expert, spots, spot] = token_slots[rows_of].astype(jnp.bfloat16)
                backward_slots[expert, spots, spot] = (
                    grad_slots[rows_of] * slot_gates[expert, spots, :]
                ).astype(jnp.bfloat16)

    def slot_stores(expert):
        return [
            pltpu.make_async_copy(
                source.at[expert], target.at[expert], expert_sems.at[2 + index, expert]
            )
            for index, (source, target) in enumerate(
                ((forward_slots, received_ref), (backward_slots, grad_returned_ref))
            )
        ]

    def narrow_stores(expert):
        buffer = expert % 2
        return [
            pltpu.make_async_copy(
                narrow.at[buffer, index], target.at[expert], expert_sems.at[4 + buffer, index]
            )
            for index, target in enumerate((act_ref, grad_gate_ref, grad_up_ref))
        ]

    def weight_loads(expert):
        buffer = expert % 2
        return [
            pltpu.make_async_copy(
                weights_ref.at[3 * expert + matrix],
                matrices.at[3 * buffer + matrix],
                expert_sems.at[6 + buffer, matrix],
            )
            for matrix in range(3)
        ]

    def fetch(expert):
        for matrix, copy in enumerate(weight_loads(expert)):
            shard_complete(3 * expert + matrix)
            copy.start()

    for expert in range(experts):
        for copy in slot_stores(expert):
            copy.start()
    fetch(0)

    @pl.loop(0, experts)
    def _(expert):
        buffer = expert % 2
        loaded = weight_loads(expert)

        @pl.when(expert >= 2)
        def _():
            for copy in narrow_stores(expert - 2):
                copy.wait()

        received = forward_slots[expert]
        grad_out = backward_slots[expert]
        loaded[0].wait()
        gate_pre = matmul(received, matrices[3 * buffer])
        loaded[1].wait()
        up_pre = matmul(received, matrices[3 * buffer + 1])
        loaded[2].wait()
        grad_act = matmul(grad_out, matrices[3 * buffer + 2])
        gate_sig = jax.nn.sigmoid(gate_pre)
        gate_act = gate_pre * gate_sig
        act = (gate_act * up_pre).astype(jnp.bfloat16)
        grad_gate = (grad_act * up_pre * gate_sig * (1.0 + gate_pre * (1.0 - gate_sig))).astype(
            jnp.bfloat16
        )
        grad_up = (grad_act * gate_act).astype(jnp.bfloat16)
        narrow[buffer, 0] = act
        narrow[buffer, 1] = grad_gate
        narrow[buffer, 2] = grad_up
        for copy in narrow_stores(expert):
            copy.start()
        for copy in slot_stores(expert):
            copy.wait()
        for block in range(3):
            rows_of = pl.ds(block * hidden, hidden)
            spot = pl.ds(block * hidden, hidden)
            out = matmul_nt(act, matrices[3 * buffer + 2, rows_of, :]).astype(jnp.bfloat16)
            forward_slots[expert, :, spot] = (
                out.astype(jnp.float32) * slot_gates[expert]
            ).astype(jnp.bfloat16)
            backward_slots[expert, :, spot] = (
                matmul_nt(grad_gate, matrices[3 * buffer, rows_of, :])
                + matmul_nt(grad_up, matrices[3 * buffer + 1, rows_of, :])
            ).astype(jnp.bfloat16)

        for done, todo in enumerate(((12,), (13,), (14,), (15, 16), (17,))):

            @pl.when(expert == done)
            def _():
                for panel in todo:
                    exchange(panel)
                if done == 4:
                    shard_last(panels - 2)
                    shard_last(panels - 1)

        @pl.when(expert + 1 < experts)
        def _():
            fetch(expert + 1)

    for expert in (experts - 2, experts - 1):
        for copy in narrow_stores(expert):
            copy.wait()
    out_copies = []
    for first, values, target in ((0, backward_slots, grad_parts_ref), (3, forward_slots, routed_parts_ref)):
        for block in range(3):
            spot = slice(block * hidden, (block + 1) * hidden)
            for source in range(4):
                slots_of = jnp.concatenate(
                    [
                        values[expert, source * slots : (source + 1) * slots, spot]
                        for expert in range(experts)
                    ],
                    0,
                )
                matrices[first + block, source * length : (source + 1) * length, :] = matmul_tn(
                    chosen[source], slots_of
                ).astype(jnp.bfloat16)
            out_copies.append(
                pltpu.make_async_copy(
                    matrices.at[first + block, pl.ds(0, 4 * length)],
                    target.at[:, pl.ds(block * hidden, hidden)],
                    load_sems.at[first + block],
                )
            )
            out_copies[-1].start()
    for copy in out_copies:
        copy.wait()

    @pl.loop(0, panels)
    def _(panel):
        shard_finish(panel)

    links.finish()


def front(stripe, gates, masters, hidden_in, cotangent, slots):
    length, width = cotangent.shape
    stripe_rows, columns = stripe.shape
    panels, rows, hidden = masters.shape
    experts = panels // 3
    low, full = jnp.bfloat16, jnp.float32
    vmem = pl.BlockSpec(memory_space=pltpu.VMEM)
    query_width = HEADS * HD
    spots = 4 * slots
    return pl.pallas_call(
        front_kernel,
        in_specs=[ANY] * 3 + [vmem] * 2,
        out_specs=[ANY] * 11 + [vmem] * 11,
        out_shape=[
            jax.ShapeDtypeStruct((stripe_rows * 32, columns), low),
            jax.ShapeDtypeStruct((panels, rows * 8, hidden), low),
            *[jax.ShapeDtypeStruct((length * 4, width), low)] * 4,
            *[jax.ShapeDtypeStruct((experts, spots, width), low)] * 2,
            *[jax.ShapeDtypeStruct((experts, spots, hidden), low)] * 3,
            jax.ShapeDtypeStruct((length, width), low),
            jax.ShapeDtypeStruct((length, query_width + 2 * KVH * HD), low),
            jax.ShapeDtypeStruct((length, query_width), low),
            jax.ShapeDtypeStruct((length, width), full),
            jax.ShapeDtypeStruct((length, 1), full),
            jax.ShapeDtypeStruct((length, width), low),
            jax.ShapeDtypeStruct((length, FFS), low),
            jax.ShapeDtypeStruct((length, 2 * FFS), low),
            jax.ShapeDtypeStruct((length, width), full),
            jax.ShapeDtypeStruct((length, width), full),
            jax.ShapeDtypeStruct((8, width), full),
        ],
        scratch_shapes=[
            pltpu.VMEM((14, width, hidden), low),
            pltpu.VMEM((width, 128), low),
            pltpu.VMEM((4, 4, 8, length), full),
            pltpu.VMEM((experts, 4, length), jnp.int32),
            pltpu.VMEM((experts, 4, length), full),
            pltpu.VMEM((4, experts * slots, length), low),
            pltpu.VMEM((experts, spots, 1), full),
            pltpu.VMEM((experts, spots, width), low),
            pltpu.VMEM((experts, spots, width), low),
            pltpu.VMEM((2, 3, spots, hidden), low),
            pltpu.VMEM((2, rows, hidden), full),
            pltpu.VMEM((2, rows, hidden), low),
            pltpu.SemaphoreType.DMA((170,)),
            pltpu.SemaphoreType.DMA((7, panels)),
            pltpu.SemaphoreType.DMA((7, panels)),
            pltpu.SemaphoreType.DMA((4,)),
            pltpu.SemaphoreType.DMA((15,)),
            pltpu.SemaphoreType.DMA((8, 6)),
        ],
        compiler_params=pltpu.CompilerParams(
            collective_id=1, has_side_effects=True, vmem_limit_bytes=63 * MIB
        ),
        name="front",
    )(stripe, gates, masters, hidden_in, cotangent)


def scatter_kernel(
    grad_parts_ref,
    routed_parts_ref,
    received_ref,
    grad_returned_ref,
    act_ref,
    grad_gate_ref,
    grad_up_ref,
    dense_ref,
    normed_mixer_ref,
    cotangent_ref,
    normed_attend_ref,
    attended_ref,
    grad_shared_pre_ref,
    shared_act_ref,
    residual_ref,
    scale_ref,
    gain_ref,
    grad_shared_ref,
    projected_ref,
    hidden_ref,
    gain_attend_ref,
    expert_sum_ref,
    stripes_ref,
    routed_received_ref,
    grad_input_ref,
    grad_gain_ref,
    grad_gain_attend_ref,
    ring,
    pair_sum,
    corner_x,
    corner_y,
    side_x,
    side_y,
    staged,
    wide,
    narrow,
    left,
    right,
    out_weights,
    grad_tokens,
    grad_attended,
    grad_pair,
    grad_residual_ref,
    key_weights,
    line_out,
    line_in,
    pair_sems,
    slot_sems,
    line_sems,
    token_sems,
    load_sems,
    free,
):
    dp, z = lax.axis_index("dp"), lax.axis_index("expert")
    core, chip = dp % 2, dp // 2
    chip_x, chip_y = flipped(chip, 0), flipped(chip, 1)
    chip_corner = flipped(chip_x, 1)
    device_core = (flipped(dp, 0), z)
    device_x = (flipped(dp, 1), z)
    device_y = (flipped(dp, 2), z)
    others = [(dp, (z + turn) % 4) for turn in range(1, 4)]
    slots = pair_sum.shape[0]
    experts = received_ref.shape[0]
    expert_panels = 3 * experts
    dense_panels = right.shape[0]
    panels = expert_panels + dense_panels
    length, width = residual_ref.shape
    share, hidden = staged.shape[1:]
    half = share // 2
    stripe = share // 4
    query_width = HEADS * HD
    kv_width = KVH * HD
    block = width // 4

    def remote(source, target, send, receive, device):
        return pltpu.make_async_remote_copy(
            src_ref=source,
            dst_ref=target,
            send_sem=send,
            recv_sem=receive,
            device_id=device,
            device_id_type=MESH,
        )

    barrier = pltpu.get_barrier_semaphore()
    for device in (device_core, device_x, device_y, *others):
        pl.semaphore_signal(barrier, inc=1, device_id=device, device_id_type=MESH)
    pl.semaphore_wait(barrier, 6)

    def token_copies(source, target, first):
        return [
            remote(
                source.at[pl.ds(pl.multiple_of(device[1] * length, length), length), :],
                target.at[turn],
                token_sems.at[first + turn],
                token_sems.at[first + 3 + turn],
                device,
            )
            for turn, device in enumerate(others)
        ]

    grad_copies = token_copies(grad_parts_ref, grad_tokens, 0)
    routed_copies = token_copies(routed_parts_ref, routed_received_ref, 6)
    for copy in grad_copies:
        copy.start()

    def expert_loads(expert):
        buffer = expert % 2
        return [
            pltpu.make_async_copy(source.at[expert], target, load_sems.at[buffer, index])
            for index, (source, target) in enumerate(
                (
                    (received_ref, wide.at[buffer, 0]),
                    (grad_returned_ref, wide.at[buffer, 1]),
                    (grad_gate_ref, narrow.at[buffer, 0]),
                    (grad_up_ref, narrow.at[buffer, 1]),
                    (act_ref, narrow.at[buffer, 2]),
                )
            )
        ]

    for copy in expert_loads(0):
        copy.start()

    def columns(ref, panel):
        return ref.at[:, pl.ds(panel * hidden, hidden)]

    sources = [
        (normed_mixer_ref, left.at[0]),
        (cotangent_ref, left.at[1]),
        (normed_attend_ref, left.at[3]),
        *[(columns(grad_shared_pre_ref, panel), right.at[panel]) for panel in range(4)],
        *[(columns(shared_act_ref, panel), right.at[4 + panel]) for panel in range(2)],
        *[(columns(attended_ref, panel), right.at[6 + panel]) for panel in range(3)],
        (dense_ref.at[:, pl.ds(query_width + 2 * kv_width, query_width)], out_weights),
        (dense_ref.at[:, pl.ds(query_width, 2 * kv_width)], key_weights),
        (
            grad_parts_ref.at[pl.ds(pl.multiple_of(z * length, length), length), :],
            grad_tokens.at[3],
        ),
    ]
    dense_loads = [
        pltpu.make_async_copy(source, target, load_sems.at[2 + index // 5, index % 5])
        for index, (source, target) in enumerate(sources)
    ]
    for copy in dense_loads:
        copy.start()
    query_load = pltpu.make_async_copy(
        dense_ref.at[:, pl.ds(0, query_width)], out_weights, pair_sems.at[4]
    )

    def fill(pair, left_ref, right_value):
        for chip_index in range(4):
            part = matmul_tn(left_ref[:, chip_index * block : (chip_index + 1) * block], right_value)
            ring[pair, chip_index] = part.astype(jnp.bfloat16).reshape(2, share, hidden)

    def total(first, *more):
        result = first.astype(jnp.float32)
        for value in more:
            result = result + value.astype(jnp.float32)
        return result

    def pair_copy(panel):
        pair, slot = panel % 2, panel % slots
        return remote(
            ring.at[pair, :, 1 - core],
            pair_sum.at[slot],
            pair_sems.at[pair],
            slot_sems.at[0, slot],
            device_core,
        )

    def corner_copies(panel):
        slot = panel % slots
        return (
            remote(
                pair_sum.at[slot, chip_corner, pl.ds(0, half)],
                corner_x.at[slot],
                slot_sems.at[1, slot],
                slot_sems.at[2, slot],
                device_x,
            ),
            remote(
                pair_sum.at[slot, chip_corner, pl.ds(half, half)],
                corner_y.at[slot],
                slot_sems.at[3, slot],
                slot_sems.at[4, slot],
                device_y,
            ),
        )

    def side_copies(panel):
        slot = panel % slots
        return (
            remote(
                pair_sum.at[slot, chip_x],
                side_x.at[slot],
                slot_sems.at[5, slot],
                slot_sems.at[6, slot],
                device_x,
            ),
            remote(
                pair_sum.at[slot, chip_y],
                side_y.at[slot],
                slot_sems.at[7, slot],
                slot_sems.at[8, slot],
                device_y,
            ),
        )

    def line_copies(panel):
        return [
            remote(
                line_out.at[panel, device[1]],
                line_in.at[panel, turn],
                line_sems.at[0, panel, turn],
                line_sems.at[1, panel, turn],
                device,
            )
            for turn, device in enumerate(others)
        ]

    def staged_copy(panel):
        return pltpu.make_async_copy(
            staged.at[panel % 2], expert_sum_ref.at[panel], pair_sems.at[2 + panel % 2]
        )

    def post(panel):
        @pl.when(panel >= slots)
        def _():
            pl.semaphore_wait(free.at[0], 1)

        pair_copy(panel).start()

    def sum_pair(panel):
        pair, slot = panel % 2, panel % slots
        pair_copy(panel).wait()
        for chip_index in range(4):
            pair_sum[slot, chip_index] = total(
                pair_sum[slot, chip_index], ring[pair, chip_index, core]
            ).astype(jnp.bfloat16)

        @pl.when(panel >= slots)
        def _():
            pl.semaphore_wait(free.at[1], 1)
            pl.semaphore_wait(free.at[2], 1)

        for copy in corner_copies(panel):
            copy.start()

    def sum_corner(panel):
        slot = panel % slots
        for copy in corner_copies(panel):
            copy.wait_recv()
        pair_sum[slot, chip_y, :half] = total(
            pair_sum[slot, chip_y, :half], corner_x[slot]
        ).astype(jnp.bfloat16)
        pair_sum[slot, chip_x, half:] = total(
            pair_sum[slot, chip_x, half:], corner_y[slot]
        ).astype(jnp.bfloat16)
        for copy in side_copies(panel):
            copy.start()

    def sum_sides(panel):
        slot = panel % slots
        for copy in corner_copies(panel):
            copy.wait_send()
        for copy in side_copies(panel):
            copy.wait()
        value = total(pair_sum[slot, chip], side_x[slot], side_y[slot]).astype(jnp.bfloat16)

        @pl.when(panel < expert_panels)
        def _():
            @pl.when(panel >= 2)
            def _():
                staged_copy(panel - 2).wait()

            staged[panel % 2] = value
            staged_copy(panel).start()

        @pl.when(panel >= expert_panels)
        def _():
            index = panel - expert_panels
            line_out[index] = value.reshape(4, stripe, hidden)
            for copy in line_copies(index):
                copy.start()

        @pl.when(panel < panels - slots)
        def _():
            for index, device in enumerate((device_core, device_x, device_y)):
                pl.semaphore_signal(
                    free.at[index], inc=1, device_id=device, device_id_type=MESH
                )

    def residual_backward(part):
        if part == 0:
            for copy in dense_loads:
                copy.wait()
            for copy in grad_copies:
                copy.wait()
            for copy in routed_copies:
                copy.start()
            grad_gain_ref[...] = jnp.zeros_like(grad_gain_ref)
        rows_step = 32
        steps = length // rows_step // 2

        @pl.loop(part * steps, (part + 1) * steps)
        def _(index):
            rows = pl.ds(index * rows_step, rows_step)
            grad_normed = (
                total(
                    grad_tokens[3, rows, :],
                    grad_tokens[0, rows, :],
                    grad_tokens[1, rows, :],
                    grad_tokens[2, rows, :],
                )
                + grad_shared_ref[rows, :]
            )
            residual, scale = residual_ref[rows, :], scale_ref[rows, :]
            grad_scaled = grad_normed * gain_ref[...]
            mean = jnp.mean(grad_scaled * residual, axis=-1, keepdims=True)
            grad_residual = (
                left[1, rows, :].astype(jnp.float32)
                + scale * grad_scaled
                - residual * (scale * scale * scale) * mean
            )
            grad_residual_ref[rows, :] = grad_residual
            left[2, rows, :] = grad_residual.astype(jnp.bfloat16)
            grad_gain_ref[...] += jnp.sum(grad_normed * residual * scale, axis=0, keepdims=True)

    def attended_backward():
        grad_attended[...] = matmul(left[2], out_weights[...]).astype(jnp.bfloat16)
        query_load.start()

    def query_backward():
        query_load.wait()
        for part in range(3):
            update = matmul_nt(right[9 + part], out_weights[:, part * hidden : (part + 1) * hidden])
            if part == 0:
                grad_input_ref[...] = update
            else:
                grad_input_ref[...] += update

    def key_backward():
        for part in range(2):
            grad_input_ref[...] += matmul_nt(
                right[12 + part], key_weights[:, part * hidden : (part + 1) * hidden]
            )

    def input_backward():
        grad_gain_attend_ref[...] = jnp.zeros_like(grad_gain_attend_ref)
        rows_step = 32

        @pl.loop(0, length // rows_step)
        def _(index):
            rows = pl.ds(index * rows_step, rows_step)
            values, grad_normed = hidden_ref[rows, :].astype(jnp.float32), grad_input_ref[rows, :]
            scale = lax.rsqrt(jnp.mean(values * values, axis=-1, keepdims=True) + 1e-06)
            grad_scaled = grad_normed * gain_attend_ref[...]
            mean = jnp.mean(grad_scaled * values, axis=-1, keepdims=True)
            grad_input_ref[rows, :] = (
                grad_residual_ref[rows, :]
                + scale * grad_scaled
                - values * (scale * scale * scale) * mean
            )
            grad_gain_attend_ref[...] += jnp.sum(
                grad_normed * values * scale, axis=0, keepdims=True
            )

    def attention_backward(head):
        score_scale = HD ** (-0.5)
        per_group = HEADS // KVH
        heads_wide = hidden // HD
        group = head // per_group
        key_rows = projected_ref[:, query_width + group * HD : query_width + (group + 1) * HD]
        value_first = query_width + kv_width + group * HD
        value_rows = projected_ref[:, value_first : value_first + HD]
        row = lax.broadcasted_iota(jnp.int32, (length, length), 0)
        column = lax.broadcasted_iota(jnp.int32, (length, length), 1)
        spot = slice(head * HD, (head + 1) * HD)
        query, grad_out = projected_ref[:, spot], grad_attended[:, spot]
        scores = jnp.where(column <= row, matmul_nt(query, key_rows) * score_scale, -1e30)
        raised = jnp.exp(scores - jnp.max(scores, axis=-1, keepdims=True))
        weights = raised / jnp.sum(raised, axis=-1, keepdims=True)
        grad_weights = matmul_nt(grad_out, value_rows)
        inner = jnp.sum(weights * grad_weights, axis=-1, keepdims=True)
        grad_scores = (weights * (grad_weights - inner)).astype(jnp.bfloat16)
        grad_query = matmul(grad_scores, key_rows) * score_scale
        place = slice(head % heads_wide * HD, (head % heads_wide + 1) * HD)
        right[9 + head // heads_wide, :, place] = grad_query.astype(jnp.bfloat16)
        grad_key = matmul_tn(grad_scores, query)
        grad_value = matmul_tn(weights.astype(jnp.bfloat16), grad_out)
        if head % per_group > 0:
            grad_key = grad_key + grad_pair[0]
            grad_value = grad_value + grad_pair[1]
        if head % per_group < per_group - 1:
            grad_pair[0] = grad_key
            grad_pair[1] = grad_value
        else:
            place = slice(group * HD, (group + 1) * HD)
            right[12, :, place] = (grad_key * score_scale).astype(jnp.bfloat16)
            right[13, :, place] = grad_value.astype(jnp.bfloat16)

    @pl.loop(0, panels + 5)
    def _(step):
        @pl.when(step < expert_panels)
        def _():
            expert, matrix = step // 3, step % 3

            @pl.when(matrix == 0)
            def _():
                for copy in expert_loads(expert):
                    copy.wait()

                @pl.when(expert + 1 < experts)
                def _():
                    for copy in expert_loads(expert + 1):
                        copy.start()

            fill(step % 2, wide.at[expert % 2, matrix // 2], narrow[expert % 2, matrix])

        backward = [
            *[functools.partial(residual_backward, part) for part in range(2)],
            attended_backward,
            *[functools.partial(attention_backward, head) for head in range(HEADS)],
            query_backward,
            key_backward,
            input_backward,
        ]
        for index, call in enumerate(backward):
            pl.when(step == GRAD_STEP + index)(call)

        @pl.when((step >= expert_panels) & (step < panels))
        def _():
            panel = step - expert_panels
            which = jnp.where(panel < 4, 0, jnp.where(panel < 6, 1, jnp.where(panel < 9, 2, 3)))
            fill(step % 2, left.at[which], right[panel])

        @pl.when(step < panels)
        def _():
            post(step)

        @pl.when((step >= 1) & (step < panels + 1))
        def _():
            sum_pair(step - 1)

        @pl.when((step >= 3) & (step < panels + 3))
        def _():
            sum_corner(step - 3)

        @pl.when(step >= 5)
        def _():
            sum_sides(step - 5)

    for panel in (expert_panels - 2, expert_panels - 1):
        staged_copy(panel).wait()

    @pl.loop(0, dense_panels)
    def _(panel):
        for copy in line_copies(panel):
            copy.wait()
        stripes_ref[panel] = total(
            line_out[panel, z], line_in[panel, 0], line_in[panel, 1], line_in[panel, 2]
        )

    for copy in routed_copies:
        copy.wait()


def scatter_grads(
    grad_parts,
    routed_parts,
    saved,
    dense_all,
    normed_mixer,
    cotangent,
    normed_attend,
    attended,
    grad_shared_pre,
    shared_act,
    residual,
    scale,
    gain,
    grad_shared,
    projected,
    hidden_in,
    gain_attend,
):
    experts, spots, width = saved[0].shape
    hidden = saved[2].shape[-1]
    length = residual.shape[0]
    share = width // 8
    stripe = share // 4
    dense_panels = 14
    low = jnp.bfloat16
    vmem = pl.BlockSpec(memory_space=pltpu.VMEM)
    return pl.pallas_call(
        scatter_kernel,
        in_specs=[ANY] * 14 + [vmem] * 7,
        out_specs=[ANY, vmem, ANY, vmem, vmem, vmem],
        out_shape=[
            jax.ShapeDtypeStruct((3 * experts, share, hidden), low),
            jax.ShapeDtypeStruct((dense_panels, stripe, hidden), jnp.float32),
            jax.ShapeDtypeStruct((3, length, width), low),
            jax.ShapeDtypeStruct((length, width), jnp.float32),
            jax.ShapeDtypeStruct((1, width), jnp.float32),
            jax.ShapeDtypeStruct((1, width), jnp.float32),
        ],
        scratch_shapes=[
            pltpu.VMEM((2, 4, 2, share, hidden), low),
            pltpu.VMEM((SLOTS, 4, share, hidden), low),
            pltpu.VMEM((SLOTS, share // 2, hidden), low),
            pltpu.VMEM((SLOTS, share // 2, hidden), low),
            pltpu.VMEM((SLOTS, share, hidden), low),
            pltpu.VMEM((SLOTS, share, hidden), low),
            pltpu.VMEM((2, share, hidden), low),
            pltpu.VMEM((2, 2, spots, width), low),
            pltpu.VMEM((2, 3, spots, hidden), low),
            pltpu.VMEM((4, length, width), low),
            pltpu.VMEM((dense_panels, length, hidden), low),
            pltpu.VMEM((width, HEADS * HD), low),
            pltpu.VMEM((4, length, width), low),
            pltpu.VMEM((length, HEADS * HD), low),
            pltpu.VMEM((2, length, HD), jnp.float32),
            pltpu.VMEM((length, width), jnp.float32),
            pltpu.VMEM((width, 2 * KVH * HD), low),
            pltpu.VMEM((dense_panels, 4, stripe, hidden), low),
            pltpu.VMEM((dense_panels, 3, stripe, hidden), low),
            pltpu.SemaphoreType.DMA((5,)),
            pltpu.SemaphoreType.DMA((9, SLOTS)),
            pltpu.SemaphoreType.DMA((2, dense_panels, 3)),
            pltpu.SemaphoreType.DMA((12,)),
            pltpu.SemaphoreType.DMA((5, 5)),
            pltpu.SemaphoreType.REGULAR((3,)),
        ],
        compiler_params=pltpu.CompilerParams(
            collective_id=3, has_side_effects=True, vmem_limit_bytes=62 * MIB
        ),
        name="scatter_grads",
    )(
        grad_parts,
        routed_parts,
        *saved,
        dense_all,
        normed_mixer,
        cotangent,
        normed_attend,
        attended,
        grad_shared_pre,
        shared_act,
        residual,
        scale,
        gain,
        grad_shared,
        projected,
        hidden_in,
        gain_attend,
    )


def muon_kernel(
    expert_ref,
    dense_ref,
    expert_out_ref,
    dense_out_ref,
    dense_back,
    moments,
    units,
    orthogonal,
    current,
    low,
    identity,
    line_sems,
    out_sems,
    in_sems,
    back_out_sems,
    back_in_sems,
    load_sems,
):
    dp, z = lax.axis_index("dp"), lax.axis_index("expert")
    count, share, _ = moments.shape
    first, dense_count = 10, 4
    stripe = dense_ref.shape[1]
    others = [(dp, (z + turn) % 4) for turn in range(1, 4)]
    peers = [((dp + turn) % 8, z) for turn in range(1, 8)]

    def remote(source, target, send, receive, device):
        return pltpu.make_async_remote_copy(
            src_ref=source,
            dst_ref=target,
            send_sem=send,
            recv_sem=receive,
            device_id=device,
            device_id_type=MESH,
        )

    def share_of(index):
        return pl.ds(pl.multiple_of(index * share, share), share)

    def stripe_of(index):
        return pl.ds(pl.multiple_of(index * stripe, stripe), stripe)

    barrier = pltpu.get_barrier_semaphore()
    for device in (*others, *peers):
        pl.semaphore_signal(barrier, inc=1, device_id=device, device_id_type=MESH)
    dense_rows = pl.ds(first, dense_count)
    loads = [
        pltpu.make_async_copy(
            expert_ref.at[pl.ds(0, first)], moments.at[pl.ds(0, first)], load_sems.at[0]
        ),
        pltpu.make_async_copy(
            expert_ref.at[pl.ds(first, count - first - dense_count)],
            moments.at[pl.ds(first + dense_count, count - first - dense_count)],
            load_sems.at[1],
        ),
        pltpu.make_async_copy(
            dense_ref.at[pl.ds(z * dense_count, dense_count)],
            moments.at[dense_rows, stripe_of(z)],
            load_sems.at[2],
        ),
    ]
    for copy in loads:
        copy.start()
    pl.semaphore_wait(barrier, len(others) + len(peers))
    line_copies = [
        remote(
            dense_ref.at[pl.ds(device[1] * dense_count, dense_count)],
            moments.at[dense_rows, stripe_of(z)],
            line_sems.at[0, turn],
            line_sems.at[1, turn],
            device,
        )
        for turn, device in enumerate(others)
    ]
    line_back = [
        remote(
            dense_back.at[:, stripe_of(device[1])],
            dense_out_ref.at[pl.ds(z * dense_count, dense_count)],
            line_sems.at[2, turn],
            line_sems.at[3, turn],
            device,
        )
        for turn, device in enumerate(others)
    ]
    own_back = pltpu.make_async_copy(
        dense_back.at[:, stripe_of(z)],
        dense_out_ref.at[pl.ds(z * dense_count, dense_count)],
        load_sems.at[2],
    )

    def out_copy(slot, turn):
        owner = peers[turn][0]
        return remote(
            moments.at[8 * slot + owner],
            units.at[slot, share_of(dp)],
            out_sems.at[slot, turn],
            in_sems.at[slot],
            peers[turn],
        )

    def own_copy(slot):
        return pltpu.make_async_copy(
            moments.at[8 * slot + dp], units.at[slot, share_of(dp)], load_sems.at[3 + slot]
        )

    def is_dense(slot, owner):
        unit = 8 * slot + owner
        return (unit >= first) & (unit < first + dense_count)

    def expert_place(slot, owner):
        unit = 8 * slot + owner
        return expert_out_ref.at[jnp.where(unit < first, unit, unit - dense_count)]

    def dense_place(slot, owner):
        return dense_back.at[8 * slot + owner - first]

    def back_copy(place, slot, turn):
        return remote(
            orthogonal.at[slot, share_of(peers[turn][0])],
            place(slot, dp),
            back_out_sems.at[slot, turn],
            back_in_sems.at[slot, dp],
            peers[turn],
        )

    def own_back_copy(place, slot):
        return pltpu.make_async_copy(
            orthogonal.at[slot, share_of(dp)], place(slot, dp), load_sems.at[3 + slot]
        )

    def send_back(place, slot):
        for turn in range(7):
            back_copy(place, slot, turn).start()
        own_back_copy(place, slot).start()

    def exists(slot, owner):
        return 8 * slot + owner < count

    def send_slot(slot):
        for turn in range(7):
            pl.when(exists(slot, peers[turn][0]))(out_copy(slot, turn).start)
        pl.when(exists(slot, dp))(own_copy(slot).start)

    for copy in line_copies:
        copy.start()
    loads[0].wait()
    send_slot(0)
    loads[1].wait()
    loads[2].wait()
    for copy in line_copies:
        copy.wait()
    send_slot(1)
    send_slot(2)

    @pl.loop(0, 3)
    def _(slot):
        @pl.when(exists(slot, dp))
        def _():
            own_copy(slot).wait()
            arrived = units.at[slot, pl.ds(0, 7 * share)]
            remote(arrived, arrived, in_sems.at[slot], in_sems.at[slot], peers[0]).wait_recv()
            newton_schulz_unit(units.at[slot], orthogonal.at[slot], current, low, identity)

            @pl.when(is_dense(slot, dp))
            def _():
                send_back(dense_place, slot)

            @pl.when(jnp.logical_not(is_dense(slot, dp)))
            def _():
                send_back(expert_place, slot)

    def own_back_wait(slot):
        def wait():
            pltpu.make_async_copy(
                orthogonal.at[slot, share_of(dp)], expert_out_ref.at[0], load_sems.at[3 + slot]
            ).wait()

        return wait

    def wait_back(slot):
        for turn in range(7):
            owner = peers[turn][0]

            @pl.when(exists(slot, owner))
            def _():
                block = expert_out_ref.at[0]
                semaphore = back_in_sems.at[slot, owner]
                remote(block, block, semaphore, semaphore, peers[0]).wait_recv()

        pl.when(exists(slot, dp))(own_back_wait(slot))

    wait_back(1)
    for copy in line_back:
        copy.start()
    own_back.start()
    wait_back(0)
    wait_back(2)
    for slot in range(3):
        for turn in range(7):
            pl.when(exists(slot, peers[turn][0]))(out_copy(slot, turn).wait_send)

        @pl.when(exists(slot, dp))
        def _():
            for turn in range(7):
                back_copy(expert_place, slot, turn).wait_send()

    for copy in line_back:
        copy.wait()
    own_back.wait()


def muon(expert_units, dense_units):
    experts, share, columns = expert_units.shape
    panels, stripe, _ = dense_units.shape
    count = experts + panels // 4
    low = jnp.bfloat16
    return pl.pallas_call(
        muon_kernel,
        in_specs=[ANY] * 2,
        out_specs=[ANY] * 2,
        out_shape=[
            jax.ShapeDtypeStruct(expert_units.shape, low),
            jax.ShapeDtypeStruct(dense_units.shape, low),
        ],
        scratch_shapes=[
            pltpu.VMEM((panels // 4, share, columns), low),
            pltpu.VMEM((count, share, columns), low),
            pltpu.VMEM((3, 8 * share, columns), low),
            pltpu.VMEM((3, 8 * share, columns), low),
            pltpu.VMEM((columns, 8 * share), jnp.float32),
            pltpu.VMEM((columns, 8 * share), low),
            pltpu.VMEM((columns, columns), low),
            pltpu.SemaphoreType.DMA((4, 3)),
            pltpu.SemaphoreType.DMA((3, 7)),
            pltpu.SemaphoreType.DMA((3,)),
            pltpu.SemaphoreType.DMA((3, 7)),
            pltpu.SemaphoreType.DMA((3, 8)),
            pltpu.SemaphoreType.DMA((6,)),
        ],
        compiler_params=pltpu.CompilerParams(
            collective_id=4, has_side_effects=True, vmem_limit_bytes=56 * MIB
        ),
        name="muon",
    )(expert_units, dense_units)


def update_kernel(weights_ref, orthogonal_ref, new_ref):
    keep_factor = 1.0 - LEARN_RATE * WEIGHT_DECAY
    new_ref[...] = keep_factor * weights_ref[...] - LEARN_RATE * orthogonal_ref[...].astype(
        jnp.float32
    )


def updated_weights(weights, orthogonal):
    panels, rows, columns = orthogonal.shape
    group = 3
    block = pl.BlockSpec((group, rows, columns), lambda index: (index, 0, 0))
    return pl.pallas_call(
        update_kernel,
        grid=(panels // group,),
        in_specs=[block, block],
        out_specs=block,
        out_shape=jax.ShapeDtypeStruct(orthogonal.shape, jnp.float32),
        name="update",
    )(weights.reshape(orthogonal.shape), orthogonal).reshape(weights.shape)


def on_device(
    hidden_in,
    cotangent,
    routes,
    route_weights,
    dense_weights,
    dense_momentum,
    expert_weights,
    expert_momentum,
    norm_gains,
    gain_first,
    gain_second,
):
    length, width = hidden_in.shape
    topk_count = routes.shape[1]
    local_experts = expert_weights.shape[0]
    expert_size = lax.axis_size("expert")
    dp_size = lax.axis_size("dp")
    expert_count = local_experts * expert_size
    capacity = 5 * length * topk_count // (4 * expert_count)
    block_rows = min(512, length)
    query_width = HEADS * HD
    kv_width = KVH * HD
    qkv_end = query_width + 2 * kv_width
    shared_base = 2 * query_width + 2 * kv_width
    gate_table = jnp.sum(
        jnp.where(
            routes.T[None, :, :] == jnp.arange(expert_count, dtype=jnp.int32)[:, None, None],
            route_weights.T[None, :, :],
            0.0,
        ),
        axis=1,
    )
    direct = dp_size == 8 and expert_size == 4
    inputs = hidden_in.astype(jnp.float32)
    scale_attend = norm_scale(inputs)
    if direct:
        stripe_rows = dense_weights.shape[0]
        extra = jnp.zeros((stripe_rows, 128 - norm_gains.shape[0]), jnp.float32)
        plane_gates = gate_table.reshape(expert_size, local_experts, length)
        (
            dense_all,
            _,
            _,
            _,
            routed_parts,
            grad_parts,
            *saved,
            normed_attend,
            projected,
            attended,
            residual,
            scale_mixer,
            normed_mixer,
            shared_act,
            grad_shared_pre,
            grad_shared,
            base_out,
            gains_all,
        ) = front(
            jnp.concatenate(
                [
                    dense_weights[:, :shared_base],
                    norm_gains.T,
                    extra,
                    dense_weights[:, shared_base:],
                ],
                1,
            ).astype(jnp.bfloat16),
            jnp.pad(plane_gates, ((0, 0), (0, 8 - local_experts), (0, 0))),
            expert_weights.reshape(-1, *expert_weights.shape[2:]),
            hidden_in,
            cotangent,
            -(-capacity // 16) * 16,
        )
        gain_attend, gain_mixer = gains_all[0], gains_all[1]
    else:
        gate_tables = lax.all_gather(gate_table, "expert", axis=0, tiled=False)
        cotangents = lax.all_gather(cotangent, "expert", axis=0, tiled=True)
        dense_all, gains_all = (
            lax.all_gather(
                dense_weights.astype(jnp.bfloat16), ("dp", "expert"), axis=0, tiled=True
            ),
            lax.all_gather(norm_gains.astype(jnp.bfloat16), ("dp", "expert"), axis=1, tiled=True),
        )
        gain_attend = gains_all[0].astype(jnp.float32)
        gain_mixer = gains_all[1].astype(jnp.float32)
        normed_attend = (inputs * scale_attend * gain_attend).astype(jnp.bfloat16)
        projected = jnp.dot(
            normed_attend, dense_all[:, :qkv_end], preferred_element_type=jnp.float32
        ).astype(jnp.bfloat16)
        query = projected[:, :query_width]
        key_rows = projected[:, query_width : query_width + kv_width]
        value_rows = projected[:, query_width + kv_width :]
        attended, saved_stats = attend_forward(query, key_rows, value_rows, block_rows)
        residual = inputs + jnp.einsum(
            "sq,dq->sd", attended, dense_all[:, qkv_end:shared_base], preferred_element_type=jnp.float32
        )
        scale_mixer = norm_scale(residual)
        normed_mixer = (residual * scale_mixer * gain_mixer).astype(jnp.bfloat16)
        expert_all = lax.all_gather(expert_weights.astype(jnp.bfloat16), "dp", axis=2, tiled=True)
        tokens = lax.all_gather(normed_mixer, "expert", axis=0, tiled=True)
        shared_pre = jnp.dot(
            normed_mixer,
            dense_all[:, shared_base : shared_base + 2 * FFS],
            preferred_element_type=jnp.float32,
        )
        shared_gate = shared_pre[:, :FFS]
        shared_up = shared_pre[:, FFS:]
        shared_act = (jax.nn.silu(shared_gate) * shared_up).astype(jnp.bfloat16)
        shared_out = jnp.einsum(
            "sf,df->sd",
            shared_act,
            dense_all[:, shared_base + 2 * FFS : shared_base + 3 * FFS],
            preferred_element_type=jnp.float32,
        )
        grad_shared_act = jnp.dot(
            cotangent,
            dense_all[:, shared_base + 2 * FFS : shared_base + 3 * FFS],
            preferred_element_type=jnp.float32,
        )
        shared_sig = jax.nn.sigmoid(shared_gate)
        grad_shared_pre = jnp.concatenate(
            [
                grad_shared_act * shared_up * shared_sig * (1.0 + shared_gate * (1.0 - shared_sig)),
                grad_shared_act * jax.nn.silu(shared_gate),
            ],
            1,
        ).astype(jnp.bfloat16)
        grad_shared = jnp.einsum(
            "sf,df->sd",
            grad_shared_pre,
            dense_all[:, shared_base : shared_base + 2 * FFS],
            preferred_element_type=jnp.float32,
        )
        base_out = residual + shared_out
        my_gates = lax.dynamic_slice_in_dim(
            gate_tables, lax.axis_index("expert") * local_experts, local_experts, 1
        ).transpose(1, 0, 2)
        hot = my_gates > 0.0
        earlier = jnp.einsum(
            "est,ut->esu",
            hot.astype(jnp.bfloat16),
            jnp.tril(jnp.ones((length, length), jnp.bfloat16), -1),
            preferred_element_type=jnp.float32,
        ).astype(jnp.int32)
        place = jnp.where(hot, earlier, -1)
        routed_parts, grad_parts, saved = grouped_experts(
            tokens, cotangents, place, my_gates, expert_all, capacity
        )
    if direct:
        (
            expert_sum,
            dense_sum,
            routed_received,
            grad_inputs,
            grad_gain_mixer,
            grad_gain_attend,
        ) = scatter_grads(
            grad_parts,
            routed_parts,
            saved,
            dense_all,
            normed_mixer,
            cotangent,
            normed_attend,
            attended,
            grad_shared_pre,
            shared_act,
            residual,
            scale_mixer,
            gain_mixer[None, :],
            grad_shared,
            projected,
            hidden_in,
            gain_attend[None, :],
        )
        routed = lax.dynamic_slice_in_dim(
            routed_parts, lax.axis_index("expert") * length, length, 0
        ).astype(jnp.float32)
        routed = routed + jnp.sum(routed_received.astype(jnp.float32), axis=0)
        expert_grad = expert_sum.reshape(expert_weights.shape).astype(jnp.float32)
        dense_grad = (
            jnp.concatenate([dense_sum[9:], dense_sum[6:9], dense_sum[:6]], 0)
            .transpose(1, 0, 2)
            .reshape(dense_weights.shape)
        )
        grad_gain_mixer, grad_gain_attend = grad_gain_mixer[0], grad_gain_attend[0]
    else:
        routed = lax.psum_scatter(routed_parts, "expert", scatter_dimension=0, tiled=True)
        grad_routed = lax.psum_scatter(grad_parts, "expert", scatter_dimension=0, tiled=True)
        expert_parts = [expert_grads(*kept) for kept in saved]
        expert_grad = lax.psum_scatter(
            sum(part.astype(jnp.float32) for part in expert_parts).astype(jnp.bfloat16),
            "dp",
            scatter_dimension=2,
            tiled=True,
        ).astype(jnp.float32)
        grad_normed = grad_routed.astype(jnp.float32) + grad_shared
        grad_scaled = grad_normed * gain_mixer
        grad_residual = (
            cotangent.astype(jnp.float32)
            + scale_mixer * grad_scaled
            - residual * scale_mixer**3 * jnp.mean(grad_scaled * residual, axis=-1, keepdims=True)
        )
        grad_gain_mixer = jnp.sum(grad_normed * residual * scale_mixer, axis=0)
        grad_attn_low = grad_residual.astype(jnp.bfloat16)
        grad_attended = jnp.dot(
            grad_attn_low, dense_all[:, qkv_end:shared_base], preferred_element_type=jnp.float32
        ).astype(jnp.bfloat16)
        grad_query, grad_key, grad_value = attend_backward(
            query, key_rows, value_rows, grad_attended, saved_stats, block_rows
        )
        grad_projected = jnp.concatenate([grad_query, grad_key, grad_value], 1)
        dense_parts = [
            jnp.einsum("sd,sf->df", left, right, preferred_element_type=jnp.float32)
            for left, right in (
                (normed_attend, grad_projected),
                (grad_attn_low, attended),
                (normed_mixer, grad_shared_pre),
                (cotangent, shared_act),
            )
        ]
        dense_grad = lax.psum_scatter(
            jnp.concatenate([part.astype(jnp.bfloat16) for part in dense_parts], 1),
            ("dp", "expert"),
            scatter_dimension=0,
            tiled=True,
        ).astype(jnp.float32)
        grad_normed_attend = jnp.einsum(
            "sc,dc->sd", grad_projected, dense_all[:, :qkv_end], preferred_element_type=jnp.float32
        )
        grad_scaled_attend = grad_normed_attend * gain_attend
        grad_inputs = (
            grad_residual
            + scale_attend * grad_scaled_attend
            - inputs * scale_attend**3 * jnp.mean(grad_scaled_attend * inputs, axis=-1, keepdims=True)
        )
        grad_gain_attend = jnp.sum(grad_normed_attend * inputs * scale_attend, axis=0)
    block_out = (base_out + routed.astype(jnp.float32)).astype(jnp.bfloat16)
    gain_grad = lax.psum_scatter(
        jnp.stack([grad_gain_attend, grad_gain_mixer], 0),
        ("dp", "expert"),
        scatter_dimension=1,
        tiled=True,
    )
    dense_moment = MOMENTUM_DECAY * dense_momentum + dense_grad
    expert_moment = MOMENTUM_DECAY * expert_momentum + expert_grad
    stripe, dense_columns = dense_weights.shape
    row_count = stripe * expert_size
    dense_total = dense_columns // FFE
    dense_share = -(-dense_total // expert_size)
    dense_padded = jnp.pad(
        dense_moment.astype(jnp.bfloat16),
        ((0, 0), (0, dense_share * expert_size * FFE - dense_columns)),
    ).reshape(stripe, dense_share * expert_size, FFE).transpose(1, 0, 2)
    expert_units = expert_moment.astype(jnp.bfloat16).reshape(-1, row_count, FFE)
    if direct:
        orth_expert, orth_stripe = muon(expert_units, dense_padded)
    else:
        dense_units = lax.all_to_all(
            dense_padded, "expert", split_axis=0, concat_axis=1, tiled=True
        )
        expert_unit_count = expert_units.shape[0]
        base_count = expert_unit_count + dense_share
        unit_count = -(-base_count // dp_size) * dp_size
        all_units = jnp.concatenate(
            [
                expert_units,
                dense_units,
                jnp.zeros((unit_count - base_count, row_count, FFE), jnp.bfloat16),
            ],
            0,
        )
        owned = lax.all_to_all(all_units, "dp", split_axis=0, concat_axis=1, tiled=True)
        orthogonal = newton_schulz(owned)
        orth_units = lax.all_to_all(orthogonal, "dp", split_axis=1, concat_axis=0, tiled=True)
        orth_expert = orth_units[:expert_unit_count]
        orth_stripe = lax.all_to_all(
            orth_units[expert_unit_count:base_count],
            "expert",
            split_axis=1,
            concat_axis=0,
            tiled=True,
        )
    orth_stripe = (
        orth_stripe[:dense_total]
        .transpose(1, 0, 2)
        .reshape(stripe, dense_columns)
        .astype(jnp.float32)
    )
    keep_factor = 1.0 - LEARN_RATE * WEIGHT_DECAY
    dense_new = keep_factor * dense_weights - LEARN_RATE * orth_stripe
    expert_new = updated_weights(expert_weights, orth_expert)
    first_new = FIRST_DECAY * gain_first + (1.0 - FIRST_DECAY) * gain_grad
    second_new = SECOND_DECAY * gain_second + (1.0 - SECOND_DECAY) * gain_grad * gain_grad
    step_ratio = (
        first_new
        / (1.0 - FIRST_DECAY**STEP)
        / (jnp.sqrt(second_new / (1.0 - SECOND_DECAY**STEP)) + 1e-08)
    )
    gain_new = norm_gains - GAIN_RATE * step_ratio
    return (
        block_out,
        grad_inputs,
        dense_grad,
        dense_moment,
        dense_new,
        expert_grad,
        expert_moment,
        expert_new,
        gain_grad,
        first_new,
        second_new,
        gain_new,
    )


def solution(mesh):
    in_specs = (
        P(("dp", "expert"), None),
        P(("dp", "expert"), None),
        P(("dp", "expert"), None),
        P(("dp", "expert"), None),
        P(("dp", "expert"), None),
        P(("dp", "expert"), None),
        P("expert", None, "dp", None),
        P("expert", None, "dp", None),
        P(None, ("dp", "expert")),
        P(None, ("dp", "expert")),
        P(None, ("dp", "expert")),
    )
    out_specs = (
        P(("dp", "expert"), None),
        P(("dp", "expert"), None),
        P(("dp", "expert"), None),
        P(("dp", "expert"), None),
        P(("dp", "expert"), None),
        P("expert", None, "dp", None),
        P("expert", None, "dp", None),
        P("expert", None, "dp", None),
        P(None, ("dp", "expert")),
        P(None, ("dp", "expert")),
        P(None, ("dp", "expert")),
        P(None, ("dp", "expert")),
    )
    return jax.shard_map(
        on_device, mesh=mesh, in_specs=in_specs, out_specs=out_specs, check_vma=False
    )
```

```python
import functools

import jax
import jax.numpy as jnp
from jax import lax
from jax.experimental import pallas as pl
from jax.experimental.pallas import tpu as pltpu
from jax.sharding import PartitionSpec as P

HEADS = 12
HD = 128
KVH = 4
FFE = 512
FFS = 1024
NS_STEPS = 5
STEP = 10


POLY_FIRST = 3.4445
POLY_SECOND = -4.775
POLY_THIRD = 2.0315
MOMENTUM_DECAY = 0.95
LEARN_RATE = 0.6
WEIGHT_DECAY = 0.1
GAIN_RATE = 0.8
FIRST_DECAY = 0.9
SECOND_DECAY = 0.95


def norm_scale(values):
    return lax.rsqrt(jnp.mean(values * values, axis=-1, keepdims=True) + 1e-06)


def block_scores(query_block, key_block, first_row, block_rows, last_row):
    score_scale = HD ** (-0.5)
    scores = (
        jnp.einsum("qgrd,kgd->grqk", query_block, key_block, preferred_element_type=jnp.float32)
        * score_scale
    )
    allowed = jnp.arange(last_row)[None, :] <= (first_row + jnp.arange(block_rows))[:, None]
    return jnp.where(allowed, scores, -1e30)


def attend_forward(query, key_rows, value_rows, block_rows):
    length = query.shape[0]
    query_heads = query.reshape(length, KVH, HEADS // KVH, HD)
    key_heads = key_rows.reshape(length, KVH, HD)
    value_heads = value_rows.reshape(length, KVH, HD)
    scores = block_scores(query_heads, key_heads, 0, block_rows, block_rows)
    highest = jnp.max(scores, axis=-1, keepdims=True)
    raised = jnp.exp(scores - highest)
    totals = jnp.sum(raised, axis=-1, keepdims=True)
    weights = (raised / totals).astype(jnp.bfloat16)
    outputs = jnp.einsum("grqk,kgd->qgrd", weights, value_heads, preferred_element_type=jnp.float32)
    saved_stats = [(highest, totals)]
    attended = outputs.reshape(length, HEADS * HD)
    return (attended.astype(jnp.bfloat16), saved_stats)


def attend_backward(query, key_rows, value_rows, grad_attended, saved_stats, block_rows):
    length = query.shape[0]
    score_scale = HD ** (-0.5)
    query_heads = query.reshape(length, KVH, HEADS // KVH, HD)
    grad_heads = grad_attended.reshape(length, KVH, HEADS // KVH, HD)
    key_heads = key_rows.reshape(length, KVH, HD)
    value_heads = value_rows.reshape(length, KVH, HD)
    grad_key = jnp.zeros((length, KVH, HD), jnp.float32)
    grad_value = jnp.zeros((length, KVH, HD), jnp.float32)
    query_parts = []
    for block_index, first_row in enumerate(range(0, length, block_rows)):
        last_row = first_row + block_rows
        scores = block_scores(query_heads, key_heads, first_row, block_rows, last_row)
        highest, totals = saved_stats[block_index]
        weights = jnp.exp(scores - highest) / totals
        grad_weights = jnp.einsum(
            "qgrd,kgd->grqk", grad_heads, value_heads, preferred_element_type=jnp.float32
        )
        inner_sum = jnp.sum(weights * grad_weights, axis=-1, keepdims=True)
        grad_scores = (weights * (grad_weights - inner_sum)).astype(jnp.bfloat16)
        query_parts.append(
            jnp.einsum("grqk,kgd->qgrd", grad_scores, key_heads, preferred_element_type=jnp.float32)
            * score_scale
        )
        grad_key = grad_key.at[:last_row].add(
            jnp.einsum(
                "grqk,qgrd->kgd", grad_scores, query_heads, preferred_element_type=jnp.float32
            )
            * score_scale
        )
        grad_value = grad_value.at[:last_row].add(
            jnp.einsum(
                "grqk,qgrd->kgd",
                weights.astype(jnp.bfloat16),
                grad_heads,
                preferred_element_type=jnp.float32,
            )
        )
    grad_query = query_parts[0].reshape(length, HEADS * HD)
    return (
        grad_query.astype(jnp.bfloat16),
        grad_key.reshape(length, KVH * HD).astype(jnp.bfloat16),
        grad_value.reshape(length, KVH * HD).astype(jnp.bfloat16),
    )


MIB = 2**20
GRAD_STEP = 14
SLOTS = 8
MESH = pl.DeviceIdType.MESH


def matmul(left, right):
    return jnp.dot(left, right, preferred_element_type=jnp.float32)


def matmul_nt(left, right):
    return lax.dot_general(left, right, (((1,), (1,)), ((), ())), preferred_element_type=jnp.float32)


def matmul_tn(left, right):
    return lax.dot_general(left, right, (((0,), (0,)), ((), ())), preferred_element_type=jnp.float32)


def newton_schulz_unit(moment_ref, orthogonal_ref, current, low, identity):
    columns, rows = current.shape
    step = 256
    parts = [pl.ds(index * step, step) for index in range(rows // step)]
    identity[...] = jnp.where(
        lax.broadcasted_iota(jnp.int32, identity.shape, 0)
        == lax.broadcasted_iota(jnp.int32, identity.shape, 1),
        1.0,
        0.0,
    ).astype(jnp.bfloat16)
    squares = jnp.zeros((1, columns), jnp.float32)
    for part in parts:
        values = moment_ref[part, :].astype(jnp.float32)
        squares = squares + jnp.sum(values * values, axis=0, keepdims=True)
    scale = 1.0 / (jnp.sqrt(jnp.sum(squares, axis=1, keepdims=True)) + 1e-07)
    for part in parts:
        scaled = matmul_nt(identity[...], moment_ref[part, :]) * scale
        current[:, part] = scaled
        low[:, part] = scaled.astype(jnp.bfloat16)

    def polynomial():
        gram = matmul_nt(low[...], low[...])
        gram_low = gram.astype(jnp.bfloat16)
        return (POLY_SECOND * gram + POLY_THIRD * matmul(gram_low, gram_low)).astype(jnp.bfloat16)

    @pl.loop(0, NS_STEPS - 1)
    def _(index):
        weights = polynomial()
        for part in parts:
            updated = POLY_FIRST * current[:, part] + matmul(weights, low[:, part])
            current[:, part] = updated
            low[:, part] = updated.astype(jnp.bfloat16)

    weights = polynomial()
    for part in parts:
        updated = POLY_FIRST * current[:, part] + matmul(weights, low[:, part])
        orthogonal_ref[part, :] = updated.T.astype(jnp.bfloat16)


def newton_schulz_kernel(moment_ref, orthogonal_ref, current, low, identity):
    newton_schulz_unit(moment_ref.at[0], orthogonal_ref.at[0], current, low, identity)


def newton_schulz(units):
    count, rows, columns = units.shape
    return pl.pallas_call(
        newton_schulz_kernel,
        grid=(count,),
        in_specs=[pl.BlockSpec((1, rows, columns), lambda unit: (unit, 0, 0))],
        out_specs=pl.BlockSpec((1, rows, columns), lambda unit: (unit, 0, 0)),
        out_shape=jax.ShapeDtypeStruct(units.shape, jnp.bfloat16),
        scratch_shapes=[
            pltpu.VMEM((columns, rows), jnp.float32),
            pltpu.VMEM((columns, rows), jnp.bfloat16),
            pltpu.VMEM((columns, columns), jnp.bfloat16),
        ],
        compiler_params=pltpu.CompilerParams(vmem_limit_bytes=48 * MIB),
        cost_estimate=pl.CostEstimate(
            flops=count * NS_STEPS * 2 * columns * columns * (2 * rows + columns),
            bytes_accessed=count * rows * columns * 4,
            transcendentals=0,
        ),
        name="newton_schulz",
    )(units)


def experts_kernel(
    tokens_ref,
    cotangent_ref,
    place_ref,
    gate_ref,
    weights_ref,
    routed_ref,
    grad_tokens_ref,
    received,
    grad_returned,
    act_ref,
    grad_gate_ref,
    grad_up_ref,
    routed_sum,
    grad_sum,
    chosen,
    weighted,
    grad_received,
):
    expert = pl.program_id(0)
    sequences, slots, length = chosen.shape

    @pl.when(expert == 0)
    def _():
        routed_sum[...] = jnp.zeros_like(routed_sum)
        grad_sum[...] = jnp.zeros_like(grad_sum)

    slot_weights = []
    for sequence in range(sequences):
        rows = pl.ds(sequence * length, length)
        spots = pl.ds(sequence * slots, slots)
        place = place_ref[0, sequence : sequence + 1, :]
        gate = gate_ref[0, sequence : sequence + 1, :]
        hot = lax.broadcasted_iota(jnp.int32, (slots, length), 0) == place
        slot_weight = jnp.sum(jnp.where(hot, gate, 0.0), axis=1, keepdims=True)
        slot_weights.append(slot_weight)
        hot_low = jnp.where(hot, 1.0, 0.0).astype(jnp.bfloat16)
        chosen[sequence] = hot_low
        received[0, spots, :] = matmul(hot_low, tokens_ref[rows, :]).astype(jnp.bfloat16)
        grad_returned[0, spots, :] = (
            matmul(hot_low, cotangent_ref[rows, :]) * slot_weight
        ).astype(jnp.bfloat16)
    tokens = received[0]
    grad_out = grad_returned[0]
    gate_pre = matmul(tokens, weights_ref[0, 0])
    up_pre = matmul(tokens, weights_ref[0, 1])
    gate_sig = jax.nn.sigmoid(gate_pre)
    gate_act = gate_pre * gate_sig
    act = (gate_act * up_pre).astype(jnp.bfloat16)
    act_ref[0] = act
    out = matmul_nt(act, weights_ref[0, 2]).astype(jnp.bfloat16).astype(jnp.float32)
    for sequence in range(sequences):
        spots = slice(sequence * slots, (sequence + 1) * slots)
        weighted[spots, :] = (out[spots] * slot_weights[sequence]).astype(jnp.bfloat16)
    grad_act = matmul(grad_out, weights_ref[0, 2])
    grad_gate = (grad_act * up_pre * gate_sig * (1.0 + gate_pre * (1.0 - gate_sig))).astype(
        jnp.bfloat16
    )
    grad_up = (grad_act * gate_act).astype(jnp.bfloat16)
    grad_gate_ref[0] = grad_gate
    grad_up_ref[0] = grad_up
    grad_received[...] = (
        matmul_nt(grad_gate, weights_ref[0, 0]) + matmul_nt(grad_up, weights_ref[0, 1])
    ).astype(jnp.bfloat16)
    for sequence in range(sequences):
        rows = pl.ds(sequence * length, length)
        spots = pl.ds(sequence * slots, slots)
        routed_sum[rows, :] += matmul_tn(chosen[sequence], weighted[spots, :])
        grad_sum[rows, :] += matmul_tn(chosen[sequence], grad_received[spots, :])

    @pl.when(expert == pl.num_programs(0) - 1)
    def _():
        routed_ref[...] = routed_sum[...].astype(jnp.bfloat16)
        grad_tokens_ref[...] = grad_sum[...].astype(jnp.bfloat16)


def run_experts(tokens, cotangents, place, gates, weights, capacity):
    experts, sequences, length = place.shape
    total, width = tokens.shape
    hidden = weights.shape[-1]
    slots = -(-capacity // 16) * 16
    spots = sequences * slots
    whole = pl.BlockSpec((total, width), lambda expert: (0, 0))
    table = pl.BlockSpec((1, sequences, length), lambda expert: (expert, 0, 0))
    matrices = pl.BlockSpec((1, 3, width, hidden), lambda expert: (expert, 0, 0, 0))
    wide = pl.BlockSpec((1, spots, width), lambda expert: (expert, 0, 0))
    narrow = pl.BlockSpec((1, spots, hidden), lambda expert: (expert, 0, 0))
    return pl.pallas_call(
        experts_kernel,
        grid=(experts,),
        in_specs=[whole, whole, table, table, matrices],
        out_specs=[whole, whole, wide, wide, narrow, narrow, narrow],
        out_shape=[
            *[jax.ShapeDtypeStruct((total, width), jnp.bfloat16)] * 2,
            *[jax.ShapeDtypeStruct((experts, spots, width), jnp.bfloat16)] * 2,
            *[jax.ShapeDtypeStruct((experts, spots, hidden), jnp.bfloat16)] * 3,
        ],
        scratch_shapes=[
            pltpu.VMEM((total, width), jnp.float32),
            pltpu.VMEM((total, width), jnp.float32),
            pltpu.VMEM((sequences, slots, length), jnp.bfloat16),
            pltpu.VMEM((spots, width), jnp.bfloat16),
            pltpu.VMEM((spots, width), jnp.bfloat16),
        ],
        compiler_params=pltpu.CompilerParams(vmem_limit_bytes=63 * MIB),
        cost_estimate=pl.CostEstimate(
            flops=experts * (12 * spots * width * hidden + 8 * spots * length * width),
            bytes_accessed=2 * weights.size + 16 * tokens.size,
            transcendentals=experts * spots * hidden,
        ),
        name="experts",
    )(tokens, cotangents, place, gates, weights)


def expert_grads_kernel(
    received_ref, grad_returned_ref, act_ref, grad_gate_ref, grad_up_ref, grad_weights_ref
):
    received, grad_returned = received_ref[0], grad_returned_ref[0]
    grad_weights_ref[0, 0] = matmul_tn(received, grad_gate_ref[0]).astype(jnp.bfloat16)
    grad_weights_ref[0, 1] = matmul_tn(received, grad_up_ref[0]).astype(jnp.bfloat16)
    grad_weights_ref[0, 2] = matmul_tn(grad_returned, act_ref[0]).astype(jnp.bfloat16)


def expert_grads(received, grad_returned, act, grad_gate, grad_up):
    experts, spots, width = received.shape
    hidden = act.shape[-1]
    wide = pl.BlockSpec((1, spots, width), lambda expert: (expert, 0, 0))
    narrow = pl.BlockSpec((1, spots, hidden), lambda expert: (expert, 0, 0))
    return pl.pallas_call(
        expert_grads_kernel,
        grid=(experts,),
        in_specs=[wide, wide, narrow, narrow, narrow],
        out_specs=pl.BlockSpec((1, 3, width, hidden), lambda expert: (expert, 0, 0, 0)),
        out_shape=jax.ShapeDtypeStruct((experts, 3, width, hidden), jnp.bfloat16),
        compiler_params=pltpu.CompilerParams(vmem_limit_bytes=48 * MIB),
        name="expert_grads",
    )(received, grad_returned, act, grad_gate, grad_up)


def grouped_experts(tokens, cotangents, place, gates, weights, capacity):
    experts, sequences, length = place.shape
    group = min(4, sequences)
    routed, grad_tokens, saved = [], [], []
    for first in range(0, sequences, group):
        rows = slice(first * length, (first + group) * length)
        part = slice(first, first + group)
        routed_part, grad_part, *kept = run_experts(
            tokens[rows], cotangents[rows], place[:, part], gates[:, part], weights, capacity
        )
        routed.append(routed_part)
        grad_tokens.append(grad_part)
        saved.append(kept)

    def joined(parts):
        return parts[0] if len(parts) == 1 else jnp.concatenate(parts, 0)

    return joined(routed), joined(grad_tokens), saved


def flipped(index, bit):
    unit = 2**bit
    return index + unit * (1 - 2 * ((index // unit) % 2))


class Links:
    def __init__(self, semaphores):
        self.semaphores = semaphores
        self.taken = 0
        self.dp = lax.axis_index("dp")
        self.z = lax.axis_index("expert")
        self.upper = self.z // 2
        self.position = self.z * (1 - 2 * self.upper) + 3 * self.upper
        self.step = 1 - 2 * self.upper
        self.core = (flipped(self.dp, 0), self.z)
        self.along_x = (flipped(self.dp, 1), self.z)
        self.along_y = (flipped(self.dp, 2), self.z)
        self.inward = (self.dp, self.z + self.step)
        self.outward = (self.dp, self.z - self.step)
        self.further = (self.dp, self.z + 2 * self.step)
        self.pending = []

    def order(self, index):
        near = (self.position + index) % 2 if index < 2 else index
        return near * self.step + 3 * self.upper

    def take(self, count=1):
        first = self.taken
        self.taken += count
        return first

    def barrier(self):
        barrier = pltpu.get_barrier_semaphore()
        for device in (self.core, self.along_x, self.along_y, self.inward, self.further):
            pl.semaphore_signal(barrier, inc=1, device_id=device, device_id_type=MESH)

        @pl.when(self.position == 1)
        def _():
            pl.semaphore_signal(barrier, inc=1, device_id=self.outward, device_id_type=MESH)

        pl.semaphore_wait(barrier, 5 + self.position)

    def copy_with(self, source, target, send, receive, device):
        return pltpu.make_async_remote_copy(
            src_ref=source,
            dst_ref=target,
            send_sem=send,
            recv_sem=receive,
            device_id=device,
            device_id_type=MESH,
        )

    def copy(self, source, target, send, receive, device):
        return self.copy_with(
            source, target, self.semaphores.at[send], self.semaphores.at[receive], device
        )

    def send(self, source, target, receive, device, position=None):
        copy = self.copy(source, target, self.take(), receive, device)
        if position is None:
            copy.start()
        else:
            pl.when(self.position == position)(copy.start)
        self.pending.append((copy, position))

    def arrived(self, region, receive):
        self.copy(region, region, receive, receive, self.core).wait_recv()

    def finish(self):
        for copy, position in self.pending:
            if position is None:
                copy.wait_send()
            else:
                pl.when(self.position == position)(copy.wait_send)


class LineGather:
    def __init__(self, links, region, own=None):
        self.links, self.region = links, region
        self.receives = links.take(4)
        self.own = region(links.z) if own is None else own

    def start(self):
        links = self.links
        target, receive = self.region(links.z), self.receives + links.z
        links.send(self.own, target, receive, links.further)
        links.send(self.own, target, receive, links.inward)
        links.send(self.own, target, receive, links.outward, 1)

    def relay(self):
        links = self.links
        source = links.order(3)
        block = self.region(source)

        @pl.when(links.position == 1)
        def _():
            links.arrived(block, self.receives + source)

        links.send(block, block, self.receives + source, links.outward, 1)

    def arrive(self, index):
        links = self.links
        source = links.order(index)

        def wait():
            links.arrived(self.region(source), self.receives + source)

        if index < 3:
            wait()
        else:
            pl.when(links.position == 0)(wait)


class PlaneGather:
    def __init__(self, links, region, parity, own=None):
        self.links, self.region, self.parity = links, region, parity
        self.receives = links.take(7)
        self.own = region(links.dp) if own is None else own

    def start(self):
        links, first = self.links, self.receives
        target = self.region(links.dp)
        links.send(self.own, target, first, links.along_x)
        links.send(self.own, target, first + 1, links.along_y)
        links.send(self.own, target, first + 2, links.core)

    def forward(self):
        links, first = self.links, self.receives
        across = self.region(flipped(links.dp, 1))
        links.arrived(across, first)
        if self.parity == 0:
            links.send(across, across, first + 3, links.along_y)
        links.send(across, across, first + 4, links.core)
        along = self.region(flipped(links.dp, 2))
        links.arrived(along, first + 1)
        if self.parity == 1:
            links.send(along, along, first + 3, links.along_x)
        links.send(along, along, first + 5, links.core)

    def last(self):
        links, first = self.links, self.receives
        corner = self.region(flipped(flipped(links.dp, 1), 2))
        links.arrived(corner, first + 3)
        links.send(corner, corner, first + 6, links.core)

    def complete(self):
        links, first = self.links, self.receives
        other = flipped(links.dp, 0)
        links.arrived(self.region(other), first + 2)
        links.arrived(self.region(flipped(other, 1)), first + 4)
        links.arrived(self.region(flipped(other, 2)), first + 5)
        links.arrived(self.region(flipped(flipped(other, 1), 2)), first + 6)


ANY = pl.BlockSpec(memory_space=pl.ANY)


def front_kernel(
    stripe_ref,
    gates_ref,
    masters_ref,
    hidden_ref,
    cotangent_ref,
    dense_ref,
    weights_ref,
    cotangents_ref,
    tokens_ref,
    routed_parts_ref,
    grad_parts_ref,
    received_ref,
    grad_returned_ref,
    act_ref,
    grad_gate_ref,
    grad_up_ref,
    normed_attend_ref,
    projected_ref,
    attended_ref,
    residual_ref,
    scale_ref,
    normed_mixer_ref,
    shared_act_ref,
    grad_shared_pre_ref,
    grad_shared_ref,
    base_ref,
    gains_ref,
    shared_sum_ref,
    matrices,
    extra,
    all_gates,
    places,
    my_gates,
    chosen,
    forward_slots,
    backward_slots,
    narrow,
    pair_sum,
    corner_x,
    corner_y,
    side_x,
    side_y,
    semaphores,
    shard_out,
    shard_in,
    local,
    load_sems,
    expert_sems,
    shared_sems,
):
    links = Links(semaphores)
    stripe, columns = stripe_ref.shape
    length, width = hidden_ref.shape
    panels, rows, hidden = masters_ref.shape
    experts = panels // 3
    slots = chosen.shape[1] // experts
    first_panels = 8
    middle = first_panels * hidden + extra.shape[1]
    halves = ((0, middle), (middle, columns - middle))
    query_width = HEADS * HD
    kv_width = KVH * HD
    ahead = 4

    def dense_region(dp, z, half):
        first, count = halves[half]
        row = pl.multiple_of((dp * 4 + z) * stripe, stripe)
        return dense_ref.at[pl.ds(row, stripe), pl.ds(first, count)]

    def own(half):
        first, count = halves[half]
        return stripe_ref.at[:, pl.ds(first, count)]

    def sequence(ref, z):
        return ref.at[pl.ds(pl.multiple_of(z * length, length), length), :]

    def shard_region(dp, panel):
        return weights_ref.at[panel, pl.ds(pl.multiple_of(dp * rows, rows), rows), :]

    lines = [
        LineGather(links, functools.partial(dense_region, links.dp, half=half), own(half))
        for half in range(2)
    ]
    cotangents = LineGather(links, functools.partial(sequence, cotangents_ref), cotangent_ref)
    tokens = LineGather(links, functools.partial(sequence, tokens_ref), normed_mixer_ref)
    gates = LineGather(links, lambda z: all_gates.at[z], gates_ref)
    planes = [
        [
            PlaneGather(
                links,
                functools.partial(dense_region, z=links.order(index), half=half),
                index % 2,
                own(half) if index == 0 else None,
            )
            for index in range(4)
        ]
        for half in range(2)
    ]

    def shard_copy(kind, panel, source_dp, device):
        block = shard_region(source_dp, panel)
        return links.copy_with(
            block, block, shard_out.at[kind, panel], shard_in.at[kind, panel], device
        )

    dp = links.dp
    dp_core, dp_x, dp_y = flipped(dp, 0), flipped(dp, 1), flipped(dp, 2)
    dp_corner = flipped(dp_x, 2)

    def hop(kind, panel):
        source, device = (
            (dp, links.along_x),
            (dp, links.along_y),
            (dp, links.core),
            None,
            (dp_x, links.core),
            (dp_y, links.core),
            (dp_corner, links.core),
        )[kind]
        return shard_copy(kind, panel, source, device)

    def corner_copy(panel, parity):
        if parity == 0:
            return shard_copy(3, panel, dp_x, links.along_y)
        return shard_copy(3, panel, dp_y, links.along_x)

    def shard_arrived(kind, panel, source_dp):
        shard_copy(kind, panel, source_dp, links.core).wait_recv()

    def shard_start(panel):
        for kind in range(3):
            hop(kind, panel).start()

    def shard_forward(panel):
        shard_arrived(0, panel, dp_x)
        pl.when(panel % 2 == 0)(corner_copy(panel, 0).start)
        hop(4, panel).start()
        shard_arrived(1, panel, dp_y)
        pl.when(panel % 2 == 1)(corner_copy(panel, 1).start)
        hop(5, panel).start()

    def shard_last(panel):
        shard_arrived(3, panel, dp_corner)
        hop(6, panel).start()

    def shard_complete(panel):
        shard_arrived(2, panel, dp_core)
        shard_arrived(4, panel, flipped(dp_core, 1))
        shard_arrived(5, panel, flipped(dp_core, 2))
        shard_arrived(6, panel, flipped(flipped(dp_core, 1), 2))

    def shard_finish(panel):
        for kind in (0, 1, 2, 4, 5, 6):
            hop(kind, panel).wait_send()
        corner_copy(panel, 0).wait_send()

    def exchange(panel):
        shard_forward(panel)
        if panel + ahead < panels:
            shard_start(panel + ahead)
        if panel >= 3:
            shard_last(panel - 3)

    local_copies = [
        pltpu.make_async_copy(source, target, local.at[index])
        for index, (source, target) in enumerate(
            (
                (
                    stripe_ref,
                    dense_ref.at[
                        pl.ds(pl.multiple_of((links.dp * 4 + links.z) * stripe, stripe), stripe), :
                    ],
                ),
                (gates_ref, all_gates.at[links.z]),
                (cotangent_ref, sequence(cotangents_ref, links.z)),
            )
        )
    ]
    token_copy = pltpu.make_async_copy(
        normed_mixer_ref, sequence(tokens_ref, links.z), local.at[3]
    )

    def dense_column(panel):
        return panel * hidden + (0 if panel < first_panels else extra.shape[1])

    loads = [
        pltpu.make_async_copy(
            dense_ref.at[:, pl.ds(dense_column(panel), hidden)],
            matrices.at[panel],
            load_sems.at[panel],
        )
        for panel in range(14)
    ]
    extra_load = pltpu.make_async_copy(
        dense_ref.at[:, pl.ds(first_panels * hidden, extra.shape[1])], extra, load_sems.at[14]
    )

    def half_columns(panel):
        return pl.ds(pl.multiple_of(panel % 2 * hidden, hidden), hidden)

    def master_load(panel):
        return pltpu.make_async_copy(
            masters_ref.at[panel],
            grad_shared_ref.at[pl.ds(0, rows), half_columns(panel)],
            expert_sems.at[0, panel % 2],
        )

    def master_store(panel):
        return pltpu.make_async_copy(
            shared_act_ref.at[pl.ds(0, rows), half_columns(panel)],
            shard_region(dp, panel),
            expert_sems.at[1, panel % 2],
        )

    master_load(0).start()
    links.barrier()
    lines[0].start()
    planes[0][0].start()
    lines[1].start()
    gates.start()
    for copy in local_copies:
        copy.start()

    def round_masters(first, last):
        @pl.loop(first, last)
        def _(panel):
            master_load(panel).wait()

            @pl.when(panel + 1 < panels)
            def _():
                master_load(panel + 1).start()

            @pl.when(panel >= 2)
            def _():
                master_store(panel - 2).wait()

            shared_act_ref[:rows, half_columns(panel)] = grad_shared_ref[
                :rows, half_columns(panel)
            ].astype(jnp.bfloat16)
            master_store(panel).start()

    lines[0].arrive(1)
    planes[0][1].start()
    lines[0].arrive(2)
    planes[0][2].start()
    round_masters(0, panels // 3)
    for panel in range(2):
        shard_start(panel)
    planes[0][0].forward()
    lines[0].relay()
    lines[0].arrive(3)
    planes[0][3].start()
    planes[0][1].forward()
    lines[1].relay()
    round_masters(panels // 3, panels)
    for panel in (panels - 2, panels - 1):
        master_store(panel).wait()
    for panel in range(2, ahead):
        shard_start(panel)
    planes[1][0].start()
    planes[0][2].forward()
    lines[1].arrive(1)
    planes[1][1].start()
    planes[0][3].forward()
    cotangents.start()
    gates.relay()
    lines[1].arrive(2)
    planes[1][2].start()
    for plane in planes[0]:
        plane.last()
    planes[1][0].forward()
    for plane in planes[0]:
        plane.complete()
    local_copies[0].wait()
    extra_load.start()
    for copy in loads[:first_panels]:
        copy.start()

    rows_step = 32

    def norm_rows(source, gain, scale_out, target):
        @pl.loop(0, length // rows_step)
        def _(index):
            part = pl.ds(index * rows_step, rows_step)
            values = source[part, :].astype(jnp.float32)
            scale = lax.rsqrt(jnp.mean(values * values, axis=-1, keepdims=True) + 1e-06)
            if scale_out is not None:
                scale_out[part, :] = scale
            target[part, :] = (values * scale * gains_ref[gain : gain + 1, :]).astype(jnp.bfloat16)

    def project():
        extra_load.wait()
        gains_ref[...] = extra[...].astype(jnp.float32).T[:8, :]
        norm_rows(hidden_ref, 0, None, normed_attend_ref)
        for panel in range(5):
            loads[panel].wait()
            projected_ref[:, panel * hidden : (panel + 1) * hidden] = matmul(
                normed_attend_ref[...], matrices[panel]
            ).astype(jnp.bfloat16)

    def attend(group):
        key_rows = projected_ref[:, query_width + group * HD : query_width + (group + 1) * HD]
        value_first = query_width + kv_width + group * HD
        value_rows = projected_ref[:, value_first : value_first + HD]
        row = lax.broadcasted_iota(jnp.int32, (length, length), 0)
        column = lax.broadcasted_iota(jnp.int32, (length, length), 1)
        per_group = HEADS // KVH
        for head in range(group * per_group, (group + 1) * per_group):
            spot = slice(head * HD, (head + 1) * HD)
            scores = matmul_nt(projected_ref[:, spot], key_rows) * HD ** (-0.5)
            scores = jnp.where(column <= row, scores, -1e30)
            raised = jnp.exp(scores - jnp.max(scores, axis=-1, keepdims=True))
            shares = (raised / jnp.sum(raised, axis=-1, keepdims=True)).astype(jnp.bfloat16)
            attended_ref[:, spot] = matmul(shares, value_rows).astype(jnp.bfloat16)

    def join():
        for part in range(3):
            loads[5 + part].wait()
            update = matmul_nt(
                attended_ref[:, part * hidden : (part + 1) * hidden], matrices[5 + part]
            )
            if part == 0:
                residual_ref[...] = hidden_ref[...].astype(jnp.float32) + update
            else:
                residual_ref[...] += update
        norm_rows(residual_ref, 1, scale_ref, normed_mixer_ref)
        tokens.start()
        token_copy.start()

    def shared(part):
        spot = slice(part * hidden, (part + 1) * hidden)
        for panel in (8, 10, 12):
            loads[panel + part].wait()
        gate = matmul(normed_mixer_ref[...], matrices[8 + part])
        up = matmul(normed_mixer_ref[...], matrices[10 + part])
        sig = jax.nn.sigmoid(gate)
        gate_act = gate * sig
        shared_act_ref[:, spot] = (gate_act * up).astype(jnp.bfloat16)
        grad_act = matmul(cotangent_ref[...], matrices[12 + part])
        grad_shared_pre_ref[:, spot] = (
            grad_act * up * sig * (1.0 + gate * (1.0 - sig))
        ).astype(jnp.bfloat16)
        up_spot = slice((2 + part) * hidden, (3 + part) * hidden)
        grad_shared_pre_ref[:, up_spot] = (grad_act * gate_act).astype(jnp.bfloat16)

    def shared_back(part):
        spot = slice(part * hidden, (part + 1) * hidden)
        up_spot = slice((2 + part) * hidden, (3 + part) * hidden)
        grad = matmul_nt(grad_shared_pre_ref[:, spot], matrices[8 + part]) + matmul_nt(
            grad_shared_pre_ref[:, up_spot], matrices[10 + part]
        )
        out = matmul_nt(shared_act_ref[:, spot], matrices[12 + part])
        if part == 0:
            grad_shared_ref[...] = grad
            base_ref[...] = residual_ref[...] + out
        else:
            grad_shared_ref[...] += grad
            base_ref[...] += out

    def place_slots():
        local_copies[1].wait()
        before = (
            lax.broadcasted_iota(jnp.int32, (length, length), 0)
            < lax.broadcasted_iota(jnp.int32, (length, length), 1)
        )
        earlier_mask = jnp.where(before, 1.0, 0.0).astype(jnp.bfloat16)
        for source in range(4):
            gate = all_gates[source, links.z]
            hot = gate > 0.0
            earlier = matmul(jnp.where(hot, 1.0, 0.0).astype(jnp.bfloat16), earlier_mask)
            place = jnp.where(hot, earlier, -1.0).astype(jnp.int32)
            for expert in range(experts):
                places[expert, source : source + 1, :] = place[expert : expert + 1, :]
                my_gates[expert, source : source + 1, :] = gate[expert : expert + 1, :]

    core, chip = dp % 2, dp // 2
    chip_x, chip_y = flipped(chip, 0), flipped(chip, 1)
    chip_corner = flipped(chip_x, 1)
    shared_panels = pair_sum.shape[0]
    half = rows // 2
    quarter = width // 4

    ring = matrices.at[13]

    def ring_rows(index, which):
        return pl.ds(pl.multiple_of((2 * index + which) * rows, rows), rows)

    def pair_copy(panel, index):
        return links.copy_with(
            ring.at[ring_rows(index, 1 - core)],
            pair_sum.at[panel, index],
            shared_sems.at[0, 0, panel],
            shared_sems.at[1, 0, panel],
            links.core,
        )

    def shared_copy(kind, panel):
        source, target, device = (
            (pair_sum.at[panel], pair_sum.at[panel], links.core),
            (pair_sum.at[panel, chip_corner, pl.ds(0, half)], corner_x.at[panel], links.along_x),
            (pair_sum.at[panel, chip_corner, pl.ds(half, half)], corner_y.at[panel], links.along_y),
            (pair_sum.at[panel, chip_x], side_x.at[panel], links.along_x),
            (pair_sum.at[panel, chip_y], side_y.at[panel], links.along_y),
        )[kind]
        return links.copy_with(
            source, target, shared_sems.at[0, kind, panel], shared_sems.at[1, kind, panel], device
        )

    def shared_fill(panel):
        left_ref = normed_mixer_ref if panel < 4 else cotangent_ref
        right_ref = grad_shared_pre_ref if panel < 4 else shared_act_ref
        first = (panel if panel < 4 else panel - 4) * hidden
        right = right_ref[:, first : first + hidden]
        for index in range(4):
            part = matmul_tn(left_ref[:, index * quarter : (index + 1) * quarter], right)
            ring[index * quarter : (index + 1) * quarter, :] = part.astype(jnp.bfloat16)
        for index in range(4):
            pair_copy(panel, index).start()

    def shared_pair(panel):
        shared_copy(0, panel).wait()
        for index in range(4):
            pair_sum[panel, index] = (
                pair_sum[panel, index].astype(jnp.float32)
                + ring[ring_rows(index, core), :].astype(jnp.float32)
            ).astype(jnp.bfloat16)

    def shared_corners(panel):
        for kind in (1, 2):
            shared_copy(kind, panel).start()

    def shared_sides(panel):
        for kind in (1, 2):
            shared_copy(kind, panel).wait()
        pair_sum[panel, chip_y, :half] = (
            pair_sum[panel, chip_y, :half].astype(jnp.float32)
            + corner_x[panel].astype(jnp.float32)
        ).astype(jnp.bfloat16)
        pair_sum[panel, chip_x, half:] = (
            pair_sum[panel, chip_x, half:].astype(jnp.float32)
            + corner_y[panel].astype(jnp.float32)
        ).astype(jnp.bfloat16)
        for kind in (3, 4):
            shared_copy(kind, panel).start()

    def shared_total(panel):
        for kind in (3, 4):
            shared_copy(kind, panel).wait()
        value = (
            pair_sum[panel, chip].astype(jnp.float32)
            + side_x[panel].astype(jnp.float32)
            + side_y[panel].astype(jnp.float32)
        )
        matrices[12, pl.ds(panel % 2 * rows, rows), :] = value.astype(jnp.bfloat16)

    def shared_store(panel):
        return pltpu.make_async_copy(
            matrices.at[12, pl.ds(panel % 2 * rows, rows)],
            shared_sum_ref.at[panel],
            local.at[4 + panel % 2],
        )

    project()
    lines[1].arrive(3)
    planes[1][3].start()
    planes[1][1].forward()
    attend(0)
    attend(1)
    planes[1][2].forward()
    attend(2)
    attend(3)
    planes[1][3].forward()
    cotangents.relay()
    join()
    for plane in planes[1]:
        plane.last()
    for index in range(1, 4):
        gates.arrive(index)
    place_slots()
    for plane in planes[1]:
        plane.complete()
    for copy in loads[first_panels:]:
        copy.start()
    exchange(0)
    shared(0)
    exchange(1)
    shared(1)
    exchange(2)
    shared_back(0)
    exchange(3)
    shared_back(1)
    exchange(4)
    shared_fill(0)
    tokens.relay()
    for panel in range(5, 11):
        exchange(panel)
        shared_pair(panel - 5)
        shared_corners(panel - 5)
        if panel < 10:
            shared_fill(panel - 4)
    for index in range(1, 4):
        cotangents.arrive(index)
        tokens.arrive(index)
    local_copies[2].wait()
    token_copy.wait()
    token_loads = [
        pltpu.make_async_copy(
            source.at[:, pl.ds(part * hidden, hidden)],
            matrices.at[first + part, pl.ds(0, 4 * length)],
            load_sems.at[first + part],
        )
        for first, source in ((6, tokens_ref), (9, cotangents_ref))
        for part in range(3)
    ]
    for copy in token_loads:
        copy.start()
    slot_iota = lax.broadcasted_iota(jnp.int32, (slots, length), 0)

    def slot_gate(expert, source):
        hot = slot_iota == places[expert, pl.ds(source, 1), :]
        return jnp.sum(
            jnp.where(hot, my_gates[expert, pl.ds(source, 1), :], 0.0), axis=1, keepdims=True
        )

    for source in range(4):
        for expert in range(experts):
            hot = slot_iota == places[expert, source : source + 1, :]
            chosen[source, expert * slots : (expert + 1) * slots, :] = jnp.where(
                hot, 1.0, 0.0
            ).astype(jnp.bfloat16)
    exchange(11)
    for copy in token_loads:
        copy.wait()

    @pl.loop(0, 4)
    def _(source):
        part = pl.ds(source * length, length)
        spots = pl.ds(pl.multiple_of(source * slots, slots), slots)
        slot_gates = [slot_gate(expert, source) for expert in range(experts)]
        for block in range(3):
            spot = pl.ds(block * hidden, hidden)
            token_slots = matmul(chosen[source], matrices[6 + block, part, :])
            grad_slots = matmul(chosen[source], matrices[9 + block, part, :])
            for expert in range(experts):
                rows_of = slice(expert * slots, (expert + 1) * slots)
                forward_slots[expert, spots, spot] = token_slots[rows_of].astype(jnp.bfloat16)
                backward_slots[expert, spots, spot] = (
                    grad_slots[rows_of] * slot_gates[expert]
                ).astype(jnp.bfloat16)

    def slot_stores(expert):
        return [
            pltpu.make_async_copy(
                source.at[expert], target.at[expert], expert_sems.at[2 + index, expert]
            )
            for index, (source, target) in enumerate(
                ((forward_slots, received_ref), (backward_slots, grad_returned_ref))
            )
        ]

    def narrow_stores(expert):
        buffer = expert % 2
        return [
            pltpu.make_async_copy(
                narrow.at[buffer, index], target.at[expert], expert_sems.at[4 + buffer, index]
            )
            for index, target in enumerate((act_ref, grad_gate_ref, grad_up_ref))
        ]

    def weight_loads(expert):
        buffer = expert % 2
        return [
            pltpu.make_async_copy(
                weights_ref.at[3 * expert + matrix],
                matrices.at[3 * buffer + matrix],
                expert_sems.at[6 + buffer, matrix],
            )
            for matrix in range(3)
        ]

    def fetch(expert):
        for matrix, copy in enumerate(weight_loads(expert)):
            shard_complete(3 * expert + matrix)
            copy.start()

    for expert in range(experts):
        for copy in slot_stores(expert):
            copy.start()
    fetch(0)

    @pl.loop(0, experts)
    def _(expert):
        buffer = expert % 2
        loaded = weight_loads(expert)

        @pl.when(expert >= 2)
        def _():
            for copy in narrow_stores(expert - 2):
                copy.wait()

        received = forward_slots[expert]
        grad_out = backward_slots[expert]
        loaded[0].wait()
        gate_pre = matmul(received, matrices[3 * buffer])
        loaded[1].wait()
        up_pre = matmul(received, matrices[3 * buffer + 1])
        loaded[2].wait()
        grad_act = matmul(grad_out, matrices[3 * buffer + 2])
        gate_sig = jax.nn.sigmoid(gate_pre)
        gate_act = gate_pre * gate_sig
        act = (gate_act * up_pre).astype(jnp.bfloat16)
        grad_gate = (grad_act * up_pre * gate_sig * (1.0 + gate_pre * (1.0 - gate_sig))).astype(
            jnp.bfloat16
        )
        grad_up = (grad_act * gate_act).astype(jnp.bfloat16)
        narrow[buffer, 0] = act
        narrow[buffer, 1] = grad_gate
        narrow[buffer, 2] = grad_up
        for copy in narrow_stores(expert):
            copy.start()
        for copy in slot_stores(expert):
            copy.wait()
        slot_gates = jnp.concatenate([slot_gate(expert, source) for source in range(4)], 0)
        for block in range(3):
            rows_of = pl.ds(block * hidden, hidden)
            spot = pl.ds(block * hidden, hidden)
            out = matmul_nt(act, matrices[3 * buffer + 2, rows_of, :]).astype(jnp.bfloat16)
            forward_slots[expert, :, spot] = (
                out.astype(jnp.float32) * slot_gates
            ).astype(jnp.bfloat16)
            backward_slots[expert, :, spot] = (
                matmul_nt(grad_gate, matrices[3 * buffer, rows_of, :])
                + matmul_nt(grad_up, matrices[3 * buffer + 1, rows_of, :])
            ).astype(jnp.bfloat16)

        later = (
            (lambda: exchange(12), lambda: shared_sides(0)),
            (lambda: exchange(13), lambda: shared_sides(1)),
            (lambda: exchange(14), lambda: shared_sides(2)),
            (lambda: exchange(15), lambda: exchange(16), lambda: shard_last(14)),
            (
                lambda: shard_forward(17),
                lambda: shared_sides(3),
                lambda: shared_sides(4),
                lambda: shared_sides(5),
                lambda: shard_last(15),
                lambda: shard_last(16),
                lambda: shard_last(17),
            ),
        )
        for done, calls in enumerate(later):

            @pl.when(expert == done)
            def _():
                for call in calls:
                    call()

        @pl.when(expert + 1 < experts)
        def _():
            fetch(expert + 1)

    for expert in (experts - 2, experts - 1):
        for copy in narrow_stores(expert):
            copy.wait()
    out_copies = []
    for first, values, target in ((0, backward_slots, grad_parts_ref), (3, forward_slots, routed_parts_ref)):
        for block in range(3):
            spot = slice(block * hidden, (block + 1) * hidden)
            for source in range(4):
                slots_of = jnp.concatenate(
                    [
                        values[expert, source * slots : (source + 1) * slots, spot]
                        for expert in range(experts)
                    ],
                    0,
                )
                matrices[first + block, source * length : (source + 1) * length, :] = matmul_tn(
                    chosen[source], slots_of
                ).astype(jnp.bfloat16)
            out_copies.append(
                pltpu.make_async_copy(
                    matrices.at[first + block, pl.ds(0, 4 * length)],
                    target.at[:, pl.ds(block * hidden, hidden)],
                    load_sems.at[first + block],
                )
            )
            out_copies[-1].start()
    @pl.loop(0, panels)
    def _(panel):
        shard_finish(panel)

    for panel in range(shared_panels):
        if panel >= 2:
            shared_store(panel - 2).wait()
        shared_total(panel)
        shared_store(panel).start()
    for panel in (shared_panels - 2, shared_panels - 1):
        shared_store(panel).wait()
    for copy in out_copies:
        copy.wait()

    links.finish()


def front(stripe, gates, masters, hidden_in, cotangent, slots):
    length, width = cotangent.shape
    stripe_rows, columns = stripe.shape
    panels, rows, hidden = masters.shape
    experts = panels // 3
    low, full = jnp.bfloat16, jnp.float32
    vmem = pl.BlockSpec(memory_space=pltpu.VMEM)
    query_width = HEADS * HD
    spots = 4 * slots
    return pl.pallas_call(
        front_kernel,
        in_specs=[ANY] * 3 + [vmem] * 2,
        out_specs=[ANY] * 11 + [vmem] * 11 + [ANY],
        out_shape=[
            jax.ShapeDtypeStruct((stripe_rows * 32, columns), low),
            jax.ShapeDtypeStruct((panels, rows * 8, hidden), low),
            *[jax.ShapeDtypeStruct((length * 4, width), low)] * 4,
            *[jax.ShapeDtypeStruct((experts, spots, width), low)] * 2,
            *[jax.ShapeDtypeStruct((experts, spots, hidden), low)] * 3,
            jax.ShapeDtypeStruct((length, width), low),
            jax.ShapeDtypeStruct((length, query_width + 2 * KVH * HD), low),
            jax.ShapeDtypeStruct((length, query_width), low),
            jax.ShapeDtypeStruct((length, width), full),
            jax.ShapeDtypeStruct((length, 1), full),
            jax.ShapeDtypeStruct((length, width), low),
            jax.ShapeDtypeStruct((length, FFS), low),
            jax.ShapeDtypeStruct((length, 2 * FFS), low),
            jax.ShapeDtypeStruct((length, width), full),
            jax.ShapeDtypeStruct((length, width), full),
            jax.ShapeDtypeStruct((8, width), full),
            jax.ShapeDtypeStruct((6, rows, hidden), low),
        ],
        scratch_shapes=[
            pltpu.VMEM((14, width, hidden), low),
            pltpu.VMEM((width, 128), low),
            pltpu.VMEM((4, 4, 8, length), full),
            pltpu.VMEM((experts, 4, length), jnp.int32),
            pltpu.VMEM((experts, 4, length), full),
            pltpu.VMEM((4, experts * slots, length), low),
            pltpu.VMEM((experts, spots, width), low),
            pltpu.VMEM((experts, spots, width), low),
            pltpu.VMEM((2, 3, spots, hidden), low),
            pltpu.VMEM((6, 4, rows, hidden), low),
            pltpu.VMEM((6, rows // 2, hidden), low),
            pltpu.VMEM((6, rows // 2, hidden), low),
            pltpu.VMEM((6, rows, hidden), low),
            pltpu.VMEM((6, rows, hidden), low),
            pltpu.SemaphoreType.DMA((170,)),
            pltpu.SemaphoreType.DMA((7, panels)),
            pltpu.SemaphoreType.DMA((7, panels)),
            pltpu.SemaphoreType.DMA((6,)),
            pltpu.SemaphoreType.DMA((15,)),
            pltpu.SemaphoreType.DMA((8, 6)),
            pltpu.SemaphoreType.DMA((2, 5, 6)),
        ],
        compiler_params=pltpu.CompilerParams(
            collective_id=1, has_side_effects=True, vmem_limit_bytes=63 * MIB
        ),
        name="front",
    )(stripe, gates, masters, hidden_in, cotangent)


def scatter_kernel(
    grad_parts_ref,
    received_ref,
    grad_returned_ref,
    act_ref,
    grad_gate_ref,
    grad_up_ref,
    dense_ref,
    shared_sum_ref,
    cotangent_ref,
    normed_attend_ref,
    attended_ref,
    residual_ref,
    scale_ref,
    gain_ref,
    grad_shared_ref,
    projected_ref,
    hidden_ref,
    gain_attend_ref,
    expert_sum_ref,
    stripes_ref,
    grad_input_ref,
    grad_gain_ref,
    grad_gain_attend_ref,
    ring,
    pair_sum,
    corner_x,
    corner_y,
    side_x,
    side_y,
    staged,
    wide,
    narrow,
    left,
    right,
    out_weights,
    grad_tokens,
    grad_attended,
    grad_pair,
    grad_residual_ref,
    key_weights,
    line_out,
    line_in,
    pair_sems,
    slot_sems,
    line_sems,
    token_sems,
    load_sems,
    free,
):
    dp, z = lax.axis_index("dp"), lax.axis_index("expert")
    core, chip = dp % 2, dp // 2
    chip_x, chip_y = flipped(chip, 0), flipped(chip, 1)
    chip_corner = flipped(chip_x, 1)
    device_core = (flipped(dp, 0), z)
    device_x = (flipped(dp, 1), z)
    device_y = (flipped(dp, 2), z)
    others = [(dp, (z + turn) % 4) for turn in range(1, 4)]
    slots = pair_sum.shape[0]
    experts = received_ref.shape[0]
    expert_panels = 3 * experts
    dense_panels = line_out.shape[0]
    shared_panels = dense_panels - right.shape[0]
    panels = expert_panels + right.shape[0]
    length, width = residual_ref.shape
    share, hidden = staged.shape[1:]
    half = share // 2
    stripe = share // 4
    query_width = HEADS * HD
    kv_width = KVH * HD
    block = width // 4

    def remote(source, target, send, receive, device):
        return pltpu.make_async_remote_copy(
            src_ref=source,
            dst_ref=target,
            send_sem=send,
            recv_sem=receive,
            device_id=device,
            device_id_type=MESH,
        )

    barrier = pltpu.get_barrier_semaphore()
    for device in (device_core, device_x, device_y, *others):
        pl.semaphore_signal(barrier, inc=1, device_id=device, device_id_type=MESH)
    pl.semaphore_wait(barrier, 6)

    grad_copies = [
        remote(
            grad_parts_ref.at[pl.ds(pl.multiple_of(device[1] * length, length), length), :],
            grad_tokens.at[turn],
            token_sems.at[turn],
            token_sems.at[3 + turn],
            device,
        )
        for turn, device in enumerate(others)
    ]
    for copy in grad_copies:
        copy.start()

    def expert_loads(expert):
        buffer = expert % 2
        return [
            pltpu.make_async_copy(source.at[expert], target, load_sems.at[buffer, index])
            for index, (source, target) in enumerate(
                (
                    (received_ref, wide.at[buffer, 0]),
                    (grad_returned_ref, wide.at[buffer, 1]),
                    (grad_gate_ref, narrow.at[buffer, 0]),
                    (grad_up_ref, narrow.at[buffer, 1]),
                    (act_ref, narrow.at[buffer, 2]),
                )
            )
        ]

    for copy in expert_loads(0):
        copy.start()

    def columns(ref, panel):
        return ref.at[:, pl.ds(panel * hidden, hidden)]

    sources = [
        (cotangent_ref, left.at[0]),
        (normed_attend_ref, left.at[2]),
        *[(columns(attended_ref, panel), right.at[panel]) for panel in range(3)],
        (shared_sum_ref, line_out.at[pl.ds(0, shared_panels)]),
        (dense_ref.at[:, pl.ds(query_width + 2 * kv_width, query_width)], out_weights),
        (dense_ref.at[:, pl.ds(query_width, 2 * kv_width)], key_weights),
        (
            grad_parts_ref.at[pl.ds(pl.multiple_of(z * length, length), length), :],
            grad_tokens.at[3],
        ),
    ]
    dense_loads = [
        pltpu.make_async_copy(source, target, load_sems.at[2 + index // 5, index % 5])
        for index, (source, target) in enumerate(sources)
    ]
    for copy in dense_loads:
        copy.start()
    query_load = pltpu.make_async_copy(
        dense_ref.at[:, pl.ds(0, query_width)], out_weights, pair_sems.at[4]
    )

    def fill(pair, left_ref, right_value):
        for chip_index in range(4):
            part = matmul_tn(left_ref[:, chip_index * block : (chip_index + 1) * block], right_value)
            ring[pair, chip_index] = part.astype(jnp.bfloat16).reshape(2, share, hidden)

    def total(first, *more):
        result = first.astype(jnp.float32)
        for value in more:
            result = result + value.astype(jnp.float32)
        return result

    def pair_copy(panel):
        pair, slot = panel % 2, panel % slots
        return remote(
            ring.at[pair, :, 1 - core],
            pair_sum.at[slot],
            pair_sems.at[pair],
            slot_sems.at[0, slot],
            device_core,
        )

    def corner_copies(panel):
        slot = panel % slots
        return (
            remote(
                pair_sum.at[slot, chip_corner, pl.ds(0, half)],
                corner_x.at[slot],
                slot_sems.at[1, slot],
                slot_sems.at[2, slot],
                device_x,
            ),
            remote(
                pair_sum.at[slot, chip_corner, pl.ds(half, half)],
                corner_y.at[slot],
                slot_sems.at[3, slot],
                slot_sems.at[4, slot],
                device_y,
            ),
        )

    def side_copies(panel):
        slot = panel % slots
        return (
            remote(
                pair_sum.at[slot, chip_x],
                side_x.at[slot],
                slot_sems.at[5, slot],
                slot_sems.at[6, slot],
                device_x,
            ),
            remote(
                pair_sum.at[slot, chip_y],
                side_y.at[slot],
                slot_sems.at[7, slot],
                slot_sems.at[8, slot],
                device_y,
            ),
        )

    def line_copies(panel):
        return [
            remote(
                line_out.at[panel, pl.ds(pl.multiple_of(device[1] * stripe, stripe), stripe)],
                line_in.at[panel, turn],
                line_sems.at[0, panel, turn],
                line_sems.at[1, panel, turn],
                device,
            )
            for turn, device in enumerate(others)
        ]

    def staged_copy(panel):
        return pltpu.make_async_copy(
            staged.at[panel % 2], expert_sum_ref.at[panel], pair_sems.at[2 + panel % 2]
        )

    def post(panel):
        @pl.when(panel >= slots)
        def _():
            pl.semaphore_wait(free.at[0], 1)

        pair_copy(panel).start()

    def sum_pair(panel):
        pair, slot = panel % 2, panel % slots
        pair_copy(panel).wait()
        for chip_index in range(4):
            pair_sum[slot, chip_index] = total(
                pair_sum[slot, chip_index], ring[pair, chip_index, core]
            ).astype(jnp.bfloat16)

        @pl.when(panel >= slots)
        def _():
            pl.semaphore_wait(free.at[1], 1)
            pl.semaphore_wait(free.at[2], 1)

        for copy in corner_copies(panel):
            copy.start()

    def sum_corner(panel):
        slot = panel % slots
        for copy in corner_copies(panel):
            copy.wait_recv()
        pair_sum[slot, chip_y, :half] = total(
            pair_sum[slot, chip_y, :half], corner_x[slot]
        ).astype(jnp.bfloat16)
        pair_sum[slot, chip_x, half:] = total(
            pair_sum[slot, chip_x, half:], corner_y[slot]
        ).astype(jnp.bfloat16)
        for copy in side_copies(panel):
            copy.start()

    def sum_sides(panel):
        slot = panel % slots
        for copy in corner_copies(panel):
            copy.wait_send()
        for copy in side_copies(panel):
            copy.wait()
        value = total(pair_sum[slot, chip], side_x[slot], side_y[slot]).astype(jnp.bfloat16)

        @pl.when(panel < expert_panels)
        def _():
            @pl.when(panel >= 2)
            def _():
                staged_copy(panel - 2).wait()

            staged[panel % 2] = value
            staged_copy(panel).start()

        @pl.when(panel >= expert_panels)
        def _():
            index = panel - expert_panels + shared_panels
            line_out[index] = value
            for copy in line_copies(index):
                copy.start()

        @pl.when(panel < panels - slots)
        def _():
            for index, device in enumerate((device_core, device_x, device_y)):
                pl.semaphore_signal(
                    free.at[index], inc=1, device_id=device, device_id_type=MESH
                )

    def residual_backward(part):
        if part == 0:
            for copy in dense_loads:
                copy.wait()
            for copy in grad_copies:
                copy.wait()
            grad_gain_ref[...] = jnp.zeros_like(grad_gain_ref)
        rows_step = 32
        steps = length // rows_step // 2

        @pl.loop(part * steps, (part + 1) * steps)
        def _(index):
            rows = pl.ds(index * rows_step, rows_step)
            grad_normed = (
                total(
                    grad_tokens[3, rows, :],
                    grad_tokens[0, rows, :],
                    grad_tokens[1, rows, :],
                    grad_tokens[2, rows, :],
                )
                + grad_shared_ref[rows, :]
            )
            residual, scale = residual_ref[rows, :], scale_ref[rows, :]
            grad_scaled = grad_normed * gain_ref[...]
            mean = jnp.mean(grad_scaled * residual, axis=-1, keepdims=True)
            grad_residual = (
                left[0, rows, :].astype(jnp.float32)
                + scale * grad_scaled
                - residual * (scale * scale * scale) * mean
            )
            grad_residual_ref[rows, :] = grad_residual
            left[1, rows, :] = grad_residual.astype(jnp.bfloat16)
            grad_gain_ref[...] += jnp.sum(grad_normed * residual * scale, axis=0, keepdims=True)

    def attended_backward():
        grad_attended[...] = matmul(left[1], out_weights[...]).astype(jnp.bfloat16)
        query_load.start()

    def query_backward():
        query_load.wait()
        for part in range(3):
            update = matmul_nt(right[3 + part], out_weights[:, part * hidden : (part + 1) * hidden])
            if part == 0:
                grad_input_ref[...] = update
            else:
                grad_input_ref[...] += update

    def key_backward():
        for part in range(2):
            grad_input_ref[...] += matmul_nt(
                right[6 + part], key_weights[:, part * hidden : (part + 1) * hidden]
            )

    def input_backward():
        grad_gain_attend_ref[...] = jnp.zeros_like(grad_gain_attend_ref)
        rows_step = 32

        @pl.loop(0, length // rows_step)
        def _(index):
            rows = pl.ds(index * rows_step, rows_step)
            values, grad_normed = hidden_ref[rows, :].astype(jnp.float32), grad_input_ref[rows, :]
            scale = lax.rsqrt(jnp.mean(values * values, axis=-1, keepdims=True) + 1e-06)
            grad_scaled = grad_normed * gain_attend_ref[...]
            mean = jnp.mean(grad_scaled * values, axis=-1, keepdims=True)
            grad_input_ref[rows, :] = (
                grad_residual_ref[rows, :]
                + scale * grad_scaled
                - values * (scale * scale * scale) * mean
            )
            grad_gain_attend_ref[...] += jnp.sum(
                grad_normed * values * scale, axis=0, keepdims=True
            )

    def attention_backward(head):
        score_scale = HD ** (-0.5)
        per_group = HEADS // KVH
        heads_wide = hidden // HD
        group = head // per_group
        key_rows = projected_ref[:, query_width + group * HD : query_width + (group + 1) * HD]
        value_first = query_width + kv_width + group * HD
        value_rows = projected_ref[:, value_first : value_first + HD]
        row = lax.broadcasted_iota(jnp.int32, (length, length), 0)
        column = lax.broadcasted_iota(jnp.int32, (length, length), 1)
        spot = slice(head * HD, (head + 1) * HD)
        query, grad_out = projected_ref[:, spot], grad_attended[:, spot]
        scores = jnp.where(column <= row, matmul_nt(query, key_rows) * score_scale, -1e30)
        raised = jnp.exp(scores - jnp.max(scores, axis=-1, keepdims=True))
        weights = raised / jnp.sum(raised, axis=-1, keepdims=True)
        grad_weights = matmul_nt(grad_out, value_rows)
        inner = jnp.sum(weights * grad_weights, axis=-1, keepdims=True)
        grad_scores = (weights * (grad_weights - inner)).astype(jnp.bfloat16)
        grad_query = matmul(grad_scores, key_rows) * score_scale
        place = slice(head % heads_wide * HD, (head % heads_wide + 1) * HD)
        right[3 + head // heads_wide, :, place] = grad_query.astype(jnp.bfloat16)
        grad_key = matmul_tn(grad_scores, query)
        grad_value = matmul_tn(weights.astype(jnp.bfloat16), grad_out)
        if head % per_group > 0:
            grad_key = grad_key + grad_pair[0]
            grad_value = grad_value + grad_pair[1]
        if head % per_group < per_group - 1:
            grad_pair[0] = grad_key
            grad_pair[1] = grad_value
        else:
            place = slice(group * HD, (group + 1) * HD)
            right[6, :, place] = (grad_key * score_scale).astype(jnp.bfloat16)
            right[7, :, place] = grad_value.astype(jnp.bfloat16)

    def two_heads_backward(head):
        attention_backward(head)
        attention_backward(head + 1)

    @pl.loop(0, panels + 5)
    def _(step):
        @pl.when(step < expert_panels)
        def _():
            expert, matrix = step // 3, step % 3

            @pl.when(matrix == 0)
            def _():
                for copy in expert_loads(expert):
                    copy.wait()

                @pl.when(expert + 1 < experts)
                def _():
                    for copy in expert_loads(expert + 1):
                        copy.start()

            fill(step % 2, wide.at[expert % 2, matrix // 2], narrow[expert % 2, matrix])

        backward = [
            *[functools.partial(residual_backward, part) for part in range(2)],
            attended_backward,
            *[functools.partial(two_heads_backward, head) for head in range(0, HEADS, 2)],
            query_backward,
            key_backward,
            input_backward,
        ]
        for index, call in enumerate(backward):
            pl.when(step == GRAD_STEP + index)(call)

        @pl.when((step >= expert_panels) & (step < panels))
        def _():
            panel = step - expert_panels
            fill(step % 2, left.at[jnp.where(panel < 3, 1, 2)], right[panel])

        @pl.when(step == GRAD_STEP + 1)
        def _():
            for panel in range(shared_panels):
                for copy in line_copies(panel):
                    copy.start()

        @pl.when(step < panels)
        def _():
            post(step)

        @pl.when((step >= 1) & (step < panels + 1))
        def _():
            sum_pair(step - 1)

        @pl.when((step >= 3) & (step < panels + 3))
        def _():
            sum_corner(step - 3)

        @pl.when(step >= 5)
        def _():
            sum_sides(step - 5)

    for panel in (expert_panels - 2, expert_panels - 1):
        staged_copy(panel).wait()

    @pl.loop(0, dense_panels)
    def _(panel):
        for copy in line_copies(panel):
            copy.wait()
        stripes_ref[panel] = total(
            line_out[panel, pl.ds(pl.multiple_of(z * stripe, stripe), stripe), :],
            line_in[panel, 0], line_in[panel, 1], line_in[panel, 2]
        )


def scatter_grads(
    grad_parts,
    saved,
    dense_all,
    shared_sum,
    cotangent,
    normed_attend,
    attended,
    residual,
    scale,
    gain,
    grad_shared,
    projected,
    hidden_in,
    gain_attend,
):
    experts, spots, width = saved[0].shape
    hidden = saved[2].shape[-1]
    length = residual.shape[0]
    share = width // 8
    stripe = share // 4
    dense_panels = 14
    low = jnp.bfloat16
    vmem = pl.BlockSpec(memory_space=pltpu.VMEM)
    return pl.pallas_call(
        scatter_kernel,
        in_specs=[ANY] * 11 + [vmem] * 7,
        out_specs=[ANY, vmem, vmem, vmem, vmem],
        out_shape=[
            jax.ShapeDtypeStruct((3 * experts, share, hidden), low),
            jax.ShapeDtypeStruct((dense_panels, stripe, hidden), jnp.float32),
            jax.ShapeDtypeStruct((length, width), jnp.float32),
            jax.ShapeDtypeStruct((1, width), jnp.float32),
            jax.ShapeDtypeStruct((1, width), jnp.float32),
        ],
        scratch_shapes=[
            pltpu.VMEM((2, 4, 2, share, hidden), low),
            pltpu.VMEM((SLOTS, 4, share, hidden), low),
            pltpu.VMEM((SLOTS, share // 2, hidden), low),
            pltpu.VMEM((SLOTS, share // 2, hidden), low),
            pltpu.VMEM((SLOTS, share, hidden), low),
            pltpu.VMEM((SLOTS, share, hidden), low),
            pltpu.VMEM((2, share, hidden), low),
            pltpu.VMEM((2, 2, spots, width), low),
            pltpu.VMEM((2, 3, spots, hidden), low),
            pltpu.VMEM((3, length, width), low),
            pltpu.VMEM((8, length, hidden), low),
            pltpu.VMEM((width, HEADS * HD), low),
            pltpu.VMEM((4, length, width), low),
            pltpu.VMEM((length, HEADS * HD), low),
            pltpu.VMEM((2, length, HD), jnp.float32),
            pltpu.VMEM((length, width), jnp.float32),
            pltpu.VMEM((width, 2 * KVH * HD), low),
            pltpu.VMEM((dense_panels, share, hidden), low),
            pltpu.VMEM((dense_panels, 3, stripe, hidden), low),
            pltpu.SemaphoreType.DMA((5,)),
            pltpu.SemaphoreType.DMA((9, SLOTS)),
            pltpu.SemaphoreType.DMA((2, dense_panels, 3)),
            pltpu.SemaphoreType.DMA((6,)),
            pltpu.SemaphoreType.DMA((5, 5)),
            pltpu.SemaphoreType.REGULAR((3,)),
        ],
        compiler_params=pltpu.CompilerParams(
            collective_id=3, has_side_effects=True, vmem_limit_bytes=62 * MIB
        ),
        name="scatter_grads",
    )(
        grad_parts,
        *saved,
        dense_all,
        shared_sum,
        cotangent,
        normed_attend,
        attended,
        residual,
        scale,
        gain,
        grad_shared,
        projected,
        hidden_in,
        gain_attend,
    )


def muon_kernel(
    expert_ref,
    dense_ref,
    routed_parts_ref,
    expert_out_ref,
    dense_out_ref,
    routed_received_ref,
    dense_back,
    moments,
    units,
    orthogonal,
    current,
    low,
    identity,
    line_sems,
    out_sems,
    in_sems,
    back_out_sems,
    back_in_sems,
    load_sems,
):
    dp, z = lax.axis_index("dp"), lax.axis_index("expert")
    count, share, _ = moments.shape
    first, dense_count = 10, 4
    stripe = dense_ref.shape[1]
    others = [(dp, (z + turn) % 4) for turn in range(1, 4)]
    peers = [((dp + turn) % 8, z) for turn in range(1, 8)]

    def remote(source, target, send, receive, device):
        return pltpu.make_async_remote_copy(
            src_ref=source,
            dst_ref=target,
            send_sem=send,
            recv_sem=receive,
            device_id=device,
            device_id_type=MESH,
        )

    def share_of(index):
        return pl.ds(pl.multiple_of(index * share, share), share)

    def stripe_of(index):
        return pl.ds(pl.multiple_of(index * stripe, stripe), stripe)

    barrier = pltpu.get_barrier_semaphore()
    for device in (*others, *peers):
        pl.semaphore_signal(barrier, inc=1, device_id=device, device_id_type=MESH)
    dense_rows = pl.ds(first, dense_count)
    loads = [
        pltpu.make_async_copy(
            expert_ref.at[pl.ds(0, first)], moments.at[pl.ds(0, first)], load_sems.at[0]
        ),
        pltpu.make_async_copy(
            expert_ref.at[pl.ds(first, count - first - dense_count)],
            moments.at[pl.ds(first + dense_count, count - first - dense_count)],
            load_sems.at[1],
        ),
        pltpu.make_async_copy(
            dense_ref.at[pl.ds(z * dense_count, dense_count)],
            moments.at[dense_rows, stripe_of(z)],
            load_sems.at[2],
        ),
    ]
    for copy in loads:
        copy.start()
    pl.semaphore_wait(barrier, len(others) + len(peers))
    line_copies = [
        remote(
            dense_ref.at[pl.ds(device[1] * dense_count, dense_count)],
            moments.at[dense_rows, stripe_of(z)],
            line_sems.at[0, turn],
            line_sems.at[1, turn],
            device,
        )
        for turn, device in enumerate(others)
    ]
    line_back = [
        remote(
            dense_back.at[:, stripe_of(device[1])],
            dense_out_ref.at[pl.ds(z * dense_count, dense_count)],
            line_sems.at[2, turn],
            line_sems.at[3, turn],
            device,
        )
        for turn, device in enumerate(others)
    ]
    own_back = pltpu.make_async_copy(
        dense_back.at[:, stripe_of(z)],
        dense_out_ref.at[pl.ds(z * dense_count, dense_count)],
        load_sems.at[2],
    )

    def out_copy(slot, turn):
        owner = peers[turn][0]
        return remote(
            moments.at[8 * slot + owner],
            units.at[slot, share_of(dp)],
            out_sems.at[slot, turn],
            in_sems.at[slot],
            peers[turn],
        )

    def own_copy(slot):
        return pltpu.make_async_copy(
            moments.at[8 * slot + dp], units.at[slot, share_of(dp)], load_sems.at[3 + slot]
        )

    def is_dense(slot, owner):
        unit = 8 * slot + owner
        return (unit >= first) & (unit < first + dense_count)

    def expert_place(slot, owner):
        unit = 8 * slot + owner
        return expert_out_ref.at[jnp.where(unit < first, unit, unit - dense_count)]

    def dense_place(slot, owner):
        return dense_back.at[8 * slot + owner - first]

    def back_copy(place, slot, turn):
        return remote(
            orthogonal.at[slot, share_of(peers[turn][0])],
            place(slot, dp),
            back_out_sems.at[slot, turn],
            back_in_sems.at[slot, dp],
            peers[turn],
        )

    def own_back_copy(place, slot):
        return pltpu.make_async_copy(
            orthogonal.at[slot, share_of(dp)], place(slot, dp), load_sems.at[3 + slot]
        )

    def send_back(place, slot):
        for turn in range(7):
            back_copy(place, slot, turn).start()
        own_back_copy(place, slot).start()

    def exists(slot, owner):
        return 8 * slot + owner < count

    def send_slot(slot):
        for turn in range(7):
            pl.when(exists(slot, peers[turn][0]))(out_copy(slot, turn).start)
        pl.when(exists(slot, dp))(own_copy(slot).start)

    length = routed_received_ref.shape[1]
    routed_copies = [
        remote(
            routed_parts_ref.at[pl.ds(pl.multiple_of(device[1] * length, length), length), :],
            routed_received_ref.at[turn],
            line_sems.at[4, turn],
            line_sems.at[5, turn],
            device,
        )
        for turn, device in enumerate(others)
    ]
    for copy in line_copies:
        copy.start()
    loads[0].wait()
    send_slot(0)
    loads[1].wait()
    loads[2].wait()
    for copy in line_copies:
        copy.wait()
    send_slot(1)
    send_slot(2)
    for copy in routed_copies:
        copy.start()

    @pl.loop(0, 3)
    def _(slot):
        @pl.when(exists(slot, dp))
        def _():
            own_copy(slot).wait()
            arrived = units.at[slot, pl.ds(0, 7 * share)]
            remote(arrived, arrived, in_sems.at[slot], in_sems.at[slot], peers[0]).wait_recv()
            newton_schulz_unit(units.at[slot], orthogonal.at[slot], current, low, identity)

            @pl.when(is_dense(slot, dp))
            def _():
                send_back(dense_place, slot)

            @pl.when(jnp.logical_not(is_dense(slot, dp)))
            def _():
                send_back(expert_place, slot)

    def own_back_wait(slot):
        def wait():
            pltpu.make_async_copy(
                orthogonal.at[slot, share_of(dp)], expert_out_ref.at[0], load_sems.at[3 + slot]
            ).wait()

        return wait

    def wait_back(slot):
        for turn in range(7):
            owner = peers[turn][0]

            @pl.when(exists(slot, owner))
            def _():
                block = expert_out_ref.at[0]
                semaphore = back_in_sems.at[slot, owner]
                remote(block, block, semaphore, semaphore, peers[0]).wait_recv()

        pl.when(exists(slot, dp))(own_back_wait(slot))

    wait_back(1)
    for copy in line_back:
        copy.start()
    own_back.start()
    wait_back(0)
    wait_back(2)
    for slot in range(3):
        for turn in range(7):
            pl.when(exists(slot, peers[turn][0]))(out_copy(slot, turn).wait_send)

        @pl.when(exists(slot, dp))
        def _():
            for turn in range(7):
                back_copy(expert_place, slot, turn).wait_send()

    for copy in line_back:
        copy.wait()
    own_back.wait()
    for copy in routed_copies:
        copy.wait()


def muon(expert_units, dense_units, routed_parts):
    experts, share, columns = expert_units.shape
    panels, stripe, _ = dense_units.shape
    count = experts + panels // 4
    low = jnp.bfloat16
    return pl.pallas_call(
        muon_kernel,
        in_specs=[ANY] * 3,
        out_specs=[ANY] * 3,
        out_shape=[
            jax.ShapeDtypeStruct(expert_units.shape, low),
            jax.ShapeDtypeStruct(dense_units.shape, low),
            jax.ShapeDtypeStruct((3, routed_parts.shape[0] // 4, routed_parts.shape[1]), low),
        ],
        scratch_shapes=[
            pltpu.VMEM((panels // 4, share, columns), low),
            pltpu.VMEM((count, share, columns), low),
            pltpu.VMEM((3, 8 * share, columns), low),
            pltpu.VMEM((3, 8 * share, columns), low),
            pltpu.VMEM((columns, 8 * share), jnp.float32),
            pltpu.VMEM((columns, 8 * share), low),
            pltpu.VMEM((columns, columns), low),
            pltpu.SemaphoreType.DMA((6, 3)),
            pltpu.SemaphoreType.DMA((3, 7)),
            pltpu.SemaphoreType.DMA((3,)),
            pltpu.SemaphoreType.DMA((3, 7)),
            pltpu.SemaphoreType.DMA((3, 8)),
            pltpu.SemaphoreType.DMA((6,)),
        ],
        compiler_params=pltpu.CompilerParams(
            collective_id=4, has_side_effects=True, vmem_limit_bytes=56 * MIB
        ),
        name="muon",
    )(expert_units, dense_units, routed_parts)


def update_kernel(weights_ref, orthogonal_ref, new_ref):
    keep_factor = 1.0 - LEARN_RATE * WEIGHT_DECAY
    new_ref[...] = keep_factor * weights_ref[...] - LEARN_RATE * orthogonal_ref[...].astype(
        jnp.float32
    )


def updated_weights(weights, orthogonal):
    panels, rows, columns = orthogonal.shape
    group = 3
    block = pl.BlockSpec((group, rows, columns), lambda index: (index, 0, 0))
    return pl.pallas_call(
        update_kernel,
        grid=(panels // group,),
        in_specs=[block, block],
        out_specs=block,
        out_shape=jax.ShapeDtypeStruct(orthogonal.shape, jnp.float32),
        name="update",
    )(weights.reshape(orthogonal.shape), orthogonal).reshape(weights.shape)


def on_device(
    hidden_in,
    cotangent,
    routes,
    route_weights,
    dense_weights,
    dense_momentum,
    expert_weights,
    expert_momentum,
    norm_gains,
    gain_first,
    gain_second,
):
    length, width = hidden_in.shape
    topk_count = routes.shape[1]
    local_experts = expert_weights.shape[0]
    expert_size = lax.axis_size("expert")
    dp_size = lax.axis_size("dp")
    expert_count = local_experts * expert_size
    capacity = 5 * length * topk_count // (4 * expert_count)
    block_rows = min(512, length)
    query_width = HEADS * HD
    kv_width = KVH * HD
    qkv_end = query_width + 2 * kv_width
    shared_base = 2 * query_width + 2 * kv_width
    gate_table = jnp.sum(
        jnp.where(
            routes.T[None, :, :] == jnp.arange(expert_count, dtype=jnp.int32)[:, None, None],
            route_weights.T[None, :, :],
            0.0,
        ),
        axis=1,
    )
    direct = dp_size == 8 and expert_size == 4
    inputs = hidden_in.astype(jnp.float32)
    scale_attend = norm_scale(inputs)
    if direct:
        stripe_rows = dense_weights.shape[0]
        extra = jnp.zeros((stripe_rows, 128 - norm_gains.shape[0]), jnp.float32)
        plane_gates = gate_table.reshape(expert_size, local_experts, length)
        (
            dense_all,
            _,
            _,
            _,
            routed_parts,
            grad_parts,
            *saved,
            normed_attend,
            projected,
            attended,
            residual,
            scale_mixer,
            normed_mixer,
            shared_act,
            grad_shared_pre,
            grad_shared,
            base_out,
            gains_all,
            shared_sum,
        ) = front(
            jnp.concatenate(
                [
                    dense_weights[:, :shared_base],
                    norm_gains.T,
                    extra,
                    dense_weights[:, shared_base:],
                ],
                1,
            ).astype(jnp.bfloat16),
            jnp.pad(plane_gates, ((0, 0), (0, 8 - local_experts), (0, 0))),
            expert_weights.reshape(-1, *expert_weights.shape[2:]),
            hidden_in,
            cotangent,
            -(-capacity // 16) * 16,
        )
        gain_attend, gain_mixer = gains_all[0], gains_all[1]
    else:
        gate_tables = lax.all_gather(gate_table, "expert", axis=0, tiled=False)
        cotangents = lax.all_gather(cotangent, "expert", axis=0, tiled=True)
        dense_all, gains_all = (
            lax.all_gather(
                dense_weights.astype(jnp.bfloat16), ("dp", "expert"), axis=0, tiled=True
            ),
            lax.all_gather(norm_gains.astype(jnp.bfloat16), ("dp", "expert"), axis=1, tiled=True),
        )
        gain_attend = gains_all[0].astype(jnp.float32)
        gain_mixer = gains_all[1].astype(jnp.float32)
        normed_attend = (inputs * scale_attend * gain_attend).astype(jnp.bfloat16)
        projected = jnp.dot(
            normed_attend, dense_all[:, :qkv_end], preferred_element_type=jnp.float32
        ).astype(jnp.bfloat16)
        query = projected[:, :query_width]
        key_rows = projected[:, query_width : query_width + kv_width]
        value_rows = projected[:, query_width + kv_width :]
        attended, saved_stats = attend_forward(query, key_rows, value_rows, block_rows)
        residual = inputs + jnp.einsum(
            "sq,dq->sd", attended, dense_all[:, qkv_end:shared_base], preferred_element_type=jnp.float32
        )
        scale_mixer = norm_scale(residual)
        normed_mixer = (residual * scale_mixer * gain_mixer).astype(jnp.bfloat16)
        expert_all = lax.all_gather(expert_weights.astype(jnp.bfloat16), "dp", axis=2, tiled=True)
        tokens = lax.all_gather(normed_mixer, "expert", axis=0, tiled=True)
        shared_pre = jnp.dot(
            normed_mixer,
            dense_all[:, shared_base : shared_base + 2 * FFS],
            preferred_element_type=jnp.float32,
        )
        shared_gate = shared_pre[:, :FFS]
        shared_up = shared_pre[:, FFS:]
        shared_act = (jax.nn.silu(shared_gate) * shared_up).astype(jnp.bfloat16)
        shared_out = jnp.einsum(
            "sf,df->sd",
            shared_act,
            dense_all[:, shared_base + 2 * FFS : shared_base + 3 * FFS],
            preferred_element_type=jnp.float32,
        )
        grad_shared_act = jnp.dot(
            cotangent,
            dense_all[:, shared_base + 2 * FFS : shared_base + 3 * FFS],
            preferred_element_type=jnp.float32,
        )
        shared_sig = jax.nn.sigmoid(shared_gate)
        grad_shared_pre = jnp.concatenate(
            [
                grad_shared_act * shared_up * shared_sig * (1.0 + shared_gate * (1.0 - shared_sig)),
                grad_shared_act * jax.nn.silu(shared_gate),
            ],
            1,
        ).astype(jnp.bfloat16)
        grad_shared = jnp.einsum(
            "sf,df->sd",
            grad_shared_pre,
            dense_all[:, shared_base : shared_base + 2 * FFS],
            preferred_element_type=jnp.float32,
        )
        base_out = residual + shared_out
        my_gates = lax.dynamic_slice_in_dim(
            gate_tables, lax.axis_index("expert") * local_experts, local_experts, 1
        ).transpose(1, 0, 2)
        hot = my_gates > 0.0
        earlier = jnp.einsum(
            "est,ut->esu",
            hot.astype(jnp.bfloat16),
            jnp.tril(jnp.ones((length, length), jnp.bfloat16), -1),
            preferred_element_type=jnp.float32,
        ).astype(jnp.int32)
        place = jnp.where(hot, earlier, -1)
        routed_parts, grad_parts, saved = grouped_experts(
            tokens, cotangents, place, my_gates, expert_all, capacity
        )
    if direct:
        (
            expert_sum,
            dense_sum,
            grad_inputs,
            grad_gain_mixer,
            grad_gain_attend,
        ) = scatter_grads(
            grad_parts,
            saved,
            dense_all,
            shared_sum,
            cotangent,
            normed_attend,
            attended,
            residual,
            scale_mixer,
            gain_mixer[None, :],
            grad_shared,
            projected,
            hidden_in,
            gain_attend[None, :],
        )
        expert_grad = expert_sum.reshape(expert_weights.shape).astype(jnp.float32)
        dense_grad = (
            jnp.concatenate([dense_sum[9:], dense_sum[6:9], dense_sum[:6]], 0)
            .transpose(1, 0, 2)
            .reshape(dense_weights.shape)
        )
        grad_gain_mixer, grad_gain_attend = grad_gain_mixer[0], grad_gain_attend[0]
    else:
        routed = lax.psum_scatter(routed_parts, "expert", scatter_dimension=0, tiled=True)
        grad_routed = lax.psum_scatter(grad_parts, "expert", scatter_dimension=0, tiled=True)
        expert_parts = [expert_grads(*kept) for kept in saved]
        expert_grad = lax.psum_scatter(
            sum(part.astype(jnp.float32) for part in expert_parts).astype(jnp.bfloat16),
            "dp",
            scatter_dimension=2,
            tiled=True,
        ).astype(jnp.float32)
        grad_normed = grad_routed.astype(jnp.float32) + grad_shared
        grad_scaled = grad_normed * gain_mixer
        grad_residual = (
            cotangent.astype(jnp.float32)
            + scale_mixer * grad_scaled
            - residual * scale_mixer**3 * jnp.mean(grad_scaled * residual, axis=-1, keepdims=True)
        )
        grad_gain_mixer = jnp.sum(grad_normed * residual * scale_mixer, axis=0)
        grad_attn_low = grad_residual.astype(jnp.bfloat16)
        grad_attended = jnp.dot(
            grad_attn_low, dense_all[:, qkv_end:shared_base], preferred_element_type=jnp.float32
        ).astype(jnp.bfloat16)
        grad_query, grad_key, grad_value = attend_backward(
            query, key_rows, value_rows, grad_attended, saved_stats, block_rows
        )
        grad_projected = jnp.concatenate([grad_query, grad_key, grad_value], 1)
        dense_parts = [
            jnp.einsum("sd,sf->df", left, right, preferred_element_type=jnp.float32)
            for left, right in (
                (normed_attend, grad_projected),
                (grad_attn_low, attended),
                (normed_mixer, grad_shared_pre),
                (cotangent, shared_act),
            )
        ]
        dense_grad = lax.psum_scatter(
            jnp.concatenate([part.astype(jnp.bfloat16) for part in dense_parts], 1),
            ("dp", "expert"),
            scatter_dimension=0,
            tiled=True,
        ).astype(jnp.float32)
        grad_normed_attend = jnp.einsum(
            "sc,dc->sd", grad_projected, dense_all[:, :qkv_end], preferred_element_type=jnp.float32
        )
        grad_scaled_attend = grad_normed_attend * gain_attend
        grad_inputs = (
            grad_residual
            + scale_attend * grad_scaled_attend
            - inputs * scale_attend**3 * jnp.mean(grad_scaled_attend * inputs, axis=-1, keepdims=True)
        )
        grad_gain_attend = jnp.sum(grad_normed_attend * inputs * scale_attend, axis=0)
    gain_grad = lax.psum_scatter(
        jnp.stack([grad_gain_attend, grad_gain_mixer], 0),
        ("dp", "expert"),
        scatter_dimension=1,
        tiled=True,
    )
    dense_moment = MOMENTUM_DECAY * dense_momentum + dense_grad
    expert_moment = MOMENTUM_DECAY * expert_momentum + expert_grad
    stripe, dense_columns = dense_weights.shape
    row_count = stripe * expert_size
    dense_total = dense_columns // FFE
    dense_share = -(-dense_total // expert_size)
    dense_padded = jnp.pad(
        dense_moment.astype(jnp.bfloat16),
        ((0, 0), (0, dense_share * expert_size * FFE - dense_columns)),
    ).reshape(stripe, dense_share * expert_size, FFE).transpose(1, 0, 2)
    expert_units = expert_moment.astype(jnp.bfloat16).reshape(-1, row_count, FFE)
    if direct:
        orth_expert, orth_stripe, routed_received = muon(expert_units, dense_padded, routed_parts)
        routed = lax.dynamic_slice_in_dim(
            routed_parts, lax.axis_index("expert") * length, length, 0
        ).astype(jnp.float32)
        routed = routed + jnp.sum(routed_received.astype(jnp.float32), axis=0)
    else:
        dense_units = lax.all_to_all(
            dense_padded, "expert", split_axis=0, concat_axis=1, tiled=True
        )
        expert_unit_count = expert_units.shape[0]
        base_count = expert_unit_count + dense_share
        unit_count = -(-base_count // dp_size) * dp_size
        all_units = jnp.concatenate(
            [
                expert_units,
                dense_units,
                jnp.zeros((unit_count - base_count, row_count, FFE), jnp.bfloat16),
            ],
            0,
        )
        owned = lax.all_to_all(all_units, "dp", split_axis=0, concat_axis=1, tiled=True)
        orthogonal = newton_schulz(owned)
        orth_units = lax.all_to_all(orthogonal, "dp", split_axis=1, concat_axis=0, tiled=True)
        orth_expert = orth_units[:expert_unit_count]
        orth_stripe = lax.all_to_all(
            orth_units[expert_unit_count:base_count],
            "expert",
            split_axis=1,
            concat_axis=0,
            tiled=True,
        )
    orth_stripe = (
        orth_stripe[:dense_total]
        .transpose(1, 0, 2)
        .reshape(stripe, dense_columns)
        .astype(jnp.float32)
    )
    block_out = (base_out + routed.astype(jnp.float32)).astype(jnp.bfloat16)
    keep_factor = 1.0 - LEARN_RATE * WEIGHT_DECAY
    dense_new = keep_factor * dense_weights - LEARN_RATE * orth_stripe
    expert_new = updated_weights(expert_weights, orth_expert)
    first_new = FIRST_DECAY * gain_first + (1.0 - FIRST_DECAY) * gain_grad
    second_new = SECOND_DECAY * gain_second + (1.0 - SECOND_DECAY) * gain_grad * gain_grad
    step_ratio = (
        first_new
        / (1.0 - FIRST_DECAY**STEP)
        / (jnp.sqrt(second_new / (1.0 - SECOND_DECAY**STEP)) + 1e-08)
    )
    gain_new = norm_gains - GAIN_RATE * step_ratio
    return (
        block_out,
        grad_inputs,
        dense_grad,
        dense_moment,
        dense_new,
        expert_grad,
        expert_moment,
        expert_new,
        gain_grad,
        first_new,
        second_new,
        gain_new,
    )


def solution(mesh):
    in_specs = (
        P(("dp", "expert"), None),
        P(("dp", "expert"), None),
        P(("dp", "expert"), None),
        P(("dp", "expert"), None),
        P(("dp", "expert"), None),
        P(("dp", "expert"), None),
        P("expert", None, "dp", None),
        P("expert", None, "dp", None),
        P(None, ("dp", "expert")),
        P(None, ("dp", "expert")),
        P(None, ("dp", "expert")),
    )
    out_specs = (
        P(("dp", "expert"), None),
        P(("dp", "expert"), None),
        P(("dp", "expert"), None),
        P(("dp", "expert"), None),
        P(("dp", "expert"), None),
        P("expert", None, "dp", None),
        P("expert", None, "dp", None),
        P("expert", None, "dp", None),
        P(None, ("dp", "expert")),
        P(None, ("dp", "expert")),
        P(None, ("dp", "expert")),
        P(None, ("dp", "expert")),
    )
    return jax.shard_map(
        on_device, mesh=mesh, in_specs=in_specs, out_specs=out_specs, check_vma=False
    )
```

```python
import functools

import jax
import jax.numpy as jnp
from jax import lax
from jax.experimental import pallas as pl
from jax.experimental.pallas import tpu as pltpu
from jax.sharding import PartitionSpec as P

HEADS = 12
HD = 128
KVH = 4
FFE = 512
FFS = 1024
NS_STEPS = 5
STEP = 10


POLY_FIRST = 3.4445
POLY_SECOND = -4.775
POLY_THIRD = 2.0315
MOMENTUM_DECAY = 0.95
LEARN_RATE = 0.6
WEIGHT_DECAY = 0.1
GAIN_RATE = 0.8
FIRST_DECAY = 0.9
SECOND_DECAY = 0.95


def norm_scale(values):
    return lax.rsqrt(jnp.mean(values * values, axis=-1, keepdims=True) + 1e-06)


def block_scores(query_block, key_block, first_row, block_rows, last_row):
    score_scale = HD ** (-0.5)
    scores = (
        jnp.einsum("qgrd,kgd->grqk", query_block, key_block, preferred_element_type=jnp.float32)
        * score_scale
    )
    allowed = jnp.arange(last_row)[None, :] <= (first_row + jnp.arange(block_rows))[:, None]
    return jnp.where(allowed, scores, -1e30)


def attend_forward(query, key_rows, value_rows, block_rows):
    length = query.shape[0]
    query_heads = query.reshape(length, KVH, HEADS // KVH, HD)
    key_heads = key_rows.reshape(length, KVH, HD)
    value_heads = value_rows.reshape(length, KVH, HD)
    scores = block_scores(query_heads, key_heads, 0, block_rows, block_rows)
    highest = jnp.max(scores, axis=-1, keepdims=True)
    raised = jnp.exp(scores - highest)
    totals = jnp.sum(raised, axis=-1, keepdims=True)
    weights = (raised / totals).astype(jnp.bfloat16)
    outputs = jnp.einsum("grqk,kgd->qgrd", weights, value_heads, preferred_element_type=jnp.float32)
    saved_stats = [(highest, totals)]
    attended = outputs.reshape(length, HEADS * HD)
    return (attended.astype(jnp.bfloat16), saved_stats)


def attend_backward(query, key_rows, value_rows, grad_attended, saved_stats, block_rows):
    length = query.shape[0]
    score_scale = HD ** (-0.5)
    query_heads = query.reshape(length, KVH, HEADS // KVH, HD)
    grad_heads = grad_attended.reshape(length, KVH, HEADS // KVH, HD)
    key_heads = key_rows.reshape(length, KVH, HD)
    value_heads = value_rows.reshape(length, KVH, HD)
    grad_key = jnp.zeros((length, KVH, HD), jnp.float32)
    grad_value = jnp.zeros((length, KVH, HD), jnp.float32)
    query_parts = []
    for block_index, first_row in enumerate(range(0, length, block_rows)):
        last_row = first_row + block_rows
        scores = block_scores(query_heads, key_heads, first_row, block_rows, last_row)
        highest, totals = saved_stats[block_index]
        weights = jnp.exp(scores - highest) / totals
        grad_weights = jnp.einsum(
            "qgrd,kgd->grqk", grad_heads, value_heads, preferred_element_type=jnp.float32
        )
        inner_sum = jnp.sum(weights * grad_weights, axis=-1, keepdims=True)
        grad_scores = (weights * (grad_weights - inner_sum)).astype(jnp.bfloat16)
        query_parts.append(
            jnp.einsum("grqk,kgd->qgrd", grad_scores, key_heads, preferred_element_type=jnp.float32)
            * score_scale
        )
        grad_key = grad_key.at[:last_row].add(
            jnp.einsum(
                "grqk,qgrd->kgd", grad_scores, query_heads, preferred_element_type=jnp.float32
            )
            * score_scale
        )
        grad_value = grad_value.at[:last_row].add(
            jnp.einsum(
                "grqk,qgrd->kgd",
                weights.astype(jnp.bfloat16),
                grad_heads,
                preferred_element_type=jnp.float32,
            )
        )
    grad_query = query_parts[0].reshape(length, HEADS * HD)
    return (
        grad_query.astype(jnp.bfloat16),
        grad_key.reshape(length, KVH * HD).astype(jnp.bfloat16),
        grad_value.reshape(length, KVH * HD).astype(jnp.bfloat16),
    )


MIB = 2**20
GRAD_STEP = 14
SLOTS = 8
MESH = pl.DeviceIdType.MESH


def matmul(left, right):
    return jnp.dot(left, right, preferred_element_type=jnp.float32)


def matmul_nt(left, right):
    return lax.dot_general(left, right, (((1,), (1,)), ((), ())), preferred_element_type=jnp.float32)


def matmul_tn(left, right):
    return lax.dot_general(left, right, (((0,), (0,)), ((), ())), preferred_element_type=jnp.float32)


def newton_schulz_unit(moment_ref, orthogonal_ref, current, low, identity):
    columns, rows = current.shape
    step = 256
    parts = [pl.ds(index * step, step) for index in range(rows // step)]
    identity[...] = jnp.where(
        lax.broadcasted_iota(jnp.int32, identity.shape, 0)
        == lax.broadcasted_iota(jnp.int32, identity.shape, 1),
        1.0,
        0.0,
    ).astype(jnp.bfloat16)
    squares = jnp.zeros((1, columns), jnp.float32)
    for part in parts:
        values = moment_ref[part, :].astype(jnp.float32)
        squares = squares + jnp.sum(values * values, axis=0, keepdims=True)
    scale = 1.0 / (jnp.sqrt(jnp.sum(squares, axis=1, keepdims=True)) + 1e-07)
    for part in parts:
        scaled = matmul_nt(identity[...], moment_ref[part, :]) * scale
        current[:, part] = scaled
        low[:, part] = scaled.astype(jnp.bfloat16)

    def polynomial():
        gram = matmul_nt(low[...], low[...])
        gram_low = gram.astype(jnp.bfloat16)
        return (POLY_SECOND * gram + POLY_THIRD * matmul(gram_low, gram_low)).astype(jnp.bfloat16)

    @pl.loop(0, NS_STEPS - 1)
    def _(index):
        weights = polynomial()
        for part in parts:
            updated = POLY_FIRST * current[:, part] + matmul(weights, low[:, part])
            current[:, part] = updated
            low[:, part] = updated.astype(jnp.bfloat16)

    weights = polynomial()
    for part in parts:
        updated = POLY_FIRST * current[:, part] + matmul(weights, low[:, part])
        orthogonal_ref[part, :] = updated.T.astype(jnp.bfloat16)


def newton_schulz_kernel(moment_ref, orthogonal_ref, current, low, identity):
    newton_schulz_unit(moment_ref.at[0], orthogonal_ref.at[0], current, low, identity)


def newton_schulz(units):
    count, rows, columns = units.shape
    return pl.pallas_call(
        newton_schulz_kernel,
        grid=(count,),
        in_specs=[pl.BlockSpec((1, rows, columns), lambda unit: (unit, 0, 0))],
        out_specs=pl.BlockSpec((1, rows, columns), lambda unit: (unit, 0, 0)),
        out_shape=jax.ShapeDtypeStruct(units.shape, jnp.bfloat16),
        scratch_shapes=[
            pltpu.VMEM((columns, rows), jnp.float32),
            pltpu.VMEM((columns, rows), jnp.bfloat16),
            pltpu.VMEM((columns, columns), jnp.bfloat16),
        ],
        compiler_params=pltpu.CompilerParams(vmem_limit_bytes=48 * MIB),
        cost_estimate=pl.CostEstimate(
            flops=count * NS_STEPS * 2 * columns * columns * (2 * rows + columns),
            bytes_accessed=count * rows * columns * 4,
            transcendentals=0,
        ),
        name="newton_schulz",
    )(units)


def experts_kernel(
    tokens_ref,
    cotangent_ref,
    place_ref,
    gate_ref,
    weights_ref,
    routed_ref,
    grad_tokens_ref,
    received,
    grad_returned,
    act_ref,
    grad_gate_ref,
    grad_up_ref,
    routed_sum,
    grad_sum,
    chosen,
    weighted,
    grad_received,
):
    expert = pl.program_id(0)
    sequences, slots, length = chosen.shape

    @pl.when(expert == 0)
    def _():
        routed_sum[...] = jnp.zeros_like(routed_sum)
        grad_sum[...] = jnp.zeros_like(grad_sum)

    slot_weights = []
    for sequence in range(sequences):
        rows = pl.ds(sequence * length, length)
        spots = pl.ds(sequence * slots, slots)
        place = place_ref[0, sequence : sequence + 1, :]
        gate = gate_ref[0, sequence : sequence + 1, :]
        hot = lax.broadcasted_iota(jnp.int32, (slots, length), 0) == place
        slot_weight = jnp.sum(jnp.where(hot, gate, 0.0), axis=1, keepdims=True)
        slot_weights.append(slot_weight)
        hot_low = jnp.where(hot, 1.0, 0.0).astype(jnp.bfloat16)
        chosen[sequence] = hot_low
        received[0, spots, :] = matmul(hot_low, tokens_ref[rows, :]).astype(jnp.bfloat16)
        grad_returned[0, spots, :] = (
            matmul(hot_low, cotangent_ref[rows, :]) * slot_weight
        ).astype(jnp.bfloat16)
    tokens = received[0]
    grad_out = grad_returned[0]
    gate_pre = matmul(tokens, weights_ref[0, 0])
    up_pre = matmul(tokens, weights_ref[0, 1])
    gate_sig = jax.nn.sigmoid(gate_pre)
    gate_act = gate_pre * gate_sig
    act = (gate_act * up_pre).astype(jnp.bfloat16)
    act_ref[0] = act
    out = matmul_nt(act, weights_ref[0, 2]).astype(jnp.bfloat16).astype(jnp.float32)
    for sequence in range(sequences):
        spots = slice(sequence * slots, (sequence + 1) * slots)
        weighted[spots, :] = (out[spots] * slot_weights[sequence]).astype(jnp.bfloat16)
    grad_act = matmul(grad_out, weights_ref[0, 2])
    grad_gate = (grad_act * up_pre * gate_sig * (1.0 + gate_pre * (1.0 - gate_sig))).astype(
        jnp.bfloat16
    )
    grad_up = (grad_act * gate_act).astype(jnp.bfloat16)
    grad_gate_ref[0] = grad_gate
    grad_up_ref[0] = grad_up
    grad_received[...] = (
        matmul_nt(grad_gate, weights_ref[0, 0]) + matmul_nt(grad_up, weights_ref[0, 1])
    ).astype(jnp.bfloat16)
    for sequence in range(sequences):
        rows = pl.ds(sequence * length, length)
        spots = pl.ds(sequence * slots, slots)
        routed_sum[rows, :] += matmul_tn(chosen[sequence], weighted[spots, :])
        grad_sum[rows, :] += matmul_tn(chosen[sequence], grad_received[spots, :])

    @pl.when(expert == pl.num_programs(0) - 1)
    def _():
        routed_ref[...] = routed_sum[...].astype(jnp.bfloat16)
        grad_tokens_ref[...] = grad_sum[...].astype(jnp.bfloat16)


def run_experts(tokens, cotangents, place, gates, weights, capacity):
    experts, sequences, length = place.shape
    total, width = tokens.shape
    hidden = weights.shape[-1]
    slots = -(-capacity // 16) * 16
    spots = sequences * slots
    whole = pl.BlockSpec((total, width), lambda expert: (0, 0))
    table = pl.BlockSpec((1, sequences, length), lambda expert: (expert, 0, 0))
    matrices = pl.BlockSpec((1, 3, width, hidden), lambda expert: (expert, 0, 0, 0))
    wide = pl.BlockSpec((1, spots, width), lambda expert: (expert, 0, 0))
    narrow = pl.BlockSpec((1, spots, hidden), lambda expert: (expert, 0, 0))
    return pl.pallas_call(
        experts_kernel,
        grid=(experts,),
        in_specs=[whole, whole, table, table, matrices],
        out_specs=[whole, whole, wide, wide, narrow, narrow, narrow],
        out_shape=[
            *[jax.ShapeDtypeStruct((total, width), jnp.bfloat16)] * 2,
            *[jax.ShapeDtypeStruct((experts, spots, width), jnp.bfloat16)] * 2,
            *[jax.ShapeDtypeStruct((experts, spots, hidden), jnp.bfloat16)] * 3,
        ],
        scratch_shapes=[
            pltpu.VMEM((total, width), jnp.float32),
            pltpu.VMEM((total, width), jnp.float32),
            pltpu.VMEM((sequences, slots, length), jnp.bfloat16),
            pltpu.VMEM((spots, width), jnp.bfloat16),
            pltpu.VMEM((spots, width), jnp.bfloat16),
        ],
        compiler_params=pltpu.CompilerParams(vmem_limit_bytes=63 * MIB),
        cost_estimate=pl.CostEstimate(
            flops=experts * (12 * spots * width * hidden + 8 * spots * length * width),
            bytes_accessed=2 * weights.size + 16 * tokens.size,
            transcendentals=experts * spots * hidden,
        ),
        name="experts",
    )(tokens, cotangents, place, gates, weights)


def expert_grads_kernel(
    received_ref, grad_returned_ref, act_ref, grad_gate_ref, grad_up_ref, grad_weights_ref
):
    received, grad_returned = received_ref[0], grad_returned_ref[0]
    grad_weights_ref[0, 0] = matmul_tn(received, grad_gate_ref[0]).astype(jnp.bfloat16)
    grad_weights_ref[0, 1] = matmul_tn(received, grad_up_ref[0]).astype(jnp.bfloat16)
    grad_weights_ref[0, 2] = matmul_tn(grad_returned, act_ref[0]).astype(jnp.bfloat16)


def expert_grads(received, grad_returned, act, grad_gate, grad_up):
    experts, spots, width = received.shape
    hidden = act.shape[-1]
    wide = pl.BlockSpec((1, spots, width), lambda expert: (expert, 0, 0))
    narrow = pl.BlockSpec((1, spots, hidden), lambda expert: (expert, 0, 0))
    return pl.pallas_call(
        expert_grads_kernel,
        grid=(experts,),
        in_specs=[wide, wide, narrow, narrow, narrow],
        out_specs=pl.BlockSpec((1, 3, width, hidden), lambda expert: (expert, 0, 0, 0)),
        out_shape=jax.ShapeDtypeStruct((experts, 3, width, hidden), jnp.bfloat16),
        compiler_params=pltpu.CompilerParams(vmem_limit_bytes=48 * MIB),
        name="expert_grads",
    )(received, grad_returned, act, grad_gate, grad_up)


def grouped_experts(tokens, cotangents, place, gates, weights, capacity):
    experts, sequences, length = place.shape
    group = min(4, sequences)
    routed, grad_tokens, saved = [], [], []
    for first in range(0, sequences, group):
        rows = slice(first * length, (first + group) * length)
        part = slice(first, first + group)
        routed_part, grad_part, *kept = run_experts(
            tokens[rows], cotangents[rows], place[:, part], gates[:, part], weights, capacity
        )
        routed.append(routed_part)
        grad_tokens.append(grad_part)
        saved.append(kept)

    def joined(parts):
        return parts[0] if len(parts) == 1 else jnp.concatenate(parts, 0)

    return joined(routed), joined(grad_tokens), saved


def flipped(index, bit):
    unit = 2**bit
    return index + unit * (1 - 2 * ((index // unit) % 2))


class Links:
    def __init__(self, semaphores):
        self.semaphores = semaphores
        self.taken = 0
        self.dp = lax.axis_index("dp")
        self.z = lax.axis_index("expert")
        self.upper = self.z // 2
        self.position = self.z * (1 - 2 * self.upper) + 3 * self.upper
        self.step = 1 - 2 * self.upper
        self.core = (flipped(self.dp, 0), self.z)
        self.along_x = (flipped(self.dp, 1), self.z)
        self.along_y = (flipped(self.dp, 2), self.z)
        self.inward = (self.dp, self.z + self.step)
        self.outward = (self.dp, self.z - self.step)
        self.further = (self.dp, self.z + 2 * self.step)
        self.pending = []

    def order(self, index):
        near = (self.position + index) % 2 if index < 2 else index
        return near * self.step + 3 * self.upper

    def take(self, count=1):
        first = self.taken
        self.taken += count
        return first

    def barrier(self):
        barrier = pltpu.get_barrier_semaphore()
        for device in (self.core, self.along_x, self.along_y, self.inward, self.further):
            pl.semaphore_signal(barrier, inc=1, device_id=device, device_id_type=MESH)

        @pl.when(self.position == 1)
        def _():
            pl.semaphore_signal(barrier, inc=1, device_id=self.outward, device_id_type=MESH)

        pl.semaphore_wait(barrier, 5 + self.position)

    def copy_with(self, source, target, send, receive, device):
        return pltpu.make_async_remote_copy(
            src_ref=source,
            dst_ref=target,
            send_sem=send,
            recv_sem=receive,
            device_id=device,
            device_id_type=MESH,
        )

    def copy(self, source, target, send, receive, device):
        return self.copy_with(
            source, target, self.semaphores.at[send], self.semaphores.at[receive], device
        )

    def send(self, source, target, receive, device, position=None):
        copy = self.copy(source, target, self.take(), receive, device)
        if position is None:
            copy.start()
        else:
            pl.when(self.position == position)(copy.start)
        self.pending.append((copy, position))

    def arrived(self, region, receive):
        self.copy(region, region, receive, receive, self.core).wait_recv()

    def finish(self):
        for copy, position in self.pending:
            if position is None:
                copy.wait_send()
            else:
                pl.when(self.position == position)(copy.wait_send)


class LineGather:
    def __init__(self, links, region, own=None):
        self.links, self.region = links, region
        self.receives = links.take(4)
        self.own = region(links.z) if own is None else own

    def start(self):
        links = self.links
        target, receive = self.region(links.z), self.receives + links.z
        links.send(self.own, target, receive, links.further)
        links.send(self.own, target, receive, links.inward)
        links.send(self.own, target, receive, links.outward, 1)

    def relay(self):
        links = self.links
        source = links.order(3)
        block = self.region(source)

        @pl.when(links.position == 1)
        def _():
            links.arrived(block, self.receives + source)

        links.send(block, block, self.receives + source, links.outward, 1)

    def arrive(self, index):
        links = self.links
        source = links.order(index)

        def wait():
            links.arrived(self.region(source), self.receives + source)

        if index < 3:
            wait()
        else:
            pl.when(links.position == 0)(wait)


class PlaneGather:
    def __init__(self, links, region, parity, own=None):
        self.links, self.region, self.parity = links, region, parity
        self.receives = links.take(7)
        self.own = region(links.dp) if own is None else own

    def start(self):
        links, first = self.links, self.receives
        target = self.region(links.dp)
        links.send(self.own, target, first, links.along_x)
        links.send(self.own, target, first + 1, links.along_y)
        links.send(self.own, target, first + 2, links.core)

    def forward(self):
        links, first = self.links, self.receives
        across = self.region(flipped(links.dp, 1))
        links.arrived(across, first)
        if self.parity == 0:
            links.send(across, across, first + 3, links.along_y)
        links.send(across, across, first + 4, links.core)
        along = self.region(flipped(links.dp, 2))
        links.arrived(along, first + 1)
        if self.parity == 1:
            links.send(along, along, first + 3, links.along_x)
        links.send(along, along, first + 5, links.core)

    def last(self):
        links, first = self.links, self.receives
        corner = self.region(flipped(flipped(links.dp, 1), 2))
        links.arrived(corner, first + 3)
        links.send(corner, corner, first + 6, links.core)

    def complete(self):
        links, first = self.links, self.receives
        other = flipped(links.dp, 0)
        links.arrived(self.region(other), first + 2)
        links.arrived(self.region(flipped(other, 1)), first + 4)
        links.arrived(self.region(flipped(other, 2)), first + 5)
        links.arrived(self.region(flipped(flipped(other, 1), 2)), first + 6)


ANY = pl.BlockSpec(memory_space=pl.ANY)


def front_kernel(
    stripe_ref,
    gates_ref,
    masters_ref,
    hidden_ref,
    cotangent_ref,
    dense_ref,
    weights_ref,
    cotangents_ref,
    tokens_ref,
    routed_parts_ref,
    grad_parts_ref,
    received_ref,
    grad_returned_ref,
    act_ref,
    grad_gate_ref,
    grad_up_ref,
    normed_attend_ref,
    projected_ref,
    attended_ref,
    residual_ref,
    scale_ref,
    normed_mixer_ref,
    shared_act_ref,
    grad_shared_pre_ref,
    grad_shared_ref,
    base_ref,
    gains_ref,
    shared_sum_ref,
    matrices,
    extra,
    all_gates,
    places,
    my_gates,
    chosen,
    forward_slots,
    backward_slots,
    narrow,
    pair_sum,
    corner_x,
    corner_y,
    side_x,
    side_y,
    semaphores,
    shard_out,
    shard_in,
    local,
    load_sems,
    expert_sems,
    shared_sems,
):
    links = Links(semaphores)
    stripe, columns = stripe_ref.shape
    length, width = hidden_ref.shape
    panels, rows, hidden = masters_ref.shape
    experts = panels // 3
    slots = chosen.shape[1] // experts
    first_panels = 8
    middle = first_panels * hidden + extra.shape[1]
    halves = ((0, middle), (middle, columns - middle))
    query_width = HEADS * HD
    kv_width = KVH * HD
    ahead = 4

    def dense_region(dp, z, half):
        first, count = halves[half]
        row = pl.multiple_of((dp * 4 + z) * stripe, stripe)
        return dense_ref.at[pl.ds(row, stripe), pl.ds(first, count)]

    def own(half):
        first, count = halves[half]
        return stripe_ref.at[:, pl.ds(first, count)]

    def sequence(ref, z):
        return ref.at[pl.ds(pl.multiple_of(z * length, length), length), :]

    def shard_region(dp, panel):
        return weights_ref.at[panel, pl.ds(pl.multiple_of(dp * rows, rows), rows), :]

    lines = [
        LineGather(links, functools.partial(dense_region, links.dp, half=half), own(half))
        for half in range(2)
    ]
    cotangents = LineGather(links, functools.partial(sequence, cotangents_ref), cotangent_ref)
    tokens = LineGather(links, functools.partial(sequence, tokens_ref), normed_mixer_ref)
    gates = LineGather(links, lambda z: all_gates.at[z], gates_ref)
    planes = [
        [
            PlaneGather(
                links,
                functools.partial(dense_region, z=links.order(index), half=half),
                index % 2,
                own(half) if index == 0 else None,
            )
            for index in range(4)
        ]
        for half in range(2)
    ]

    def shard_copy(kind, panel, source_dp, device):
        block = shard_region(source_dp, panel)
        return links.copy_with(
            block, block, shard_out.at[kind, panel], shard_in.at[kind, panel], device
        )

    dp = links.dp
    dp_core, dp_x, dp_y = flipped(dp, 0), flipped(dp, 1), flipped(dp, 2)
    dp_corner = flipped(dp_x, 2)

    def hop(kind, panel):
        source, device = (
            (dp, links.along_x),
            (dp, links.along_y),
            (dp, links.core),
            None,
            (dp_x, links.core),
            (dp_y, links.core),
            (dp_corner, links.core),
        )[kind]
        return shard_copy(kind, panel, source, device)

    def corner_copy(panel, parity):
        if parity == 0:
            return shard_copy(3, panel, dp_x, links.along_y)
        return shard_copy(3, panel, dp_y, links.along_x)

    def shard_arrived(kind, panel, source_dp):
        shard_copy(kind, panel, source_dp, links.core).wait_recv()

    def shard_start(panel):
        for kind in range(3):
            hop(kind, panel).start()

    def shard_forward(panel):
        shard_arrived(0, panel, dp_x)
        pl.when(panel % 2 == 0)(corner_copy(panel, 0).start)
        hop(4, panel).start()
        shard_arrived(1, panel, dp_y)
        pl.when(panel % 2 == 1)(corner_copy(panel, 1).start)
        hop(5, panel).start()

    def shard_last(panel):
        shard_arrived(3, panel, dp_corner)
        hop(6, panel).start()

    def shard_complete(panel):
        shard_arrived(2, panel, dp_core)
        shard_arrived(4, panel, flipped(dp_core, 1))
        shard_arrived(5, panel, flipped(dp_core, 2))
        shard_arrived(6, panel, flipped(flipped(dp_core, 1), 2))

    def shard_finish(panel):
        for kind in (0, 1, 2, 4, 5, 6):
            hop(kind, panel).wait_send()
        corner_copy(panel, 0).wait_send()

    def exchange(panel):
        shard_forward(panel)
        if panel + ahead < panels:
            shard_start(panel + ahead)
        if panel >= 3:
            shard_last(panel - 3)

    local_copies = [
        pltpu.make_async_copy(source, target, local.at[index])
        for index, (source, target) in enumerate(
            (
                (
                    stripe_ref,
                    dense_ref.at[
                        pl.ds(pl.multiple_of((links.dp * 4 + links.z) * stripe, stripe), stripe), :
                    ],
                ),
                (gates_ref, all_gates.at[links.z]),
                (cotangent_ref, sequence(cotangents_ref, links.z)),
            )
        )
    ]
    token_copy = pltpu.make_async_copy(
        normed_mixer_ref, sequence(tokens_ref, links.z), local.at[3]
    )

    def dense_column(panel):
        return panel * hidden + (0 if panel < first_panels else extra.shape[1])

    loads = [
        pltpu.make_async_copy(
            dense_ref.at[:, pl.ds(dense_column(panel), hidden)],
            matrices.at[panel],
            load_sems.at[panel],
        )
        for panel in range(14)
    ]
    extra_load = pltpu.make_async_copy(
        dense_ref.at[:, pl.ds(first_panels * hidden, extra.shape[1])], extra, load_sems.at[14]
    )

    def half_columns(panel):
        return pl.ds(pl.multiple_of(panel % 2 * hidden, hidden), hidden)

    def master_load(panel):
        return pltpu.make_async_copy(
            masters_ref.at[panel],
            grad_shared_ref.at[pl.ds(0, rows), half_columns(panel)],
            expert_sems.at[0, panel % 2],
        )

    def master_store(panel):
        return pltpu.make_async_copy(
            shared_act_ref.at[pl.ds(0, rows), half_columns(panel)],
            shard_region(dp, panel),
            expert_sems.at[1, panel % 2],
        )

    master_load(0).start()
    links.barrier()
    lines[0].start()
    planes[0][0].start()
    lines[1].start()
    gates.start()
    for copy in local_copies:
        copy.start()

    def round_masters(first, last):
        @pl.loop(first, last)
        def _(panel):
            master_load(panel).wait()

            @pl.when(panel + 1 < panels)
            def _():
                master_load(panel + 1).start()

            @pl.when(panel >= 2)
            def _():
                master_store(panel - 2).wait()

            shared_act_ref[:rows, half_columns(panel)] = grad_shared_ref[
                :rows, half_columns(panel)
            ].astype(jnp.bfloat16)
            master_store(panel).start()

    lines[0].arrive(1)
    planes[0][1].start()
    lines[0].arrive(2)
    planes[0][2].start()
    round_masters(0, panels // 3)
    for panel in range(2):
        shard_start(panel)
    planes[0][0].forward()
    lines[0].relay()
    lines[0].arrive(3)
    planes[0][3].start()
    planes[0][1].forward()
    lines[1].relay()
    round_masters(panels // 3, panels)
    for panel in (panels - 2, panels - 1):
        master_store(panel).wait()
    for panel in range(2, ahead):
        shard_start(panel)
    planes[1][0].start()
    planes[0][2].forward()
    lines[1].arrive(1)
    planes[1][1].start()
    planes[0][3].forward()
    cotangents.start()
    gates.relay()
    lines[1].arrive(2)
    planes[1][2].start()
    for plane in planes[0]:
        plane.last()
    planes[1][0].forward()
    for plane in planes[0]:
        plane.complete()
    local_copies[0].wait()
    extra_load.start()
    for copy in loads[:first_panels]:
        copy.start()

    rows_step = 32

    def norm_rows(source, gain, scale_out, target):
        @pl.loop(0, length // rows_step)
        def _(index):
            part = pl.ds(index * rows_step, rows_step)
            values = source[part, :].astype(jnp.float32)
            scale = lax.rsqrt(jnp.mean(values * values, axis=-1, keepdims=True) + 1e-06)
            if scale_out is not None:
                scale_out[part, :] = scale
            target[part, :] = (values * scale * gains_ref[gain : gain + 1, :]).astype(jnp.bfloat16)

    def project():
        extra_load.wait()
        gains_ref[...] = extra[...].astype(jnp.float32).T[:8, :]
        norm_rows(hidden_ref, 0, None, normed_attend_ref)
        for panel in range(5):
            loads[panel].wait()
            projected_ref[:, panel * hidden : (panel + 1) * hidden] = matmul(
                normed_attend_ref[...], matrices[panel]
            ).astype(jnp.bfloat16)

    def attend(group):
        key_rows = projected_ref[:, query_width + group * HD : query_width + (group + 1) * HD]
        value_first = query_width + kv_width + group * HD
        value_rows = projected_ref[:, value_first : value_first + HD]
        row = lax.broadcasted_iota(jnp.int32, (length, length), 0)
        column = lax.broadcasted_iota(jnp.int32, (length, length), 1)
        per_group = HEADS // KVH
        for head in range(group * per_group, (group + 1) * per_group):
            spot = slice(head * HD, (head + 1) * HD)
            scores = matmul_nt(projected_ref[:, spot], key_rows) * HD ** (-0.5)
            scores = jnp.where(column <= row, scores, -1e30)
            raised = jnp.exp(scores - jnp.max(scores, axis=-1, keepdims=True))
            shares = (raised / jnp.sum(raised, axis=-1, keepdims=True)).astype(jnp.bfloat16)
            attended_ref[:, spot] = matmul(shares, value_rows).astype(jnp.bfloat16)

    def join():
        for part in range(3):
            loads[5 + part].wait()
            update = matmul_nt(
                attended_ref[:, part * hidden : (part + 1) * hidden], matrices[5 + part]
            )
            if part == 0:
                residual_ref[...] = hidden_ref[...].astype(jnp.float32) + update
            else:
                residual_ref[...] += update
        norm_rows(residual_ref, 1, scale_ref, normed_mixer_ref)
        tokens.start()
        token_copy.start()

    def shared(part):
        spot = slice(part * hidden, (part + 1) * hidden)
        for panel in (8, 10, 12):
            loads[panel + part].wait()
        gate = matmul(normed_mixer_ref[...], matrices[8 + part])
        up = matmul(normed_mixer_ref[...], matrices[10 + part])
        sig = jax.nn.sigmoid(gate)
        gate_act = gate * sig
        shared_act_ref[:, spot] = (gate_act * up).astype(jnp.bfloat16)
        grad_act = matmul(cotangent_ref[...], matrices[12 + part])
        grad_shared_pre_ref[:, spot] = (
            grad_act * up * sig * (1.0 + gate * (1.0 - sig))
        ).astype(jnp.bfloat16)
        up_spot = slice((2 + part) * hidden, (3 + part) * hidden)
        grad_shared_pre_ref[:, up_spot] = (grad_act * gate_act).astype(jnp.bfloat16)

    def shared_back(part):
        spot = slice(part * hidden, (part + 1) * hidden)
        up_spot = slice((2 + part) * hidden, (3 + part) * hidden)
        grad = matmul_nt(grad_shared_pre_ref[:, spot], matrices[8 + part]) + matmul_nt(
            grad_shared_pre_ref[:, up_spot], matrices[10 + part]
        )
        out = matmul_nt(shared_act_ref[:, spot], matrices[12 + part])
        if part == 0:
            grad_shared_ref[...] = grad
            base_ref[...] = residual_ref[...] + out
        else:
            grad_shared_ref[...] += grad
            base_ref[...] += out

    def place_slots():
        local_copies[1].wait()
        before = (
            lax.broadcasted_iota(jnp.int32, (length, length), 0)
            < lax.broadcasted_iota(jnp.int32, (length, length), 1)
        )
        earlier_mask = jnp.where(before, 1.0, 0.0).astype(jnp.bfloat16)
        for source in range(4):
            gate = all_gates[source, links.z]
            hot = gate > 0.0
            earlier = matmul(jnp.where(hot, 1.0, 0.0).astype(jnp.bfloat16), earlier_mask)
            place = jnp.where(hot, earlier, -1.0).astype(jnp.int32)
            for expert in range(experts):
                places[expert, source : source + 1, :] = place[expert : expert + 1, :]
                my_gates[expert, source : source + 1, :] = gate[expert : expert + 1, :]

    core, chip = dp % 2, dp // 2
    chip_x, chip_y = flipped(chip, 0), flipped(chip, 1)
    chip_corner = flipped(chip_x, 1)
    shared_panels = pair_sum.shape[0]
    half = rows // 2
    quarter = width // 4

    ring = matrices.at[13]

    def ring_rows(index, which):
        return pl.ds(pl.multiple_of((2 * index + which) * rows, rows), rows)

    def pair_copy(panel, index):
        return links.copy_with(
            ring.at[ring_rows(index, 1 - core)],
            pair_sum.at[panel, index],
            shared_sems.at[0, 0, panel],
            shared_sems.at[1, 0, panel],
            links.core,
        )

    def shared_copy(kind, panel):
        source, target, device = (
            (pair_sum.at[panel], pair_sum.at[panel], links.core),
            (pair_sum.at[panel, chip_corner, pl.ds(0, half)], corner_x.at[panel], links.along_x),
            (pair_sum.at[panel, chip_corner, pl.ds(half, half)], corner_y.at[panel], links.along_y),
            (pair_sum.at[panel, chip_x], side_x.at[panel], links.along_x),
            (pair_sum.at[panel, chip_y], side_y.at[panel], links.along_y),
        )[kind]
        return links.copy_with(
            source, target, shared_sems.at[0, kind, panel], shared_sems.at[1, kind, panel], device
        )

    def shared_fill(panel):
        left_ref = normed_mixer_ref if panel < 4 else cotangent_ref
        right_ref = grad_shared_pre_ref if panel < 4 else shared_act_ref
        first = (panel if panel < 4 else panel - 4) * hidden
        right = right_ref[:, first : first + hidden]
        for index in range(4):
            part = matmul_tn(left_ref[:, index * quarter : (index + 1) * quarter], right)
            ring[index * quarter : (index + 1) * quarter, :] = part.astype(jnp.bfloat16)
        for index in range(4):
            pair_copy(panel, index).start()

    def shared_pair(panel):
        shared_copy(0, panel).wait()
        for index in range(4):
            pair_sum[panel, index] = (
                pair_sum[panel, index].astype(jnp.float32)
                + ring[ring_rows(index, core), :].astype(jnp.float32)
            ).astype(jnp.bfloat16)

    def shared_corners(panel):
        for kind in (1, 2):
            shared_copy(kind, panel).start()

    def shared_sides(panel):
        for kind in (1, 2):
            shared_copy(kind, panel).wait()
        pair_sum[panel, chip_y, :half] = (
            pair_sum[panel, chip_y, :half].astype(jnp.float32)
            + corner_x[panel].astype(jnp.float32)
        ).astype(jnp.bfloat16)
        pair_sum[panel, chip_x, half:] = (
            pair_sum[panel, chip_x, half:].astype(jnp.float32)
            + corner_y[panel].astype(jnp.float32)
        ).astype(jnp.bfloat16)
        for kind in (3, 4):
            shared_copy(kind, panel).start()

    def shared_total(panel):
        for kind in (3, 4):
            shared_copy(kind, panel).wait()
        value = (
            pair_sum[panel, chip].astype(jnp.float32)
            + side_x[panel].astype(jnp.float32)
            + side_y[panel].astype(jnp.float32)
        )
        matrices[12, pl.ds(panel % 2 * rows, rows), :] = value.astype(jnp.bfloat16)

    def shared_store(panel):
        return pltpu.make_async_copy(
            matrices.at[12, pl.ds(panel % 2 * rows, rows)],
            shared_sum_ref.at[panel],
            local.at[4 + panel % 2],
        )

    project()
    lines[1].arrive(3)
    planes[1][3].start()
    planes[1][1].forward()
    attend(0)
    attend(1)
    planes[1][2].forward()
    attend(2)
    attend(3)
    planes[1][3].forward()
    cotangents.relay()
    join()
    for plane in planes[1]:
        plane.last()
    for index in range(1, 4):
        gates.arrive(index)
    place_slots()
    for plane in planes[1]:
        plane.complete()
    for copy in loads[first_panels:]:
        copy.start()
    exchange(0)
    shared(0)
    exchange(1)
    shared(1)
    exchange(2)
    shared_back(0)
    exchange(3)
    shared_back(1)
    exchange(4)
    shared_fill(0)
    tokens.relay()
    for panel in range(5, 11):
        exchange(panel)
        shared_pair(panel - 5)
        shared_corners(panel - 5)
        if panel < 10:
            shared_fill(panel - 4)
    for index in range(1, 4):
        cotangents.arrive(index)
        tokens.arrive(index)
    local_copies[2].wait()
    token_copy.wait()
    token_loads = [
        pltpu.make_async_copy(
            source.at[:, pl.ds(part * hidden, hidden)],
            matrices.at[first + part, pl.ds(0, 4 * length)],
            load_sems.at[first + part],
        )
        for first, source in ((6, tokens_ref), (9, cotangents_ref))
        for part in range(3)
    ]
    for copy in token_loads:
        copy.start()
    slot_iota = lax.broadcasted_iota(jnp.int32, (slots, length), 0)

    def slot_gate(expert, source):
        hot = slot_iota == places[expert, pl.ds(source, 1), :]
        return jnp.sum(
            jnp.where(hot, my_gates[expert, pl.ds(source, 1), :], 0.0), axis=1, keepdims=True
        )

    for source in range(4):
        for expert in range(experts):
            hot = slot_iota == places[expert, source : source + 1, :]
            chosen[source, expert * slots : (expert + 1) * slots, :] = jnp.where(
                hot, 1.0, 0.0
            ).astype(jnp.bfloat16)
    exchange(11)
    for copy in token_loads:
        copy.wait()

    @pl.loop(0, 4)
    def _(source):
        part = pl.ds(source * length, length)
        spots = pl.ds(pl.multiple_of(source * slots, slots), slots)
        slot_gates = [slot_gate(expert, source) for expert in range(experts)]
        for block in range(3):
            spot = pl.ds(block * hidden, hidden)
            token_slots = matmul(chosen[source], matrices[6 + block, part, :])
            grad_slots = matmul(chosen[source], matrices[9 + block, part, :])
            for expert in range(experts):
                rows_of = slice(expert * slots, (expert + 1) * slots)
                forward_slots[expert, spots, spot] = token_slots[rows_of].astype(jnp.bfloat16)
                backward_slots[expert, spots, spot] = (
                    grad_slots[rows_of] * slot_gates[expert]
                ).astype(jnp.bfloat16)

    def slot_stores(expert):
        return [
            pltpu.make_async_copy(
                source.at[expert], target.at[expert], expert_sems.at[2 + index, expert]
            )
            for index, (source, target) in enumerate(
                ((forward_slots, received_ref), (backward_slots, grad_returned_ref))
            )
        ]

    def narrow_stores(expert):
        buffer = expert % 2
        return [
            pltpu.make_async_copy(
                narrow.at[buffer, index], target.at[expert], expert_sems.at[4 + buffer, index]
            )
            for index, target in enumerate((act_ref, grad_gate_ref, grad_up_ref))
        ]

    def weight_loads(expert):
        buffer = expert % 2
        return [
            pltpu.make_async_copy(
                weights_ref.at[3 * expert + matrix],
                matrices.at[3 * buffer + matrix],
                expert_sems.at[6 + buffer, matrix],
            )
            for matrix in range(3)
        ]

    def fetch(expert):
        for matrix, copy in enumerate(weight_loads(expert)):
            shard_complete(3 * expert + matrix)
            copy.start()

    for expert in range(experts):
        for copy in slot_stores(expert):
            copy.start()
    fetch(0)

    @pl.loop(0, experts)
    def _(expert):
        buffer = expert % 2
        loaded = weight_loads(expert)

        @pl.when(expert >= 2)
        def _():
            for copy in narrow_stores(expert - 2):
                copy.wait()

        received = forward_slots[expert]
        grad_out = backward_slots[expert]
        loaded[0].wait()
        gate_pre = matmul(received, matrices[3 * buffer])
        loaded[1].wait()
        up_pre = matmul(received, matrices[3 * buffer + 1])
        loaded[2].wait()
        grad_act = matmul(grad_out, matrices[3 * buffer + 2])
        gate_sig = jax.nn.sigmoid(gate_pre)
        gate_act = gate_pre * gate_sig
        act = (gate_act * up_pre).astype(jnp.bfloat16)
        grad_gate = (grad_act * up_pre * gate_sig * (1.0 + gate_pre * (1.0 - gate_sig))).astype(
            jnp.bfloat16
        )
        grad_up = (grad_act * gate_act).astype(jnp.bfloat16)
        narrow[buffer, 0] = act
        narrow[buffer, 1] = grad_gate
        narrow[buffer, 2] = grad_up
        for copy in narrow_stores(expert):
            copy.start()
        for copy in slot_stores(expert):
            copy.wait()
        slot_gates = jnp.concatenate([slot_gate(expert, source) for source in range(4)], 0)
        for block in range(3):
            rows_of = pl.ds(block * hidden, hidden)
            spot = pl.ds(block * hidden, hidden)
            out = matmul_nt(act, matrices[3 * buffer + 2, rows_of, :]).astype(jnp.bfloat16)
            forward_slots[expert, :, spot] = (
                out.astype(jnp.float32) * slot_gates
            ).astype(jnp.bfloat16)
            backward_slots[expert, :, spot] = (
                matmul_nt(grad_gate, matrices[3 * buffer, rows_of, :])
                + matmul_nt(grad_up, matrices[3 * buffer + 1, rows_of, :])
            ).astype(jnp.bfloat16)

        later = (
            (lambda: exchange(12), lambda: shared_sides(0)),
            (lambda: exchange(13), lambda: shared_sides(1)),
            (lambda: exchange(14), lambda: shared_sides(2)),
            (lambda: exchange(15), lambda: exchange(16), lambda: shard_last(14)),
            (
                lambda: shard_forward(17),
                lambda: shared_sides(3),
                lambda: shared_sides(4),
                lambda: shared_sides(5),
                lambda: shard_last(15),
                lambda: shard_last(16),
                lambda: shard_last(17),
            ),
        )
        for done, calls in enumerate(later):

            @pl.when(expert == done)
            def _():
                for call in calls:
                    call()

        @pl.when(expert + 1 < experts)
        def _():
            fetch(expert + 1)

    for expert in (experts - 2, experts - 1):
        for copy in narrow_stores(expert):
            copy.wait()
    out_copies = []
    for first, values, target in ((0, backward_slots, grad_parts_ref), (3, forward_slots, routed_parts_ref)):
        for block in range(3):
            spot = slice(block * hidden, (block + 1) * hidden)
            for source in range(4):
                slots_of = jnp.concatenate(
                    [
                        values[expert, source * slots : (source + 1) * slots, spot]
                        for expert in range(experts)
                    ],
                    0,
                )
                matrices[first + block, source * length : (source + 1) * length, :] = matmul_tn(
                    chosen[source], slots_of
                ).astype(jnp.bfloat16)
            out_copies.append(
                pltpu.make_async_copy(
                    matrices.at[first + block, pl.ds(0, 4 * length)],
                    target.at[:, pl.ds(block * hidden, hidden)],
                    load_sems.at[first + block],
                )
            )
            out_copies[-1].start()
    @pl.loop(0, panels)
    def _(panel):
        shard_finish(panel)

    for panel in range(shared_panels):
        if panel >= 2:
            shared_store(panel - 2).wait()
        shared_total(panel)
        shared_store(panel).start()
    for panel in (shared_panels - 2, shared_panels - 1):
        shared_store(panel).wait()
    for copy in out_copies:
        copy.wait()

    links.finish()


def front(stripe, gates, masters, hidden_in, cotangent, slots):
    length, width = cotangent.shape
    stripe_rows, columns = stripe.shape
    panels, rows, hidden = masters.shape
    experts = panels // 3
    low, full = jnp.bfloat16, jnp.float32
    vmem = pl.BlockSpec(memory_space=pltpu.VMEM)
    query_width = HEADS * HD
    spots = 4 * slots
    return pl.pallas_call(
        front_kernel,
        in_specs=[ANY] * 3 + [vmem] * 2,
        out_specs=[ANY] * 11 + [vmem] * 11 + [ANY],
        out_shape=[
            jax.ShapeDtypeStruct((stripe_rows * 32, columns), low),
            jax.ShapeDtypeStruct((panels, rows * 8, hidden), low),
            *[jax.ShapeDtypeStruct((length * 4, width), low)] * 4,
            *[jax.ShapeDtypeStruct((experts, spots, width), low)] * 2,
            *[jax.ShapeDtypeStruct((experts, spots, hidden), low)] * 3,
            jax.ShapeDtypeStruct((length, width), low),
            jax.ShapeDtypeStruct((length, query_width + 2 * KVH * HD), low),
            jax.ShapeDtypeStruct((length, query_width), low),
            jax.ShapeDtypeStruct((length, width), full),
            jax.ShapeDtypeStruct((length, 1), full),
            jax.ShapeDtypeStruct((length, width), low),
            jax.ShapeDtypeStruct((length, FFS), low),
            jax.ShapeDtypeStruct((length, 2 * FFS), low),
            jax.ShapeDtypeStruct((length, width), full),
            jax.ShapeDtypeStruct((length, width), full),
            jax.ShapeDtypeStruct((8, width), full),
            jax.ShapeDtypeStruct((6, rows, hidden), low),
        ],
        scratch_shapes=[
            pltpu.VMEM((14, width, hidden), low),
            pltpu.VMEM((width, 128), low),
            pltpu.VMEM((4, 4, 8, length), full),
            pltpu.VMEM((experts, 4, length), jnp.int32),
            pltpu.VMEM((experts, 4, length), full),
            pltpu.VMEM((4, experts * slots, length), low),
            pltpu.VMEM((experts, spots, width), low),
            pltpu.VMEM((experts, spots, width), low),
            pltpu.VMEM((2, 3, spots, hidden), low),
            pltpu.VMEM((6, 4, rows, hidden), low),
            pltpu.VMEM((6, rows // 2, hidden), low),
            pltpu.VMEM((6, rows // 2, hidden), low),
            pltpu.VMEM((6, rows, hidden), low),
            pltpu.VMEM((6, rows, hidden), low),
            pltpu.SemaphoreType.DMA((170,)),
            pltpu.SemaphoreType.DMA((7, panels)),
            pltpu.SemaphoreType.DMA((7, panels)),
            pltpu.SemaphoreType.DMA((6,)),
            pltpu.SemaphoreType.DMA((15,)),
            pltpu.SemaphoreType.DMA((8, 6)),
            pltpu.SemaphoreType.DMA((2, 5, 6)),
        ],
        compiler_params=pltpu.CompilerParams(
            collective_id=1, has_side_effects=True, vmem_limit_bytes=63 * MIB
        ),
        name="front",
    )(stripe, gates, masters, hidden_in, cotangent)


def scatter_kernel(
    grad_parts_ref,
    received_ref,
    grad_returned_ref,
    act_ref,
    grad_gate_ref,
    grad_up_ref,
    dense_ref,
    shared_sum_ref,
    cotangent_ref,
    normed_attend_ref,
    attended_ref,
    residual_ref,
    scale_ref,
    gain_ref,
    grad_shared_ref,
    projected_ref,
    hidden_ref,
    gain_attend_ref,
    momentum_ref,
    expert_sum_ref,
    dense_grad_ref,
    dense_moment_ref,
    dense_units_ref,
    grad_input_ref,
    grad_gain_ref,
    ring,
    pair_sum,
    corner_x,
    corner_y,
    side_x,
    side_y,
    staged,
    wide,
    narrow,
    left,
    right,
    out_weights,
    grad_tokens,
    grad_attended,
    grad_pair,
    grad_residual_ref,
    key_weights,
    line_out,
    line_in,
    pair_sems,
    slot_sems,
    line_sems,
    token_sems,
    load_sems,
    free,
):
    dp, z = lax.axis_index("dp"), lax.axis_index("expert")
    core, chip = dp % 2, dp // 2
    chip_x, chip_y = flipped(chip, 0), flipped(chip, 1)
    chip_corner = flipped(chip_x, 1)
    device_core = (flipped(dp, 0), z)
    device_x = (flipped(dp, 1), z)
    device_y = (flipped(dp, 2), z)
    others = [(dp, (z + turn) % 4) for turn in range(1, 4)]
    slots = pair_sum.shape[0]
    experts = received_ref.shape[0]
    expert_panels = 3 * experts
    dense_panels = line_out.shape[0]
    shared_panels = dense_panels - right.shape[0]
    panels = expert_panels + right.shape[0]
    length, width = residual_ref.shape
    share, hidden = staged.shape[1:]
    half = share // 2
    stripe = share // 4
    query_width = HEADS * HD
    kv_width = KVH * HD
    block = width // 4

    def remote(source, target, send, receive, device):
        return pltpu.make_async_remote_copy(
            src_ref=source,
            dst_ref=target,
            send_sem=send,
            recv_sem=receive,
            device_id=device,
            device_id_type=MESH,
        )

    barrier = pltpu.get_barrier_semaphore()
    for device in (device_core, device_x, device_y, *others):
        pl.semaphore_signal(barrier, inc=1, device_id=device, device_id_type=MESH)
    pl.semaphore_wait(barrier, 6)

    grad_copies = [
        remote(
            grad_parts_ref.at[pl.ds(pl.multiple_of(device[1] * length, length), length), :],
            grad_tokens.at[turn],
            token_sems.at[turn],
            token_sems.at[3 + turn],
            device,
        )
        for turn, device in enumerate(others)
    ]
    for copy in grad_copies:
        copy.start()

    def expert_loads(expert):
        buffer = expert % 2
        return [
            pltpu.make_async_copy(source.at[expert], target, load_sems.at[buffer, index])
            for index, (source, target) in enumerate(
                (
                    (received_ref, wide.at[buffer, 0]),
                    (grad_returned_ref, wide.at[buffer, 1]),
                    (grad_gate_ref, narrow.at[buffer, 0]),
                    (grad_up_ref, narrow.at[buffer, 1]),
                    (act_ref, narrow.at[buffer, 2]),
                )
            )
        ]

    for copy in expert_loads(0):
        copy.start()

    def columns(ref, panel):
        return ref.at[:, pl.ds(panel * hidden, hidden)]

    sources = [
        (cotangent_ref, left.at[0]),
        (normed_attend_ref, left.at[2]),
        *[(columns(attended_ref, panel), right.at[panel]) for panel in range(3)],
        (shared_sum_ref, line_out.at[pl.ds(0, shared_panels)]),
        (dense_ref.at[:, pl.ds(query_width + 2 * kv_width, query_width)], out_weights),
        (dense_ref.at[:, pl.ds(query_width, 2 * kv_width)], key_weights),
        (
            grad_parts_ref.at[pl.ds(pl.multiple_of(z * length, length), length), :],
            grad_tokens.at[3],
        ),
    ]
    dense_loads = [
        pltpu.make_async_copy(source, target, load_sems.at[2 + index // 5, index % 5])
        for index, (source, target) in enumerate(sources)
    ]
    for copy in dense_loads:
        copy.start()
    query_load = pltpu.make_async_copy(
        dense_ref.at[:, pl.ds(0, query_width)], out_weights, pair_sems.at[4]
    )

    def fill(pair, left_ref, right_value):
        for chip_index in range(4):
            part = matmul_tn(left_ref[:, chip_index * block : (chip_index + 1) * block], right_value)
            ring[pair, chip_index] = part.astype(jnp.bfloat16).reshape(2, share, hidden)

    def total(first, *more):
        result = first.astype(jnp.float32)
        for value in more:
            result = result + value.astype(jnp.float32)
        return result

    def pair_copy(panel):
        pair, slot = panel % 2, panel % slots
        return remote(
            ring.at[pair, :, 1 - core],
            pair_sum.at[slot],
            pair_sems.at[pair],
            slot_sems.at[0, slot],
            device_core,
        )

    def corner_copies(panel):
        slot = panel % slots
        return (
            remote(
                pair_sum.at[slot, chip_corner, pl.ds(0, half)],
                corner_x.at[slot],
                slot_sems.at[1, slot],
                slot_sems.at[2, slot],
                device_x,
            ),
            remote(
                pair_sum.at[slot, chip_corner, pl.ds(half, half)],
                corner_y.at[slot],
                slot_sems.at[3, slot],
                slot_sems.at[4, slot],
                device_y,
            ),
        )

    def side_copies(panel):
        slot = panel % slots
        return (
            remote(
                pair_sum.at[slot, chip_x],
                side_x.at[slot],
                slot_sems.at[5, slot],
                slot_sems.at[6, slot],
                device_x,
            ),
            remote(
                pair_sum.at[slot, chip_y],
                side_y.at[slot],
                slot_sems.at[7, slot],
                slot_sems.at[8, slot],
                device_y,
            ),
        )

    def line_copies(panel):
        return [
            remote(
                line_out.at[panel, pl.ds(pl.multiple_of(device[1] * stripe, stripe), stripe)],
                line_in.at[panel, turn],
                line_sems.at[0, panel, turn],
                line_sems.at[1, panel, turn],
                device,
            )
            for turn, device in enumerate(others)
        ]

    def staged_copy(panel):
        return pltpu.make_async_copy(
            staged.at[panel % 2], expert_sum_ref.at[panel], pair_sems.at[2 + panel % 2]
        )

    def post(panel):
        @pl.when(panel >= slots)
        def _():
            pl.semaphore_wait(free.at[0], 1)

        pair_copy(panel).start()

    def sum_pair(panel):
        pair, slot = panel % 2, panel % slots
        pair_copy(panel).wait()
        for chip_index in range(4):
            pair_sum[slot, chip_index] = total(
                pair_sum[slot, chip_index], ring[pair, chip_index, core]
            ).astype(jnp.bfloat16)

        @pl.when(panel >= slots)
        def _():
            pl.semaphore_wait(free.at[1], 1)
            pl.semaphore_wait(free.at[2], 1)

        for copy in corner_copies(panel):
            copy.start()

    def sum_corner(panel):
        slot = panel % slots
        for copy in corner_copies(panel):
            copy.wait_recv()
        pair_sum[slot, chip_y, :half] = total(
            pair_sum[slot, chip_y, :half], corner_x[slot]
        ).astype(jnp.bfloat16)
        pair_sum[slot, chip_x, half:] = total(
            pair_sum[slot, chip_x, half:], corner_y[slot]
        ).astype(jnp.bfloat16)
        for copy in side_copies(panel):
            copy.start()

    def sum_sides(panel):
        slot = panel % slots
        for copy in corner_copies(panel):
            copy.wait_send()
        for copy in side_copies(panel):
            copy.wait()
        value = total(pair_sum[slot, chip], side_x[slot], side_y[slot]).astype(jnp.bfloat16)

        @pl.when(panel < expert_panels)
        def _():
            @pl.when(panel >= 2)
            def _():
                staged_copy(panel - 2).wait()

            staged[panel % 2] = value
            staged_copy(panel).start()

        @pl.when(panel >= expert_panels)
        def _():
            index = panel - expert_panels + shared_panels
            line_out[index] = value
            for copy in line_copies(index):
                copy.start()

        @pl.when(panel < panels - slots)
        def _():
            for index, device in enumerate((device_core, device_x, device_y)):
                pl.semaphore_signal(
                    free.at[index], inc=1, device_id=device, device_id_type=MESH
                )

    def residual_backward(part):
        if part == 0:
            for copy in dense_loads:
                copy.wait()
            for copy in grad_copies:
                copy.wait()
            grad_gain_ref[...] = jnp.zeros_like(grad_gain_ref)
        rows_step = 32
        steps = length // rows_step // 2

        @pl.loop(part * steps, (part + 1) * steps)
        def _(index):
            rows = pl.ds(index * rows_step, rows_step)
            grad_normed = (
                total(
                    grad_tokens[3, rows, :],
                    grad_tokens[0, rows, :],
                    grad_tokens[1, rows, :],
                    grad_tokens[2, rows, :],
                )
                + grad_shared_ref[rows, :]
            )
            residual, scale = residual_ref[rows, :], scale_ref[rows, :]
            grad_scaled = grad_normed * gain_ref[...]
            mean = jnp.mean(grad_scaled * residual, axis=-1, keepdims=True)
            grad_residual = (
                left[0, rows, :].astype(jnp.float32)
                + scale * grad_scaled
                - residual * (scale * scale * scale) * mean
            )
            grad_residual_ref[rows, :] = grad_residual
            left[1, rows, :] = grad_residual.astype(jnp.bfloat16)
            grad_gain_ref[1:2, :] += jnp.sum(
                grad_normed * residual * scale, axis=0, keepdims=True
            )

    def attended_backward():
        grad_attended[...] = matmul(left[1], out_weights[...]).astype(jnp.bfloat16)
        query_load.start()

    def query_backward():
        query_load.wait()
        for part in range(3):
            update = matmul_nt(right[3 + part], out_weights[:, part * hidden : (part + 1) * hidden])
            if part == 0:
                grad_input_ref[...] = update
            else:
                grad_input_ref[...] += update

    def key_backward():
        for part in range(2):
            grad_input_ref[...] += matmul_nt(
                right[6 + part], key_weights[:, part * hidden : (part + 1) * hidden]
            )

    def input_backward():
        rows_step = 32

        @pl.loop(0, length // rows_step)
        def _(index):
            rows = pl.ds(index * rows_step, rows_step)
            values, grad_normed = hidden_ref[rows, :].astype(jnp.float32), grad_input_ref[rows, :]
            scale = lax.rsqrt(jnp.mean(values * values, axis=-1, keepdims=True) + 1e-06)
            grad_scaled = grad_normed * gain_attend_ref[...]
            mean = jnp.mean(grad_scaled * values, axis=-1, keepdims=True)
            grad_input_ref[rows, :] = (
                grad_residual_ref[rows, :]
                + scale * grad_scaled
                - values * (scale * scale * scale) * mean
            )
            grad_gain_ref[0:1, :] += jnp.sum(
                grad_normed * values * scale, axis=0, keepdims=True
            )

    def attention_backward(head):
        score_scale = HD ** (-0.5)
        per_group = HEADS // KVH
        heads_wide = hidden // HD
        group = head // per_group
        key_rows = projected_ref[:, query_width + group * HD : query_width + (group + 1) * HD]
        value_first = query_width + kv_width + group * HD
        value_rows = projected_ref[:, value_first : value_first + HD]
        row = lax.broadcasted_iota(jnp.int32, (length, length), 0)
        column = lax.broadcasted_iota(jnp.int32, (length, length), 1)
        spot = slice(head * HD, (head + 1) * HD)
        query, grad_out = projected_ref[:, spot], grad_attended[:, spot]
        scores = jnp.where(column <= row, matmul_nt(query, key_rows) * score_scale, -1e30)
        raised = jnp.exp(scores - jnp.max(scores, axis=-1, keepdims=True))
        weights = raised / jnp.sum(raised, axis=-1, keepdims=True)
        grad_weights = matmul_nt(grad_out, value_rows)
        inner = jnp.sum(weights * grad_weights, axis=-1, keepdims=True)
        grad_scores = (weights * (grad_weights - inner)).astype(jnp.bfloat16)
        grad_query = matmul(grad_scores, key_rows) * score_scale
        place = slice(head % heads_wide * HD, (head % heads_wide + 1) * HD)
        right[3 + head // heads_wide, :, place] = grad_query.astype(jnp.bfloat16)
        grad_key = matmul_tn(grad_scores, query)
        grad_value = matmul_tn(weights.astype(jnp.bfloat16), grad_out)
        if head % per_group > 0:
            grad_key = grad_key + grad_pair[0]
            grad_value = grad_value + grad_pair[1]
        if head % per_group < per_group - 1:
            grad_pair[0] = grad_key
            grad_pair[1] = grad_value
        else:
            place = slice(group * HD, (group + 1) * HD)
            right[6, :, place] = (grad_key * score_scale).astype(jnp.bfloat16)
            right[7, :, place] = grad_value.astype(jnp.bfloat16)

    def two_heads_backward(head):
        attention_backward(head)
        attention_backward(head + 1)

    @pl.loop(0, panels + 5)
    def _(step):
        @pl.when(step < expert_panels)
        def _():
            expert, matrix = step // 3, step % 3

            @pl.when(matrix == 0)
            def _():
                for copy in expert_loads(expert):
                    copy.wait()

                @pl.when(expert + 1 < experts)
                def _():
                    for copy in expert_loads(expert + 1):
                        copy.start()

            fill(step % 2, wide.at[expert % 2, matrix // 2], narrow[expert % 2, matrix])

        backward = [
            *[functools.partial(residual_backward, part) for part in range(2)],
            attended_backward,
            *[functools.partial(two_heads_backward, head) for head in range(0, HEADS, 2)],
            query_backward,
            key_backward,
            input_backward,
        ]
        for index, call in enumerate(backward):
            pl.when(step == GRAD_STEP + index)(call)

        @pl.when((step >= expert_panels) & (step < panels))
        def _():
            panel = step - expert_panels
            fill(step % 2, left.at[jnp.where(panel < 3, 1, 2)], right[panel])

        @pl.when(step == GRAD_STEP + 1)
        def _():
            for panel in range(shared_panels):
                for copy in line_copies(panel):
                    copy.start()

        @pl.when(step < panels)
        def _():
            post(step)

        @pl.when((step >= 1) & (step < panels + 1))
        def _():
            sum_pair(step - 1)

        @pl.when((step >= 3) & (step < panels + 3))
        def _():
            sum_corner(step - 3)

        @pl.when(step >= 5)
        def _():
            sum_sides(step - 5)

    for panel in (expert_panels - 2, expert_panels - 1):
        staged_copy(panel).wait()

    for panel in range(dense_panels):
        for copy in line_copies(panel):
            copy.wait()
        place = panel + 8 if panel < 6 else panel - 1 if panel < 9 else panel - 9
        spot = slice(place * hidden, (place + 1) * hidden)
        grad = total(
            line_out[panel, pl.ds(pl.multiple_of(z * stripe, stripe), stripe), :],
            line_in[panel, 0],
            line_in[panel, 1],
            line_in[panel, 2],
        )
        moment = MOMENTUM_DECAY * momentum_ref[:, spot] + grad
        dense_grad_ref[:, spot] = grad
        dense_moment_ref[:, spot] = moment
        dense_units_ref[place] = moment.astype(jnp.bfloat16)
    for panel in range(dense_panels, dense_units_ref.shape[0]):
        dense_units_ref[panel] = jnp.zeros_like(dense_units_ref[panel])


def scatter_grads(
    grad_parts,
    saved,
    dense_all,
    shared_sum,
    cotangent,
    normed_attend,
    attended,
    residual,
    scale,
    gain,
    grad_shared,
    projected,
    hidden_in,
    gain_attend,
    dense_momentum,
):
    experts, spots, width = saved[0].shape
    hidden = saved[2].shape[-1]
    length = residual.shape[0]
    share = width // 8
    stripe = share // 4
    dense_panels = 14
    low = jnp.bfloat16
    vmem = pl.BlockSpec(memory_space=pltpu.VMEM)
    return pl.pallas_call(
        scatter_kernel,
        in_specs=[ANY] * 11 + [vmem] * 8,
        out_specs=[ANY] + [vmem] * 5,
        out_shape=[
            jax.ShapeDtypeStruct((3 * experts, share, hidden), low),
            jax.ShapeDtypeStruct(dense_momentum.shape, jnp.float32),
            jax.ShapeDtypeStruct(dense_momentum.shape, jnp.float32),
            jax.ShapeDtypeStruct((16, stripe, hidden), low),
            jax.ShapeDtypeStruct((length, width), jnp.float32),
            jax.ShapeDtypeStruct((2, width), jnp.float32),
        ],
        scratch_shapes=[
            pltpu.VMEM((2, 4, 2, share, hidden), low),
            pltpu.VMEM((SLOTS, 4, share, hidden), low),
            pltpu.VMEM((SLOTS, share // 2, hidden), low),
            pltpu.VMEM((SLOTS, share // 2, hidden), low),
            pltpu.VMEM((SLOTS, share, hidden), low),
            pltpu.VMEM((SLOTS, share, hidden), low),
            pltpu.VMEM((2, share, hidden), low),
            pltpu.VMEM((2, 2, spots, width), low),
            pltpu.VMEM((2, 3, spots, hidden), low),
            pltpu.VMEM((3, length, width), low),
            pltpu.VMEM((8, length, hidden), low),
            pltpu.VMEM((width, HEADS * HD), low),
            pltpu.VMEM((4, length, width), low),
            pltpu.VMEM((length, HEADS * HD), low),
            pltpu.VMEM((2, length, HD), jnp.float32),
            pltpu.VMEM((length, width), jnp.float32),
            pltpu.VMEM((width, 2 * KVH * HD), low),
            pltpu.VMEM((dense_panels, share, hidden), low),
            pltpu.VMEM((dense_panels, 3, stripe, hidden), low),
            pltpu.SemaphoreType.DMA((5,)),
            pltpu.SemaphoreType.DMA((9, SLOTS)),
            pltpu.SemaphoreType.DMA((2, dense_panels, 3)),
            pltpu.SemaphoreType.DMA((6,)),
            pltpu.SemaphoreType.DMA((5, 5)),
            pltpu.SemaphoreType.REGULAR((3,)),
        ],
        compiler_params=pltpu.CompilerParams(
            collective_id=3, has_side_effects=True, vmem_limit_bytes=62 * MIB
        ),
        name="scatter_grads",
    )(
        grad_parts,
        *saved,
        dense_all,
        shared_sum,
        cotangent,
        normed_attend,
        attended,
        residual,
        scale,
        gain,
        grad_shared,
        projected,
        hidden_in,
        gain_attend,
        dense_momentum,
    )


def muon_kernel(
    expert_ref,
    dense_ref,
    routed_parts_ref,
    base_ref,
    dense_weights_ref,
    expert_out_ref,
    block_out_ref,
    dense_new_ref,
    dense_out_ref,
    routed,
    dense_back,
    moments,
    units,
    orthogonal,
    current,
    low,
    identity,
    line_sems,
    out_sems,
    in_sems,
    back_out_sems,
    back_in_sems,
    load_sems,
):
    dp, z = lax.axis_index("dp"), lax.axis_index("expert")
    count, share, _ = moments.shape
    first, dense_count = 10, 4
    stripe = dense_ref.shape[1]
    others = [(dp, (z + turn) % 4) for turn in range(1, 4)]
    peers = [((dp + turn) % 8, z) for turn in range(1, 8)]

    def remote(source, target, send, receive, device):
        return pltpu.make_async_remote_copy(
            src_ref=source,
            dst_ref=target,
            send_sem=send,
            recv_sem=receive,
            device_id=device,
            device_id_type=MESH,
        )

    def share_of(index):
        return pl.ds(pl.multiple_of(index * share, share), share)

    def stripe_of(index):
        return pl.ds(pl.multiple_of(index * stripe, stripe), stripe)

    barrier = pltpu.get_barrier_semaphore()
    for device in (*others, *peers):
        pl.semaphore_signal(barrier, inc=1, device_id=device, device_id_type=MESH)
    dense_rows = pl.ds(first, dense_count)
    loads = [
        pltpu.make_async_copy(
            expert_ref.at[pl.ds(0, first)], moments.at[pl.ds(0, first)], load_sems.at[0]
        ),
        pltpu.make_async_copy(
            expert_ref.at[pl.ds(first, count - first - dense_count)],
            moments.at[pl.ds(first + dense_count, count - first - dense_count)],
            load_sems.at[1],
        ),
        pltpu.make_async_copy(
            dense_ref.at[pl.ds(z * dense_count, dense_count)],
            moments.at[dense_rows, stripe_of(z)],
            load_sems.at[2],
        ),
    ]
    for copy in loads:
        copy.start()
    pl.semaphore_wait(barrier, len(others) + len(peers))
    line_copies = [
        remote(
            dense_ref.at[pl.ds(device[1] * dense_count, dense_count)],
            moments.at[dense_rows, stripe_of(z)],
            line_sems.at[0, turn],
            line_sems.at[1, turn],
            device,
        )
        for turn, device in enumerate(others)
    ]
    line_back = [
        remote(
            dense_back.at[:, stripe_of(device[1])],
            dense_out_ref.at[pl.ds(z * dense_count, dense_count)],
            line_sems.at[2, turn],
            line_sems.at[3, turn],
            device,
        )
        for turn, device in enumerate(others)
    ]
    own_back = pltpu.make_async_copy(
        dense_back.at[:, stripe_of(z)],
        dense_out_ref.at[pl.ds(z * dense_count, dense_count)],
        load_sems.at[2],
    )

    def out_copy(slot, turn):
        owner = peers[turn][0]
        return remote(
            moments.at[8 * slot + owner],
            units.at[slot, share_of(dp)],
            out_sems.at[slot, turn],
            in_sems.at[slot],
            peers[turn],
        )

    def own_copy(slot):
        return pltpu.make_async_copy(
            moments.at[8 * slot + dp], units.at[slot, share_of(dp)], load_sems.at[3 + slot]
        )

    def is_dense(slot, owner):
        unit = 8 * slot + owner
        return (unit >= first) & (unit < first + dense_count)

    def expert_place(slot, owner):
        unit = 8 * slot + owner
        return expert_out_ref.at[jnp.where(unit < first, unit, unit - dense_count)]

    def dense_place(slot, owner):
        return dense_back.at[8 * slot + owner - first]

    def back_copy(place, slot, turn):
        return remote(
            orthogonal.at[slot, share_of(peers[turn][0])],
            place(slot, dp),
            back_out_sems.at[slot, turn],
            back_in_sems.at[slot, dp],
            peers[turn],
        )

    def own_back_copy(place, slot):
        return pltpu.make_async_copy(
            orthogonal.at[slot, share_of(dp)], place(slot, dp), load_sems.at[3 + slot]
        )

    def send_back(place, slot):
        for turn in range(7):
            back_copy(place, slot, turn).start()
        own_back_copy(place, slot).start()

    def exists(slot, owner):
        return 8 * slot + owner < count

    def send_slot(slot):
        for turn in range(7):
            pl.when(exists(slot, peers[turn][0]))(out_copy(slot, turn).start)
        pl.when(exists(slot, dp))(own_copy(slot).start)

    length = base_ref.shape[0]
    own_routed = pltpu.make_async_copy(
        routed_parts_ref.at[pl.ds(pl.multiple_of(z * length, length), length), :],
        routed.at[3],
        load_sems.at[6],
    )
    own_routed.start()
    routed_copies = [
        remote(
            routed_parts_ref.at[pl.ds(pl.multiple_of(device[1] * length, length), length), :],
            routed.at[turn],
            line_sems.at[4, turn],
            line_sems.at[5, turn],
            device,
        )
        for turn, device in enumerate(others)
    ]
    for copy in line_copies:
        copy.start()
    loads[0].wait()
    send_slot(0)
    loads[1].wait()
    loads[2].wait()
    for copy in line_copies:
        copy.wait()
    send_slot(1)
    send_slot(2)
    for copy in routed_copies:
        copy.start()

    @pl.loop(0, 3)
    def _(slot):
        @pl.when(exists(slot, dp))
        def _():
            own_copy(slot).wait()
            arrived = units.at[slot, pl.ds(0, 7 * share)]
            remote(arrived, arrived, in_sems.at[slot], in_sems.at[slot], peers[0]).wait_recv()
            newton_schulz_unit(units.at[slot], orthogonal.at[slot], current, low, identity)

            @pl.when(is_dense(slot, dp))
            def _():
                send_back(dense_place, slot)

            @pl.when(jnp.logical_not(is_dense(slot, dp)))
            def _():
                send_back(expert_place, slot)

    def own_back_wait(slot):
        def wait():
            pltpu.make_async_copy(
                orthogonal.at[slot, share_of(dp)], expert_out_ref.at[0], load_sems.at[3 + slot]
            ).wait()

        return wait

    def wait_back(slot):
        for turn in range(7):
            owner = peers[turn][0]

            @pl.when(exists(slot, owner))
            def _():
                block = expert_out_ref.at[0]
                semaphore = back_in_sems.at[slot, owner]
                remote(block, block, semaphore, semaphore, peers[0]).wait_recv()

        pl.when(exists(slot, dp))(own_back_wait(slot))

    wait_back(1)
    for copy in line_back:
        copy.start()
    own_back.start()
    wait_back(0)
    own_routed.wait()
    for copy in routed_copies:
        copy.wait()
    rows_step = 32

    @pl.loop(0, length // rows_step)
    def _(index):
        part = pl.ds(index * rows_step, rows_step)
        total = base_ref[part, :]
        for source in (3, 0, 1, 2):
            total = total + routed[source, part, :].astype(jnp.float32)
        block_out_ref[part, :] = total.astype(jnp.bfloat16)

    wait_back(2)
    for slot in range(3):
        for turn in range(7):
            pl.when(exists(slot, peers[turn][0]))(out_copy(slot, turn).wait_send)

        @pl.when(exists(slot, dp))
        def _():
            for turn in range(7):
                back_copy(expert_place, slot, turn).wait_send()

    for copy in line_back:
        copy.wait()
    own_back.wait()
    keep_factor = 1.0 - LEARN_RATE * WEIGHT_DECAY
    columns = current.shape[0]
    for panel in range(dense_new_ref.shape[1] // columns):
        spot = slice(panel * columns, (panel + 1) * columns)
        dense_new_ref[:, spot] = keep_factor * dense_weights_ref[:, spot] - LEARN_RATE * (
            dense_out_ref[panel].astype(jnp.float32)
        )


def muon(expert_units, dense_units, routed_parts, base_out, dense_weights):
    experts, share, columns = expert_units.shape
    panels, stripe, _ = dense_units.shape
    count = experts + panels // 4
    low = jnp.bfloat16
    vmem = pl.BlockSpec(memory_space=pltpu.VMEM)
    return pl.pallas_call(
        muon_kernel,
        in_specs=[ANY] * 3 + [vmem] * 2,
        out_specs=[ANY] + [vmem] * 2,
        out_shape=[
            jax.ShapeDtypeStruct(expert_units.shape, low),
            jax.ShapeDtypeStruct(base_out.shape, low),
            jax.ShapeDtypeStruct(dense_weights.shape, jnp.float32),
        ],
        scratch_shapes=[
            pltpu.VMEM(dense_units.shape, low),
            pltpu.VMEM((4, *base_out.shape), low),
            pltpu.VMEM((panels // 4, share, columns), low),
            pltpu.VMEM((count, share, columns), low),
            pltpu.VMEM((3, 8 * share, columns), low),
            pltpu.VMEM((3, 8 * share, columns), low),
            pltpu.VMEM((columns, 8 * share), jnp.float32),
            pltpu.VMEM((columns, 8 * share), low),
            pltpu.VMEM((columns, columns), low),
            pltpu.SemaphoreType.DMA((6, 3)),
            pltpu.SemaphoreType.DMA((3, 7)),
            pltpu.SemaphoreType.DMA((3,)),
            pltpu.SemaphoreType.DMA((3, 7)),
            pltpu.SemaphoreType.DMA((3, 8)),
            pltpu.SemaphoreType.DMA((7,)),
        ],
        compiler_params=pltpu.CompilerParams(
            collective_id=4, has_side_effects=True, vmem_limit_bytes=56 * MIB
        ),
        name="muon",
    )(expert_units, dense_units, routed_parts, base_out, dense_weights)


def moments_kernel(momentum_ref, sum_ref, grad_ref, moment_ref, units_ref):
    grad = sum_ref[...].astype(jnp.float32)
    moment = MOMENTUM_DECAY * momentum_ref[...] + grad
    grad_ref[...] = grad
    moment_ref[...] = moment
    units_ref[...] = moment.astype(jnp.bfloat16)


def moments(momentum, grad_sum):
    panels, rows, columns = grad_sum.shape
    group = 3
    block = pl.BlockSpec((group, rows, columns), lambda index: (index, 0, 0))
    full = jax.ShapeDtypeStruct(grad_sum.shape, jnp.float32)
    grad, moment, units = pl.pallas_call(
        moments_kernel,
        grid=(panels // group,),
        in_specs=[block] * 2,
        out_specs=[block] * 3,
        out_shape=[full, full, jax.ShapeDtypeStruct(grad_sum.shape, jnp.bfloat16)],
        compiler_params=pltpu.CompilerParams(vmem_limit_bytes=32 * MIB),
        name="moments",
    )(momentum.reshape(grad_sum.shape), grad_sum)
    return grad.reshape(momentum.shape), moment.reshape(momentum.shape), units


def update_kernel(weights_ref, orthogonal_ref, new_ref):
    keep_factor = 1.0 - LEARN_RATE * WEIGHT_DECAY
    new_ref[...] = keep_factor * weights_ref[...] - LEARN_RATE * orthogonal_ref[...].astype(
        jnp.float32
    )


def updated_weights(weights, orthogonal):
    panels, rows, columns = orthogonal.shape
    group = 6
    block = pl.BlockSpec((group, rows, columns), lambda index: (index, 0, 0))
    return pl.pallas_call(
        update_kernel,
        grid=(panels // group,),
        in_specs=[block, block],
        out_specs=block,
        out_shape=jax.ShapeDtypeStruct(orthogonal.shape, jnp.float32),
        compiler_params=pltpu.CompilerParams(vmem_limit_bytes=32 * MIB),
        name="update",
    )(weights.reshape(orthogonal.shape), orthogonal).reshape(weights.shape)


def on_device(
    hidden_in,
    cotangent,
    routes,
    route_weights,
    dense_weights,
    dense_momentum,
    expert_weights,
    expert_momentum,
    norm_gains,
    gain_first,
    gain_second,
):
    length, width = hidden_in.shape
    topk_count = routes.shape[1]
    local_experts = expert_weights.shape[0]
    expert_size = lax.axis_size("expert")
    dp_size = lax.axis_size("dp")
    expert_count = local_experts * expert_size
    capacity = 5 * length * topk_count // (4 * expert_count)
    block_rows = min(512, length)
    query_width = HEADS * HD
    kv_width = KVH * HD
    qkv_end = query_width + 2 * kv_width
    shared_base = 2 * query_width + 2 * kv_width
    gate_table = jnp.sum(
        jnp.where(
            routes.T[None, :, :] == jnp.arange(expert_count, dtype=jnp.int32)[:, None, None],
            route_weights.T[None, :, :],
            0.0,
        ),
        axis=1,
    )
    direct = dp_size == 8 and expert_size == 4
    inputs = hidden_in.astype(jnp.float32)
    scale_attend = norm_scale(inputs)
    if direct:
        stripe_rows = dense_weights.shape[0]
        extra = jnp.zeros((stripe_rows, 128 - norm_gains.shape[0]), jnp.float32)
        plane_gates = gate_table.reshape(expert_size, local_experts, length)
        (
            dense_all,
            _,
            _,
            _,
            routed_parts,
            grad_parts,
            *saved,
            normed_attend,
            projected,
            attended,
            residual,
            scale_mixer,
            normed_mixer,
            shared_act,
            grad_shared_pre,
            grad_shared,
            base_out,
            gains_all,
            shared_sum,
        ) = front(
            jnp.concatenate(
                [
                    dense_weights[:, :shared_base],
                    norm_gains.T,
                    extra,
                    dense_weights[:, shared_base:],
                ],
                1,
            ).astype(jnp.bfloat16),
            jnp.pad(plane_gates, ((0, 0), (0, 8 - local_experts), (0, 0))),
            expert_weights.reshape(-1, *expert_weights.shape[2:]),
            hidden_in,
            cotangent,
            -(-capacity // 16) * 16,
        )
        gain_attend, gain_mixer = gains_all[0], gains_all[1]
    else:
        gate_tables = lax.all_gather(gate_table, "expert", axis=0, tiled=False)
        cotangents = lax.all_gather(cotangent, "expert", axis=0, tiled=True)
        dense_all, gains_all = (
            lax.all_gather(
                dense_weights.astype(jnp.bfloat16), ("dp", "expert"), axis=0, tiled=True
            ),
            lax.all_gather(norm_gains.astype(jnp.bfloat16), ("dp", "expert"), axis=1, tiled=True),
        )
        gain_attend = gains_all[0].astype(jnp.float32)
        gain_mixer = gains_all[1].astype(jnp.float32)
        normed_attend = (inputs * scale_attend * gain_attend).astype(jnp.bfloat16)
        projected = jnp.dot(
            normed_attend, dense_all[:, :qkv_end], preferred_element_type=jnp.float32
        ).astype(jnp.bfloat16)
        query = projected[:, :query_width]
        key_rows = projected[:, query_width : query_width + kv_width]
        value_rows = projected[:, query_width + kv_width :]
        attended, saved_stats = attend_forward(query, key_rows, value_rows, block_rows)
        residual = inputs + jnp.einsum(
            "sq,dq->sd", attended, dense_all[:, qkv_end:shared_base], preferred_element_type=jnp.float32
        )
        scale_mixer = norm_scale(residual)
        normed_mixer = (residual * scale_mixer * gain_mixer).astype(jnp.bfloat16)
        expert_all = lax.all_gather(expert_weights.astype(jnp.bfloat16), "dp", axis=2, tiled=True)
        tokens = lax.all_gather(normed_mixer, "expert", axis=0, tiled=True)
        shared_pre = jnp.dot(
            normed_mixer,
            dense_all[:, shared_base : shared_base + 2 * FFS],
            preferred_element_type=jnp.float32,
        )
        shared_gate = shared_pre[:, :FFS]
        shared_up = shared_pre[:, FFS:]
        shared_act = (jax.nn.silu(shared_gate) * shared_up).astype(jnp.bfloat16)
        shared_out = jnp.einsum(
            "sf,df->sd",
            shared_act,
            dense_all[:, shared_base + 2 * FFS : shared_base + 3 * FFS],
            preferred_element_type=jnp.float32,
        )
        grad_shared_act = jnp.dot(
            cotangent,
            dense_all[:, shared_base + 2 * FFS : shared_base + 3 * FFS],
            preferred_element_type=jnp.float32,
        )
        shared_sig = jax.nn.sigmoid(shared_gate)
        grad_shared_pre = jnp.concatenate(
            [
                grad_shared_act * shared_up * shared_sig * (1.0 + shared_gate * (1.0 - shared_sig)),
                grad_shared_act * jax.nn.silu(shared_gate),
            ],
            1,
        ).astype(jnp.bfloat16)
        grad_shared = jnp.einsum(
            "sf,df->sd",
            grad_shared_pre,
            dense_all[:, shared_base : shared_base + 2 * FFS],
            preferred_element_type=jnp.float32,
        )
        base_out = residual + shared_out
        my_gates = lax.dynamic_slice_in_dim(
            gate_tables, lax.axis_index("expert") * local_experts, local_experts, 1
        ).transpose(1, 0, 2)
        hot = my_gates > 0.0
        earlier = jnp.einsum(
            "est,ut->esu",
            hot.astype(jnp.bfloat16),
            jnp.tril(jnp.ones((length, length), jnp.bfloat16), -1),
            preferred_element_type=jnp.float32,
        ).astype(jnp.int32)
        place = jnp.where(hot, earlier, -1)
        routed_parts, grad_parts, saved = grouped_experts(
            tokens, cotangents, place, my_gates, expert_all, capacity
        )
    if direct:
        (
            expert_sum,
            dense_grad,
            dense_moment,
            dense_units,
            grad_inputs,
            grad_gains,
        ) = scatter_grads(
            grad_parts,
            saved,
            dense_all,
            shared_sum,
            cotangent,
            normed_attend,
            attended,
            residual,
            scale_mixer,
            gain_mixer[None, :],
            grad_shared,
            projected,
            hidden_in,
            gain_attend[None, :],
            dense_momentum,
        )
        expert_grad, expert_moment, expert_units = moments(expert_momentum, expert_sum)
        orth_expert, block_out, dense_new = muon(
            expert_units, dense_units, routed_parts, base_out, dense_weights
        )
    else:
        routed = lax.psum_scatter(routed_parts, "expert", scatter_dimension=0, tiled=True)
        grad_routed = lax.psum_scatter(grad_parts, "expert", scatter_dimension=0, tiled=True)
        expert_parts = [expert_grads(*kept) for kept in saved]
        expert_grad = lax.psum_scatter(
            sum(part.astype(jnp.float32) for part in expert_parts).astype(jnp.bfloat16),
            "dp",
            scatter_dimension=2,
            tiled=True,
        ).astype(jnp.float32)
        grad_normed = grad_routed.astype(jnp.float32) + grad_shared
        grad_scaled = grad_normed * gain_mixer
        grad_residual = (
            cotangent.astype(jnp.float32)
            + scale_mixer * grad_scaled
            - residual * scale_mixer**3 * jnp.mean(grad_scaled * residual, axis=-1, keepdims=True)
        )
        grad_gain_mixer = jnp.sum(grad_normed * residual * scale_mixer, axis=0)
        grad_attn_low = grad_residual.astype(jnp.bfloat16)
        grad_attended = jnp.dot(
            grad_attn_low, dense_all[:, qkv_end:shared_base], preferred_element_type=jnp.float32
        ).astype(jnp.bfloat16)
        grad_query, grad_key, grad_value = attend_backward(
            query, key_rows, value_rows, grad_attended, saved_stats, block_rows
        )
        grad_projected = jnp.concatenate([grad_query, grad_key, grad_value], 1)
        dense_parts = [
            jnp.einsum("sd,sf->df", left, right, preferred_element_type=jnp.float32)
            for left, right in (
                (normed_attend, grad_projected),
                (grad_attn_low, attended),
                (normed_mixer, grad_shared_pre),
                (cotangent, shared_act),
            )
        ]
        dense_grad = lax.psum_scatter(
            jnp.concatenate([part.astype(jnp.bfloat16) for part in dense_parts], 1),
            ("dp", "expert"),
            scatter_dimension=0,
            tiled=True,
        ).astype(jnp.float32)
        grad_normed_attend = jnp.einsum(
            "sc,dc->sd", grad_projected, dense_all[:, :qkv_end], preferred_element_type=jnp.float32
        )
        grad_scaled_attend = grad_normed_attend * gain_attend
        grad_inputs = (
            grad_residual
            + scale_attend * grad_scaled_attend
            - inputs * scale_attend**3 * jnp.mean(grad_scaled_attend * inputs, axis=-1, keepdims=True)
        )
        grad_gain_attend = jnp.sum(grad_normed_attend * inputs * scale_attend, axis=0)
        block_out = (base_out + routed.astype(jnp.float32)).astype(jnp.bfloat16)
        grad_gains = jnp.stack([grad_gain_attend, grad_gain_mixer], 0)
        dense_moment = MOMENTUM_DECAY * dense_momentum + dense_grad
        expert_moment = MOMENTUM_DECAY * expert_momentum + expert_grad
        stripe, dense_columns = dense_weights.shape
        row_count = stripe * expert_size
        dense_total = dense_columns // FFE
        dense_share = -(-dense_total // expert_size)
        dense_padded = jnp.pad(
            dense_moment.astype(jnp.bfloat16),
            ((0, 0), (0, dense_share * expert_size * FFE - dense_columns)),
        ).reshape(stripe, dense_share * expert_size, FFE).transpose(1, 0, 2)
        expert_units = expert_moment.astype(jnp.bfloat16).reshape(-1, row_count, FFE)
        dense_units = lax.all_to_all(
            dense_padded, "expert", split_axis=0, concat_axis=1, tiled=True
        )
        expert_unit_count = expert_units.shape[0]
        base_count = expert_unit_count + dense_share
        unit_count = -(-base_count // dp_size) * dp_size
        all_units = jnp.concatenate(
            [
                expert_units,
                dense_units,
                jnp.zeros((unit_count - base_count, row_count, FFE), jnp.bfloat16),
            ],
            0,
        )
        owned = lax.all_to_all(all_units, "dp", split_axis=0, concat_axis=1, tiled=True)
        orthogonal = newton_schulz(owned)
        orth_units = lax.all_to_all(orthogonal, "dp", split_axis=1, concat_axis=0, tiled=True)
        orth_expert = orth_units[:expert_unit_count]
        orth_stripe = lax.all_to_all(
            orth_units[expert_unit_count:base_count],
            "expert",
            split_axis=1,
            concat_axis=0,
            tiled=True,
        )
        orth_stripe = (
            orth_stripe[:dense_total]
            .transpose(1, 0, 2)
            .reshape(stripe, dense_columns)
            .astype(jnp.float32)
        )
        keep_factor = 1.0 - LEARN_RATE * WEIGHT_DECAY
        dense_new = keep_factor * dense_weights - LEARN_RATE * orth_stripe
    gain_grad = lax.psum_scatter(
        grad_gains,
        ("dp", "expert"),
        scatter_dimension=1,
        tiled=True,
    )
    expert_new = updated_weights(expert_weights, orth_expert)
    first_new = FIRST_DECAY * gain_first + (1.0 - FIRST_DECAY) * gain_grad
    second_new = SECOND_DECAY * gain_second + (1.0 - SECOND_DECAY) * gain_grad * gain_grad
    step_ratio = (
        first_new
        / (1.0 - FIRST_DECAY**STEP)
        / (jnp.sqrt(second_new / (1.0 - SECOND_DECAY**STEP)) + 1e-08)
    )
    gain_new = norm_gains - GAIN_RATE * step_ratio
    return (
        block_out,
        grad_inputs,
        dense_grad,
        dense_moment,
        dense_new,
        expert_grad,
        expert_moment,
        expert_new,
        gain_grad,
        first_new,
        second_new,
        gain_new,
    )


def solution(mesh):
    in_specs = (
        P(("dp", "expert"), None),
        P(("dp", "expert"), None),
        P(("dp", "expert"), None),
        P(("dp", "expert"), None),
        P(("dp", "expert"), None),
        P(("dp", "expert"), None),
        P("expert", None, "dp", None),
        P("expert", None, "dp", None),
        P(None, ("dp", "expert")),
        P(None, ("dp", "expert")),
        P(None, ("dp", "expert")),
    )
    out_specs = (
        P(("dp", "expert"), None),
        P(("dp", "expert"), None),
        P(("dp", "expert"), None),
        P(("dp", "expert"), None),
        P(("dp", "expert"), None),
        P("expert", None, "dp", None),
        P("expert", None, "dp", None),
        P("expert", None, "dp", None),
        P(None, ("dp", "expert")),
        P(None, ("dp", "expert")),
        P(None, ("dp", "expert")),
        P(None, ("dp", "expert")),
    )
    return jax.shard_map(
        on_device, mesh=mesh, in_specs=in_specs, out_specs=out_specs, check_vma=False
    )
```

```python
import functools

import jax
import jax.numpy as jnp
from jax import lax
from jax.experimental import pallas as pl
from jax.experimental.pallas import tpu as pltpu
from jax.sharding import PartitionSpec as P

HEADS = 12
HD = 128
KVH = 4
FFE = 512
FFS = 1024
NS_STEPS = 5
STEP = 10


POLY_FIRST = 3.4445
POLY_SECOND = -4.775
POLY_THIRD = 2.0315
MOMENTUM_DECAY = 0.95
LEARN_RATE = 0.6
WEIGHT_DECAY = 0.1
GAIN_RATE = 0.8
FIRST_DECAY = 0.9
SECOND_DECAY = 0.95


def norm_scale(values):
    return lax.rsqrt(jnp.mean(values * values, axis=-1, keepdims=True) + 1e-06)


def block_scores(query_block, key_block, first_row, block_rows, last_row):
    score_scale = HD ** (-0.5)
    scores = (
        jnp.einsum("qgrd,kgd->grqk", query_block, key_block, preferred_element_type=jnp.float32)
        * score_scale
    )
    allowed = jnp.arange(last_row)[None, :] <= (first_row + jnp.arange(block_rows))[:, None]
    return jnp.where(allowed, scores, -1e30)


def attend_forward(query, key_rows, value_rows, block_rows):
    length = query.shape[0]
    query_heads = query.reshape(length, KVH, HEADS // KVH, HD)
    key_heads = key_rows.reshape(length, KVH, HD)
    value_heads = value_rows.reshape(length, KVH, HD)
    scores = block_scores(query_heads, key_heads, 0, block_rows, block_rows)
    highest = jnp.max(scores, axis=-1, keepdims=True)
    raised = jnp.exp(scores - highest)
    totals = jnp.sum(raised, axis=-1, keepdims=True)
    weights = (raised / totals).astype(jnp.bfloat16)
    outputs = jnp.einsum("grqk,kgd->qgrd", weights, value_heads, preferred_element_type=jnp.float32)
    saved_stats = [(highest, totals)]
    attended = outputs.reshape(length, HEADS * HD)
    return (attended.astype(jnp.bfloat16), saved_stats)


def attend_backward(query, key_rows, value_rows, grad_attended, saved_stats, block_rows):
    length = query.shape[0]
    score_scale = HD ** (-0.5)
    query_heads = query.reshape(length, KVH, HEADS // KVH, HD)
    grad_heads = grad_attended.reshape(length, KVH, HEADS // KVH, HD)
    key_heads = key_rows.reshape(length, KVH, HD)
    value_heads = value_rows.reshape(length, KVH, HD)
    grad_key = jnp.zeros((length, KVH, HD), jnp.float32)
    grad_value = jnp.zeros((length, KVH, HD), jnp.float32)
    query_parts = []
    for block_index, first_row in enumerate(range(0, length, block_rows)):
        last_row = first_row + block_rows
        scores = block_scores(query_heads, key_heads, first_row, block_rows, last_row)
        highest, totals = saved_stats[block_index]
        weights = jnp.exp(scores - highest) / totals
        grad_weights = jnp.einsum(
            "qgrd,kgd->grqk", grad_heads, value_heads, preferred_element_type=jnp.float32
        )
        inner_sum = jnp.sum(weights * grad_weights, axis=-1, keepdims=True)
        grad_scores = (weights * (grad_weights - inner_sum)).astype(jnp.bfloat16)
        query_parts.append(
            jnp.einsum("grqk,kgd->qgrd", grad_scores, key_heads, preferred_element_type=jnp.float32)
            * score_scale
        )
        grad_key = grad_key.at[:last_row].add(
            jnp.einsum(
                "grqk,qgrd->kgd", grad_scores, query_heads, preferred_element_type=jnp.float32
            )
            * score_scale
        )
        grad_value = grad_value.at[:last_row].add(
            jnp.einsum(
                "grqk,qgrd->kgd",
                weights.astype(jnp.bfloat16),
                grad_heads,
                preferred_element_type=jnp.float32,
            )
        )
    grad_query = query_parts[0].reshape(length, HEADS * HD)
    return (
        grad_query.astype(jnp.bfloat16),
        grad_key.reshape(length, KVH * HD).astype(jnp.bfloat16),
        grad_value.reshape(length, KVH * HD).astype(jnp.bfloat16),
    )


MIB = 2**20
GRAD_STEP = 14
SLOTS = 8
MESH = pl.DeviceIdType.MESH


def matmul(left, right):
    return jnp.dot(left, right, preferred_element_type=jnp.float32)


def matmul_nt(left, right):
    return lax.dot_general(left, right, (((1,), (1,)), ((), ())), preferred_element_type=jnp.float32)


def matmul_tn(left, right):
    return lax.dot_general(left, right, (((0,), (0,)), ((), ())), preferred_element_type=jnp.float32)


def newton_schulz_unit(moment_ref, orthogonal_ref, current, low, identity):
    columns, rows = current.shape
    step = 256
    parts = [pl.ds(index * step, step) for index in range(rows // step)]
    identity[...] = jnp.where(
        lax.broadcasted_iota(jnp.int32, identity.shape, 0)
        == lax.broadcasted_iota(jnp.int32, identity.shape, 1),
        1.0,
        0.0,
    ).astype(jnp.bfloat16)
    squares = jnp.zeros((1, columns), jnp.float32)
    for part in parts:
        values = moment_ref[part, :].astype(jnp.float32)
        squares = squares + jnp.sum(values * values, axis=0, keepdims=True)
    scale = 1.0 / (jnp.sqrt(jnp.sum(squares, axis=1, keepdims=True)) + 1e-07)
    for part in parts:
        scaled = matmul_nt(identity[...], moment_ref[part, :]) * scale
        current[:, part] = scaled
        low[:, part] = scaled.astype(jnp.bfloat16)

    def polynomial():
        gram = matmul_nt(low[...], low[...])
        gram_low = gram.astype(jnp.bfloat16)
        return (POLY_SECOND * gram + POLY_THIRD * matmul(gram_low, gram_low)).astype(jnp.bfloat16)

    @pl.loop(0, NS_STEPS - 1)
    def _(index):
        weights = polynomial()
        for part in parts:
            updated = POLY_FIRST * current[:, part] + matmul(weights, low[:, part])
            current[:, part] = updated
            low[:, part] = updated.astype(jnp.bfloat16)

    weights = polynomial()
    for part in parts:
        updated = POLY_FIRST * current[:, part] + matmul(weights, low[:, part])
        orthogonal_ref[part, :] = updated.T.astype(jnp.bfloat16)


def newton_schulz_kernel(moment_ref, orthogonal_ref, current, low, identity):
    newton_schulz_unit(moment_ref.at[0], orthogonal_ref.at[0], current, low, identity)


def newton_schulz(units):
    count, rows, columns = units.shape
    return pl.pallas_call(
        newton_schulz_kernel,
        grid=(count,),
        in_specs=[pl.BlockSpec((1, rows, columns), lambda unit: (unit, 0, 0))],
        out_specs=pl.BlockSpec((1, rows, columns), lambda unit: (unit, 0, 0)),
        out_shape=jax.ShapeDtypeStruct(units.shape, jnp.bfloat16),
        scratch_shapes=[
            pltpu.VMEM((columns, rows), jnp.float32),
            pltpu.VMEM((columns, rows), jnp.bfloat16),
            pltpu.VMEM((columns, columns), jnp.bfloat16),
        ],
        compiler_params=pltpu.CompilerParams(vmem_limit_bytes=48 * MIB),
        cost_estimate=pl.CostEstimate(
            flops=count * NS_STEPS * 2 * columns * columns * (2 * rows + columns),
            bytes_accessed=count * rows * columns * 4,
            transcendentals=0,
        ),
        name="newton_schulz",
    )(units)


def experts_kernel(
    tokens_ref,
    cotangent_ref,
    place_ref,
    gate_ref,
    weights_ref,
    routed_ref,
    grad_tokens_ref,
    received,
    grad_returned,
    act_ref,
    grad_gate_ref,
    grad_up_ref,
    routed_sum,
    grad_sum,
    chosen,
    weighted,
    grad_received,
):
    expert = pl.program_id(0)
    sequences, slots, length = chosen.shape

    @pl.when(expert == 0)
    def _():
        routed_sum[...] = jnp.zeros_like(routed_sum)
        grad_sum[...] = jnp.zeros_like(grad_sum)

    slot_weights = []
    for sequence in range(sequences):
        rows = pl.ds(sequence * length, length)
        spots = pl.ds(sequence * slots, slots)
        place = place_ref[0, sequence : sequence + 1, :]
        gate = gate_ref[0, sequence : sequence + 1, :]
        hot = lax.broadcasted_iota(jnp.int32, (slots, length), 0) == place
        slot_weight = jnp.sum(jnp.where(hot, gate, 0.0), axis=1, keepdims=True)
        slot_weights.append(slot_weight)
        hot_low = jnp.where(hot, 1.0, 0.0).astype(jnp.bfloat16)
        chosen[sequence] = hot_low
        received[0, spots, :] = matmul(hot_low, tokens_ref[rows, :]).astype(jnp.bfloat16)
        grad_returned[0, spots, :] = (
            matmul(hot_low, cotangent_ref[rows, :]) * slot_weight
        ).astype(jnp.bfloat16)
    tokens = received[0]
    grad_out = grad_returned[0]
    gate_pre = matmul(tokens, weights_ref[0, 0])
    up_pre = matmul(tokens, weights_ref[0, 1])
    gate_sig = jax.nn.sigmoid(gate_pre)
    gate_act = gate_pre * gate_sig
    act = (gate_act * up_pre).astype(jnp.bfloat16)
    act_ref[0] = act
    out = matmul_nt(act, weights_ref[0, 2]).astype(jnp.bfloat16).astype(jnp.float32)
    for sequence in range(sequences):
        spots = slice(sequence * slots, (sequence + 1) * slots)
        weighted[spots, :] = (out[spots] * slot_weights[sequence]).astype(jnp.bfloat16)
    grad_act = matmul(grad_out, weights_ref[0, 2])
    grad_gate = (grad_act * up_pre * gate_sig * (1.0 + gate_pre * (1.0 - gate_sig))).astype(
        jnp.bfloat16
    )
    grad_up = (grad_act * gate_act).astype(jnp.bfloat16)
    grad_gate_ref[0] = grad_gate
    grad_up_ref[0] = grad_up
    grad_received[...] = (
        matmul_nt(grad_gate, weights_ref[0, 0]) + matmul_nt(grad_up, weights_ref[0, 1])
    ).astype(jnp.bfloat16)
    for sequence in range(sequences):
        rows = pl.ds(sequence * length, length)
        spots = pl.ds(sequence * slots, slots)
        routed_sum[rows, :] += matmul_tn(chosen[sequence], weighted[spots, :])
        grad_sum[rows, :] += matmul_tn(chosen[sequence], grad_received[spots, :])

    @pl.when(expert == pl.num_programs(0) - 1)
    def _():
        routed_ref[...] = routed_sum[...].astype(jnp.bfloat16)
        grad_tokens_ref[...] = grad_sum[...].astype(jnp.bfloat16)


def run_experts(tokens, cotangents, place, gates, weights, capacity):
    experts, sequences, length = place.shape
    total, width = tokens.shape
    hidden = weights.shape[-1]
    slots = -(-capacity // 16) * 16
    spots = sequences * slots
    whole = pl.BlockSpec((total, width), lambda expert: (0, 0))
    table = pl.BlockSpec((1, sequences, length), lambda expert: (expert, 0, 0))
    matrices = pl.BlockSpec((1, 3, width, hidden), lambda expert: (expert, 0, 0, 0))
    wide = pl.BlockSpec((1, spots, width), lambda expert: (expert, 0, 0))
    narrow = pl.BlockSpec((1, spots, hidden), lambda expert: (expert, 0, 0))
    return pl.pallas_call(
        experts_kernel,
        grid=(experts,),
        in_specs=[whole, whole, table, table, matrices],
        out_specs=[whole, whole, wide, wide, narrow, narrow, narrow],
        out_shape=[
            *[jax.ShapeDtypeStruct((total, width), jnp.bfloat16)] * 2,
            *[jax.ShapeDtypeStruct((experts, spots, width), jnp.bfloat16)] * 2,
            *[jax.ShapeDtypeStruct((experts, spots, hidden), jnp.bfloat16)] * 3,
        ],
        scratch_shapes=[
            pltpu.VMEM((total, width), jnp.float32),
            pltpu.VMEM((total, width), jnp.float32),
            pltpu.VMEM((sequences, slots, length), jnp.bfloat16),
            pltpu.VMEM((spots, width), jnp.bfloat16),
            pltpu.VMEM((spots, width), jnp.bfloat16),
        ],
        compiler_params=pltpu.CompilerParams(vmem_limit_bytes=63 * MIB),
        cost_estimate=pl.CostEstimate(
            flops=experts * (12 * spots * width * hidden + 8 * spots * length * width),
            bytes_accessed=2 * weights.size + 16 * tokens.size,
            transcendentals=experts * spots * hidden,
        ),
        name="experts",
    )(tokens, cotangents, place, gates, weights)


def expert_grads_kernel(
    received_ref, grad_returned_ref, act_ref, grad_gate_ref, grad_up_ref, grad_weights_ref
):
    received, grad_returned = received_ref[0], grad_returned_ref[0]
    grad_weights_ref[0, 0] = matmul_tn(received, grad_gate_ref[0]).astype(jnp.bfloat16)
    grad_weights_ref[0, 1] = matmul_tn(received, grad_up_ref[0]).astype(jnp.bfloat16)
    grad_weights_ref[0, 2] = matmul_tn(grad_returned, act_ref[0]).astype(jnp.bfloat16)


def expert_grads(received, grad_returned, act, grad_gate, grad_up):
    experts, spots, width = received.shape
    hidden = act.shape[-1]
    wide = pl.BlockSpec((1, spots, width), lambda expert: (expert, 0, 0))
    narrow = pl.BlockSpec((1, spots, hidden), lambda expert: (expert, 0, 0))
    return pl.pallas_call(
        expert_grads_kernel,
        grid=(experts,),
        in_specs=[wide, wide, narrow, narrow, narrow],
        out_specs=pl.BlockSpec((1, 3, width, hidden), lambda expert: (expert, 0, 0, 0)),
        out_shape=jax.ShapeDtypeStruct((experts, 3, width, hidden), jnp.bfloat16),
        compiler_params=pltpu.CompilerParams(vmem_limit_bytes=48 * MIB),
        name="expert_grads",
    )(received, grad_returned, act, grad_gate, grad_up)


def grouped_experts(tokens, cotangents, place, gates, weights, capacity):
    experts, sequences, length = place.shape
    group = min(4, sequences)
    routed, grad_tokens, saved = [], [], []
    for first in range(0, sequences, group):
        rows = slice(first * length, (first + group) * length)
        part = slice(first, first + group)
        routed_part, grad_part, *kept = run_experts(
            tokens[rows], cotangents[rows], place[:, part], gates[:, part], weights, capacity
        )
        routed.append(routed_part)
        grad_tokens.append(grad_part)
        saved.append(kept)

    def joined(parts):
        return parts[0] if len(parts) == 1 else jnp.concatenate(parts, 0)

    return joined(routed), joined(grad_tokens), saved


def flipped(index, bit):
    unit = 2**bit
    return index + unit * (1 - 2 * ((index // unit) % 2))


class Links:
    def __init__(self, semaphores):
        self.semaphores = semaphores
        self.taken = 0
        self.dp = lax.axis_index("dp")
        self.z = lax.axis_index("expert")
        self.upper = self.z // 2
        self.position = self.z * (1 - 2 * self.upper) + 3 * self.upper
        self.step = 1 - 2 * self.upper
        self.core = (flipped(self.dp, 0), self.z)
        self.along_x = (flipped(self.dp, 1), self.z)
        self.along_y = (flipped(self.dp, 2), self.z)
        self.inward = (self.dp, self.z + self.step)
        self.outward = (self.dp, self.z - self.step)
        self.further = (self.dp, self.z + 2 * self.step)
        self.pending = []

    def order(self, index):
        near = (self.position + index) % 2 if index < 2 else index
        return near * self.step + 3 * self.upper

    def take(self, count=1):
        first = self.taken
        self.taken += count
        return first

    def barrier(self):
        barrier = pltpu.get_barrier_semaphore()
        for device in (self.core, self.along_x, self.along_y, self.inward, self.further):
            pl.semaphore_signal(barrier, inc=1, device_id=device, device_id_type=MESH)

        @pl.when(self.position == 1)
        def _():
            pl.semaphore_signal(barrier, inc=1, device_id=self.outward, device_id_type=MESH)

        pl.semaphore_wait(barrier, 5 + self.position)

    def copy_with(self, source, target, send, receive, device):
        return pltpu.make_async_remote_copy(
            src_ref=source,
            dst_ref=target,
            send_sem=send,
            recv_sem=receive,
            device_id=device,
            device_id_type=MESH,
        )

    def copy(self, source, target, send, receive, device):
        return self.copy_with(
            source, target, self.semaphores.at[send], self.semaphores.at[receive], device
        )

    def send(self, source, target, receive, device, position=None):
        copy = self.copy(source, target, self.take(), receive, device)
        if position is None:
            copy.start()
        else:
            pl.when(self.position == position)(copy.start)
        self.pending.append((copy, position))

    def arrived(self, region, receive):
        self.copy(region, region, receive, receive, self.core).wait_recv()

    def finish(self):
        for copy, position in self.pending:
            if position is None:
                copy.wait_send()
            else:
                pl.when(self.position == position)(copy.wait_send)


class LineGather:
    def __init__(self, links, region, own=None):
        self.links, self.region = links, region
        self.receives = links.take(4)
        self.own = region(links.z) if own is None else own

    def start(self):
        links = self.links
        target, receive = self.region(links.z), self.receives + links.z
        links.send(self.own, target, receive, links.further)
        links.send(self.own, target, receive, links.inward)
        links.send(self.own, target, receive, links.outward, 1)

    def relay(self):
        links = self.links
        source = links.order(3)
        block = self.region(source)

        @pl.when(links.position == 1)
        def _():
            links.arrived(block, self.receives + source)

        links.send(block, block, self.receives + source, links.outward, 1)

    def arrive(self, index):
        links = self.links
        source = links.order(index)

        def wait():
            links.arrived(self.region(source), self.receives + source)

        if index < 3:
            wait()
        else:
            pl.when(links.position == 0)(wait)


class PlaneGather:
    def __init__(self, links, region, parity, own=None):
        self.links, self.region, self.parity = links, region, parity
        self.receives = links.take(7)
        self.own = region(links.dp) if own is None else own

    def start(self):
        links, first = self.links, self.receives
        target = self.region(links.dp)
        links.send(self.own, target, first, links.along_x)
        links.send(self.own, target, first + 1, links.along_y)
        links.send(self.own, target, first + 2, links.core)

    def forward(self):
        links, first = self.links, self.receives
        across = self.region(flipped(links.dp, 1))
        links.arrived(across, first)
        if self.parity == 0:
            links.send(across, across, first + 3, links.along_y)
        links.send(across, across, first + 4, links.core)
        along = self.region(flipped(links.dp, 2))
        links.arrived(along, first + 1)
        if self.parity == 1:
            links.send(along, along, first + 3, links.along_x)
        links.send(along, along, first + 5, links.core)

    def last(self):
        links, first = self.links, self.receives
        corner = self.region(flipped(flipped(links.dp, 1), 2))
        links.arrived(corner, first + 3)
        links.send(corner, corner, first + 6, links.core)

    def complete(self):
        links, first = self.links, self.receives
        other = flipped(links.dp, 0)
        links.arrived(self.region(other), first + 2)
        links.arrived(self.region(flipped(other, 1)), first + 4)
        links.arrived(self.region(flipped(other, 2)), first + 5)
        links.arrived(self.region(flipped(flipped(other, 1), 2)), first + 6)


ANY = pl.BlockSpec(memory_space=pl.ANY)


def front_kernel(
    stripe_ref,
    gates_ref,
    masters_ref,
    hidden_ref,
    cotangent_ref,
    dense_ref,
    weights_ref,
    cotangents_ref,
    tokens_ref,
    routed_parts_ref,
    grad_parts_ref,
    received_ref,
    grad_returned_ref,
    act_ref,
    grad_gate_ref,
    grad_up_ref,
    normed_attend_out,
    projected_out,
    attended_out,
    residual_out,
    grad_shared_out,
    base_out,
    shared_sum_ref,
    scale_ref,
    gains_ref,
    normed_attend_ref,
    projected_ref,
    attended_ref,
    residual_ref,
    grad_shared_ref,
    base_ref,
    normed_mixer_ref,
    shared_act_ref,
    grad_shared_pre_ref,
    matrices,
    extra,
    all_gates,
    places,
    my_gates,
    chosen,
    forward_slots,
    backward_slots,
    narrow,
    pair_sum,
    corner_x,
    corner_y,
    side_x,
    side_y,
    semaphores,
    shard_out,
    shard_in,
    local,
    load_sems,
    expert_sems,
    shared_sems,
    keep_sems,
):
    links = Links(semaphores)
    stripe, columns = stripe_ref.shape
    length, width = hidden_ref.shape
    panels, rows, hidden = masters_ref.shape
    experts = panels // 3
    slots = chosen.shape[1] // experts
    first_panels = 8
    middle = first_panels * hidden + extra.shape[1]
    halves = ((0, middle), (middle, columns - middle))
    query_width = HEADS * HD
    kv_width = KVH * HD
    ahead = 4

    def dense_region(dp, z, half):
        first, count = halves[half]
        row = pl.multiple_of((dp * 4 + z) * stripe, stripe)
        return dense_ref.at[pl.ds(row, stripe), pl.ds(first, count)]

    def own(half):
        first, count = halves[half]
        return stripe_ref.at[:, pl.ds(first, count)]

    def sequence(ref, z):
        return ref.at[pl.ds(pl.multiple_of(z * length, length), length), :]

    def shard_region(dp, panel):
        return weights_ref.at[panel, pl.ds(pl.multiple_of(dp * rows, rows), rows), :]

    lines = [
        LineGather(links, functools.partial(dense_region, links.dp, half=half), own(half))
        for half in range(2)
    ]
    cotangents = LineGather(links, functools.partial(sequence, cotangents_ref), cotangent_ref)
    tokens = LineGather(links, functools.partial(sequence, tokens_ref), normed_mixer_ref)
    gates = LineGather(links, lambda z: all_gates.at[z], gates_ref)
    planes = [
        [
            PlaneGather(
                links,
                functools.partial(dense_region, z=links.order(index), half=half),
                index % 2,
                own(half) if index == 0 else None,
            )
            for index in range(4)
        ]
        for half in range(2)
    ]

    def shard_copy(kind, panel, source_dp, device):
        block = shard_region(source_dp, panel)
        return links.copy_with(
            block, block, shard_out.at[kind, panel], shard_in.at[kind, panel], device
        )

    dp = links.dp
    dp_core, dp_x, dp_y = flipped(dp, 0), flipped(dp, 1), flipped(dp, 2)
    dp_corner = flipped(dp_x, 2)

    def hop(kind, panel):
        source, device = (
            (dp, links.along_x),
            (dp, links.along_y),
            (dp, links.core),
            None,
            (dp_x, links.core),
            (dp_y, links.core),
            (dp_corner, links.core),
        )[kind]
        return shard_copy(kind, panel, source, device)

    def corner_copy(panel, parity):
        if parity == 0:
            return shard_copy(3, panel, dp_x, links.along_y)
        return shard_copy(3, panel, dp_y, links.along_x)

    def shard_arrived(kind, panel, source_dp):
        shard_copy(kind, panel, source_dp, links.core).wait_recv()

    def shard_start(panel):
        for kind in range(3):
            hop(kind, panel).start()

    def shard_forward(panel):
        shard_arrived(0, panel, dp_x)
        pl.when(panel % 2 == 0)(corner_copy(panel, 0).start)
        hop(4, panel).start()
        shard_arrived(1, panel, dp_y)
        pl.when(panel % 2 == 1)(corner_copy(panel, 1).start)
        hop(5, panel).start()

    def shard_last(panel):
        shard_arrived(3, panel, dp_corner)
        hop(6, panel).start()

    def shard_complete(panel):
        shard_arrived(2, panel, dp_core)
        shard_arrived(4, panel, flipped(dp_core, 1))
        shard_arrived(5, panel, flipped(dp_core, 2))
        shard_arrived(6, panel, flipped(flipped(dp_core, 1), 2))

    def shard_finish(panel):
        for kind in (0, 1, 2, 4, 5, 6):
            hop(kind, panel).wait_send()
        corner_copy(panel, 0).wait_send()

    def exchange(panel):
        shard_forward(panel)
        if panel + ahead < panels:
            shard_start(panel + ahead)
        if panel >= 3:
            shard_last(panel - 3)

    local_copies = [
        pltpu.make_async_copy(source, target, local.at[index])
        for index, (source, target) in enumerate(
            (
                (
                    stripe_ref,
                    dense_ref.at[
                        pl.ds(pl.multiple_of((links.dp * 4 + links.z) * stripe, stripe), stripe), :
                    ],
                ),
                (gates_ref, all_gates.at[links.z]),
                (cotangent_ref, sequence(cotangents_ref, links.z)),
            )
        )
    ]
    token_copy = pltpu.make_async_copy(
        normed_mixer_ref, sequence(tokens_ref, links.z), local.at[3]
    )

    def dense_column(panel):
        return panel * hidden + (0 if panel < first_panels else extra.shape[1])

    loads = [
        pltpu.make_async_copy(
            dense_ref.at[:, pl.ds(dense_column(panel), hidden)],
            matrices.at[panel],
            load_sems.at[panel],
        )
        for panel in range(14)
    ]
    extra_load = pltpu.make_async_copy(
        dense_ref.at[:, pl.ds(first_panels * hidden, extra.shape[1])], extra, load_sems.at[14]
    )

    def half_columns(panel):
        return pl.ds(pl.multiple_of(panel % 2 * hidden, hidden), hidden)

    def master_load(panel):
        return pltpu.make_async_copy(
            masters_ref.at[panel],
            grad_shared_ref.at[pl.ds(0, rows), half_columns(panel)],
            expert_sems.at[0, panel % 2],
        )

    def master_store(panel):
        return pltpu.make_async_copy(
            shared_act_ref.at[pl.ds(0, rows), half_columns(panel)],
            shard_region(dp, panel),
            expert_sems.at[1, panel % 2],
        )

    master_load(0).start()
    links.barrier()
    lines[0].start()
    planes[0][0].start()
    lines[1].start()
    gates.start()
    for copy in local_copies:
        copy.start()

    def round_masters(first, last):
        @pl.loop(first, last)
        def _(panel):
            master_load(panel).wait()

            @pl.when(panel + 1 < panels)
            def _():
                master_load(panel + 1).start()

            @pl.when(panel >= 2)
            def _():
                master_store(panel - 2).wait()

            shared_act_ref[:rows, half_columns(panel)] = grad_shared_ref[
                :rows, half_columns(panel)
            ].astype(jnp.bfloat16)
            master_store(panel).start()

    lines[0].arrive(1)
    planes[0][1].start()
    lines[0].arrive(2)
    planes[0][2].start()
    round_masters(0, panels // 3)
    for panel in range(2):
        shard_start(panel)
    planes[0][0].forward()
    lines[0].relay()
    lines[0].arrive(3)
    planes[0][3].start()
    planes[0][1].forward()
    lines[1].relay()
    round_masters(panels // 3, panels)
    for panel in (panels - 2, panels - 1):
        master_store(panel).wait()
    for panel in range(2, ahead):
        shard_start(panel)
    planes[1][0].start()
    planes[0][2].forward()
    lines[1].arrive(1)
    planes[1][1].start()
    planes[0][3].forward()
    cotangents.start()
    gates.relay()
    lines[1].arrive(2)
    planes[1][2].start()
    for plane in planes[0]:
        plane.last()
    planes[1][0].forward()
    for plane in planes[0]:
        plane.complete()
    local_copies[0].wait()
    extra_load.start()
    for copy in loads[:first_panels]:
        copy.start()

    rows_step = 32

    def norm_rows(source, gain, scale_out, target):
        @pl.loop(0, length // rows_step)
        def _(index):
            part = pl.ds(index * rows_step, rows_step)
            values = source[part, :].astype(jnp.float32)
            scale = lax.rsqrt(jnp.mean(values * values, axis=-1, keepdims=True) + 1e-06)
            if scale_out is not None:
                scale_out[part, :] = scale
            target[part, :] = (values * scale * gains_ref[gain : gain + 1, :]).astype(jnp.bfloat16)

    def project():
        extra_load.wait()
        gains_ref[...] = extra[...].astype(jnp.float32).T[:8, :]
        norm_rows(hidden_ref, 0, None, normed_attend_ref)
        for panel in range(5):
            loads[panel].wait()
            projected_ref[:, panel * hidden : (panel + 1) * hidden] = matmul(
                normed_attend_ref[...], matrices[panel]
            ).astype(jnp.bfloat16)

    def attend(group):
        key_rows = projected_ref[:, query_width + group * HD : query_width + (group + 1) * HD]
        value_first = query_width + kv_width + group * HD
        value_rows = projected_ref[:, value_first : value_first + HD]
        row = lax.broadcasted_iota(jnp.int32, (length, length), 0)
        column = lax.broadcasted_iota(jnp.int32, (length, length), 1)
        per_group = HEADS // KVH
        for head in range(group * per_group, (group + 1) * per_group):
            spot = slice(head * HD, (head + 1) * HD)
            scores = matmul_nt(projected_ref[:, spot], key_rows) * HD ** (-0.5)
            scores = jnp.where(column <= row, scores, -1e30)
            raised = jnp.exp(scores - jnp.max(scores, axis=-1, keepdims=True))
            shares = (raised / jnp.sum(raised, axis=-1, keepdims=True)).astype(jnp.bfloat16)
            attended_ref[:, spot] = matmul(shares, value_rows).astype(jnp.bfloat16)

    def join():
        for part in range(3):
            loads[5 + part].wait()
            update = matmul_nt(
                attended_ref[:, part * hidden : (part + 1) * hidden], matrices[5 + part]
            )
            if part == 0:
                residual_ref[...] = hidden_ref[...].astype(jnp.float32) + update
            else:
                residual_ref[...] += update
        norm_rows(residual_ref, 1, scale_ref, normed_mixer_ref)
        tokens.start()
        token_copy.start()

    def shared(part):
        spot = slice(part * hidden, (part + 1) * hidden)
        for panel in (8, 10, 12):
            loads[panel + part].wait()
        gate = matmul(normed_mixer_ref[...], matrices[8 + part])
        up = matmul(normed_mixer_ref[...], matrices[10 + part])
        sig = jax.nn.sigmoid(gate)
        gate_act = gate * sig
        shared_act_ref[:, spot] = (gate_act * up).astype(jnp.bfloat16)
        grad_act = matmul(cotangent_ref[...], matrices[12 + part])
        grad_shared_pre_ref[:, spot] = (
            grad_act * up * sig * (1.0 + gate * (1.0 - sig))
        ).astype(jnp.bfloat16)
        up_spot = slice((2 + part) * hidden, (3 + part) * hidden)
        grad_shared_pre_ref[:, up_spot] = (grad_act * gate_act).astype(jnp.bfloat16)

    def shared_back(part):
        spot = slice(part * hidden, (part + 1) * hidden)
        up_spot = slice((2 + part) * hidden, (3 + part) * hidden)
        grad = matmul_nt(grad_shared_pre_ref[:, spot], matrices[8 + part]) + matmul_nt(
            grad_shared_pre_ref[:, up_spot], matrices[10 + part]
        )
        out = matmul_nt(shared_act_ref[:, spot], matrices[12 + part])
        if part == 0:
            grad_shared_ref[...] = grad
            base_ref[...] = residual_ref[...] + out
        else:
            grad_shared_ref[...] += grad
            base_ref[...] += out

    kept = [
        pltpu.make_async_copy(source, target, keep_sems.at[index])
        for index, (source, target) in enumerate(
            (
                (normed_attend_ref, normed_attend_out),
                (projected_ref, projected_out),
                (attended_ref, attended_out),
                (residual_ref, residual_out),
                (grad_shared_ref, grad_shared_out),
                (base_ref, base_out),
            )
        )
    ]

    def place_slots():
        local_copies[1].wait()
        before = (
            lax.broadcasted_iota(jnp.int32, (length, length), 0)
            < lax.broadcasted_iota(jnp.int32, (length, length), 1)
        )
        earlier_mask = jnp.where(before, 1.0, 0.0).astype(jnp.bfloat16)
        for source in range(4):
            gate = all_gates[source, links.z]
            hot = gate > 0.0
            earlier = matmul(jnp.where(hot, 1.0, 0.0).astype(jnp.bfloat16), earlier_mask)
            place = jnp.where(hot, earlier, -1.0).astype(jnp.int32)
            for expert in range(experts):
                places[expert, source : source + 1, :] = place[expert : expert + 1, :]
                my_gates[expert, source : source + 1, :] = gate[expert : expert + 1, :]

    core, chip = dp % 2, dp // 2
    chip_x, chip_y = flipped(chip, 0), flipped(chip, 1)
    chip_corner = flipped(chip_x, 1)
    shared_panels = pair_sum.shape[0]
    half = rows // 2
    quarter = width // 4

    ring = matrices.at[13]

    def ring_rows(index, which):
        return pl.ds(pl.multiple_of((2 * index + which) * rows, rows), rows)

    def pair_copy(panel, index):
        return links.copy_with(
            ring.at[ring_rows(index, 1 - core)],
            pair_sum.at[panel, index],
            shared_sems.at[0, 0, panel],
            shared_sems.at[1, 0, panel],
            links.core,
        )

    def shared_copy(kind, panel):
        source, target, device = (
            (pair_sum.at[panel], pair_sum.at[panel], links.core),
            (pair_sum.at[panel, chip_corner, pl.ds(0, half)], corner_x.at[panel], links.along_x),
            (pair_sum.at[panel, chip_corner, pl.ds(half, half)], corner_y.at[panel], links.along_y),
            (pair_sum.at[panel, chip_x], side_x.at[panel], links.along_x),
            (pair_sum.at[panel, chip_y], side_y.at[panel], links.along_y),
        )[kind]
        return links.copy_with(
            source, target, shared_sems.at[0, kind, panel], shared_sems.at[1, kind, panel], device
        )

    def shared_fill(panel):
        left_ref = normed_mixer_ref if panel < 4 else cotangent_ref
        right_ref = grad_shared_pre_ref if panel < 4 else shared_act_ref
        first = (panel if panel < 4 else panel - 4) * hidden
        right = right_ref[:, first : first + hidden]
        for index in range(4):
            part = matmul_tn(left_ref[:, index * quarter : (index + 1) * quarter], right)
            ring[index * quarter : (index + 1) * quarter, :] = part.astype(jnp.bfloat16)
        for index in range(4):
            pair_copy(panel, index).start()

    def shared_pair(panel):
        shared_copy(0, panel).wait()
        for index in range(4):
            pair_sum[panel, index] = (
                pair_sum[panel, index].astype(jnp.float32)
                + ring[ring_rows(index, core), :].astype(jnp.float32)
            ).astype(jnp.bfloat16)

    def shared_corners(panel):
        for kind in (1, 2):
            shared_copy(kind, panel).start()

    def shared_sides(panel):
        for kind in (1, 2):
            shared_copy(kind, panel).wait()
        pair_sum[panel, chip_y, :half] = (
            pair_sum[panel, chip_y, :half].astype(jnp.float32)
            + corner_x[panel].astype(jnp.float32)
        ).astype(jnp.bfloat16)
        pair_sum[panel, chip_x, half:] = (
            pair_sum[panel, chip_x, half:].astype(jnp.float32)
            + corner_y[panel].astype(jnp.float32)
        ).astype(jnp.bfloat16)
        for kind in (3, 4):
            shared_copy(kind, panel).start()

    def shared_total(panel):
        for kind in (3, 4):
            shared_copy(kind, panel).wait()
        value = (
            pair_sum[panel, chip].astype(jnp.float32)
            + side_x[panel].astype(jnp.float32)
            + side_y[panel].astype(jnp.float32)
        )
        matrices[12, pl.ds(panel % 2 * rows, rows), :] = value.astype(jnp.bfloat16)

    def shared_store(panel):
        return pltpu.make_async_copy(
            matrices.at[12, pl.ds(panel % 2 * rows, rows)],
            shared_sum_ref.at[panel],
            local.at[4 + panel % 2],
        )

    project()
    lines[1].arrive(3)
    planes[1][3].start()
    planes[1][1].forward()
    attend(0)
    attend(1)
    planes[1][2].forward()
    attend(2)
    attend(3)
    planes[1][3].forward()
    cotangents.relay()
    join()
    for plane in planes[1]:
        plane.last()
    for index in range(1, 4):
        gates.arrive(index)
    place_slots()
    for plane in planes[1]:
        plane.complete()
    for copy in loads[first_panels:]:
        copy.start()
    exchange(0)
    shared(0)
    exchange(1)
    shared(1)
    exchange(2)
    shared_back(0)
    exchange(3)
    shared_back(1)
    for copy in kept:
        copy.start()
    exchange(4)
    shared_fill(0)
    tokens.relay()
    for panel in range(5, 11):
        exchange(panel)
        shared_pair(panel - 5)
        shared_corners(panel - 5)
        if panel < 10:
            shared_fill(panel - 4)
    for index in range(1, 4):
        cotangents.arrive(index)
        tokens.arrive(index)
    local_copies[2].wait()
    token_copy.wait()
    token_loads = [
        pltpu.make_async_copy(
            source.at[:, pl.ds(part * hidden, hidden)],
            matrices.at[first + part, pl.ds(0, 4 * length)],
            load_sems.at[first + part],
        )
        for first, source in ((6, tokens_ref), (9, cotangents_ref))
        for part in range(3)
    ]
    for copy in token_loads:
        copy.start()
    slot_iota = lax.broadcasted_iota(jnp.int32, (slots, length), 0)

    def slot_gate(expert, source):
        hot = slot_iota == places[expert, pl.ds(source, 1), :]
        return jnp.sum(
            jnp.where(hot, my_gates[expert, pl.ds(source, 1), :], 0.0), axis=1, keepdims=True
        )

    for source in range(4):
        for expert in range(experts):
            hot = slot_iota == places[expert, source : source + 1, :]
            chosen[source, expert * slots : (expert + 1) * slots, :] = jnp.where(
                hot, 1.0, 0.0
            ).astype(jnp.bfloat16)
    exchange(11)
    for copy in token_loads:
        copy.wait()

    @pl.loop(0, 4)
    def _(source):
        part = pl.ds(source * length, length)
        spots = pl.ds(pl.multiple_of(source * slots, slots), slots)
        slot_gates = [slot_gate(expert, source) for expert in range(experts)]
        for block in range(3):
            spot = pl.ds(block * hidden, hidden)
            token_slots = matmul(chosen[source], matrices[6 + block, part, :])
            grad_slots = matmul(chosen[source], matrices[9 + block, part, :])
            for expert in range(experts):
                rows_of = slice(expert * slots, (expert + 1) * slots)
                forward_slots[expert, spots, spot] = token_slots[rows_of].astype(jnp.bfloat16)
                backward_slots[expert, spots, spot] = (
                    grad_slots[rows_of] * slot_gates[expert]
                ).astype(jnp.bfloat16)

    def slot_stores(expert):
        return [
            pltpu.make_async_copy(
                source.at[expert], target.at[expert], expert_sems.at[2 + index, expert]
            )
            for index, (source, target) in enumerate(
                ((forward_slots, received_ref), (backward_slots, grad_returned_ref))
            )
        ]

    def narrow_stores(expert):
        buffer = expert % 2
        return [
            pltpu.make_async_copy(
                narrow.at[buffer, index], target.at[expert], expert_sems.at[4 + buffer, index]
            )
            for index, target in enumerate((act_ref, grad_gate_ref, grad_up_ref))
        ]

    def weight_loads(expert):
        buffer = expert % 2
        return [
            pltpu.make_async_copy(
                weights_ref.at[3 * expert + matrix],
                matrices.at[3 * buffer + matrix],
                expert_sems.at[6 + buffer, matrix],
            )
            for matrix in range(3)
        ]

    def fetch(expert):
        for matrix, copy in enumerate(weight_loads(expert)):
            shard_complete(3 * expert + matrix)
            copy.start()

    for expert in range(experts):
        for copy in slot_stores(expert):
            copy.start()
    fetch(0)

    @pl.loop(0, experts)
    def _(expert):
        buffer = expert % 2
        loaded = weight_loads(expert)

        @pl.when(expert >= 2)
        def _():
            for copy in narrow_stores(expert - 2):
                copy.wait()

        received = forward_slots[expert]
        grad_out = backward_slots[expert]
        loaded[0].wait()
        gate_pre = matmul(received, matrices[3 * buffer])
        loaded[1].wait()
        up_pre = matmul(received, matrices[3 * buffer + 1])
        loaded[2].wait()
        grad_act = matmul(grad_out, matrices[3 * buffer + 2])
        gate_sig = jax.nn.sigmoid(gate_pre)
        gate_act = gate_pre * gate_sig
        act = (gate_act * up_pre).astype(jnp.bfloat16)
        grad_gate = (grad_act * up_pre * gate_sig * (1.0 + gate_pre * (1.0 - gate_sig))).astype(
            jnp.bfloat16
        )
        grad_up = (grad_act * gate_act).astype(jnp.bfloat16)
        narrow[buffer, 0] = act
        narrow[buffer, 1] = grad_gate
        narrow[buffer, 2] = grad_up
        for copy in narrow_stores(expert):
            copy.start()
        for copy in slot_stores(expert):
            copy.wait()
        slot_gates = jnp.concatenate([slot_gate(expert, source) for source in range(4)], 0)
        for block in range(3):
            rows_of = pl.ds(block * hidden, hidden)
            spot = pl.ds(block * hidden, hidden)
            out = matmul_nt(act, matrices[3 * buffer + 2, rows_of, :]).astype(jnp.bfloat16)
            forward_slots[expert, :, spot] = (
                out.astype(jnp.float32) * slot_gates
            ).astype(jnp.bfloat16)
            backward_slots[expert, :, spot] = (
                matmul_nt(grad_gate, matrices[3 * buffer, rows_of, :])
                + matmul_nt(grad_up, matrices[3 * buffer + 1, rows_of, :])
            ).astype(jnp.bfloat16)

        later = (
            (lambda: exchange(12), lambda: shared_sides(0)),
            (lambda: exchange(13), lambda: shared_sides(1)),
            (lambda: exchange(14), lambda: shared_sides(2)),
            (lambda: exchange(15), lambda: exchange(16), lambda: shard_last(14)),
            (
                lambda: shard_forward(17),
                lambda: shared_sides(3),
                lambda: shared_sides(4),
                lambda: shared_sides(5),
                lambda: shard_last(15),
                lambda: shard_last(16),
                lambda: shard_last(17),
            ),
        )
        for done, calls in enumerate(later):

            @pl.when(expert == done)
            def _():
                for call in calls:
                    call()

        @pl.when(expert + 1 < experts)
        def _():
            fetch(expert + 1)

    for expert in (experts - 2, experts - 1):
        for copy in narrow_stores(expert):
            copy.wait()
    out_copies = []
    for first, values, target in ((0, backward_slots, grad_parts_ref), (3, forward_slots, routed_parts_ref)):
        for block in range(3):
            spot = slice(block * hidden, (block + 1) * hidden)
            for source in range(4):
                slots_of = jnp.concatenate(
                    [
                        values[expert, source * slots : (source + 1) * slots, spot]
                        for expert in range(experts)
                    ],
                    0,
                )
                matrices[first + block, source * length : (source + 1) * length, :] = matmul_tn(
                    chosen[source], slots_of
                ).astype(jnp.bfloat16)
            out_copies.append(
                pltpu.make_async_copy(
                    matrices.at[first + block, pl.ds(0, 4 * length)],
                    target.at[:, pl.ds(block * hidden, hidden)],
                    load_sems.at[first + block],
                )
            )
            out_copies[-1].start()
    @pl.loop(0, panels)
    def _(panel):
        shard_finish(panel)

    for panel in range(shared_panels):
        if panel >= 2:
            shared_store(panel - 2).wait()
        shared_total(panel)
        shared_store(panel).start()
    for panel in (shared_panels - 2, shared_panels - 1):
        shared_store(panel).wait()
    for copy in (*kept, *out_copies):
        copy.wait()

    links.finish()


def front(stripe, gates, masters, hidden_in, cotangent, slots):
    length, width = cotangent.shape
    stripe_rows, columns = stripe.shape
    panels, rows, hidden = masters.shape
    experts = panels // 3
    low, full = jnp.bfloat16, jnp.float32
    vmem = pl.BlockSpec(memory_space=pltpu.VMEM)
    query_width = HEADS * HD
    spots = 4 * slots
    return pl.pallas_call(
        front_kernel,
        in_specs=[ANY] * 3 + [vmem] * 2,
        out_specs=[ANY] * 18 + [vmem] * 2,
        out_shape=[
            jax.ShapeDtypeStruct((stripe_rows * 32, columns), low),
            jax.ShapeDtypeStruct((panels, rows * 8, hidden), low),
            *[jax.ShapeDtypeStruct((length * 4, width), low)] * 4,
            *[jax.ShapeDtypeStruct((experts, spots, width), low)] * 2,
            *[jax.ShapeDtypeStruct((experts, spots, hidden), low)] * 3,
            jax.ShapeDtypeStruct((length, width), low),
            jax.ShapeDtypeStruct((length, query_width + 2 * KVH * HD), low),
            jax.ShapeDtypeStruct((length, query_width), low),
            jax.ShapeDtypeStruct((length, width), full),
            jax.ShapeDtypeStruct((length, width), full),
            jax.ShapeDtypeStruct((length, width), full),
            jax.ShapeDtypeStruct((6, rows, hidden), low),
            jax.ShapeDtypeStruct((length, 1), full),
            jax.ShapeDtypeStruct((8, width), full),
        ],
        scratch_shapes=[
            pltpu.VMEM((length, width), low),
            pltpu.VMEM((length, query_width + 2 * KVH * HD), low),
            pltpu.VMEM((length, query_width), low),
            pltpu.VMEM((length, width), full),
            pltpu.VMEM((length, width), full),
            pltpu.VMEM((length, width), full),
            pltpu.VMEM((length, width), low),
            pltpu.VMEM((length, FFS), low),
            pltpu.VMEM((length, 2 * FFS), low),
            pltpu.VMEM((14, width, hidden), low),
            pltpu.VMEM((width, 128), low),
            pltpu.VMEM((4, 4, 8, length), full),
            pltpu.VMEM((experts, 4, length), jnp.int32),
            pltpu.VMEM((experts, 4, length), full),
            pltpu.VMEM((4, experts * slots, length), low),
            pltpu.VMEM((experts, spots, width), low),
            pltpu.VMEM((experts, spots, width), low),
            pltpu.VMEM((2, 3, spots, hidden), low),
            pltpu.VMEM((6, 4, rows, hidden), low),
            pltpu.VMEM((6, rows // 2, hidden), low),
            pltpu.VMEM((6, rows // 2, hidden), low),
            pltpu.VMEM((6, rows, hidden), low),
            pltpu.VMEM((6, rows, hidden), low),
            pltpu.SemaphoreType.DMA((170,)),
            pltpu.SemaphoreType.DMA((7, panels)),
            pltpu.SemaphoreType.DMA((7, panels)),
            pltpu.SemaphoreType.DMA((6,)),
            pltpu.SemaphoreType.DMA((15,)),
            pltpu.SemaphoreType.DMA((8, 6)),
            pltpu.SemaphoreType.DMA((2, 5, 6)),
            pltpu.SemaphoreType.DMA((6,)),
        ],
        compiler_params=pltpu.CompilerParams(
            collective_id=1, has_side_effects=True, vmem_limit_bytes=63 * MIB
        ),
        name="front",
    )(stripe, gates, masters, hidden_in, cotangent)


def scatter_kernel(
    grad_parts_ref,
    received_ref,
    grad_returned_ref,
    act_ref,
    grad_gate_ref,
    grad_up_ref,
    dense_ref,
    shared_sum_ref,
    cotangent_ref,
    normed_attend_ref,
    attended_ref,
    residual_in,
    grad_shared_in,
    projected_in,
    hidden_in,
    scale_ref,
    gains_ref,
    expert_sum_ref,
    stripes_ref,
    grad_input_ref,
    grad_gain_ref,
    residual_ref,
    grad_shared_ref,
    projected_ref,
    hidden_ref,
    ring,
    pair_sum,
    corner_x,
    corner_y,
    side_x,
    side_y,
    staged,
    wide,
    narrow,
    left,
    right,
    out_weights,
    grad_tokens,
    grad_attended,
    grad_pair,
    grad_residual_ref,
    key_weights,
    line_out,
    line_in,
    pair_sems,
    slot_sems,
    line_sems,
    token_sems,
    load_sems,
    free,
):
    dp, z = lax.axis_index("dp"), lax.axis_index("expert")
    core, chip = dp % 2, dp // 2
    chip_x, chip_y = flipped(chip, 0), flipped(chip, 1)
    chip_corner = flipped(chip_x, 1)
    device_core = (flipped(dp, 0), z)
    device_x = (flipped(dp, 1), z)
    device_y = (flipped(dp, 2), z)
    others = [(dp, (z + turn) % 4) for turn in range(1, 4)]
    slots = pair_sum.shape[0]
    experts = received_ref.shape[0]
    expert_panels = 3 * experts
    dense_panels = line_out.shape[0]
    shared_panels = dense_panels - right.shape[0]
    panels = expert_panels + right.shape[0]
    length, width = residual_ref.shape
    share, hidden = staged.shape[1:]
    half = share // 2
    stripe = share // 4
    query_width = HEADS * HD
    kv_width = KVH * HD
    block = width // 4

    def remote(source, target, send, receive, device):
        return pltpu.make_async_remote_copy(
            src_ref=source,
            dst_ref=target,
            send_sem=send,
            recv_sem=receive,
            device_id=device,
            device_id_type=MESH,
        )

    barrier = pltpu.get_barrier_semaphore()
    for device in (device_core, device_x, device_y, *others):
        pl.semaphore_signal(barrier, inc=1, device_id=device, device_id_type=MESH)
    pl.semaphore_wait(barrier, 6)

    grad_copies = [
        remote(
            grad_parts_ref.at[pl.ds(pl.multiple_of(device[1] * length, length), length), :],
            grad_tokens.at[turn],
            token_sems.at[turn],
            token_sems.at[3 + turn],
            device,
        )
        for turn, device in enumerate(others)
    ]
    for copy in grad_copies:
        copy.start()

    def expert_loads(expert):
        buffer = expert % 2
        return [
            pltpu.make_async_copy(source.at[expert], target, load_sems.at[buffer, index])
            for index, (source, target) in enumerate(
                (
                    (received_ref, wide.at[buffer, 0]),
                    (grad_returned_ref, wide.at[buffer, 1]),
                    (grad_gate_ref, narrow.at[buffer, 0]),
                    (grad_up_ref, narrow.at[buffer, 1]),
                    (act_ref, narrow.at[buffer, 2]),
                )
            )
        ]

    for copy in expert_loads(0):
        copy.start()

    def columns(ref, panel):
        return ref.at[:, pl.ds(panel * hidden, hidden)]

    sources = [
        (cotangent_ref, left.at[0]),
        (normed_attend_ref, left.at[2]),
        *[(columns(attended_ref, panel), right.at[panel]) for panel in range(3)],
        (shared_sum_ref, line_out.at[pl.ds(0, shared_panels)]),
        (residual_in, residual_ref),
        (grad_shared_in, grad_shared_ref),
        (projected_in, projected_ref),
        (hidden_in, hidden_ref),
        (dense_ref.at[:, pl.ds(query_width + 2 * kv_width, query_width)], out_weights),
        (dense_ref.at[:, pl.ds(query_width, 2 * kv_width)], key_weights),
        (
            grad_parts_ref.at[pl.ds(pl.multiple_of(z * length, length), length), :],
            grad_tokens.at[3],
        ),
    ]
    dense_loads = [
        pltpu.make_async_copy(source, target, load_sems.at[2 + index // 5, index % 5])
        for index, (source, target) in enumerate(sources)
    ]
    for copy in dense_loads:
        copy.start()
    query_load = pltpu.make_async_copy(
        dense_ref.at[:, pl.ds(0, query_width)], out_weights, pair_sems.at[4]
    )

    def fill(pair, left_ref, right_value):
        for chip_index in range(4):
            part = matmul_tn(left_ref[:, chip_index * block : (chip_index + 1) * block], right_value)
            ring[pair, chip_index] = part.astype(jnp.bfloat16).reshape(2, share, hidden)

    def total(first, *more):
        result = first.astype(jnp.float32)
        for value in more:
            result = result + value.astype(jnp.float32)
        return result

    def pair_copy(panel):
        pair, slot = panel % 2, panel % slots
        return remote(
            ring.at[pair, :, 1 - core],
            pair_sum.at[slot],
            pair_sems.at[pair],
            slot_sems.at[0, slot],
            device_core,
        )

    def corner_copies(panel):
        slot = panel % slots
        return (
            remote(
                pair_sum.at[slot, chip_corner, pl.ds(0, half)],
                corner_x.at[slot],
                slot_sems.at[1, slot],
                slot_sems.at[2, slot],
                device_x,
            ),
            remote(
                pair_sum.at[slot, chip_corner, pl.ds(half, half)],
                corner_y.at[slot],
                slot_sems.at[3, slot],
                slot_sems.at[4, slot],
                device_y,
            ),
        )

    def side_copies(panel):
        slot = panel % slots
        return (
            remote(
                pair_sum.at[slot, chip_x],
                side_x.at[slot],
                slot_sems.at[5, slot],
                slot_sems.at[6, slot],
                device_x,
            ),
            remote(
                pair_sum.at[slot, chip_y],
                side_y.at[slot],
                slot_sems.at[7, slot],
                slot_sems.at[8, slot],
                device_y,
            ),
        )

    def line_copies(panel):
        return [
            remote(
                line_out.at[panel, pl.ds(pl.multiple_of(device[1] * stripe, stripe), stripe)],
                line_in.at[panel, turn],
                line_sems.at[0, panel, turn],
                line_sems.at[1, panel, turn],
                device,
            )
            for turn, device in enumerate(others)
        ]

    def staged_copy(panel):
        return pltpu.make_async_copy(
            staged.at[panel % 2], expert_sum_ref.at[panel], pair_sems.at[2 + panel % 2]
        )

    def post(panel):
        @pl.when(panel >= slots)
        def _():
            pl.semaphore_wait(free.at[0], 1)

        pair_copy(panel).start()

    def sum_pair(panel):
        pair, slot = panel % 2, panel % slots
        pair_copy(panel).wait()
        for chip_index in range(4):
            pair_sum[slot, chip_index] = total(
                pair_sum[slot, chip_index], ring[pair, chip_index, core]
            ).astype(jnp.bfloat16)

        @pl.when(panel >= slots)
        def _():
            pl.semaphore_wait(free.at[1], 1)
            pl.semaphore_wait(free.at[2], 1)

        for copy in corner_copies(panel):
            copy.start()

    def sum_corner(panel):
        slot = panel % slots
        for copy in corner_copies(panel):
            copy.wait_recv()
        pair_sum[slot, chip_y, :half] = total(
            pair_sum[slot, chip_y, :half], corner_x[slot]
        ).astype(jnp.bfloat16)
        pair_sum[slot, chip_x, half:] = total(
            pair_sum[slot, chip_x, half:], corner_y[slot]
        ).astype(jnp.bfloat16)
        for copy in side_copies(panel):
            copy.start()

    def sum_sides(panel):
        slot = panel % slots
        for copy in corner_copies(panel):
            copy.wait_send()
        for copy in side_copies(panel):
            copy.wait()
        value = total(pair_sum[slot, chip], side_x[slot], side_y[slot]).astype(jnp.bfloat16)

        @pl.when(panel < expert_panels)
        def _():
            @pl.when(panel >= 2)
            def _():
                staged_copy(panel - 2).wait()

            staged[panel % 2] = value
            staged_copy(panel).start()

        @pl.when(panel >= expert_panels)
        def _():
            index = panel - expert_panels + shared_panels
            line_out[index] = value
            for copy in line_copies(index):
                copy.start()

        @pl.when(panel < panels - slots)
        def _():
            for index, device in enumerate((device_core, device_x, device_y)):
                pl.semaphore_signal(
                    free.at[index], inc=1, device_id=device, device_id_type=MESH
                )

    def residual_backward(part):
        if part == 0:
            for copy in dense_loads:
                copy.wait()
            for copy in grad_copies:
                copy.wait()
            grad_gain_ref[...] = jnp.zeros_like(grad_gain_ref)
        rows_step = 32
        steps = length // rows_step // 2

        @pl.loop(part * steps, (part + 1) * steps)
        def _(index):
            rows = pl.ds(index * rows_step, rows_step)
            grad_normed = (
                total(
                    grad_tokens[3, rows, :],
                    grad_tokens[0, rows, :],
                    grad_tokens[1, rows, :],
                    grad_tokens[2, rows, :],
                )
                + grad_shared_ref[rows, :]
            )
            residual, scale = residual_ref[rows, :], scale_ref[rows, :]
            grad_scaled = grad_normed * gains_ref[1:2, :]
            mean = jnp.mean(grad_scaled * residual, axis=-1, keepdims=True)
            grad_residual = (
                left[0, rows, :].astype(jnp.float32)
                + scale * grad_scaled
                - residual * (scale * scale * scale) * mean
            )
            grad_residual_ref[rows, :] = grad_residual
            left[1, rows, :] = grad_residual.astype(jnp.bfloat16)
            grad_gain_ref[1:2, :] += jnp.sum(
                grad_normed * residual * scale, axis=0, keepdims=True
            )

    def attended_backward():
        grad_attended[...] = matmul(left[1], out_weights[...]).astype(jnp.bfloat16)
        query_load.start()

    def query_backward():
        query_load.wait()
        for part in range(3):
            update = matmul_nt(right[3 + part], out_weights[:, part * hidden : (part + 1) * hidden])
            if part == 0:
                grad_input_ref[...] = update
            else:
                grad_input_ref[...] += update

    def key_backward():
        for part in range(2):
            grad_input_ref[...] += matmul_nt(
                right[6 + part], key_weights[:, part * hidden : (part + 1) * hidden]
            )

    def input_backward():
        rows_step = 32

        @pl.loop(0, length // rows_step)
        def _(index):
            rows = pl.ds(index * rows_step, rows_step)
            values, grad_normed = hidden_ref[rows, :].astype(jnp.float32), grad_input_ref[rows, :]
            scale = lax.rsqrt(jnp.mean(values * values, axis=-1, keepdims=True) + 1e-06)
            grad_scaled = grad_normed * gains_ref[0:1, :]
            mean = jnp.mean(grad_scaled * values, axis=-1, keepdims=True)
            grad_input_ref[rows, :] = (
                grad_residual_ref[rows, :]
                + scale * grad_scaled
                - values * (scale * scale * scale) * mean
            )
            grad_gain_ref[0:1, :] += jnp.sum(
                grad_normed * values * scale, axis=0, keepdims=True
            )

    def attention_backward(head):
        score_scale = HD ** (-0.5)
        per_group = HEADS // KVH
        heads_wide = hidden // HD
        group = head // per_group
        key_rows = projected_ref[:, query_width + group * HD : query_width + (group + 1) * HD]
        value_first = query_width + kv_width + group * HD
        value_rows = projected_ref[:, value_first : value_first + HD]
        row = lax.broadcasted_iota(jnp.int32, (length, length), 0)
        column = lax.broadcasted_iota(jnp.int32, (length, length), 1)
        spot = slice(head * HD, (head + 1) * HD)
        query, grad_out = projected_ref[:, spot], grad_attended[:, spot]
        scores = jnp.where(column <= row, matmul_nt(query, key_rows) * score_scale, -1e30)
        raised = jnp.exp(scores - jnp.max(scores, axis=-1, keepdims=True))
        weights = raised / jnp.sum(raised, axis=-1, keepdims=True)
        grad_weights = matmul_nt(grad_out, value_rows)
        inner = jnp.sum(weights * grad_weights, axis=-1, keepdims=True)
        grad_scores = (weights * (grad_weights - inner)).astype(jnp.bfloat16)
        grad_query = matmul(grad_scores, key_rows) * score_scale
        place = slice(head % heads_wide * HD, (head % heads_wide + 1) * HD)
        right[3 + head // heads_wide, :, place] = grad_query.astype(jnp.bfloat16)
        grad_key = matmul_tn(grad_scores, query)
        grad_value = matmul_tn(weights.astype(jnp.bfloat16), grad_out)
        if head % per_group > 0:
            grad_key = grad_key + grad_pair[0]
            grad_value = grad_value + grad_pair[1]
        if head % per_group < per_group - 1:
            grad_pair[0] = grad_key
            grad_pair[1] = grad_value
        else:
            place = slice(group * HD, (group + 1) * HD)
            right[6, :, place] = (grad_key * score_scale).astype(jnp.bfloat16)
            right[7, :, place] = grad_value.astype(jnp.bfloat16)

    def two_heads_backward(head):
        attention_backward(head)
        attention_backward(head + 1)

    @pl.loop(0, panels + 5)
    def _(step):
        @pl.when(step < expert_panels)
        def _():
            expert, matrix = step // 3, step % 3

            @pl.when(matrix == 0)
            def _():
                for copy in expert_loads(expert):
                    copy.wait()

                @pl.when(expert + 1 < experts)
                def _():
                    for copy in expert_loads(expert + 1):
                        copy.start()

            fill(step % 2, wide.at[expert % 2, matrix // 2], narrow[expert % 2, matrix])

        backward = [
            *[functools.partial(residual_backward, part) for part in range(2)],
            attended_backward,
            *[functools.partial(two_heads_backward, head) for head in range(0, HEADS, 2)],
            query_backward,
            key_backward,
            input_backward,
        ]
        for index, call in enumerate(backward):
            pl.when(step == GRAD_STEP + index)(call)

        @pl.when((step >= expert_panels) & (step < panels))
        def _():
            panel = step - expert_panels
            fill(step % 2, left.at[jnp.where(panel < 3, 1, 2)], right[panel])

        @pl.when(step == GRAD_STEP + 1)
        def _():
            for panel in range(shared_panels):
                for copy in line_copies(panel):
                    copy.start()

        @pl.when(step < panels)
        def _():
            post(step)

        @pl.when((step >= 1) & (step < panels + 1))
        def _():
            sum_pair(step - 1)

        @pl.when((step >= 3) & (step < panels + 3))
        def _():
            sum_corner(step - 3)

        @pl.when(step >= 5)
        def _():
            sum_sides(step - 5)

    for panel in (expert_panels - 2, expert_panels - 1):
        staged_copy(panel).wait()

    for panel in range(dense_panels):
        for copy in line_copies(panel):
            copy.wait()
        place = panel + 8 if panel < 6 else panel - 1 if panel < 9 else panel - 9
        stripes_ref[place] = total(
            line_out[panel, pl.ds(pl.multiple_of(z * stripe, stripe), stripe), :],
            line_in[panel, 0],
            line_in[panel, 1],
            line_in[panel, 2],
        )


def scatter_grads(
    grad_parts,
    saved,
    dense_all,
    shared_sum,
    cotangent,
    normed_attend,
    attended,
    residual,
    grad_shared,
    projected,
    hidden_in,
    scale,
    gains,
):
    experts, spots, width = saved[0].shape
    hidden = saved[2].shape[-1]
    length = residual.shape[0]
    share = width // 8
    stripe = share // 4
    dense_panels = 14
    low = jnp.bfloat16
    vmem = pl.BlockSpec(memory_space=pltpu.VMEM)
    return pl.pallas_call(
        scatter_kernel,
        in_specs=[ANY] * 15 + [vmem] * 2,
        out_specs=[ANY] + [vmem] * 3,
        out_shape=[
            jax.ShapeDtypeStruct((3 * experts, share, hidden), low),
            jax.ShapeDtypeStruct((dense_panels, stripe, hidden), jnp.float32),
            jax.ShapeDtypeStruct((length, width), jnp.float32),
            jax.ShapeDtypeStruct((2, width), jnp.float32),
        ],
        scratch_shapes=[
            pltpu.VMEM((length, width), jnp.float32),
            pltpu.VMEM((length, width), jnp.float32),
            pltpu.VMEM(projected.shape, low),
            pltpu.VMEM((length, width), low),
            pltpu.VMEM((2, 4, 2, share, hidden), low),
            pltpu.VMEM((SLOTS, 4, share, hidden), low),
            pltpu.VMEM((SLOTS, share // 2, hidden), low),
            pltpu.VMEM((SLOTS, share // 2, hidden), low),
            pltpu.VMEM((SLOTS, share, hidden), low),
            pltpu.VMEM((SLOTS, share, hidden), low),
            pltpu.VMEM((2, share, hidden), low),
            pltpu.VMEM((2, 2, spots, width), low),
            pltpu.VMEM((2, 3, spots, hidden), low),
            pltpu.VMEM((3, length, width), low),
            pltpu.VMEM((8, length, hidden), low),
            pltpu.VMEM((width, HEADS * HD), low),
            pltpu.VMEM((4, length, width), low),
            pltpu.VMEM((length, HEADS * HD), low),
            pltpu.VMEM((2, length, HD), jnp.float32),
            pltpu.VMEM((length, width), jnp.float32),
            pltpu.VMEM((width, 2 * KVH * HD), low),
            pltpu.VMEM((dense_panels, share, hidden), low),
            pltpu.VMEM((dense_panels, 3, stripe, hidden), low),
            pltpu.SemaphoreType.DMA((5,)),
            pltpu.SemaphoreType.DMA((9, SLOTS)),
            pltpu.SemaphoreType.DMA((2, dense_panels, 3)),
            pltpu.SemaphoreType.DMA((6,)),
            pltpu.SemaphoreType.DMA((5, 5)),
            pltpu.SemaphoreType.REGULAR((3,)),
        ],
        compiler_params=pltpu.CompilerParams(
            collective_id=3, has_side_effects=True, vmem_limit_bytes=62 * MIB
        ),
        name="scatter_grads",
    )(
        grad_parts,
        *saved,
        dense_all,
        shared_sum,
        cotangent,
        normed_attend,
        attended,
        residual,
        grad_shared,
        projected,
        hidden_in,
        scale,
        gains,
    )


def muon_kernel(
    expert_ref,
    dense_ref,
    routed_parts_ref,
    expert_out_ref,
    dense_out_ref,
    routed_received_ref,
    dense_back,
    moments,
    units,
    orthogonal,
    current,
    low,
    identity,
    line_sems,
    out_sems,
    in_sems,
    back_out_sems,
    back_in_sems,
    load_sems,
):
    dp, z = lax.axis_index("dp"), lax.axis_index("expert")
    count, share, _ = moments.shape
    first, dense_count = 10, 4
    stripe = dense_ref.shape[1]
    others = [(dp, (z + turn) % 4) for turn in range(1, 4)]
    peers = [((dp + turn) % 8, z) for turn in range(1, 8)]

    def remote(source, target, send, receive, device):
        return pltpu.make_async_remote_copy(
            src_ref=source,
            dst_ref=target,
            send_sem=send,
            recv_sem=receive,
            device_id=device,
            device_id_type=MESH,
        )

    def share_of(index):
        return pl.ds(pl.multiple_of(index * share, share), share)

    def stripe_of(index):
        return pl.ds(pl.multiple_of(index * stripe, stripe), stripe)

    barrier = pltpu.get_barrier_semaphore()
    for device in (*others, *peers):
        pl.semaphore_signal(barrier, inc=1, device_id=device, device_id_type=MESH)
    dense_rows = pl.ds(first, dense_count)
    loads = [
        pltpu.make_async_copy(
            expert_ref.at[pl.ds(0, first)], moments.at[pl.ds(0, first)], load_sems.at[0]
        ),
        pltpu.make_async_copy(
            expert_ref.at[pl.ds(first, count - first - dense_count)],
            moments.at[pl.ds(first + dense_count, count - first - dense_count)],
            load_sems.at[1],
        ),
        pltpu.make_async_copy(
            dense_ref.at[pl.ds(z * dense_count, dense_count)],
            moments.at[dense_rows, stripe_of(z)],
            load_sems.at[2],
        ),
    ]
    for copy in loads:
        copy.start()
    pl.semaphore_wait(barrier, len(others) + len(peers))
    line_copies = [
        remote(
            dense_ref.at[pl.ds(device[1] * dense_count, dense_count)],
            moments.at[dense_rows, stripe_of(z)],
            line_sems.at[0, turn],
            line_sems.at[1, turn],
            device,
        )
        for turn, device in enumerate(others)
    ]
    line_back = [
        remote(
            dense_back.at[:, stripe_of(device[1])],
            dense_out_ref.at[pl.ds(z * dense_count, dense_count)],
            line_sems.at[2, turn],
            line_sems.at[3, turn],
            device,
        )
        for turn, device in enumerate(others)
    ]
    own_back = pltpu.make_async_copy(
        dense_back.at[:, stripe_of(z)],
        dense_out_ref.at[pl.ds(z * dense_count, dense_count)],
        load_sems.at[2],
    )

    def out_copy(slot, turn):
        owner = peers[turn][0]
        return remote(
            moments.at[8 * slot + owner],
            units.at[slot, share_of(dp)],
            out_sems.at[slot, turn],
            in_sems.at[slot],
            peers[turn],
        )

    def own_copy(slot):
        return pltpu.make_async_copy(
            moments.at[8 * slot + dp], units.at[slot, share_of(dp)], load_sems.at[3 + slot]
        )

    def is_dense(slot, owner):
        unit = 8 * slot + owner
        return (unit >= first) & (unit < first + dense_count)

    def expert_place(slot, owner):
        unit = 8 * slot + owner
        return expert_out_ref.at[jnp.where(unit < first, unit, unit - dense_count)]

    def dense_place(slot, owner):
        return dense_back.at[8 * slot + owner - first]

    def back_copy(place, slot, turn):
        return remote(
            orthogonal.at[slot, share_of(peers[turn][0])],
            place(slot, dp),
            back_out_sems.at[slot, turn],
            back_in_sems.at[slot, dp],
            peers[turn],
        )

    def own_back_copy(place, slot):
        return pltpu.make_async_copy(
            orthogonal.at[slot, share_of(dp)], place(slot, dp), load_sems.at[3 + slot]
        )

    def send_back(place, slot):
        for turn in range(7):
            back_copy(place, slot, turn).start()
        own_back_copy(place, slot).start()

    def exists(slot, owner):
        return 8 * slot + owner < count

    def send_slot(slot):
        for turn in range(7):
            pl.when(exists(slot, peers[turn][0]))(out_copy(slot, turn).start)
        pl.when(exists(slot, dp))(own_copy(slot).start)

    length = routed_received_ref.shape[1]
    own_routed = pltpu.make_async_copy(
        routed_parts_ref.at[pl.ds(pl.multiple_of(z * length, length), length), :],
        routed_received_ref.at[3],
        load_sems.at[6],
    )
    own_routed.start()
    routed_copies = [
        remote(
            routed_parts_ref.at[pl.ds(pl.multiple_of(device[1] * length, length), length), :],
            routed_received_ref.at[turn],
            line_sems.at[4, turn],
            line_sems.at[5, turn],
            device,
        )
        for turn, device in enumerate(others)
    ]
    for copy in line_copies:
        copy.start()
    loads[0].wait()
    send_slot(0)
    loads[1].wait()
    loads[2].wait()
    for copy in line_copies:
        copy.wait()
    send_slot(1)
    send_slot(2)
    for copy in routed_copies:
        copy.start()

    @pl.loop(0, 3)
    def _(slot):
        @pl.when(exists(slot, dp))
        def _():
            own_copy(slot).wait()
            arrived = units.at[slot, pl.ds(0, 7 * share)]
            remote(arrived, arrived, in_sems.at[slot], in_sems.at[slot], peers[0]).wait_recv()
            newton_schulz_unit(units.at[slot], orthogonal.at[slot], current, low, identity)

            @pl.when(is_dense(slot, dp))
            def _():
                send_back(dense_place, slot)

            @pl.when(jnp.logical_not(is_dense(slot, dp)))
            def _():
                send_back(expert_place, slot)

    def own_back_wait(slot):
        def wait():
            pltpu.make_async_copy(
                orthogonal.at[slot, share_of(dp)], expert_out_ref.at[0], load_sems.at[3 + slot]
            ).wait()

        return wait

    def wait_back(slot):
        for turn in range(7):
            owner = peers[turn][0]

            @pl.when(exists(slot, owner))
            def _():
                block = expert_out_ref.at[0]
                semaphore = back_in_sems.at[slot, owner]
                remote(block, block, semaphore, semaphore, peers[0]).wait_recv()

        pl.when(exists(slot, dp))(own_back_wait(slot))

    wait_back(1)
    for copy in line_back:
        copy.start()
    own_back.start()
    wait_back(0)
    wait_back(2)
    for slot in range(3):
        for turn in range(7):
            pl.when(exists(slot, peers[turn][0]))(out_copy(slot, turn).wait_send)

        @pl.when(exists(slot, dp))
        def _():
            for turn in range(7):
                back_copy(expert_place, slot, turn).wait_send()

    for copy in line_back:
        copy.wait()
    own_back.wait()
    own_routed.wait()
    for copy in routed_copies:
        copy.wait()


def muon(expert_units, dense_units, routed_parts):
    experts, share, columns = expert_units.shape
    panels, stripe, _ = dense_units.shape
    count = experts + panels // 4
    low = jnp.bfloat16
    return pl.pallas_call(
        muon_kernel,
        in_specs=[ANY] * 3,
        out_specs=[ANY] * 3,
        out_shape=[
            jax.ShapeDtypeStruct(expert_units.shape, low),
            jax.ShapeDtypeStruct(dense_units.shape, low),
            jax.ShapeDtypeStruct((4, routed_parts.shape[0] // 4, routed_parts.shape[1]), low),
        ],
        scratch_shapes=[
            pltpu.VMEM((panels // 4, share, columns), low),
            pltpu.VMEM((count, share, columns), low),
            pltpu.VMEM((3, 8 * share, columns), low),
            pltpu.VMEM((3, 8 * share, columns), low),
            pltpu.VMEM((columns, 8 * share), jnp.float32),
            pltpu.VMEM((columns, 8 * share), low),
            pltpu.VMEM((columns, columns), low),
            pltpu.SemaphoreType.DMA((6, 3)),
            pltpu.SemaphoreType.DMA((3, 7)),
            pltpu.SemaphoreType.DMA((3,)),
            pltpu.SemaphoreType.DMA((3, 7)),
            pltpu.SemaphoreType.DMA((3, 8)),
            pltpu.SemaphoreType.DMA((7,)),
        ],
        compiler_params=pltpu.CompilerParams(
            collective_id=4, has_side_effects=True, vmem_limit_bytes=56 * MIB
        ),
        name="muon",
    )(expert_units, dense_units, routed_parts)


GROUP = 2


def blocks_over(steps, shape, axis):
    def place(index):
        return tuple(
            jnp.minimum(index, steps - 1) if position == axis else 0
            for position in range(len(shape))
        )

    return pl.BlockSpec(shape, place)


def moments_kernel(
    momentum_ref,
    sum_ref,
    dense_momentum_ref,
    dense_sum_ref,
    grad_ref,
    moment_ref,
    units_ref,
    dense_grad_ref,
    dense_moment_ref,
    dense_units_ref,
):
    grad = sum_ref[...].astype(jnp.float32)
    moment = MOMENTUM_DECAY * momentum_ref[...] + grad
    grad_ref[...] = grad
    moment_ref[...] = moment
    units_ref[...] = moment.astype(jnp.bfloat16)
    columns = dense_sum_ref.shape[2]
    real = pl.program_id(0) < pl.num_programs(0) - 2
    for panel in range(GROUP):
        spot = slice(panel * columns, (panel + 1) * columns)
        dense_grad = dense_sum_ref[panel]
        dense_moment = MOMENTUM_DECAY * dense_momentum_ref[:, spot] + dense_grad
        dense_grad_ref[:, spot] = dense_grad
        dense_moment_ref[:, spot] = dense_moment
        dense_units_ref[panel] = jnp.where(real, dense_moment, 0.0).astype(jnp.bfloat16)


def moments(momentum, grad_sum, dense_momentum, dense_sum):
    panels, rows, columns = grad_sum.shape
    dense_panels, stripe, _ = dense_sum.shape
    steps = panels // GROUP
    block = pl.BlockSpec((GROUP, rows, columns), lambda index: (index, 0, 0))
    wide = blocks_over(dense_panels // GROUP, (stripe, GROUP * columns), 1)
    full = jax.ShapeDtypeStruct(grad_sum.shape, jnp.float32)
    dense_full = jax.ShapeDtypeStruct(dense_momentum.shape, jnp.float32)
    grad, moment, *rest = pl.pallas_call(
        moments_kernel,
        grid=(steps,),
        in_specs=[
            block,
            block,
            wide,
            blocks_over(dense_panels // GROUP, (GROUP, stripe, columns), 0),
        ],
        out_specs=[
            block,
            block,
            block,
            wide,
            wide,
            blocks_over(dense_panels // GROUP + 1, (GROUP, stripe, columns), 0),
        ],
        out_shape=[
            full,
            full,
            jax.ShapeDtypeStruct(grad_sum.shape, jnp.bfloat16),
            dense_full,
            dense_full,
            jax.ShapeDtypeStruct((dense_panels + GROUP, stripe, columns), jnp.bfloat16),
        ],
        compiler_params=pltpu.CompilerParams(vmem_limit_bytes=60 * MIB),
        name="moments",
    )(momentum.reshape(grad_sum.shape), grad_sum, dense_momentum, dense_sum)
    return grad.reshape(momentum.shape), moment.reshape(momentum.shape), *rest


def update_kernel(
    weights_ref,
    orthogonal_ref,
    dense_weights_ref,
    dense_orthogonal_ref,
    base_ref,
    routed_ref,
    grad_ref,
    new_ref,
    dense_new_ref,
    out_ref,
    grad_out_ref,
):
    keep_factor = 1.0 - LEARN_RATE * WEIGHT_DECAY
    new_ref[...] = keep_factor * weights_ref[...] - LEARN_RATE * orthogonal_ref[...].astype(
        jnp.float32
    )
    columns = dense_orthogonal_ref.shape[2]
    for panel in range(GROUP):
        spot = slice(panel * columns, (panel + 1) * columns)
        dense_new_ref[:, spot] = keep_factor * dense_weights_ref[:, spot] - LEARN_RATE * (
            dense_orthogonal_ref[panel].astype(jnp.float32)
        )
    total = base_ref[...]
    for source in (3, 0, 1, 2):
        total = total + routed_ref[source].astype(jnp.float32)
    out_ref[...] = total.astype(jnp.bfloat16)
    grad_out_ref[...] = grad_ref[...]


def updated(weights, orthogonal, dense_weights, dense_orthogonal, base, routed, grad):
    panels, rows, columns = orthogonal.shape
    stripe, dense_columns = dense_weights.shape
    length, width = base.shape
    dense_steps = dense_columns // (GROUP * columns)
    row_steps = 8
    block = pl.BlockSpec((GROUP, rows, columns), lambda index: (index, 0, 0))
    wide = blocks_over(dense_steps, (stripe, GROUP * columns), 1)
    part = blocks_over(row_steps, (length // row_steps, width), 0)
    new, *rest = pl.pallas_call(
        update_kernel,
        grid=(panels // GROUP,),
        in_specs=[
            block,
            block,
            wide,
            blocks_over(dense_steps, (GROUP, stripe, columns), 0),
            part,
            blocks_over(row_steps, (4, length // row_steps, width), 1),
            part,
        ],
        out_specs=[block, wide, part, part],
        out_shape=[
            jax.ShapeDtypeStruct(orthogonal.shape, jnp.float32),
            jax.ShapeDtypeStruct(dense_weights.shape, jnp.float32),
            jax.ShapeDtypeStruct(base.shape, jnp.bfloat16),
            jax.ShapeDtypeStruct(base.shape, jnp.float32),
        ],
        compiler_params=pltpu.CompilerParams(vmem_limit_bytes=32 * MIB),
        name="update",
    )(
        weights.reshape(orthogonal.shape),
        orthogonal,
        dense_weights,
        dense_orthogonal,
        base,
        routed,
        grad,
    )
    return new.reshape(weights.shape), *rest


def on_device(
    hidden_in,
    cotangent,
    routes,
    route_weights,
    dense_weights,
    dense_momentum,
    expert_weights,
    expert_momentum,
    norm_gains,
    gain_first,
    gain_second,
):
    length, width = hidden_in.shape
    topk_count = routes.shape[1]
    local_experts = expert_weights.shape[0]
    expert_size = lax.axis_size("expert")
    dp_size = lax.axis_size("dp")
    expert_count = local_experts * expert_size
    capacity = 5 * length * topk_count // (4 * expert_count)
    block_rows = min(512, length)
    query_width = HEADS * HD
    kv_width = KVH * HD
    qkv_end = query_width + 2 * kv_width
    shared_base = 2 * query_width + 2 * kv_width
    gate_table = jnp.sum(
        jnp.where(
            routes.T[None, :, :] == jnp.arange(expert_count, dtype=jnp.int32)[:, None, None],
            route_weights.T[None, :, :],
            0.0,
        ),
        axis=1,
    )
    direct = dp_size == 8 and expert_size == 4
    inputs = hidden_in.astype(jnp.float32)
    scale_attend = norm_scale(inputs)
    if direct:
        stripe_rows = dense_weights.shape[0]
        extra = jnp.zeros((stripe_rows, 128 - norm_gains.shape[0]), jnp.float32)
        plane_gates = gate_table.reshape(expert_size, local_experts, length)
        (
            dense_all,
            _,
            _,
            _,
            routed_parts,
            grad_parts,
            *saved,
            normed_attend,
            projected,
            attended,
            residual,
            grad_shared,
            base_out,
            shared_sum,
            scale_mixer,
            gains_all,
        ) = front(
            jnp.concatenate(
                [
                    dense_weights[:, :shared_base],
                    norm_gains.T,
                    extra,
                    dense_weights[:, shared_base:],
                ],
                1,
            ).astype(jnp.bfloat16),
            jnp.pad(plane_gates, ((0, 0), (0, 8 - local_experts), (0, 0))),
            expert_weights.reshape(-1, *expert_weights.shape[2:]),
            hidden_in,
            cotangent,
            -(-capacity // 16) * 16,
        )
    else:
        gate_tables = lax.all_gather(gate_table, "expert", axis=0, tiled=False)
        cotangents = lax.all_gather(cotangent, "expert", axis=0, tiled=True)
        dense_all, gains_all = (
            lax.all_gather(
                dense_weights.astype(jnp.bfloat16), ("dp", "expert"), axis=0, tiled=True
            ),
            lax.all_gather(norm_gains.astype(jnp.bfloat16), ("dp", "expert"), axis=1, tiled=True),
        )
        gain_attend = gains_all[0].astype(jnp.float32)
        gain_mixer = gains_all[1].astype(jnp.float32)
        normed_attend = (inputs * scale_attend * gain_attend).astype(jnp.bfloat16)
        projected = jnp.dot(
            normed_attend, dense_all[:, :qkv_end], preferred_element_type=jnp.float32
        ).astype(jnp.bfloat16)
        query = projected[:, :query_width]
        key_rows = projected[:, query_width : query_width + kv_width]
        value_rows = projected[:, query_width + kv_width :]
        attended, saved_stats = attend_forward(query, key_rows, value_rows, block_rows)
        residual = inputs + jnp.einsum(
            "sq,dq->sd", attended, dense_all[:, qkv_end:shared_base], preferred_element_type=jnp.float32
        )
        scale_mixer = norm_scale(residual)
        normed_mixer = (residual * scale_mixer * gain_mixer).astype(jnp.bfloat16)
        expert_all = lax.all_gather(expert_weights.astype(jnp.bfloat16), "dp", axis=2, tiled=True)
        tokens = lax.all_gather(normed_mixer, "expert", axis=0, tiled=True)
        shared_pre = jnp.dot(
            normed_mixer,
            dense_all[:, shared_base : shared_base + 2 * FFS],
            preferred_element_type=jnp.float32,
        )
        shared_gate = shared_pre[:, :FFS]
        shared_up = shared_pre[:, FFS:]
        shared_act = (jax.nn.silu(shared_gate) * shared_up).astype(jnp.bfloat16)
        shared_out = jnp.einsum(
            "sf,df->sd",
            shared_act,
            dense_all[:, shared_base + 2 * FFS : shared_base + 3 * FFS],
            preferred_element_type=jnp.float32,
        )
        grad_shared_act = jnp.dot(
            cotangent,
            dense_all[:, shared_base + 2 * FFS : shared_base + 3 * FFS],
            preferred_element_type=jnp.float32,
        )
        shared_sig = jax.nn.sigmoid(shared_gate)
        grad_shared_pre = jnp.concatenate(
            [
                grad_shared_act * shared_up * shared_sig * (1.0 + shared_gate * (1.0 - shared_sig)),
                grad_shared_act * jax.nn.silu(shared_gate),
            ],
            1,
        ).astype(jnp.bfloat16)
        grad_shared = jnp.einsum(
            "sf,df->sd",
            grad_shared_pre,
            dense_all[:, shared_base : shared_base + 2 * FFS],
            preferred_element_type=jnp.float32,
        )
        base_out = residual + shared_out
        my_gates = lax.dynamic_slice_in_dim(
            gate_tables, lax.axis_index("expert") * local_experts, local_experts, 1
        ).transpose(1, 0, 2)
        hot = my_gates > 0.0
        earlier = jnp.einsum(
            "est,ut->esu",
            hot.astype(jnp.bfloat16),
            jnp.tril(jnp.ones((length, length), jnp.bfloat16), -1),
            preferred_element_type=jnp.float32,
        ).astype(jnp.int32)
        place = jnp.where(hot, earlier, -1)
        routed_parts, grad_parts, saved = grouped_experts(
            tokens, cotangents, place, my_gates, expert_all, capacity
        )
    if direct:
        expert_sum, dense_sum, grad_inputs, grad_gains = scatter_grads(
            grad_parts,
            saved,
            dense_all,
            shared_sum,
            cotangent,
            normed_attend,
            attended,
            residual,
            grad_shared,
            projected,
            hidden_in,
            scale_mixer,
            gains_all,
        )
        expert_grad, expert_moment, expert_units, dense_grad, dense_moment, dense_units = moments(
            expert_momentum, expert_sum, dense_momentum, dense_sum
        )
        orth_expert, orth_dense, routed = muon(expert_units, dense_units, routed_parts)
        expert_new, dense_new, block_out, grad_inputs = updated(
            expert_weights,
            orth_expert,
            dense_weights,
            orth_dense,
            base_out,
            routed,
            grad_inputs,
        )
    else:
        routed = lax.psum_scatter(routed_parts, "expert", scatter_dimension=0, tiled=True)
        grad_routed = lax.psum_scatter(grad_parts, "expert", scatter_dimension=0, tiled=True)
        expert_parts = [expert_grads(*kept) for kept in saved]
        expert_grad = lax.psum_scatter(
            sum(part.astype(jnp.float32) for part in expert_parts).astype(jnp.bfloat16),
            "dp",
            scatter_dimension=2,
            tiled=True,
        ).astype(jnp.float32)
        grad_normed = grad_routed.astype(jnp.float32) + grad_shared
        grad_scaled = grad_normed * gain_mixer
        grad_residual = (
            cotangent.astype(jnp.float32)
            + scale_mixer * grad_scaled
            - residual * scale_mixer**3 * jnp.mean(grad_scaled * residual, axis=-1, keepdims=True)
        )
        grad_gain_mixer = jnp.sum(grad_normed * residual * scale_mixer, axis=0)
        grad_attn_low = grad_residual.astype(jnp.bfloat16)
        grad_attended = jnp.dot(
            grad_attn_low, dense_all[:, qkv_end:shared_base], preferred_element_type=jnp.float32
        ).astype(jnp.bfloat16)
        grad_query, grad_key, grad_value = attend_backward(
            query, key_rows, value_rows, grad_attended, saved_stats, block_rows
        )
        grad_projected = jnp.concatenate([grad_query, grad_key, grad_value], 1)
        dense_parts = [
            jnp.einsum("sd,sf->df", left, right, preferred_element_type=jnp.float32)
            for left, right in (
                (normed_attend, grad_projected),
                (grad_attn_low, attended),
                (normed_mixer, grad_shared_pre),
                (cotangent, shared_act),
            )
        ]
        dense_grad = lax.psum_scatter(
            jnp.concatenate([part.astype(jnp.bfloat16) for part in dense_parts], 1),
            ("dp", "expert"),
            scatter_dimension=0,
            tiled=True,
        ).astype(jnp.float32)
        grad_normed_attend = jnp.einsum(
            "sc,dc->sd", grad_projected, dense_all[:, :qkv_end], preferred_element_type=jnp.float32
        )
        grad_scaled_attend = grad_normed_attend * gain_attend
        grad_inputs = (
            grad_residual
            + scale_attend * grad_scaled_attend
            - inputs * scale_attend**3 * jnp.mean(grad_scaled_attend * inputs, axis=-1, keepdims=True)
        )
        grad_gain_attend = jnp.sum(grad_normed_attend * inputs * scale_attend, axis=0)
        block_out = (base_out + routed.astype(jnp.float32)).astype(jnp.bfloat16)
        grad_gains = jnp.stack([grad_gain_attend, grad_gain_mixer], 0)
        dense_moment = MOMENTUM_DECAY * dense_momentum + dense_grad
        expert_moment = MOMENTUM_DECAY * expert_momentum + expert_grad
        stripe, dense_columns = dense_weights.shape
        row_count = stripe * expert_size
        dense_total = dense_columns // FFE
        dense_share = -(-dense_total // expert_size)
        dense_padded = jnp.pad(
            dense_moment.astype(jnp.bfloat16),
            ((0, 0), (0, dense_share * expert_size * FFE - dense_columns)),
        ).reshape(stripe, dense_share * expert_size, FFE).transpose(1, 0, 2)
        expert_units = expert_moment.astype(jnp.bfloat16).reshape(-1, row_count, FFE)
        dense_units = lax.all_to_all(
            dense_padded, "expert", split_axis=0, concat_axis=1, tiled=True
        )
        expert_unit_count = expert_units.shape[0]
        base_count = expert_unit_count + dense_share
        unit_count = -(-base_count // dp_size) * dp_size
        all_units = jnp.concatenate(
            [
                expert_units,
                dense_units,
                jnp.zeros((unit_count - base_count, row_count, FFE), jnp.bfloat16),
            ],
            0,
        )
        owned = lax.all_to_all(all_units, "dp", split_axis=0, concat_axis=1, tiled=True)
        orthogonal = newton_schulz(owned)
        orth_units = lax.all_to_all(orthogonal, "dp", split_axis=1, concat_axis=0, tiled=True)
        orth_expert = orth_units[:expert_unit_count]
        orth_stripe = lax.all_to_all(
            orth_units[expert_unit_count:base_count],
            "expert",
            split_axis=1,
            concat_axis=0,
            tiled=True,
        )
        orth_stripe = (
            orth_stripe[:dense_total]
            .transpose(1, 0, 2)
            .reshape(stripe, dense_columns)
            .astype(jnp.float32)
        )
        keep_factor = 1.0 - LEARN_RATE * WEIGHT_DECAY
        dense_new = keep_factor * dense_weights - LEARN_RATE * orth_stripe
        expert_new = keep_factor * expert_weights - LEARN_RATE * orth_expert.reshape(
            expert_weights.shape
        ).astype(jnp.float32)
    gain_grad = lax.psum_scatter(
        grad_gains,
        ("dp", "expert"),
        scatter_dimension=1,
        tiled=True,
    )
    first_new = FIRST_DECAY * gain_first + (1.0 - FIRST_DECAY) * gain_grad
    second_new = SECOND_DECAY * gain_second + (1.0 - SECOND_DECAY) * gain_grad * gain_grad
    step_ratio = (
        first_new
        / (1.0 - FIRST_DECAY**STEP)
        / (jnp.sqrt(second_new / (1.0 - SECOND_DECAY**STEP)) + 1e-08)
    )
    gain_new = norm_gains - GAIN_RATE * step_ratio
    return (
        block_out,
        grad_inputs,
        dense_grad,
        dense_moment,
        dense_new,
        expert_grad,
        expert_moment,
        expert_new,
        gain_grad,
        first_new,
        second_new,
        gain_new,
    )


def solution(mesh):
    in_specs = (
        P(("dp", "expert"), None),
        P(("dp", "expert"), None),
        P(("dp", "expert"), None),
        P(("dp", "expert"), None),
        P(("dp", "expert"), None),
        P(("dp", "expert"), None),
        P("expert", None, "dp", None),
        P("expert", None, "dp", None),
        P(None, ("dp", "expert")),
        P(None, ("dp", "expert")),
        P(None, ("dp", "expert")),
    )
    out_specs = (
        P(("dp", "expert"), None),
        P(("dp", "expert"), None),
        P(("dp", "expert"), None),
        P(("dp", "expert"), None),
        P(("dp", "expert"), None),
        P("expert", None, "dp", None),
        P("expert", None, "dp", None),
        P("expert", None, "dp", None),
        P(None, ("dp", "expert")),
        P(None, ("dp", "expert")),
        P(None, ("dp", "expert")),
        P(None, ("dp", "expert")),
    )
    return jax.shard_map(
        on_device, mesh=mesh, in_specs=in_specs, out_specs=out_specs, check_vma=False
    )
```

```python
import functools

import jax
import jax.numpy as jnp
from jax import lax
from jax.experimental import pallas as pl
from jax.experimental.pallas import tpu as pltpu
from jax.sharding import PartitionSpec as P

HEADS = 12
HD = 128
KVH = 4
FFE = 512
FFS = 1024
NS_STEPS = 5
STEP = 10


POLY_FIRST = 3.4445
POLY_SECOND = -4.775
POLY_THIRD = 2.0315
MOMENTUM_DECAY = 0.95
LEARN_RATE = 0.6
WEIGHT_DECAY = 0.1
GAIN_RATE = 0.8
FIRST_DECAY = 0.9
SECOND_DECAY = 0.95


def norm_scale(values):
    return lax.rsqrt(jnp.mean(values * values, axis=-1, keepdims=True) + 1e-06)


def block_scores(query_block, key_block, first_row, block_rows, last_row):
    score_scale = HD ** (-0.5)
    scores = (
        jnp.einsum("qgrd,kgd->grqk", query_block, key_block, preferred_element_type=jnp.float32)
        * score_scale
    )
    allowed = jnp.arange(last_row)[None, :] <= (first_row + jnp.arange(block_rows))[:, None]
    return jnp.where(allowed, scores, -1e30)


def attend_forward(query, key_rows, value_rows, block_rows):
    length = query.shape[0]
    query_heads = query.reshape(length, KVH, HEADS // KVH, HD)
    key_heads = key_rows.reshape(length, KVH, HD)
    value_heads = value_rows.reshape(length, KVH, HD)
    scores = block_scores(query_heads, key_heads, 0, block_rows, block_rows)
    highest = jnp.max(scores, axis=-1, keepdims=True)
    raised = jnp.exp(scores - highest)
    totals = jnp.sum(raised, axis=-1, keepdims=True)
    weights = (raised / totals).astype(jnp.bfloat16)
    outputs = jnp.einsum("grqk,kgd->qgrd", weights, value_heads, preferred_element_type=jnp.float32)
    saved_stats = [(highest, totals)]
    attended = outputs.reshape(length, HEADS * HD)
    return (attended.astype(jnp.bfloat16), saved_stats)


def attend_backward(query, key_rows, value_rows, grad_attended, saved_stats, block_rows):
    length = query.shape[0]
    score_scale = HD ** (-0.5)
    query_heads = query.reshape(length, KVH, HEADS // KVH, HD)
    grad_heads = grad_attended.reshape(length, KVH, HEADS // KVH, HD)
    key_heads = key_rows.reshape(length, KVH, HD)
    value_heads = value_rows.reshape(length, KVH, HD)
    grad_key = jnp.zeros((length, KVH, HD), jnp.float32)
    grad_value = jnp.zeros((length, KVH, HD), jnp.float32)
    query_parts = []
    for block_index, first_row in enumerate(range(0, length, block_rows)):
        last_row = first_row + block_rows
        scores = block_scores(query_heads, key_heads, first_row, block_rows, last_row)
        highest, totals = saved_stats[block_index]
        weights = jnp.exp(scores - highest) / totals
        grad_weights = jnp.einsum(
            "qgrd,kgd->grqk", grad_heads, value_heads, preferred_element_type=jnp.float32
        )
        inner_sum = jnp.sum(weights * grad_weights, axis=-1, keepdims=True)
        grad_scores = (weights * (grad_weights - inner_sum)).astype(jnp.bfloat16)
        query_parts.append(
            jnp.einsum("grqk,kgd->qgrd", grad_scores, key_heads, preferred_element_type=jnp.float32)
            * score_scale
        )
        grad_key = grad_key.at[:last_row].add(
            jnp.einsum(
                "grqk,qgrd->kgd", grad_scores, query_heads, preferred_element_type=jnp.float32
            )
            * score_scale
        )
        grad_value = grad_value.at[:last_row].add(
            jnp.einsum(
                "grqk,qgrd->kgd",
                weights.astype(jnp.bfloat16),
                grad_heads,
                preferred_element_type=jnp.float32,
            )
        )
    grad_query = query_parts[0].reshape(length, HEADS * HD)
    return (
        grad_query.astype(jnp.bfloat16),
        grad_key.reshape(length, KVH * HD).astype(jnp.bfloat16),
        grad_value.reshape(length, KVH * HD).astype(jnp.bfloat16),
    )


MIB = 2**20
GRAD_STEP = 14
SLOTS = 8
MESH = pl.DeviceIdType.MESH


def matmul(left, right):
    return jnp.dot(left, right, preferred_element_type=jnp.float32)


def matmul_nt(left, right):
    return lax.dot_general(left, right, (((1,), (1,)), ((), ())), preferred_element_type=jnp.float32)


def matmul_tn(left, right):
    return lax.dot_general(left, right, (((0,), (0,)), ((), ())), preferred_element_type=jnp.float32)


def newton_schulz_unit(moment_ref, orthogonal_ref, current, low, identity):
    columns, rows = current.shape
    step = 256
    parts = [pl.ds(index * step, step) for index in range(rows // step)]
    identity[...] = jnp.where(
        lax.broadcasted_iota(jnp.int32, identity.shape, 0)
        == lax.broadcasted_iota(jnp.int32, identity.shape, 1),
        1.0,
        0.0,
    ).astype(jnp.bfloat16)
    squares = jnp.zeros((1, columns), jnp.float32)
    for part in parts:
        values = moment_ref[part, :].astype(jnp.float32)
        squares = squares + jnp.sum(values * values, axis=0, keepdims=True)
    scale = 1.0 / (jnp.sqrt(jnp.sum(squares, axis=1, keepdims=True)) + 1e-07)
    for part in parts:
        scaled = matmul_nt(identity[...], moment_ref[part, :]) * scale
        current[:, part] = scaled
        low[:, part] = scaled.astype(jnp.bfloat16)

    def polynomial():
        gram = matmul_nt(low[...], low[...])
        gram_low = gram.astype(jnp.bfloat16)
        return (POLY_SECOND * gram + POLY_THIRD * matmul(gram_low, gram_low)).astype(jnp.bfloat16)

    @pl.loop(0, NS_STEPS - 1)
    def _(index):
        weights = polynomial()
        for part in parts:
            updated = POLY_FIRST * current[:, part] + matmul(weights, low[:, part])
            current[:, part] = updated
            low[:, part] = updated.astype(jnp.bfloat16)

    weights = polynomial()
    for part in parts:
        updated = POLY_FIRST * current[:, part] + matmul(weights, low[:, part])
        orthogonal_ref[part, :] = updated.T.astype(jnp.bfloat16)


def newton_schulz_kernel(moment_ref, orthogonal_ref, current, low, identity):
    newton_schulz_unit(moment_ref.at[0], orthogonal_ref.at[0], current, low, identity)


def newton_schulz(units):
    count, rows, columns = units.shape
    return pl.pallas_call(
        newton_schulz_kernel,
        grid=(count,),
        in_specs=[pl.BlockSpec((1, rows, columns), lambda unit: (unit, 0, 0))],
        out_specs=pl.BlockSpec((1, rows, columns), lambda unit: (unit, 0, 0)),
        out_shape=jax.ShapeDtypeStruct(units.shape, jnp.bfloat16),
        scratch_shapes=[
            pltpu.VMEM((columns, rows), jnp.float32),
            pltpu.VMEM((columns, rows), jnp.bfloat16),
            pltpu.VMEM((columns, columns), jnp.bfloat16),
        ],
        compiler_params=pltpu.CompilerParams(vmem_limit_bytes=48 * MIB),
        cost_estimate=pl.CostEstimate(
            flops=count * NS_STEPS * 2 * columns * columns * (2 * rows + columns),
            bytes_accessed=count * rows * columns * 4,
            transcendentals=0,
        ),
        name="newton_schulz",
    )(units)


def experts_kernel(
    tokens_ref,
    cotangent_ref,
    place_ref,
    gate_ref,
    weights_ref,
    routed_ref,
    grad_tokens_ref,
    received,
    grad_returned,
    act_ref,
    grad_gate_ref,
    grad_up_ref,
    routed_sum,
    grad_sum,
    chosen,
    weighted,
    grad_received,
):
    expert = pl.program_id(0)
    sequences, slots, length = chosen.shape

    @pl.when(expert == 0)
    def _():
        routed_sum[...] = jnp.zeros_like(routed_sum)
        grad_sum[...] = jnp.zeros_like(grad_sum)

    slot_weights = []
    for sequence in range(sequences):
        rows = pl.ds(sequence * length, length)
        spots = pl.ds(sequence * slots, slots)
        place = place_ref[0, sequence : sequence + 1, :]
        gate = gate_ref[0, sequence : sequence + 1, :]
        hot = lax.broadcasted_iota(jnp.int32, (slots, length), 0) == place
        slot_weight = jnp.sum(jnp.where(hot, gate, 0.0), axis=1, keepdims=True)
        slot_weights.append(slot_weight)
        hot_low = jnp.where(hot, 1.0, 0.0).astype(jnp.bfloat16)
        chosen[sequence] = hot_low
        received[0, spots, :] = matmul(hot_low, tokens_ref[rows, :]).astype(jnp.bfloat16)
        grad_returned[0, spots, :] = (
            matmul(hot_low, cotangent_ref[rows, :]) * slot_weight
        ).astype(jnp.bfloat16)
    tokens = received[0]
    grad_out = grad_returned[0]
    gate_pre = matmul(tokens, weights_ref[0, 0])
    up_pre = matmul(tokens, weights_ref[0, 1])
    gate_sig = jax.nn.sigmoid(gate_pre)
    gate_act = gate_pre * gate_sig
    act = (gate_act * up_pre).astype(jnp.bfloat16)
    act_ref[0] = act
    out = matmul_nt(act, weights_ref[0, 2]).astype(jnp.bfloat16).astype(jnp.float32)
    for sequence in range(sequences):
        spots = slice(sequence * slots, (sequence + 1) * slots)
        weighted[spots, :] = (out[spots] * slot_weights[sequence]).astype(jnp.bfloat16)
    grad_act = matmul(grad_out, weights_ref[0, 2])
    grad_gate = (grad_act * up_pre * gate_sig * (1.0 + gate_pre * (1.0 - gate_sig))).astype(
        jnp.bfloat16
    )
    grad_up = (grad_act * gate_act).astype(jnp.bfloat16)
    grad_gate_ref[0] = grad_gate
    grad_up_ref[0] = grad_up
    grad_received[...] = (
        matmul_nt(grad_gate, weights_ref[0, 0]) + matmul_nt(grad_up, weights_ref[0, 1])
    ).astype(jnp.bfloat16)
    for sequence in range(sequences):
        rows = pl.ds(sequence * length, length)
        spots = pl.ds(sequence * slots, slots)
        routed_sum[rows, :] += matmul_tn(chosen[sequence], weighted[spots, :])
        grad_sum[rows, :] += matmul_tn(chosen[sequence], grad_received[spots, :])

    @pl.when(expert == pl.num_programs(0) - 1)
    def _():
        routed_ref[...] = routed_sum[...].astype(jnp.bfloat16)
        grad_tokens_ref[...] = grad_sum[...].astype(jnp.bfloat16)


def run_experts(tokens, cotangents, place, gates, weights, capacity):
    experts, sequences, length = place.shape
    total, width = tokens.shape
    hidden = weights.shape[-1]
    slots = -(-capacity // 16) * 16
    spots = sequences * slots
    whole = pl.BlockSpec((total, width), lambda expert: (0, 0))
    table = pl.BlockSpec((1, sequences, length), lambda expert: (expert, 0, 0))
    matrices = pl.BlockSpec((1, 3, width, hidden), lambda expert: (expert, 0, 0, 0))
    wide = pl.BlockSpec((1, spots, width), lambda expert: (expert, 0, 0))
    narrow = pl.BlockSpec((1, spots, hidden), lambda expert: (expert, 0, 0))
    return pl.pallas_call(
        experts_kernel,
        grid=(experts,),
        in_specs=[whole, whole, table, table, matrices],
        out_specs=[whole, whole, wide, wide, narrow, narrow, narrow],
        out_shape=[
            *[jax.ShapeDtypeStruct((total, width), jnp.bfloat16)] * 2,
            *[jax.ShapeDtypeStruct((experts, spots, width), jnp.bfloat16)] * 2,
            *[jax.ShapeDtypeStruct((experts, spots, hidden), jnp.bfloat16)] * 3,
        ],
        scratch_shapes=[
            pltpu.VMEM((total, width), jnp.float32),
            pltpu.VMEM((total, width), jnp.float32),
            pltpu.VMEM((sequences, slots, length), jnp.bfloat16),
            pltpu.VMEM((spots, width), jnp.bfloat16),
            pltpu.VMEM((spots, width), jnp.bfloat16),
        ],
        compiler_params=pltpu.CompilerParams(vmem_limit_bytes=63 * MIB),
        cost_estimate=pl.CostEstimate(
            flops=experts * (12 * spots * width * hidden + 8 * spots * length * width),
            bytes_accessed=2 * weights.size + 16 * tokens.size,
            transcendentals=experts * spots * hidden,
        ),
        name="experts",
    )(tokens, cotangents, place, gates, weights)


def expert_grads_kernel(
    received_ref, grad_returned_ref, act_ref, grad_gate_ref, grad_up_ref, grad_weights_ref
):
    received, grad_returned = received_ref[0], grad_returned_ref[0]
    grad_weights_ref[0, 0] = matmul_tn(received, grad_gate_ref[0]).astype(jnp.bfloat16)
    grad_weights_ref[0, 1] = matmul_tn(received, grad_up_ref[0]).astype(jnp.bfloat16)
    grad_weights_ref[0, 2] = matmul_tn(grad_returned, act_ref[0]).astype(jnp.bfloat16)


def expert_grads(received, grad_returned, act, grad_gate, grad_up):
    experts, spots, width = received.shape
    hidden = act.shape[-1]
    wide = pl.BlockSpec((1, spots, width), lambda expert: (expert, 0, 0))
    narrow = pl.BlockSpec((1, spots, hidden), lambda expert: (expert, 0, 0))
    return pl.pallas_call(
        expert_grads_kernel,
        grid=(experts,),
        in_specs=[wide, wide, narrow, narrow, narrow],
        out_specs=pl.BlockSpec((1, 3, width, hidden), lambda expert: (expert, 0, 0, 0)),
        out_shape=jax.ShapeDtypeStruct((experts, 3, width, hidden), jnp.bfloat16),
        compiler_params=pltpu.CompilerParams(vmem_limit_bytes=48 * MIB),
        name="expert_grads",
    )(received, grad_returned, act, grad_gate, grad_up)


def grouped_experts(tokens, cotangents, place, gates, weights, capacity):
    experts, sequences, length = place.shape
    group = min(4, sequences)
    routed, grad_tokens, saved = [], [], []
    for first in range(0, sequences, group):
        rows = slice(first * length, (first + group) * length)
        part = slice(first, first + group)
        routed_part, grad_part, *kept = run_experts(
            tokens[rows], cotangents[rows], place[:, part], gates[:, part], weights, capacity
        )
        routed.append(routed_part)
        grad_tokens.append(grad_part)
        saved.append(kept)

    def joined(parts):
        return parts[0] if len(parts) == 1 else jnp.concatenate(parts, 0)

    return joined(routed), joined(grad_tokens), saved


def flipped(index, bit):
    unit = 2**bit
    return index + unit * (1 - 2 * ((index // unit) % 2))


class Links:
    def __init__(self, semaphores):
        self.semaphores = semaphores
        self.taken = 0
        self.dp = lax.axis_index("dp")
        self.z = lax.axis_index("expert")
        self.upper = self.z // 2
        self.position = self.z * (1 - 2 * self.upper) + 3 * self.upper
        self.step = 1 - 2 * self.upper
        self.core = (flipped(self.dp, 0), self.z)
        self.along_x = (flipped(self.dp, 1), self.z)
        self.along_y = (flipped(self.dp, 2), self.z)
        self.inward = (self.dp, self.z + self.step)
        self.outward = (self.dp, self.z - self.step)
        self.further = (self.dp, self.z + 2 * self.step)
        self.pending = []

    def order(self, index):
        near = (self.position + index) % 2 if index < 2 else index
        return near * self.step + 3 * self.upper

    def take(self, count=1):
        first = self.taken
        self.taken += count
        return first

    def barrier(self):
        barrier = pltpu.get_barrier_semaphore()
        for device in (self.core, self.along_x, self.along_y, self.inward, self.further):
            pl.semaphore_signal(barrier, inc=1, device_id=device, device_id_type=MESH)

        @pl.when(self.position == 1)
        def _():
            pl.semaphore_signal(barrier, inc=1, device_id=self.outward, device_id_type=MESH)

        pl.semaphore_wait(barrier, 5 + self.position)

    def copy_with(self, source, target, send, receive, device):
        return pltpu.make_async_remote_copy(
            src_ref=source,
            dst_ref=target,
            send_sem=send,
            recv_sem=receive,
            device_id=device,
            device_id_type=MESH,
        )

    def copy(self, source, target, send, receive, device):
        return self.copy_with(
            source, target, self.semaphores.at[send], self.semaphores.at[receive], device
        )

    def send(self, source, target, receive, device, position=None):
        copy = self.copy(source, target, self.take(), receive, device)
        if position is None:
            copy.start()
        else:
            pl.when(self.position == position)(copy.start)
        self.pending.append((copy, position))

    def arrived(self, region, receive):
        self.copy(region, region, receive, receive, self.core).wait_recv()

    def finish(self):
        for copy, position in self.pending:
            if position is None:
                copy.wait_send()
            else:
                pl.when(self.position == position)(copy.wait_send)


class LineGather:
    def __init__(self, links, region, own=None):
        self.links, self.region = links, region
        self.receives = links.take(4)
        self.own = region(links.z) if own is None else own

    def start(self):
        links = self.links
        target, receive = self.region(links.z), self.receives + links.z
        links.send(self.own, target, receive, links.further)
        links.send(self.own, target, receive, links.inward)
        links.send(self.own, target, receive, links.outward, 1)

    def relay(self):
        links = self.links
        source = links.order(3)
        block = self.region(source)

        @pl.when(links.position == 1)
        def _():
            links.arrived(block, self.receives + source)

        links.send(block, block, self.receives + source, links.outward, 1)

    def arrive(self, index):
        links = self.links
        source = links.order(index)

        def wait():
            links.arrived(self.region(source), self.receives + source)

        if index < 3:
            wait()
        else:
            pl.when(links.position == 0)(wait)


class PlaneGather:
    def __init__(self, links, region, parity, own=None):
        self.links, self.region, self.parity = links, region, parity
        self.receives = links.take(7)
        self.own = region(links.dp) if own is None else own

    def start(self):
        links, first = self.links, self.receives
        target = self.region(links.dp)
        links.send(self.own, target, first, links.along_x)
        links.send(self.own, target, first + 1, links.along_y)
        links.send(self.own, target, first + 2, links.core)

    def forward(self):
        links, first = self.links, self.receives
        across = self.region(flipped(links.dp, 1))
        links.arrived(across, first)
        if self.parity == 0:
            links.send(across, across, first + 3, links.along_y)
        links.send(across, across, first + 4, links.core)
        along = self.region(flipped(links.dp, 2))
        links.arrived(along, first + 1)
        if self.parity == 1:
            links.send(along, along, first + 3, links.along_x)
        links.send(along, along, first + 5, links.core)

    def last(self):
        links, first = self.links, self.receives
        corner = self.region(flipped(flipped(links.dp, 1), 2))
        links.arrived(corner, first + 3)
        links.send(corner, corner, first + 6, links.core)

    def complete(self):
        links, first = self.links, self.receives
        other = flipped(links.dp, 0)
        links.arrived(self.region(other), first + 2)
        links.arrived(self.region(flipped(other, 1)), first + 4)
        links.arrived(self.region(flipped(other, 2)), first + 5)
        links.arrived(self.region(flipped(flipped(other, 1), 2)), first + 6)


ANY = pl.BlockSpec(memory_space=pl.ANY)


def front_kernel(
    stripe_ref,
    gates_ref,
    masters_ref,
    hidden_ref,
    cotangent_ref,
    dense_ref,
    weights_ref,
    cotangents_ref,
    tokens_ref,
    routed_parts_ref,
    grad_parts_ref,
    received_ref,
    grad_returned_ref,
    act_ref,
    grad_gate_ref,
    grad_up_ref,
    normed_attend_out,
    projected_out,
    attended_out,
    residual_out,
    grad_shared_out,
    base_out,
    shared_sum_ref,
    scale_ref,
    gains_ref,
    normed_attend_ref,
    projected_ref,
    attended_ref,
    residual_ref,
    grad_shared_ref,
    base_ref,
    normed_mixer_ref,
    shared_act_ref,
    grad_shared_pre_ref,
    matrices,
    extra,
    all_gates,
    places,
    my_gates,
    chosen,
    forward_slots,
    backward_slots,
    narrow,
    pair_sum,
    corner_x,
    corner_y,
    side_x,
    side_y,
    semaphores,
    shard_out,
    shard_in,
    local,
    load_sems,
    expert_sems,
    shared_sems,
    keep_sems,
):
    links = Links(semaphores)
    stripe, columns = stripe_ref.shape
    length, width = hidden_ref.shape
    panels, rows, hidden = masters_ref.shape
    experts = panels // 3
    slots = chosen.shape[1] // experts
    first_panels = 8
    middle = first_panels * hidden + extra.shape[1]
    halves = ((0, middle), (middle, columns - middle))
    query_width = HEADS * HD
    kv_width = KVH * HD
    ahead = 4

    def dense_region(dp, z, half):
        first, count = halves[half]
        row = pl.multiple_of((dp * 4 + z) * stripe, stripe)
        return dense_ref.at[pl.ds(row, stripe), pl.ds(first, count)]

    def own(half):
        first, count = halves[half]
        return stripe_ref.at[:, pl.ds(first, count)]

    def sequence(ref, z):
        return ref.at[pl.ds(pl.multiple_of(z * length, length), length), :]

    def shard_region(dp, panel):
        return weights_ref.at[panel, pl.ds(pl.multiple_of(dp * rows, rows), rows), :]

    lines = [
        LineGather(links, functools.partial(dense_region, links.dp, half=half), own(half))
        for half in range(2)
    ]
    cotangents = LineGather(links, functools.partial(sequence, cotangents_ref), cotangent_ref)
    tokens = LineGather(links, functools.partial(sequence, tokens_ref), normed_mixer_ref)
    gates = LineGather(links, lambda z: all_gates.at[z], gates_ref)
    planes = [
        [
            PlaneGather(
                links,
                functools.partial(dense_region, z=links.order(index), half=half),
                index % 2,
                own(half) if index == 0 else None,
            )
            for index in range(4)
        ]
        for half in range(2)
    ]

    def shard_copy(kind, panel, source_dp, device):
        block = shard_region(source_dp, panel)
        return links.copy_with(
            block, block, shard_out.at[kind, panel], shard_in.at[kind, panel], device
        )

    dp = links.dp
    dp_core, dp_x, dp_y = flipped(dp, 0), flipped(dp, 1), flipped(dp, 2)
    dp_corner = flipped(dp_x, 2)

    def hop(kind, panel):
        source, device = (
            (dp, links.along_x),
            (dp, links.along_y),
            (dp, links.core),
            None,
            (dp_x, links.core),
            (dp_y, links.core),
            (dp_corner, links.core),
        )[kind]
        return shard_copy(kind, panel, source, device)

    def corner_copy(panel, parity):
        if parity == 0:
            return shard_copy(3, panel, dp_x, links.along_y)
        return shard_copy(3, panel, dp_y, links.along_x)

    def shard_arrived(kind, panel, source_dp):
        shard_copy(kind, panel, source_dp, links.core).wait_recv()

    def shard_start(panel):
        for kind in range(3):
            hop(kind, panel).start()

    def shard_forward(panel):
        shard_arrived(0, panel, dp_x)
        pl.when(panel % 2 == 0)(corner_copy(panel, 0).start)
        hop(4, panel).start()
        shard_arrived(1, panel, dp_y)
        pl.when(panel % 2 == 1)(corner_copy(panel, 1).start)
        hop(5, panel).start()

    def shard_last(panel):
        shard_arrived(3, panel, dp_corner)
        hop(6, panel).start()

    def shard_complete(panel):
        shard_arrived(2, panel, dp_core)
        shard_arrived(4, panel, flipped(dp_core, 1))
        shard_arrived(5, panel, flipped(dp_core, 2))
        shard_arrived(6, panel, flipped(flipped(dp_core, 1), 2))

    def shard_finish(panel):
        for kind in (0, 1, 2, 4, 5, 6):
            hop(kind, panel).wait_send()
        corner_copy(panel, 0).wait_send()

    def exchange(panel):
        shard_forward(panel)
        if panel + ahead < panels:
            shard_start(panel + ahead)
        if panel >= 3:
            shard_last(panel - 3)

    local_copies = [
        pltpu.make_async_copy(source, target, local.at[index])
        for index, (source, target) in enumerate(
            (
                (
                    stripe_ref,
                    dense_ref.at[
                        pl.ds(pl.multiple_of((links.dp * 4 + links.z) * stripe, stripe), stripe), :
                    ],
                ),
                (gates_ref, all_gates.at[links.z]),
                (cotangent_ref, sequence(cotangents_ref, links.z)),
            )
        )
    ]
    token_copy = pltpu.make_async_copy(
        normed_mixer_ref, sequence(tokens_ref, links.z), local.at[3]
    )

    def dense_column(panel):
        return panel * hidden + (0 if panel < first_panels else extra.shape[1])

    loads = [
        pltpu.make_async_copy(
            dense_ref.at[:, pl.ds(dense_column(panel), hidden)],
            matrices.at[panel],
            load_sems.at[panel],
        )
        for panel in range(14)
    ]
    extra_load = pltpu.make_async_copy(
        dense_ref.at[:, pl.ds(first_panels * hidden, extra.shape[1])], extra, load_sems.at[14]
    )

    def half_columns(panel):
        return pl.ds(pl.multiple_of(panel % 2 * hidden, hidden), hidden)

    def master_load(panel):
        return pltpu.make_async_copy(
            masters_ref.at[panel],
            grad_shared_ref.at[pl.ds(0, rows), half_columns(panel)],
            expert_sems.at[0, panel % 2],
        )

    def master_store(panel):
        return pltpu.make_async_copy(
            shared_act_ref.at[pl.ds(0, rows), half_columns(panel)],
            shard_region(dp, panel),
            expert_sems.at[1, panel % 2],
        )

    master_load(0).start()
    links.barrier()
    lines[0].start()
    planes[0][0].start()
    lines[1].start()
    gates.start()
    for copy in local_copies:
        copy.start()

    def round_masters(first, last):
        @pl.loop(first, last)
        def _(panel):
            master_load(panel).wait()

            @pl.when(panel + 1 < panels)
            def _():
                master_load(panel + 1).start()

            @pl.when(panel >= 2)
            def _():
                master_store(panel - 2).wait()

            shared_act_ref[:rows, half_columns(panel)] = grad_shared_ref[
                :rows, half_columns(panel)
            ].astype(jnp.bfloat16)
            master_store(panel).start()

    lines[0].arrive(1)
    planes[0][1].start()
    lines[0].arrive(2)
    planes[0][2].start()
    round_masters(0, panels // 3)
    for panel in range(2):
        shard_start(panel)
    planes[0][0].forward()
    lines[0].relay()
    lines[0].arrive(3)
    planes[0][3].start()
    planes[0][1].forward()
    lines[1].relay()
    round_masters(panels // 3, panels)
    for panel in (panels - 2, panels - 1):
        master_store(panel).wait()
    for panel in range(2, ahead):
        shard_start(panel)
    planes[1][0].start()
    planes[0][2].forward()
    lines[1].arrive(1)
    planes[1][1].start()
    planes[0][3].forward()
    cotangents.start()
    gates.relay()
    lines[1].arrive(2)
    planes[1][2].start()
    for plane in planes[0]:
        plane.last()
    planes[1][0].forward()
    for plane in planes[0]:
        plane.complete()
    local_copies[0].wait()
    extra_load.start()
    for copy in loads[:first_panels]:
        copy.start()

    rows_step = 32

    def norm_rows(source, gain, scale_out, target):
        @pl.loop(0, length // rows_step)
        def _(index):
            part = pl.ds(index * rows_step, rows_step)
            values = source[part, :].astype(jnp.float32)
            scale = lax.rsqrt(jnp.mean(values * values, axis=-1, keepdims=True) + 1e-06)
            if scale_out is not None:
                scale_out[part, :] = scale
            target[part, :] = (values * scale * gains_ref[gain : gain + 1, :]).astype(jnp.bfloat16)

    def project():
        extra_load.wait()
        gains_ref[...] = extra[...].astype(jnp.float32).T[:8, :]
        norm_rows(hidden_ref, 0, None, normed_attend_ref)
        for panel in range(5):
            loads[panel].wait()
            projected_ref[:, panel * hidden : (panel + 1) * hidden] = matmul(
                normed_attend_ref[...], matrices[panel]
            ).astype(jnp.bfloat16)

    def attend(group):
        key_rows = projected_ref[:, query_width + group * HD : query_width + (group + 1) * HD]
        value_first = query_width + kv_width + group * HD
        value_rows = projected_ref[:, value_first : value_first + HD]
        row = lax.broadcasted_iota(jnp.int32, (length, length), 0)
        column = lax.broadcasted_iota(jnp.int32, (length, length), 1)
        per_group = HEADS // KVH
        for head in range(group * per_group, (group + 1) * per_group):
            spot = slice(head * HD, (head + 1) * HD)
            scores = matmul_nt(projected_ref[:, spot], key_rows) * HD ** (-0.5)
            scores = jnp.where(column <= row, scores, -1e30)
            raised = jnp.exp(scores - jnp.max(scores, axis=-1, keepdims=True))
            shares = (raised / jnp.sum(raised, axis=-1, keepdims=True)).astype(jnp.bfloat16)
            attended_ref[:, spot] = matmul(shares, value_rows).astype(jnp.bfloat16)

    def join():
        for part in range(3):
            loads[5 + part].wait()
            update = matmul_nt(
                attended_ref[:, part * hidden : (part + 1) * hidden], matrices[5 + part]
            )
            if part == 0:
                residual_ref[...] = hidden_ref[...].astype(jnp.float32) + update
            else:
                residual_ref[...] += update
        norm_rows(residual_ref, 1, scale_ref, normed_mixer_ref)
        tokens.start()
        token_copy.start()

    def shared(part):
        spot = slice(part * hidden, (part + 1) * hidden)
        for panel in (8, 10, 12):
            loads[panel + part].wait()
        gate = matmul(normed_mixer_ref[...], matrices[8 + part])
        up = matmul(normed_mixer_ref[...], matrices[10 + part])
        sig = jax.nn.sigmoid(gate)
        gate_act = gate * sig
        shared_act_ref[:, spot] = (gate_act * up).astype(jnp.bfloat16)
        grad_act = matmul(cotangent_ref[...], matrices[12 + part])
        grad_shared_pre_ref[:, spot] = (
            grad_act * up * sig * (1.0 + gate * (1.0 - sig))
        ).astype(jnp.bfloat16)
        up_spot = slice((2 + part) * hidden, (3 + part) * hidden)
        grad_shared_pre_ref[:, up_spot] = (grad_act * gate_act).astype(jnp.bfloat16)

    def shared_back(part):
        spot = slice(part * hidden, (part + 1) * hidden)
        up_spot = slice((2 + part) * hidden, (3 + part) * hidden)
        grad = matmul_nt(grad_shared_pre_ref[:, spot], matrices[8 + part]) + matmul_nt(
            grad_shared_pre_ref[:, up_spot], matrices[10 + part]
        )
        out = matmul_nt(shared_act_ref[:, spot], matrices[12 + part])
        if part == 0:
            grad_shared_ref[...] = grad
            base_ref[...] = residual_ref[...] + out
        else:
            grad_shared_ref[...] += grad
            base_ref[...] += out

    kept = [
        pltpu.make_async_copy(source, target, keep_sems.at[index])
        for index, (source, target) in enumerate(
            (
                (normed_attend_ref, normed_attend_out),
                (projected_ref, projected_out),
                (attended_ref, attended_out),
                (residual_ref, residual_out),
                (grad_shared_ref, grad_shared_out),
                (base_ref, base_out),
            )
        )
    ]

    def place_slots():
        local_copies[1].wait()
        before = (
            lax.broadcasted_iota(jnp.int32, (length, length), 0)
            < lax.broadcasted_iota(jnp.int32, (length, length), 1)
        )
        earlier_mask = jnp.where(before, 1.0, 0.0).astype(jnp.bfloat16)
        for source in range(4):
            gate = all_gates[source, links.z]
            hot = gate > 0.0
            earlier = matmul(jnp.where(hot, 1.0, 0.0).astype(jnp.bfloat16), earlier_mask)
            place = jnp.where(hot, earlier, -1.0).astype(jnp.int32)
            for expert in range(experts):
                places[expert, source : source + 1, :] = place[expert : expert + 1, :]
                my_gates[expert, source : source + 1, :] = gate[expert : expert + 1, :]

    core, chip = dp % 2, dp // 2
    chip_x, chip_y = flipped(chip, 0), flipped(chip, 1)
    chip_corner = flipped(chip_x, 1)
    shared_panels = pair_sum.shape[0]
    half = rows // 2
    quarter = width // 4

    ring = matrices.at[13]

    def ring_rows(index, which):
        return pl.ds(pl.multiple_of((2 * index + which) * rows, rows), rows)

    def pair_copy(panel, index):
        return links.copy_with(
            ring.at[ring_rows(index, 1 - core)],
            pair_sum.at[panel, index],
            shared_sems.at[0, 0, panel],
            shared_sems.at[1, 0, panel],
            links.core,
        )

    def shared_copy(kind, panel):
        source, target, device = (
            (pair_sum.at[panel], pair_sum.at[panel], links.core),
            (pair_sum.at[panel, chip_corner, pl.ds(0, half)], corner_x.at[panel], links.along_x),
            (pair_sum.at[panel, chip_corner, pl.ds(half, half)], corner_y.at[panel], links.along_y),
            (pair_sum.at[panel, chip_x], side_x.at[panel], links.along_x),
            (pair_sum.at[panel, chip_y], side_y.at[panel], links.along_y),
        )[kind]
        return links.copy_with(
            source, target, shared_sems.at[0, kind, panel], shared_sems.at[1, kind, panel], device
        )

    def shared_fill(panel):
        left_ref = normed_mixer_ref if panel < 4 else cotangent_ref
        right_ref = grad_shared_pre_ref if panel < 4 else shared_act_ref
        first = (panel if panel < 4 else panel - 4) * hidden
        right = right_ref[:, first : first + hidden]
        for index in range(4):
            part = matmul_tn(left_ref[:, index * quarter : (index + 1) * quarter], right)
            ring[index * quarter : (index + 1) * quarter, :] = part.astype(jnp.bfloat16)
        for index in range(4):
            pair_copy(panel, index).start()

    def shared_pair(panel):
        shared_copy(0, panel).wait()
        for index in range(4):
            pair_sum[panel, index] = (
                pair_sum[panel, index].astype(jnp.float32)
                + ring[ring_rows(index, core), :].astype(jnp.float32)
            ).astype(jnp.bfloat16)

    def shared_corners(panel):
        for kind in (1, 2):
            shared_copy(kind, panel).start()

    def shared_sides(panel):
        for kind in (1, 2):
            shared_copy(kind, panel).wait()
        pair_sum[panel, chip_y, :half] = (
            pair_sum[panel, chip_y, :half].astype(jnp.float32)
            + corner_x[panel].astype(jnp.float32)
        ).astype(jnp.bfloat16)
        pair_sum[panel, chip_x, half:] = (
            pair_sum[panel, chip_x, half:].astype(jnp.float32)
            + corner_y[panel].astype(jnp.float32)
        ).astype(jnp.bfloat16)
        for kind in (3, 4):
            shared_copy(kind, panel).start()

    def shared_total(panel):
        for kind in (3, 4):
            shared_copy(kind, panel).wait()
        value = (
            pair_sum[panel, chip].astype(jnp.float32)
            + side_x[panel].astype(jnp.float32)
            + side_y[panel].astype(jnp.float32)
        )
        matrices[12, pl.ds(panel % 2 * rows, rows), :] = value.astype(jnp.bfloat16)

    def shared_store(panel):
        return pltpu.make_async_copy(
            matrices.at[12, pl.ds(panel % 2 * rows, rows)],
            shared_sum_ref.at[panel],
            local.at[4 + panel % 2],
        )

    project()
    lines[1].arrive(3)
    planes[1][3].start()
    planes[1][1].forward()
    attend(0)
    attend(1)
    planes[1][2].forward()
    attend(2)
    attend(3)
    planes[1][3].forward()
    cotangents.relay()
    join()
    for plane in planes[1]:
        plane.last()
    for index in range(1, 4):
        gates.arrive(index)
    place_slots()
    for plane in planes[1]:
        plane.complete()
    for copy in loads[first_panels:]:
        copy.start()
    exchange(0)
    shared(0)
    exchange(1)
    shared(1)
    exchange(2)
    shared_back(0)
    exchange(3)
    shared_back(1)
    for copy in kept:
        copy.start()
    exchange(4)
    shared_fill(0)
    tokens.relay()
    for panel in range(5, 11):
        exchange(panel)
        shared_pair(panel - 5)
        shared_corners(panel - 5)
        if panel < 10:
            shared_fill(panel - 4)
    for index in range(1, 4):
        cotangents.arrive(index)
        tokens.arrive(index)
    local_copies[2].wait()
    token_copy.wait()
    token_loads = [
        pltpu.make_async_copy(
            source.at[:, pl.ds(part * hidden, hidden)],
            matrices.at[first + part, pl.ds(0, 4 * length)],
            load_sems.at[first + part],
        )
        for first, source in ((6, tokens_ref), (9, cotangents_ref))
        for part in range(3)
    ]
    for copy in token_loads:
        copy.start()
    slot_iota = lax.broadcasted_iota(jnp.int32, (slots, length), 0)

    def slot_gate(expert, source):
        hot = slot_iota == places[expert, pl.ds(source, 1), :]
        return jnp.sum(
            jnp.where(hot, my_gates[expert, pl.ds(source, 1), :], 0.0), axis=1, keepdims=True
        )

    for source in range(4):
        for expert in range(experts):
            hot = slot_iota == places[expert, source : source + 1, :]
            chosen[source, expert * slots : (expert + 1) * slots, :] = jnp.where(
                hot, 1.0, 0.0
            ).astype(jnp.bfloat16)
    exchange(11)
    for copy in token_loads:
        copy.wait()

    @pl.loop(0, 4)
    def _(source):
        part = pl.ds(source * length, length)
        spots = pl.ds(pl.multiple_of(source * slots, slots), slots)
        slot_gates = [slot_gate(expert, source) for expert in range(experts)]
        for block in range(3):
            spot = pl.ds(block * hidden, hidden)
            token_slots = matmul(chosen[source], matrices[6 + block, part, :])
            grad_slots = matmul(chosen[source], matrices[9 + block, part, :])
            for expert in range(experts):
                rows_of = slice(expert * slots, (expert + 1) * slots)
                forward_slots[expert, spots, spot] = token_slots[rows_of].astype(jnp.bfloat16)
                backward_slots[expert, spots, spot] = (
                    grad_slots[rows_of] * slot_gates[expert]
                ).astype(jnp.bfloat16)

    def slot_stores(expert):
        return [
            pltpu.make_async_copy(
                source.at[expert], target.at[expert], expert_sems.at[2 + index, expert]
            )
            for index, (source, target) in enumerate(
                ((forward_slots, received_ref), (backward_slots, grad_returned_ref))
            )
        ]

    def narrow_stores(expert):
        buffer = expert % 2
        return [
            pltpu.make_async_copy(
                narrow.at[buffer, index], target.at[expert], expert_sems.at[4 + buffer, index]
            )
            for index, target in enumerate((act_ref, grad_gate_ref, grad_up_ref))
        ]

    def weight_loads(expert):
        buffer = expert % 2
        return [
            pltpu.make_async_copy(
                weights_ref.at[3 * expert + matrix],
                matrices.at[3 * buffer + matrix],
                expert_sems.at[6 + buffer, matrix],
            )
            for matrix in range(3)
        ]

    def fetch(expert):
        for matrix, copy in enumerate(weight_loads(expert)):
            shard_complete(3 * expert + matrix)
            copy.start()

    for expert in range(experts):
        for copy in slot_stores(expert):
            copy.start()
    fetch(0)

    @pl.loop(0, experts)
    def _(expert):
        buffer = expert % 2
        loaded = weight_loads(expert)

        @pl.when(expert >= 2)
        def _():
            for copy in narrow_stores(expert - 2):
                copy.wait()

        received = forward_slots[expert]
        grad_out = backward_slots[expert]
        loaded[0].wait()
        gate_pre = matmul(received, matrices[3 * buffer])
        loaded[1].wait()
        up_pre = matmul(received, matrices[3 * buffer + 1])
        loaded[2].wait()
        grad_act = matmul(grad_out, matrices[3 * buffer + 2])
        gate_sig = jax.nn.sigmoid(gate_pre)
        gate_act = gate_pre * gate_sig
        act = (gate_act * up_pre).astype(jnp.bfloat16)
        grad_gate = (grad_act * up_pre * gate_sig * (1.0 + gate_pre * (1.0 - gate_sig))).astype(
            jnp.bfloat16
        )
        grad_up = (grad_act * gate_act).astype(jnp.bfloat16)
        narrow[buffer, 0] = act
        narrow[buffer, 1] = grad_gate
        narrow[buffer, 2] = grad_up
        for copy in narrow_stores(expert):
            copy.start()
        for copy in slot_stores(expert):
            copy.wait()
        slot_gates = jnp.concatenate([slot_gate(expert, source) for source in range(4)], 0)
        for block in range(3):
            rows_of = pl.ds(block * hidden, hidden)
            spot = pl.ds(block * hidden, hidden)
            out = matmul_nt(act, matrices[3 * buffer + 2, rows_of, :]).astype(jnp.bfloat16)
            forward_slots[expert, :, spot] = (
                out.astype(jnp.float32) * slot_gates
            ).astype(jnp.bfloat16)
            backward_slots[expert, :, spot] = (
                matmul_nt(grad_gate, matrices[3 * buffer, rows_of, :])
                + matmul_nt(grad_up, matrices[3 * buffer + 1, rows_of, :])
            ).astype(jnp.bfloat16)

        later = (
            (lambda: exchange(12),),
            (lambda: exchange(13),),
            (lambda: exchange(14),),
            (
                lambda: exchange(15),
                lambda: exchange(16),
                lambda: shard_last(14),
                lambda: shared_sides(0),
                lambda: shared_sides(1),
            ),
            (
                lambda: shard_forward(17),
                lambda: shared_sides(2),
                lambda: shared_sides(3),
                lambda: shared_sides(4),
                lambda: shared_sides(5),
                lambda: shard_last(15),
                lambda: shard_last(16),
                lambda: shard_last(17),
            ),
        )
        for done, calls in enumerate(later):

            @pl.when(expert == done)
            def _():
                for call in calls:
                    call()

        @pl.when(expert + 1 < experts)
        def _():
            fetch(expert + 1)

    for expert in (experts - 2, experts - 1):
        for copy in narrow_stores(expert):
            copy.wait()
    out_copies = []
    for first, values, target in ((0, backward_slots, grad_parts_ref), (3, forward_slots, routed_parts_ref)):
        for block in range(3):
            spot = slice(block * hidden, (block + 1) * hidden)
            for source in range(4):
                slots_of = jnp.concatenate(
                    [
                        values[expert, source * slots : (source + 1) * slots, spot]
                        for expert in range(experts)
                    ],
                    0,
                )
                matrices[first + block, source * length : (source + 1) * length, :] = matmul_tn(
                    chosen[source], slots_of
                ).astype(jnp.bfloat16)
            out_copies.append(
                pltpu.make_async_copy(
                    matrices.at[first + block, pl.ds(0, 4 * length)],
                    target.at[:, pl.ds(block * hidden, hidden)],
                    load_sems.at[first + block],
                )
            )
            out_copies[-1].start()
    @pl.loop(0, panels)
    def _(panel):
        shard_finish(panel)

    for panel in range(shared_panels):
        if panel >= 2:
            shared_store(panel - 2).wait()
        shared_total(panel)
        shared_store(panel).start()
    for panel in (shared_panels - 2, shared_panels - 1):
        shared_store(panel).wait()
    for copy in (*kept, *out_copies):
        copy.wait()

    links.finish()


def front(stripe, gates, masters, hidden_in, cotangent, slots):
    length, width = cotangent.shape
    stripe_rows, columns = stripe.shape
    panels, rows, hidden = masters.shape
    experts = panels // 3
    low, full = jnp.bfloat16, jnp.float32
    vmem = pl.BlockSpec(memory_space=pltpu.VMEM)
    query_width = HEADS * HD
    spots = 4 * slots
    return pl.pallas_call(
        front_kernel,
        in_specs=[ANY] * 3 + [vmem] * 2,
        out_specs=[ANY] * 18 + [vmem] * 2,
        out_shape=[
            jax.ShapeDtypeStruct((stripe_rows * 32, columns), low),
            jax.ShapeDtypeStruct((panels, rows * 8, hidden), low),
            *[jax.ShapeDtypeStruct((length * 4, width), low)] * 4,
            *[jax.ShapeDtypeStruct((experts, spots, width), low)] * 2,
            *[jax.ShapeDtypeStruct((experts, spots, hidden), low)] * 3,
            jax.ShapeDtypeStruct((length, width), low),
            jax.ShapeDtypeStruct((length, query_width + 2 * KVH * HD), low),
            jax.ShapeDtypeStruct((length, query_width), low),
            jax.ShapeDtypeStruct((length, width), full),
            jax.ShapeDtypeStruct((length, width), full),
            jax.ShapeDtypeStruct((length, width), full),
            jax.ShapeDtypeStruct((6, rows, hidden), low),
            jax.ShapeDtypeStruct((length, 1), full),
            jax.ShapeDtypeStruct((8, width), full),
        ],
        scratch_shapes=[
            pltpu.VMEM((length, width), low),
            pltpu.VMEM((length, query_width + 2 * KVH * HD), low),
            pltpu.VMEM((length, query_width), low),
            pltpu.VMEM((length, width), full),
            pltpu.VMEM((length, width), full),
            pltpu.VMEM((length, width), full),
            pltpu.VMEM((length, width), low),
            pltpu.VMEM((length, FFS), low),
            pltpu.VMEM((length, 2 * FFS), low),
            pltpu.VMEM((14, width, hidden), low),
            pltpu.VMEM((width, 128), low),
            pltpu.VMEM((4, 4, 8, length), full),
            pltpu.VMEM((experts, 4, length), jnp.int32),
            pltpu.VMEM((experts, 4, length), full),
            pltpu.VMEM((4, experts * slots, length), low),
            pltpu.VMEM((experts, spots, width), low),
            pltpu.VMEM((experts, spots, width), low),
            pltpu.VMEM((2, 3, spots, hidden), low),
            pltpu.VMEM((6, 4, rows, hidden), low),
            pltpu.VMEM((6, rows // 2, hidden), low),
            pltpu.VMEM((6, rows // 2, hidden), low),
            pltpu.VMEM((6, rows, hidden), low),
            pltpu.VMEM((6, rows, hidden), low),
            pltpu.SemaphoreType.DMA((170,)),
            pltpu.SemaphoreType.DMA((7, panels)),
            pltpu.SemaphoreType.DMA((7, panels)),
            pltpu.SemaphoreType.DMA((6,)),
            pltpu.SemaphoreType.DMA((15,)),
            pltpu.SemaphoreType.DMA((8, 6)),
            pltpu.SemaphoreType.DMA((2, 5, 6)),
            pltpu.SemaphoreType.DMA((6,)),
        ],
        compiler_params=pltpu.CompilerParams(
            collective_id=1, has_side_effects=True, vmem_limit_bytes=63 * MIB
        ),
        name="front",
    )(stripe, gates, masters, hidden_in, cotangent)


def scatter_kernel(
    grad_parts_ref,
    received_ref,
    grad_returned_ref,
    act_ref,
    grad_gate_ref,
    grad_up_ref,
    dense_ref,
    shared_sum_ref,
    cotangent_ref,
    normed_attend_ref,
    attended_ref,
    residual_in,
    grad_shared_in,
    projected_in,
    hidden_in,
    scale_ref,
    gains_ref,
    expert_sum_ref,
    stripes_ref,
    grad_input_ref,
    grad_gain_ref,
    residual_ref,
    grad_shared_ref,
    projected_ref,
    hidden_ref,
    ring,
    pair_sum,
    corner_x,
    corner_y,
    side_x,
    side_y,
    staged,
    wide,
    narrow,
    left,
    right,
    out_weights,
    grad_tokens,
    grad_attended,
    grad_pair,
    grad_residual_ref,
    key_weights,
    line_out,
    line_in,
    pair_sems,
    slot_sems,
    line_sems,
    token_sems,
    load_sems,
    free,
):
    dp, z = lax.axis_index("dp"), lax.axis_index("expert")
    core, chip = dp % 2, dp // 2
    chip_x, chip_y = flipped(chip, 0), flipped(chip, 1)
    chip_corner = flipped(chip_x, 1)
    device_core = (flipped(dp, 0), z)
    device_x = (flipped(dp, 1), z)
    device_y = (flipped(dp, 2), z)
    others = [(dp, (z + turn) % 4) for turn in range(1, 4)]
    slots = pair_sum.shape[0]
    experts = received_ref.shape[0]
    expert_panels = 3 * experts
    dense_panels = line_out.shape[0]
    shared_panels = dense_panels - right.shape[0]
    panels = expert_panels + right.shape[0]
    length, width = residual_ref.shape
    share, hidden = staged.shape[1:]
    half = share // 2
    stripe = share // 4
    query_width = HEADS * HD
    kv_width = KVH * HD
    block = width // 4

    def remote(source, target, send, receive, device):
        return pltpu.make_async_remote_copy(
            src_ref=source,
            dst_ref=target,
            send_sem=send,
            recv_sem=receive,
            device_id=device,
            device_id_type=MESH,
        )

    barrier = pltpu.get_barrier_semaphore()
    for device in (device_core, device_x, device_y, *others):
        pl.semaphore_signal(barrier, inc=1, device_id=device, device_id_type=MESH)
    pl.semaphore_wait(barrier, 6)

    grad_copies = [
        remote(
            grad_parts_ref.at[pl.ds(pl.multiple_of(device[1] * length, length), length), :],
            grad_tokens.at[turn],
            token_sems.at[turn],
            token_sems.at[3 + turn],
            device,
        )
        for turn, device in enumerate(others)
    ]
    for copy in grad_copies:
        copy.start()

    def expert_loads(expert):
        buffer = expert % 2
        return [
            pltpu.make_async_copy(source.at[expert], target, load_sems.at[buffer, index])
            for index, (source, target) in enumerate(
                (
                    (received_ref, wide.at[buffer, 0]),
                    (grad_returned_ref, wide.at[buffer, 1]),
                    (grad_gate_ref, narrow.at[buffer, 0]),
                    (grad_up_ref, narrow.at[buffer, 1]),
                    (act_ref, narrow.at[buffer, 2]),
                )
            )
        ]

    for copy in expert_loads(0):
        copy.start()

    def columns(ref, panel):
        return ref.at[:, pl.ds(panel * hidden, hidden)]

    sources = [
        (cotangent_ref, left.at[0]),
        (normed_attend_ref, left.at[2]),
        *[(columns(attended_ref, panel), right.at[panel]) for panel in range(3)],
        (shared_sum_ref, line_out.at[pl.ds(0, shared_panels)]),
        (residual_in, residual_ref),
        (grad_shared_in, grad_shared_ref),
        (projected_in, projected_ref),
        (hidden_in, hidden_ref),
        (dense_ref.at[:, pl.ds(query_width + 2 * kv_width, query_width)], out_weights),
        (dense_ref.at[:, pl.ds(query_width, 2 * kv_width)], key_weights),
        (
            grad_parts_ref.at[pl.ds(pl.multiple_of(z * length, length), length), :],
            grad_tokens.at[3],
        ),
    ]
    dense_loads = [
        pltpu.make_async_copy(source, target, load_sems.at[2 + index // 5, index % 5])
        for index, (source, target) in enumerate(sources)
    ]
    for copy in dense_loads:
        copy.start()
    query_load = pltpu.make_async_copy(
        dense_ref.at[:, pl.ds(0, query_width)], out_weights, pair_sems.at[4]
    )

    def fill(pair, left_ref, right_value):
        for chip_index in range(4):
            part = matmul_tn(left_ref[:, chip_index * block : (chip_index + 1) * block], right_value)
            ring[pair, chip_index] = part.astype(jnp.bfloat16).reshape(2, share, hidden)

    def total(first, *more):
        result = first.astype(jnp.float32)
        for value in more:
            result = result + value.astype(jnp.float32)
        return result

    def pair_copy(panel):
        pair, slot = panel % 2, panel % slots
        return remote(
            ring.at[pair, :, 1 - core],
            pair_sum.at[slot],
            pair_sems.at[pair],
            slot_sems.at[0, slot],
            device_core,
        )

    def corner_copies(panel):
        slot = panel % slots
        return (
            remote(
                pair_sum.at[slot, chip_corner, pl.ds(0, half)],
                corner_x.at[slot],
                slot_sems.at[1, slot],
                slot_sems.at[2, slot],
                device_x,
            ),
            remote(
                pair_sum.at[slot, chip_corner, pl.ds(half, half)],
                corner_y.at[slot],
                slot_sems.at[3, slot],
                slot_sems.at[4, slot],
                device_y,
            ),
        )

    def side_copies(panel):
        slot = panel % slots
        return (
            remote(
                pair_sum.at[slot, chip_x],
                side_x.at[slot],
                slot_sems.at[5, slot],
                slot_sems.at[6, slot],
                device_x,
            ),
            remote(
                pair_sum.at[slot, chip_y],
                side_y.at[slot],
                slot_sems.at[7, slot],
                slot_sems.at[8, slot],
                device_y,
            ),
        )

    def line_copies(panel):
        return [
            remote(
                line_out.at[panel, pl.ds(pl.multiple_of(device[1] * stripe, stripe), stripe)],
                line_in.at[panel, turn],
                line_sems.at[0, panel, turn],
                line_sems.at[1, panel, turn],
                device,
            )
            for turn, device in enumerate(others)
        ]

    def staged_copy(panel):
        return pltpu.make_async_copy(
            staged.at[panel % 2], expert_sum_ref.at[panel], pair_sems.at[2 + panel % 2]
        )

    def post(panel):
        @pl.when(panel >= slots)
        def _():
            pl.semaphore_wait(free.at[0], 1)

        pair_copy(panel).start()

    def sum_pair(panel):
        pair, slot = panel % 2, panel % slots
        pair_copy(panel).wait()
        for chip_index in range(4):
            pair_sum[slot, chip_index] = total(
                pair_sum[slot, chip_index], ring[pair, chip_index, core]
            ).astype(jnp.bfloat16)

        @pl.when(panel >= slots)
        def _():
            pl.semaphore_wait(free.at[1], 1)
            pl.semaphore_wait(free.at[2], 1)

        for copy in corner_copies(panel):
            copy.start()

    def sum_corner(panel):
        slot = panel % slots
        for copy in corner_copies(panel):
            copy.wait_recv()
        pair_sum[slot, chip_y, :half] = total(
            pair_sum[slot, chip_y, :half], corner_x[slot]
        ).astype(jnp.bfloat16)
        pair_sum[slot, chip_x, half:] = total(
            pair_sum[slot, chip_x, half:], corner_y[slot]
        ).astype(jnp.bfloat16)
        for copy in side_copies(panel):
            copy.start()

    def sum_sides(panel):
        slot = panel % slots
        for copy in corner_copies(panel):
            copy.wait_send()
        for copy in side_copies(panel):
            copy.wait()
        value = total(pair_sum[slot, chip], side_x[slot], side_y[slot]).astype(jnp.bfloat16)

        @pl.when(panel < expert_panels)
        def _():
            @pl.when(panel >= 2)
            def _():
                staged_copy(panel - 2).wait()

            staged[panel % 2] = value
            staged_copy(panel).start()

        @pl.when(panel >= expert_panels)
        def _():
            index = panel - expert_panels + shared_panels
            line_out[index] = value
            for copy in line_copies(index):
                copy.start()

        @pl.when(panel < panels - slots)
        def _():
            for index, device in enumerate((device_core, device_x, device_y)):
                pl.semaphore_signal(
                    free.at[index], inc=1, device_id=device, device_id_type=MESH
                )

    def residual_backward(part):
        if part == 0:
            for copy in dense_loads:
                copy.wait()
            for copy in grad_copies:
                copy.wait()
            grad_gain_ref[...] = jnp.zeros_like(grad_gain_ref)
        rows_step = 32
        steps = length // rows_step // 2

        @pl.loop(part * steps, (part + 1) * steps)
        def _(index):
            rows = pl.ds(index * rows_step, rows_step)
            grad_normed = (
                total(
                    grad_tokens[3, rows, :],
                    grad_tokens[0, rows, :],
                    grad_tokens[1, rows, :],
                    grad_tokens[2, rows, :],
                )
                + grad_shared_ref[rows, :]
            )
            residual, scale = residual_ref[rows, :], scale_ref[rows, :]
            grad_scaled = grad_normed * gains_ref[1:2, :]
            mean = jnp.mean(grad_scaled * residual, axis=-1, keepdims=True)
            grad_residual = (
                left[0, rows, :].astype(jnp.float32)
                + scale * grad_scaled
                - residual * (scale * scale * scale) * mean
            )
            grad_residual_ref[rows, :] = grad_residual
            left[1, rows, :] = grad_residual.astype(jnp.bfloat16)
            grad_gain_ref[1:2, :] += jnp.sum(
                grad_normed * residual * scale, axis=0, keepdims=True
            )

    def attended_backward():
        grad_attended[...] = matmul(left[1], out_weights[...]).astype(jnp.bfloat16)
        query_load.start()

    def query_backward():
        query_load.wait()
        for part in range(3):
            update = matmul_nt(right[3 + part], out_weights[:, part * hidden : (part + 1) * hidden])
            if part == 0:
                grad_input_ref[...] = update
            else:
                grad_input_ref[...] += update

    def key_backward():
        for part in range(2):
            grad_input_ref[...] += matmul_nt(
                right[6 + part], key_weights[:, part * hidden : (part + 1) * hidden]
            )

    def input_backward():
        rows_step = 32

        @pl.loop(0, length // rows_step)
        def _(index):
            rows = pl.ds(index * rows_step, rows_step)
            values, grad_normed = hidden_ref[rows, :].astype(jnp.float32), grad_input_ref[rows, :]
            scale = lax.rsqrt(jnp.mean(values * values, axis=-1, keepdims=True) + 1e-06)
            grad_scaled = grad_normed * gains_ref[0:1, :]
            mean = jnp.mean(grad_scaled * values, axis=-1, keepdims=True)
            grad_input_ref[rows, :] = (
                grad_residual_ref[rows, :]
                + scale * grad_scaled
                - values * (scale * scale * scale) * mean
            )
            grad_gain_ref[0:1, :] += jnp.sum(
                grad_normed * values * scale, axis=0, keepdims=True
            )

    def attention_backward(head):
        score_scale = HD ** (-0.5)
        per_group = HEADS // KVH
        heads_wide = hidden // HD
        group = head // per_group
        key_rows = projected_ref[:, query_width + group * HD : query_width + (group + 1) * HD]
        value_first = query_width + kv_width + group * HD
        value_rows = projected_ref[:, value_first : value_first + HD]
        row = lax.broadcasted_iota(jnp.int32, (length, length), 0)
        column = lax.broadcasted_iota(jnp.int32, (length, length), 1)
        spot = slice(head * HD, (head + 1) * HD)
        query, grad_out = projected_ref[:, spot], grad_attended[:, spot]
        scores = jnp.where(column <= row, matmul_nt(query, key_rows) * score_scale, -1e30)
        raised = jnp.exp(scores - jnp.max(scores, axis=-1, keepdims=True))
        weights = raised / jnp.sum(raised, axis=-1, keepdims=True)
        grad_weights = matmul_nt(grad_out, value_rows)
        inner = jnp.sum(weights * grad_weights, axis=-1, keepdims=True)
        grad_scores = (weights * (grad_weights - inner)).astype(jnp.bfloat16)
        grad_query = matmul(grad_scores, key_rows) * score_scale
        place = slice(head % heads_wide * HD, (head % heads_wide + 1) * HD)
        right[3 + head // heads_wide, :, place] = grad_query.astype(jnp.bfloat16)
        grad_key = matmul_tn(grad_scores, query)
        grad_value = matmul_tn(weights.astype(jnp.bfloat16), grad_out)
        if head % per_group > 0:
            grad_key = grad_key + grad_pair[0]
            grad_value = grad_value + grad_pair[1]
        if head % per_group < per_group - 1:
            grad_pair[0] = grad_key
            grad_pair[1] = grad_value
        else:
            place = slice(group * HD, (group + 1) * HD)
            right[6, :, place] = (grad_key * score_scale).astype(jnp.bfloat16)
            right[7, :, place] = grad_value.astype(jnp.bfloat16)

    def two_heads_backward(head):
        attention_backward(head)
        attention_backward(head + 1)

    @pl.loop(0, panels + 5)
    def _(step):
        @pl.when(step < expert_panels)
        def _():
            expert, matrix = step // 3, step % 3

            @pl.when(matrix == 0)
            def _():
                for copy in expert_loads(expert):
                    copy.wait()

                @pl.when(expert + 1 < experts)
                def _():
                    for copy in expert_loads(expert + 1):
                        copy.start()

            fill(step % 2, wide.at[expert % 2, matrix // 2], narrow[expert % 2, matrix])

        backward = [
            *[functools.partial(residual_backward, part) for part in range(2)],
            attended_backward,
            *[functools.partial(two_heads_backward, head) for head in range(0, HEADS, 2)],
            query_backward,
            key_backward,
            input_backward,
        ]
        for index, call in enumerate(backward):
            pl.when(step == GRAD_STEP + index)(call)

        @pl.when((step >= expert_panels) & (step < panels))
        def _():
            panel = step - expert_panels
            fill(step % 2, left.at[jnp.where(panel < 3, 1, 2)], right[panel])

        @pl.when(step == GRAD_STEP + 1)
        def _():
            for panel in range(shared_panels):
                for copy in line_copies(panel):
                    copy.start()

        @pl.when(step < panels)
        def _():
            post(step)

        @pl.when((step >= 1) & (step < panels + 1))
        def _():
            sum_pair(step - 1)

        @pl.when((step >= 3) & (step < panels + 3))
        def _():
            sum_corner(step - 3)

        @pl.when(step >= 5)
        def _():
            sum_sides(step - 5)

    for panel in (expert_panels - 2, expert_panels - 1):
        staged_copy(panel).wait()

    for panel in range(dense_panels):
        for copy in line_copies(panel):
            copy.wait()
        place = panel + 8 if panel < 6 else panel - 1 if panel < 9 else panel - 9
        stripes_ref[place] = total(
            line_out[panel, pl.ds(pl.multiple_of(z * stripe, stripe), stripe), :],
            line_in[panel, 0],
            line_in[panel, 1],
            line_in[panel, 2],
        )


def scatter_grads(
    grad_parts,
    saved,
    dense_all,
    shared_sum,
    cotangent,
    normed_attend,
    attended,
    residual,
    grad_shared,
    projected,
    hidden_in,
    scale,
    gains,
):
    experts, spots, width = saved[0].shape
    hidden = saved[2].shape[-1]
    length = residual.shape[0]
    share = width // 8
    stripe = share // 4
    dense_panels = 14
    low = jnp.bfloat16
    vmem = pl.BlockSpec(memory_space=pltpu.VMEM)
    return pl.pallas_call(
        scatter_kernel,
        in_specs=[ANY] * 15 + [vmem] * 2,
        out_specs=[ANY] + [vmem] * 3,
        out_shape=[
            jax.ShapeDtypeStruct((3 * experts, share, hidden), low),
            jax.ShapeDtypeStruct((dense_panels, stripe, hidden), jnp.float32),
            jax.ShapeDtypeStruct((length, width), jnp.float32),
            jax.ShapeDtypeStruct((2, width), jnp.float32),
        ],
        scratch_shapes=[
            pltpu.VMEM((length, width), jnp.float32),
            pltpu.VMEM((length, width), jnp.float32),
            pltpu.VMEM(projected.shape, low),
            pltpu.VMEM((length, width), low),
            pltpu.VMEM((2, 4, 2, share, hidden), low),
            pltpu.VMEM((SLOTS, 4, share, hidden), low),
            pltpu.VMEM((SLOTS, share // 2, hidden), low),
            pltpu.VMEM((SLOTS, share // 2, hidden), low),
            pltpu.VMEM((SLOTS, share, hidden), low),
            pltpu.VMEM((SLOTS, share, hidden), low),
            pltpu.VMEM((2, share, hidden), low),
            pltpu.VMEM((2, 2, spots, width), low),
            pltpu.VMEM((2, 3, spots, hidden), low),
            pltpu.VMEM((3, length, width), low),
            pltpu.VMEM((8, length, hidden), low),
            pltpu.VMEM((width, HEADS * HD), low),
            pltpu.VMEM((4, length, width), low),
            pltpu.VMEM((length, HEADS * HD), low),
            pltpu.VMEM((2, length, HD), jnp.float32),
            pltpu.VMEM((length, width), jnp.float32),
            pltpu.VMEM((width, 2 * KVH * HD), low),
            pltpu.VMEM((dense_panels, share, hidden), low),
            pltpu.VMEM((dense_panels, 3, stripe, hidden), low),
            pltpu.SemaphoreType.DMA((5,)),
            pltpu.SemaphoreType.DMA((9, SLOTS)),
            pltpu.SemaphoreType.DMA((2, dense_panels, 3)),
            pltpu.SemaphoreType.DMA((6,)),
            pltpu.SemaphoreType.DMA((5, 5)),
            pltpu.SemaphoreType.REGULAR((3,)),
        ],
        compiler_params=pltpu.CompilerParams(
            collective_id=3, has_side_effects=True, vmem_limit_bytes=62 * MIB
        ),
        name="scatter_grads",
    )(
        grad_parts,
        *saved,
        dense_all,
        shared_sum,
        cotangent,
        normed_attend,
        attended,
        residual,
        grad_shared,
        projected,
        hidden_in,
        scale,
        gains,
    )


def muon_kernel(
    expert_ref,
    dense_ref,
    routed_parts_ref,
    expert_out_ref,
    dense_out_ref,
    routed_received_ref,
    dense_back,
    moments,
    units,
    orthogonal,
    current,
    low,
    identity,
    line_sems,
    out_sems,
    in_sems,
    back_out_sems,
    back_in_sems,
    load_sems,
):
    dp, z = lax.axis_index("dp"), lax.axis_index("expert")
    count, share, _ = moments.shape
    first, dense_count = 10, 4
    stripe = dense_ref.shape[1]
    others = [(dp, (z + turn) % 4) for turn in range(1, 4)]
    peers = [((dp + turn) % 8, z) for turn in range(1, 8)]

    def remote(source, target, send, receive, device):
        return pltpu.make_async_remote_copy(
            src_ref=source,
            dst_ref=target,
            send_sem=send,
            recv_sem=receive,
            device_id=device,
            device_id_type=MESH,
        )

    def share_of(index):
        return pl.ds(pl.multiple_of(index * share, share), share)

    def stripe_of(index):
        return pl.ds(pl.multiple_of(index * stripe, stripe), stripe)

    barrier = pltpu.get_barrier_semaphore()
    for device in (*others, *peers):
        pl.semaphore_signal(barrier, inc=1, device_id=device, device_id_type=MESH)
    dense_rows = pl.ds(first, dense_count)
    loads = [
        pltpu.make_async_copy(
            expert_ref.at[pl.ds(0, first)], moments.at[pl.ds(0, first)], load_sems.at[0]
        ),
        pltpu.make_async_copy(
            expert_ref.at[pl.ds(first, count - first - dense_count)],
            moments.at[pl.ds(first + dense_count, count - first - dense_count)],
            load_sems.at[1],
        ),
        pltpu.make_async_copy(
            dense_ref.at[pl.ds(z * dense_count, dense_count)],
            moments.at[dense_rows, stripe_of(z)],
            load_sems.at[2],
        ),
    ]
    for copy in loads:
        copy.start()
    pl.semaphore_wait(barrier, len(others) + len(peers))
    line_copies = [
        remote(
            dense_ref.at[pl.ds(device[1] * dense_count, dense_count)],
            moments.at[dense_rows, stripe_of(z)],
            line_sems.at[0, turn],
            line_sems.at[1, turn],
            device,
        )
        for turn, device in enumerate(others)
    ]
    line_back = [
        remote(
            dense_back.at[:, stripe_of(device[1])],
            dense_out_ref.at[pl.ds(z * dense_count, dense_count)],
            line_sems.at[2, turn],
            line_sems.at[3, turn],
            device,
        )
        for turn, device in enumerate(others)
    ]
    own_back = pltpu.make_async_copy(
        dense_back.at[:, stripe_of(z)],
        dense_out_ref.at[pl.ds(z * dense_count, dense_count)],
        load_sems.at[2],
    )

    def out_copy(slot, turn):
        owner = peers[turn][0]
        return remote(
            moments.at[8 * slot + owner],
            units.at[slot, share_of(dp)],
            out_sems.at[slot, turn],
            in_sems.at[slot],
            peers[turn],
        )

    def own_copy(slot):
        return pltpu.make_async_copy(
            moments.at[8 * slot + dp], units.at[slot, share_of(dp)], load_sems.at[3 + slot]
        )

    def is_dense(slot, owner):
        unit = 8 * slot + owner
        return (unit >= first) & (unit < first + dense_count)

    def expert_place(slot, owner):
        unit = 8 * slot + owner
        return expert_out_ref.at[jnp.where(unit < first, unit, unit - dense_count)]

    def dense_place(slot, owner):
        return dense_back.at[8 * slot + owner - first]

    def back_copy(place, slot, turn):
        return remote(
            orthogonal.at[slot, share_of(peers[turn][0])],
            place(slot, dp),
            back_out_sems.at[slot, turn],
            back_in_sems.at[slot, dp],
            peers[turn],
        )

    def own_back_copy(place, slot):
        return pltpu.make_async_copy(
            orthogonal.at[slot, share_of(dp)], place(slot, dp), load_sems.at[3 + slot]
        )

    def send_back(place, slot):
        for turn in range(7):
            back_copy(place, slot, turn).start()
        own_back_copy(place, slot).start()

    def exists(slot, owner):
        return 8 * slot + owner < count

    def send_slot(slot):
        for turn in range(7):
            pl.when(exists(slot, peers[turn][0]))(out_copy(slot, turn).start)
        pl.when(exists(slot, dp))(own_copy(slot).start)

    length = routed_received_ref.shape[1]
    own_routed = pltpu.make_async_copy(
        routed_parts_ref.at[pl.ds(pl.multiple_of(z * length, length), length), :],
        routed_received_ref.at[3],
        load_sems.at[6],
    )
    own_routed.start()
    routed_copies = [
        remote(
            routed_parts_ref.at[pl.ds(pl.multiple_of(device[1] * length, length), length), :],
            routed_received_ref.at[turn],
            line_sems.at[4, turn],
            line_sems.at[5, turn],
            device,
        )
        for turn, device in enumerate(others)
    ]
    for copy in line_copies:
        copy.start()
    loads[0].wait()
    send_slot(0)
    loads[1].wait()
    loads[2].wait()
    for copy in line_copies:
        copy.wait()
    send_slot(1)
    send_slot(2)
    for copy in routed_copies:
        copy.start()

    @pl.loop(0, 3)
    def _(slot):
        @pl.when(exists(slot, dp))
        def _():
            own_copy(slot).wait()
            arrived = units.at[slot, pl.ds(0, 7 * share)]
            remote(arrived, arrived, in_sems.at[slot], in_sems.at[slot], peers[0]).wait_recv()
            newton_schulz_unit(units.at[slot], orthogonal.at[slot], current, low, identity)

            @pl.when(is_dense(slot, dp))
            def _():
                send_back(dense_place, slot)

            @pl.when(jnp.logical_not(is_dense(slot, dp)))
            def _():
                send_back(expert_place, slot)

    def own_back_wait(slot):
        def wait():
            pltpu.make_async_copy(
                orthogonal.at[slot, share_of(dp)], expert_out_ref.at[0], load_sems.at[3 + slot]
            ).wait()

        return wait

    def wait_back(slot):
        for turn in range(7):
            owner = peers[turn][0]

            @pl.when(exists(slot, owner))
            def _():
                block = expert_out_ref.at[0]
                semaphore = back_in_sems.at[slot, owner]
                remote(block, block, semaphore, semaphore, peers[0]).wait_recv()

        pl.when(exists(slot, dp))(own_back_wait(slot))

    wait_back(1)
    for copy in line_back:
        copy.start()
    own_back.start()
    wait_back(0)
    wait_back(2)
    for slot in range(3):
        for turn in range(7):
            pl.when(exists(slot, peers[turn][0]))(out_copy(slot, turn).wait_send)

        @pl.when(exists(slot, dp))
        def _():
            for turn in range(7):
                back_copy(expert_place, slot, turn).wait_send()

    for copy in line_back:
        copy.wait()
    own_back.wait()
    own_routed.wait()
    for copy in routed_copies:
        copy.wait()


def muon(expert_units, dense_units, routed_parts):
    experts, share, columns = expert_units.shape
    panels, stripe, _ = dense_units.shape
    count = experts + panels // 4
    low = jnp.bfloat16
    return pl.pallas_call(
        muon_kernel,
        in_specs=[ANY] * 3,
        out_specs=[ANY] * 3,
        out_shape=[
            jax.ShapeDtypeStruct(expert_units.shape, low),
            jax.ShapeDtypeStruct(dense_units.shape, low),
            jax.ShapeDtypeStruct((4, routed_parts.shape[0] // 4, routed_parts.shape[1]), low),
        ],
        scratch_shapes=[
            pltpu.VMEM((panels // 4, share, columns), low),
            pltpu.VMEM((count, share, columns), low),
            pltpu.VMEM((3, 8 * share, columns), low),
            pltpu.VMEM((3, 8 * share, columns), low),
            pltpu.VMEM((columns, 8 * share), jnp.float32),
            pltpu.VMEM((columns, 8 * share), low),
            pltpu.VMEM((columns, columns), low),
            pltpu.SemaphoreType.DMA((6, 3)),
            pltpu.SemaphoreType.DMA((3, 7)),
            pltpu.SemaphoreType.DMA((3,)),
            pltpu.SemaphoreType.DMA((3, 7)),
            pltpu.SemaphoreType.DMA((3, 8)),
            pltpu.SemaphoreType.DMA((7,)),
        ],
        compiler_params=pltpu.CompilerParams(
            collective_id=4, has_side_effects=True, vmem_limit_bytes=56 * MIB
        ),
        name="muon",
    )(expert_units, dense_units, routed_parts)


GROUP = 2


def blocks_over(steps, shape, axis):
    def place(index):
        return tuple(
            jnp.minimum(index, steps - 1) if position == axis else 0
            for position in range(len(shape))
        )

    return pl.BlockSpec(shape, place)


def moments_kernel(
    momentum_ref,
    sum_ref,
    dense_momentum_ref,
    dense_sum_ref,
    grad_ref,
    moment_ref,
    units_ref,
    dense_grad_ref,
    dense_moment_ref,
    dense_units_ref,
):
    grad = sum_ref[...].astype(jnp.float32)
    moment = MOMENTUM_DECAY * momentum_ref[...] + grad
    grad_ref[...] = grad
    moment_ref[...] = moment
    units_ref[...] = moment.astype(jnp.bfloat16)
    columns = dense_sum_ref.shape[2]
    real = pl.program_id(0) < pl.num_programs(0) - 2
    for panel in range(GROUP):
        spot = slice(panel * columns, (panel + 1) * columns)
        dense_grad = dense_sum_ref[panel]
        dense_moment = MOMENTUM_DECAY * dense_momentum_ref[:, spot] + dense_grad
        dense_grad_ref[:, spot] = dense_grad
        dense_moment_ref[:, spot] = dense_moment
        dense_units_ref[panel] = jnp.where(real, dense_moment, 0.0).astype(jnp.bfloat16)


def moments(momentum, grad_sum, dense_momentum, dense_sum):
    panels, rows, columns = grad_sum.shape
    dense_panels, stripe, _ = dense_sum.shape
    steps = panels // GROUP
    block = pl.BlockSpec((GROUP, rows, columns), lambda index: (index, 0, 0))
    wide = blocks_over(dense_panels // GROUP, (stripe, GROUP * columns), 1)
    full = jax.ShapeDtypeStruct(grad_sum.shape, jnp.float32)
    dense_full = jax.ShapeDtypeStruct(dense_momentum.shape, jnp.float32)
    grad, moment, *rest = pl.pallas_call(
        moments_kernel,
        grid=(steps,),
        in_specs=[
            block,
            block,
            wide,
            blocks_over(dense_panels // GROUP, (GROUP, stripe, columns), 0),
        ],
        out_specs=[
            block,
            block,
            block,
            wide,
            wide,
            blocks_over(dense_panels // GROUP + 1, (GROUP, stripe, columns), 0),
        ],
        out_shape=[
            full,
            full,
            jax.ShapeDtypeStruct(grad_sum.shape, jnp.bfloat16),
            dense_full,
            dense_full,
            jax.ShapeDtypeStruct((dense_panels + GROUP, stripe, columns), jnp.bfloat16),
        ],
        compiler_params=pltpu.CompilerParams(vmem_limit_bytes=60 * MIB),
        name="moments",
    )(momentum.reshape(grad_sum.shape), grad_sum, dense_momentum, dense_sum)
    return grad.reshape(momentum.shape), moment.reshape(momentum.shape), *rest


def update_kernel(
    weights_ref,
    orthogonal_ref,
    dense_weights_ref,
    dense_orthogonal_ref,
    base_ref,
    routed_ref,
    grad_ref,
    new_ref,
    dense_new_ref,
    out_ref,
    grad_out_ref,
):
    keep_factor = 1.0 - LEARN_RATE * WEIGHT_DECAY
    new_ref[...] = keep_factor * weights_ref[...] - LEARN_RATE * orthogonal_ref[...].astype(
        jnp.float32
    )
    columns = dense_orthogonal_ref.shape[2]
    for panel in range(GROUP):
        spot = slice(panel * columns, (panel + 1) * columns)
        dense_new_ref[:, spot] = keep_factor * dense_weights_ref[:, spot] - LEARN_RATE * (
            dense_orthogonal_ref[panel].astype(jnp.float32)
        )
    total = base_ref[...]
    for source in (3, 0, 1, 2):
        total = total + routed_ref[source].astype(jnp.float32)
    out_ref[...] = total.astype(jnp.bfloat16)
    grad_out_ref[...] = grad_ref[...]


def updated(weights, orthogonal, dense_weights, dense_orthogonal, base, routed, grad):
    panels, rows, columns = orthogonal.shape
    stripe, dense_columns = dense_weights.shape
    length, width = base.shape
    dense_steps = dense_columns // (GROUP * columns)
    row_steps = 8
    block = pl.BlockSpec((GROUP, rows, columns), lambda index: (index, 0, 0))
    wide = blocks_over(dense_steps, (stripe, GROUP * columns), 1)
    part = blocks_over(row_steps, (length // row_steps, width), 0)
    new, *rest = pl.pallas_call(
        update_kernel,
        grid=(panels // GROUP,),
        in_specs=[
            block,
            block,
            wide,
            blocks_over(dense_steps, (GROUP, stripe, columns), 0),
            part,
            blocks_over(row_steps, (4, length // row_steps, width), 1),
            part,
        ],
        out_specs=[block, wide, part, part],
        out_shape=[
            jax.ShapeDtypeStruct(orthogonal.shape, jnp.float32),
            jax.ShapeDtypeStruct(dense_weights.shape, jnp.float32),
            jax.ShapeDtypeStruct(base.shape, jnp.bfloat16),
            jax.ShapeDtypeStruct(base.shape, jnp.float32),
        ],
        compiler_params=pltpu.CompilerParams(vmem_limit_bytes=60 * MIB),
        name="update",
    )(
        weights.reshape(orthogonal.shape),
        orthogonal,
        dense_weights,
        dense_orthogonal,
        base,
        routed,
        grad,
    )
    return new.reshape(weights.shape), *rest


def on_device(
    hidden_in,
    cotangent,
    routes,
    route_weights,
    dense_weights,
    dense_momentum,
    expert_weights,
    expert_momentum,
    norm_gains,
    gain_first,
    gain_second,
):
    length, width = hidden_in.shape
    topk_count = routes.shape[1]
    local_experts = expert_weights.shape[0]
    expert_size = lax.axis_size("expert")
    dp_size = lax.axis_size("dp")
    expert_count = local_experts * expert_size
    capacity = 5 * length * topk_count // (4 * expert_count)
    block_rows = min(512, length)
    query_width = HEADS * HD
    kv_width = KVH * HD
    qkv_end = query_width + 2 * kv_width
    shared_base = 2 * query_width + 2 * kv_width
    gate_table = jnp.sum(
        jnp.where(
            routes.T[None, :, :] == jnp.arange(expert_count, dtype=jnp.int32)[:, None, None],
            route_weights.T[None, :, :],
            0.0,
        ),
        axis=1,
    )
    direct = dp_size == 8 and expert_size == 4
    inputs = hidden_in.astype(jnp.float32)
    scale_attend = norm_scale(inputs)
    if direct:
        stripe_rows = dense_weights.shape[0]
        extra = jnp.zeros((stripe_rows, 128 - norm_gains.shape[0]), jnp.float32)
        plane_gates = gate_table.reshape(expert_size, local_experts, length)
        (
            dense_all,
            _,
            _,
            _,
            routed_parts,
            grad_parts,
            *saved,
            normed_attend,
            projected,
            attended,
            residual,
            grad_shared,
            base_out,
            shared_sum,
            scale_mixer,
            gains_all,
        ) = front(
            jnp.concatenate(
                [
                    dense_weights[:, :shared_base],
                    norm_gains.T,
                    extra,
                    dense_weights[:, shared_base:],
                ],
                1,
            ).astype(jnp.bfloat16),
            jnp.pad(plane_gates, ((0, 0), (0, 8 - local_experts), (0, 0))),
            expert_weights.reshape(-1, *expert_weights.shape[2:]),
            hidden_in,
            cotangent,
            -(-capacity // 16) * 16,
        )
    else:
        gate_tables = lax.all_gather(gate_table, "expert", axis=0, tiled=False)
        cotangents = lax.all_gather(cotangent, "expert", axis=0, tiled=True)
        dense_all, gains_all = (
            lax.all_gather(
                dense_weights.astype(jnp.bfloat16), ("dp", "expert"), axis=0, tiled=True
            ),
            lax.all_gather(norm_gains.astype(jnp.bfloat16), ("dp", "expert"), axis=1, tiled=True),
        )
        gain_attend = gains_all[0].astype(jnp.float32)
        gain_mixer = gains_all[1].astype(jnp.float32)
        normed_attend = (inputs * scale_attend * gain_attend).astype(jnp.bfloat16)
        projected = jnp.dot(
            normed_attend, dense_all[:, :qkv_end], preferred_element_type=jnp.float32
        ).astype(jnp.bfloat16)
        query = projected[:, :query_width]
        key_rows = projected[:, query_width : query_width + kv_width]
        value_rows = projected[:, query_width + kv_width :]
        attended, saved_stats = attend_forward(query, key_rows, value_rows, block_rows)
        residual = inputs + jnp.einsum(
            "sq,dq->sd", attended, dense_all[:, qkv_end:shared_base], preferred_element_type=jnp.float32
        )
        scale_mixer = norm_scale(residual)
        normed_mixer = (residual * scale_mixer * gain_mixer).astype(jnp.bfloat16)
        expert_all = lax.all_gather(expert_weights.astype(jnp.bfloat16), "dp", axis=2, tiled=True)
        tokens = lax.all_gather(normed_mixer, "expert", axis=0, tiled=True)
        shared_pre = jnp.dot(
            normed_mixer,
            dense_all[:, shared_base : shared_base + 2 * FFS],
            preferred_element_type=jnp.float32,
        )
        shared_gate = shared_pre[:, :FFS]
        shared_up = shared_pre[:, FFS:]
        shared_act = (jax.nn.silu(shared_gate) * shared_up).astype(jnp.bfloat16)
        shared_out = jnp.einsum(
            "sf,df->sd",
            shared_act,
            dense_all[:, shared_base + 2 * FFS : shared_base + 3 * FFS],
            preferred_element_type=jnp.float32,
        )
        grad_shared_act = jnp.dot(
            cotangent,
            dense_all[:, shared_base + 2 * FFS : shared_base + 3 * FFS],
            preferred_element_type=jnp.float32,
        )
        shared_sig = jax.nn.sigmoid(shared_gate)
        grad_shared_pre = jnp.concatenate(
            [
                grad_shared_act * shared_up * shared_sig * (1.0 + shared_gate * (1.0 - shared_sig)),
                grad_shared_act * jax.nn.silu(shared_gate),
            ],
            1,
        ).astype(jnp.bfloat16)
        grad_shared = jnp.einsum(
            "sf,df->sd",
            grad_shared_pre,
            dense_all[:, shared_base : shared_base + 2 * FFS],
            preferred_element_type=jnp.float32,
        )
        base_out = residual + shared_out
        my_gates = lax.dynamic_slice_in_dim(
            gate_tables, lax.axis_index("expert") * local_experts, local_experts, 1
        ).transpose(1, 0, 2)
        hot = my_gates > 0.0
        earlier = jnp.einsum(
            "est,ut->esu",
            hot.astype(jnp.bfloat16),
            jnp.tril(jnp.ones((length, length), jnp.bfloat16), -1),
            preferred_element_type=jnp.float32,
        ).astype(jnp.int32)
        place = jnp.where(hot, earlier, -1)
        routed_parts, grad_parts, saved = grouped_experts(
            tokens, cotangents, place, my_gates, expert_all, capacity
        )
    if direct:
        expert_sum, dense_sum, grad_inputs, grad_gains = scatter_grads(
            grad_parts,
            saved,
            dense_all,
            shared_sum,
            cotangent,
            normed_attend,
            attended,
            residual,
            grad_shared,
            projected,
            hidden_in,
            scale_mixer,
            gains_all,
        )
        expert_grad, expert_moment, expert_units, dense_grad, dense_moment, dense_units = moments(
            expert_momentum, expert_sum, dense_momentum, dense_sum
        )
        orth_expert, orth_dense, routed = muon(expert_units, dense_units, routed_parts)
        expert_new, dense_new, block_out, grad_inputs = updated(
            expert_weights,
            orth_expert,
            dense_weights,
            orth_dense,
            base_out,
            routed,
            grad_inputs,
        )
    else:
        routed = lax.psum_scatter(routed_parts, "expert", scatter_dimension=0, tiled=True)
        grad_routed = lax.psum_scatter(grad_parts, "expert", scatter_dimension=0, tiled=True)
        expert_parts = [expert_grads(*kept) for kept in saved]
        expert_grad = lax.psum_scatter(
            sum(part.astype(jnp.float32) for part in expert_parts).astype(jnp.bfloat16),
            "dp",
            scatter_dimension=2,
            tiled=True,
        ).astype(jnp.float32)
        grad_normed = grad_routed.astype(jnp.float32) + grad_shared
        grad_scaled = grad_normed * gain_mixer
        grad_residual = (
            cotangent.astype(jnp.float32)
            + scale_mixer * grad_scaled
            - residual * scale_mixer**3 * jnp.mean(grad_scaled * residual, axis=-1, keepdims=True)
        )
        grad_gain_mixer = jnp.sum(grad_normed * residual * scale_mixer, axis=0)
        grad_attn_low = grad_residual.astype(jnp.bfloat16)
        grad_attended = jnp.dot(
            grad_attn_low, dense_all[:, qkv_end:shared_base], preferred_element_type=jnp.float32
        ).astype(jnp.bfloat16)
        grad_query, grad_key, grad_value = attend_backward(
            query, key_rows, value_rows, grad_attended, saved_stats, block_rows
        )
        grad_projected = jnp.concatenate([grad_query, grad_key, grad_value], 1)
        dense_parts = [
            jnp.einsum("sd,sf->df", left, right, preferred_element_type=jnp.float32)
            for left, right in (
                (normed_attend, grad_projected),
                (grad_attn_low, attended),
                (normed_mixer, grad_shared_pre),
                (cotangent, shared_act),
            )
        ]
        dense_grad = lax.psum_scatter(
            jnp.concatenate([part.astype(jnp.bfloat16) for part in dense_parts], 1),
            ("dp", "expert"),
            scatter_dimension=0,
            tiled=True,
        ).astype(jnp.float32)
        grad_normed_attend = jnp.einsum(
            "sc,dc->sd", grad_projected, dense_all[:, :qkv_end], preferred_element_type=jnp.float32
        )
        grad_scaled_attend = grad_normed_attend * gain_attend
        grad_inputs = (
            grad_residual
            + scale_attend * grad_scaled_attend
            - inputs * scale_attend**3 * jnp.mean(grad_scaled_attend * inputs, axis=-1, keepdims=True)
        )
        grad_gain_attend = jnp.sum(grad_normed_attend * inputs * scale_attend, axis=0)
        block_out = (base_out + routed.astype(jnp.float32)).astype(jnp.bfloat16)
        grad_gains = jnp.stack([grad_gain_attend, grad_gain_mixer], 0)
        dense_moment = MOMENTUM_DECAY * dense_momentum + dense_grad
        expert_moment = MOMENTUM_DECAY * expert_momentum + expert_grad
        stripe, dense_columns = dense_weights.shape
        row_count = stripe * expert_size
        dense_total = dense_columns // FFE
        dense_share = -(-dense_total // expert_size)
        dense_padded = jnp.pad(
            dense_moment.astype(jnp.bfloat16),
            ((0, 0), (0, dense_share * expert_size * FFE - dense_columns)),
        ).reshape(stripe, dense_share * expert_size, FFE).transpose(1, 0, 2)
        expert_units = expert_moment.astype(jnp.bfloat16).reshape(-1, row_count, FFE)
        dense_units = lax.all_to_all(
            dense_padded, "expert", split_axis=0, concat_axis=1, tiled=True
        )
        expert_unit_count = expert_units.shape[0]
        base_count = expert_unit_count + dense_share
        unit_count = -(-base_count // dp_size) * dp_size
        all_units = jnp.concatenate(
            [
                expert_units,
                dense_units,
                jnp.zeros((unit_count - base_count, row_count, FFE), jnp.bfloat16),
            ],
            0,
        )
        owned = lax.all_to_all(all_units, "dp", split_axis=0, concat_axis=1, tiled=True)
        orthogonal = newton_schulz(owned)
        orth_units = lax.all_to_all(orthogonal, "dp", split_axis=1, concat_axis=0, tiled=True)
        orth_expert = orth_units[:expert_unit_count]
        orth_stripe = lax.all_to_all(
            orth_units[expert_unit_count:base_count],
            "expert",
            split_axis=1,
            concat_axis=0,
            tiled=True,
        )
        orth_stripe = (
            orth_stripe[:dense_total]
            .transpose(1, 0, 2)
            .reshape(stripe, dense_columns)
            .astype(jnp.float32)
        )
        keep_factor = 1.0 - LEARN_RATE * WEIGHT_DECAY
        dense_new = keep_factor * dense_weights - LEARN_RATE * orth_stripe
        expert_new = keep_factor * expert_weights - LEARN_RATE * orth_expert.reshape(
            expert_weights.shape
        ).astype(jnp.float32)
    gain_columns = norm_gains.shape[1]
    gain_grad = lax.dynamic_slice_in_dim(
        lax.psum(grad_gains, ("dp", "expert")),
        lax.axis_index(("dp", "expert")) * gain_columns,
        gain_columns,
        1,
    )
    first_new = FIRST_DECAY * gain_first + (1.0 - FIRST_DECAY) * gain_grad
    second_new = SECOND_DECAY * gain_second + (1.0 - SECOND_DECAY) * gain_grad * gain_grad
    step_ratio = (
        first_new
        / (1.0 - FIRST_DECAY**STEP)
        / (jnp.sqrt(second_new / (1.0 - SECOND_DECAY**STEP)) + 1e-08)
    )
    gain_new = norm_gains - GAIN_RATE * step_ratio
    return (
        block_out,
        grad_inputs,
        dense_grad,
        dense_moment,
        dense_new,
        expert_grad,
        expert_moment,
        expert_new,
        gain_grad,
        first_new,
        second_new,
        gain_new,
    )


def solution(mesh):
    in_specs = (
        P(("dp", "expert"), None),
        P(("dp", "expert"), None),
        P(("dp", "expert"), None),
        P(("dp", "expert"), None),
        P(("dp", "expert"), None),
        P(("dp", "expert"), None),
        P("expert", None, "dp", None),
        P("expert", None, "dp", None),
        P(None, ("dp", "expert")),
        P(None, ("dp", "expert")),
        P(None, ("dp", "expert")),
    )
    out_specs = (
        P(("dp", "expert"), None),
        P(("dp", "expert"), None),
        P(("dp", "expert"), None),
        P(("dp", "expert"), None),
        P(("dp", "expert"), None),
        P("expert", None, "dp", None),
        P("expert", None, "dp", None),
        P("expert", None, "dp", None),
        P(None, ("dp", "expert")),
        P(None, ("dp", "expert")),
        P(None, ("dp", "expert")),
        P(None, ("dp", "expert")),
    )
    return jax.shard_map(
        on_device, mesh=mesh, in_specs=in_specs, out_specs=out_specs, check_vma=False
    )
```

```python
import functools

import jax
import jax.numpy as jnp
from jax import lax
from jax.experimental import pallas as pl
from jax.experimental.pallas import tpu as pltpu
from jax.sharding import PartitionSpec as P

HEADS = 12
HD = 128
KVH = 4
FFE = 512
FFS = 1024
NS_STEPS = 5
STEP = 10


POLY_FIRST = 3.4445
POLY_SECOND = -4.775
POLY_THIRD = 2.0315
MOMENTUM_DECAY = 0.95
LEARN_RATE = 0.6
WEIGHT_DECAY = 0.1
GAIN_RATE = 0.8
FIRST_DECAY = 0.9
SECOND_DECAY = 0.95


def norm_scale(values):
    return lax.rsqrt(jnp.mean(values * values, axis=-1, keepdims=True) + 1e-06)


def block_scores(query_block, key_block, first_row, block_rows, last_row):
    score_scale = HD ** (-0.5)
    scores = (
        jnp.einsum("qgrd,kgd->grqk", query_block, key_block, preferred_element_type=jnp.float32)
        * score_scale
    )
    allowed = jnp.arange(last_row)[None, :] <= (first_row + jnp.arange(block_rows))[:, None]
    return jnp.where(allowed, scores, -1e30)


def attend_forward(query, key_rows, value_rows, block_rows):
    length = query.shape[0]
    query_heads = query.reshape(length, KVH, HEADS // KVH, HD)
    key_heads = key_rows.reshape(length, KVH, HD)
    value_heads = value_rows.reshape(length, KVH, HD)
    scores = block_scores(query_heads, key_heads, 0, block_rows, block_rows)
    highest = jnp.max(scores, axis=-1, keepdims=True)
    raised = jnp.exp(scores - highest)
    totals = jnp.sum(raised, axis=-1, keepdims=True)
    weights = (raised / totals).astype(jnp.bfloat16)
    outputs = jnp.einsum("grqk,kgd->qgrd", weights, value_heads, preferred_element_type=jnp.float32)
    saved_stats = [(highest, totals)]
    attended = outputs.reshape(length, HEADS * HD)
    return (attended.astype(jnp.bfloat16), saved_stats)


def attend_backward(query, key_rows, value_rows, grad_attended, saved_stats, block_rows):
    length = query.shape[0]
    score_scale = HD ** (-0.5)
    query_heads = query.reshape(length, KVH, HEADS // KVH, HD)
    grad_heads = grad_attended.reshape(length, KVH, HEADS // KVH, HD)
    key_heads = key_rows.reshape(length, KVH, HD)
    value_heads = value_rows.reshape(length, KVH, HD)
    grad_key = jnp.zeros((length, KVH, HD), jnp.float32)
    grad_value = jnp.zeros((length, KVH, HD), jnp.float32)
    query_parts = []
    for block_index, first_row in enumerate(range(0, length, block_rows)):
        last_row = first_row + block_rows
        scores = block_scores(query_heads, key_heads, first_row, block_rows, last_row)
        highest, totals = saved_stats[block_index]
        weights = jnp.exp(scores - highest) / totals
        grad_weights = jnp.einsum(
            "qgrd,kgd->grqk", grad_heads, value_heads, preferred_element_type=jnp.float32
        )
        inner_sum = jnp.sum(weights * grad_weights, axis=-1, keepdims=True)
        grad_scores = (weights * (grad_weights - inner_sum)).astype(jnp.bfloat16)
        query_parts.append(
            jnp.einsum("grqk,kgd->qgrd", grad_scores, key_heads, preferred_element_type=jnp.float32)
            * score_scale
        )
        grad_key = grad_key.at[:last_row].add(
            jnp.einsum(
                "grqk,qgrd->kgd", grad_scores, query_heads, preferred_element_type=jnp.float32
            )
            * score_scale
        )
        grad_value = grad_value.at[:last_row].add(
            jnp.einsum(
                "grqk,qgrd->kgd",
                weights.astype(jnp.bfloat16),
                grad_heads,
                preferred_element_type=jnp.float32,
            )
        )
    grad_query = query_parts[0].reshape(length, HEADS * HD)
    return (
        grad_query.astype(jnp.bfloat16),
        grad_key.reshape(length, KVH * HD).astype(jnp.bfloat16),
        grad_value.reshape(length, KVH * HD).astype(jnp.bfloat16),
    )


MIB = 2**20
GRAD_STEP = 14
SLOTS = 8
MESH = pl.DeviceIdType.MESH


def matmul(left, right):
    return jnp.dot(left, right, preferred_element_type=jnp.float32)


def matmul_nt(left, right):
    return lax.dot_general(left, right, (((1,), (1,)), ((), ())), preferred_element_type=jnp.float32)


def matmul_tn(left, right):
    return lax.dot_general(left, right, (((0,), (0,)), ((), ())), preferred_element_type=jnp.float32)


def newton_schulz_unit(moment_ref, orthogonal_ref, current, low, identity):
    columns, rows = current.shape
    step = 256
    parts = [pl.ds(index * step, step) for index in range(rows // step)]
    identity[...] = jnp.where(
        lax.broadcasted_iota(jnp.int32, identity.shape, 0)
        == lax.broadcasted_iota(jnp.int32, identity.shape, 1),
        1.0,
        0.0,
    ).astype(jnp.bfloat16)
    squares = jnp.zeros((1, columns), jnp.float32)
    for part in parts:
        values = moment_ref[part, :].astype(jnp.float32)
        squares = squares + jnp.sum(values * values, axis=0, keepdims=True)
    scale = 1.0 / (jnp.sqrt(jnp.sum(squares, axis=1, keepdims=True)) + 1e-07)
    for part in parts:
        scaled = matmul_nt(identity[...], moment_ref[part, :]) * scale
        current[:, part] = scaled
        low[:, part] = scaled.astype(jnp.bfloat16)

    def polynomial():
        gram = matmul_nt(low[...], low[...])
        gram_low = gram.astype(jnp.bfloat16)
        return (POLY_SECOND * gram + POLY_THIRD * matmul(gram_low, gram_low)).astype(jnp.bfloat16)

    @pl.loop(0, NS_STEPS - 1)
    def _(index):
        weights = polynomial()
        for part in parts:
            updated = POLY_FIRST * current[:, part] + matmul(weights, low[:, part])
            current[:, part] = updated
            low[:, part] = updated.astype(jnp.bfloat16)

    weights = polynomial()
    for part in parts:
        updated = POLY_FIRST * current[:, part] + matmul(weights, low[:, part])
        orthogonal_ref[part, :] = updated.T.astype(jnp.bfloat16)


def newton_schulz_kernel(moment_ref, orthogonal_ref, current, low, identity):
    newton_schulz_unit(moment_ref.at[0], orthogonal_ref.at[0], current, low, identity)


def newton_schulz(units):
    count, rows, columns = units.shape
    return pl.pallas_call(
        newton_schulz_kernel,
        grid=(count,),
        in_specs=[pl.BlockSpec((1, rows, columns), lambda unit: (unit, 0, 0))],
        out_specs=pl.BlockSpec((1, rows, columns), lambda unit: (unit, 0, 0)),
        out_shape=jax.ShapeDtypeStruct(units.shape, jnp.bfloat16),
        scratch_shapes=[
            pltpu.VMEM((columns, rows), jnp.float32),
            pltpu.VMEM((columns, rows), jnp.bfloat16),
            pltpu.VMEM((columns, columns), jnp.bfloat16),
        ],
        compiler_params=pltpu.CompilerParams(vmem_limit_bytes=48 * MIB),
        cost_estimate=pl.CostEstimate(
            flops=count * NS_STEPS * 2 * columns * columns * (2 * rows + columns),
            bytes_accessed=count * rows * columns * 4,
            transcendentals=0,
        ),
        name="newton_schulz",
    )(units)


def experts_kernel(
    tokens_ref,
    cotangent_ref,
    place_ref,
    gate_ref,
    weights_ref,
    routed_ref,
    grad_tokens_ref,
    received,
    grad_returned,
    act_ref,
    grad_gate_ref,
    grad_up_ref,
    routed_sum,
    grad_sum,
    chosen,
    weighted,
    grad_received,
):
    expert = pl.program_id(0)
    sequences, slots, length = chosen.shape

    @pl.when(expert == 0)
    def _():
        routed_sum[...] = jnp.zeros_like(routed_sum)
        grad_sum[...] = jnp.zeros_like(grad_sum)

    slot_weights = []
    for sequence in range(sequences):
        rows = pl.ds(sequence * length, length)
        spots = pl.ds(sequence * slots, slots)
        place = place_ref[0, sequence : sequence + 1, :]
        gate = gate_ref[0, sequence : sequence + 1, :]
        hot = lax.broadcasted_iota(jnp.int32, (slots, length), 0) == place
        slot_weight = jnp.sum(jnp.where(hot, gate, 0.0), axis=1, keepdims=True)
        slot_weights.append(slot_weight)
        hot_low = jnp.where(hot, 1.0, 0.0).astype(jnp.bfloat16)
        chosen[sequence] = hot_low
        received[0, spots, :] = matmul(hot_low, tokens_ref[rows, :]).astype(jnp.bfloat16)
        grad_returned[0, spots, :] = (
            matmul(hot_low, cotangent_ref[rows, :]) * slot_weight
        ).astype(jnp.bfloat16)
    tokens = received[0]
    grad_out = grad_returned[0]
    gate_pre = matmul(tokens, weights_ref[0, 0])
    up_pre = matmul(tokens, weights_ref[0, 1])
    gate_sig = jax.nn.sigmoid(gate_pre)
    gate_act = gate_pre * gate_sig
    act = (gate_act * up_pre).astype(jnp.bfloat16)
    act_ref[0] = act
    out = matmul_nt(act, weights_ref[0, 2]).astype(jnp.bfloat16).astype(jnp.float32)
    for sequence in range(sequences):
        spots = slice(sequence * slots, (sequence + 1) * slots)
        weighted[spots, :] = (out[spots] * slot_weights[sequence]).astype(jnp.bfloat16)
    grad_act = matmul(grad_out, weights_ref[0, 2])
    grad_gate = (grad_act * up_pre * gate_sig * (1.0 + gate_pre * (1.0 - gate_sig))).astype(
        jnp.bfloat16
    )
    grad_up = (grad_act * gate_act).astype(jnp.bfloat16)
    grad_gate_ref[0] = grad_gate
    grad_up_ref[0] = grad_up
    grad_received[...] = (
        matmul_nt(grad_gate, weights_ref[0, 0]) + matmul_nt(grad_up, weights_ref[0, 1])
    ).astype(jnp.bfloat16)
    for sequence in range(sequences):
        rows = pl.ds(sequence * length, length)
        spots = pl.ds(sequence * slots, slots)
        routed_sum[rows, :] += matmul_tn(chosen[sequence], weighted[spots, :])
        grad_sum[rows, :] += matmul_tn(chosen[sequence], grad_received[spots, :])

    @pl.when(expert == pl.num_programs(0) - 1)
    def _():
        routed_ref[...] = routed_sum[...].astype(jnp.bfloat16)
        grad_tokens_ref[...] = grad_sum[...].astype(jnp.bfloat16)


def run_experts(tokens, cotangents, place, gates, weights, capacity):
    experts, sequences, length = place.shape
    total, width = tokens.shape
    hidden = weights.shape[-1]
    slots = -(-capacity // 16) * 16
    spots = sequences * slots
    whole = pl.BlockSpec((total, width), lambda expert: (0, 0))
    table = pl.BlockSpec((1, sequences, length), lambda expert: (expert, 0, 0))
    matrices = pl.BlockSpec((1, 3, width, hidden), lambda expert: (expert, 0, 0, 0))
    wide = pl.BlockSpec((1, spots, width), lambda expert: (expert, 0, 0))
    narrow = pl.BlockSpec((1, spots, hidden), lambda expert: (expert, 0, 0))
    return pl.pallas_call(
        experts_kernel,
        grid=(experts,),
        in_specs=[whole, whole, table, table, matrices],
        out_specs=[whole, whole, wide, wide, narrow, narrow, narrow],
        out_shape=[
            *[jax.ShapeDtypeStruct((total, width), jnp.bfloat16)] * 2,
            *[jax.ShapeDtypeStruct((experts, spots, width), jnp.bfloat16)] * 2,
            *[jax.ShapeDtypeStruct((experts, spots, hidden), jnp.bfloat16)] * 3,
        ],
        scratch_shapes=[
            pltpu.VMEM((total, width), jnp.float32),
            pltpu.VMEM((total, width), jnp.float32),
            pltpu.VMEM((sequences, slots, length), jnp.bfloat16),
            pltpu.VMEM((spots, width), jnp.bfloat16),
            pltpu.VMEM((spots, width), jnp.bfloat16),
        ],
        compiler_params=pltpu.CompilerParams(vmem_limit_bytes=63 * MIB),
        cost_estimate=pl.CostEstimate(
            flops=experts * (12 * spots * width * hidden + 8 * spots * length * width),
            bytes_accessed=2 * weights.size + 16 * tokens.size,
            transcendentals=experts * spots * hidden,
        ),
        name="experts",
    )(tokens, cotangents, place, gates, weights)


def expert_grads_kernel(
    received_ref, grad_returned_ref, act_ref, grad_gate_ref, grad_up_ref, grad_weights_ref
):
    received, grad_returned = received_ref[0], grad_returned_ref[0]
    grad_weights_ref[0, 0] = matmul_tn(received, grad_gate_ref[0]).astype(jnp.bfloat16)
    grad_weights_ref[0, 1] = matmul_tn(received, grad_up_ref[0]).astype(jnp.bfloat16)
    grad_weights_ref[0, 2] = matmul_tn(grad_returned, act_ref[0]).astype(jnp.bfloat16)


def expert_grads(received, grad_returned, act, grad_gate, grad_up):
    experts, spots, width = received.shape
    hidden = act.shape[-1]
    wide = pl.BlockSpec((1, spots, width), lambda expert: (expert, 0, 0))
    narrow = pl.BlockSpec((1, spots, hidden), lambda expert: (expert, 0, 0))
    return pl.pallas_call(
        expert_grads_kernel,
        grid=(experts,),
        in_specs=[wide, wide, narrow, narrow, narrow],
        out_specs=pl.BlockSpec((1, 3, width, hidden), lambda expert: (expert, 0, 0, 0)),
        out_shape=jax.ShapeDtypeStruct((experts, 3, width, hidden), jnp.bfloat16),
        compiler_params=pltpu.CompilerParams(vmem_limit_bytes=48 * MIB),
        name="expert_grads",
    )(received, grad_returned, act, grad_gate, grad_up)


def grouped_experts(tokens, cotangents, place, gates, weights, capacity):
    experts, sequences, length = place.shape
    group = min(4, sequences)
    routed, grad_tokens, saved = [], [], []
    for first in range(0, sequences, group):
        rows = slice(first * length, (first + group) * length)
        part = slice(first, first + group)
        routed_part, grad_part, *kept = run_experts(
            tokens[rows], cotangents[rows], place[:, part], gates[:, part], weights, capacity
        )
        routed.append(routed_part)
        grad_tokens.append(grad_part)
        saved.append(kept)

    def joined(parts):
        return parts[0] if len(parts) == 1 else jnp.concatenate(parts, 0)

    return joined(routed), joined(grad_tokens), saved


def flipped(index, bit):
    unit = 2**bit
    return index + unit * (1 - 2 * ((index // unit) % 2))


class Links:
    def __init__(self, semaphores):
        self.semaphores = semaphores
        self.taken = 0
        self.dp = lax.axis_index("dp")
        self.z = lax.axis_index("expert")
        self.upper = self.z // 2
        self.position = self.z * (1 - 2 * self.upper) + 3 * self.upper
        self.step = 1 - 2 * self.upper
        self.core = (flipped(self.dp, 0), self.z)
        self.along_x = (flipped(self.dp, 1), self.z)
        self.along_y = (flipped(self.dp, 2), self.z)
        self.inward = (self.dp, self.z + self.step)
        self.outward = (self.dp, self.z - self.step)
        self.further = (self.dp, self.z + 2 * self.step)
        self.pending = []

    def order(self, index):
        near = (self.position + index) % 2 if index < 2 else index
        return near * self.step + 3 * self.upper

    def take(self, count=1):
        first = self.taken
        self.taken += count
        return first

    def barrier(self):
        barrier = pltpu.get_barrier_semaphore()
        for device in (self.core, self.along_x, self.along_y, self.inward, self.further):
            pl.semaphore_signal(barrier, inc=1, device_id=device, device_id_type=MESH)

        @pl.when(self.position == 1)
        def _():
            pl.semaphore_signal(barrier, inc=1, device_id=self.outward, device_id_type=MESH)

        pl.semaphore_wait(barrier, 5 + self.position)

    def copy_with(self, source, target, send, receive, device):
        return pltpu.make_async_remote_copy(
            src_ref=source,
            dst_ref=target,
            send_sem=send,
            recv_sem=receive,
            device_id=device,
            device_id_type=MESH,
        )

    def copy(self, source, target, send, receive, device):
        return self.copy_with(
            source, target, self.semaphores.at[send], self.semaphores.at[receive], device
        )

    def send(self, source, target, receive, device, position=None):
        copy = self.copy(source, target, self.take(), receive, device)
        if position is None:
            copy.start()
        else:
            pl.when(self.position == position)(copy.start)
        self.pending.append((copy, position))

    def arrived(self, region, receive):
        self.copy(region, region, receive, receive, self.core).wait_recv()

    def finish(self):
        for copy, position in self.pending:
            if position is None:
                copy.wait_send()
            else:
                pl.when(self.position == position)(copy.wait_send)


class LineGather:
    def __init__(self, links, region, own=None):
        self.links, self.region = links, region
        self.receives = links.take(4)
        self.own = region(links.z) if own is None else own

    def start(self):
        links = self.links
        target, receive = self.region(links.z), self.receives + links.z
        links.send(self.own, target, receive, links.further)
        links.send(self.own, target, receive, links.inward)
        links.send(self.own, target, receive, links.outward, 1)

    def relay(self):
        links = self.links
        source = links.order(3)
        block = self.region(source)

        @pl.when(links.position == 1)
        def _():
            links.arrived(block, self.receives + source)

        links.send(block, block, self.receives + source, links.outward, 1)

    def arrive(self, index):
        links = self.links
        source = links.order(index)

        def wait():
            links.arrived(self.region(source), self.receives + source)

        if index < 3:
            wait()
        else:
            pl.when(links.position == 0)(wait)


class PlaneGather:
    def __init__(self, links, region, parity, own=None):
        self.links, self.region, self.parity = links, region, parity
        self.receives = links.take(7)
        self.own = region(links.dp) if own is None else own

    def start(self):
        links, first = self.links, self.receives
        target = self.region(links.dp)
        links.send(self.own, target, first, links.along_x)
        links.send(self.own, target, first + 1, links.along_y)
        links.send(self.own, target, first + 2, links.core)

    def forward(self):
        links, first = self.links, self.receives
        across = self.region(flipped(links.dp, 1))
        links.arrived(across, first)
        if self.parity == 0:
            links.send(across, across, first + 3, links.along_y)
        links.send(across, across, first + 4, links.core)
        along = self.region(flipped(links.dp, 2))
        links.arrived(along, first + 1)
        if self.parity == 1:
            links.send(along, along, first + 3, links.along_x)
        links.send(along, along, first + 5, links.core)

    def last(self):
        links, first = self.links, self.receives
        corner = self.region(flipped(flipped(links.dp, 1), 2))
        links.arrived(corner, first + 3)
        links.send(corner, corner, first + 6, links.core)

    def complete(self):
        links, first = self.links, self.receives
        other = flipped(links.dp, 0)
        links.arrived(self.region(other), first + 2)
        links.arrived(self.region(flipped(other, 1)), first + 4)
        links.arrived(self.region(flipped(other, 2)), first + 5)
        links.arrived(self.region(flipped(flipped(other, 1), 2)), first + 6)


ANY = pl.BlockSpec(memory_space=pl.ANY)


def front_kernel(
    stripe_ref,
    gates_ref,
    masters_ref,
    hidden_ref,
    cotangent_ref,
    dense_ref,
    weights_ref,
    cotangents_ref,
    tokens_ref,
    routed_parts_ref,
    grad_parts_ref,
    received_ref,
    grad_returned_ref,
    act_ref,
    grad_gate_ref,
    grad_up_ref,
    normed_attend_out,
    projected_out,
    attended_out,
    residual_out,
    grad_shared_out,
    base_out,
    shared_sum_ref,
    scale_ref,
    gains_ref,
    normed_attend_ref,
    projected_ref,
    attended_ref,
    residual_ref,
    grad_shared_ref,
    base_ref,
    normed_mixer_ref,
    shared_act_ref,
    grad_shared_pre_ref,
    matrices,
    extra,
    all_gates,
    places,
    my_gates,
    chosen,
    forward_slots,
    backward_slots,
    narrow,
    pair_sum,
    corner_x,
    corner_y,
    side_x,
    side_y,
    semaphores,
    shard_out,
    shard_in,
    local,
    load_sems,
    expert_sems,
    shared_sems,
    keep_sems,
):
    links = Links(semaphores)
    stripe, columns = stripe_ref.shape
    length, width = hidden_ref.shape
    panels, rows, hidden = masters_ref.shape
    experts = panels // 3
    slots = chosen.shape[1] // experts
    first_panels = 8
    middle = first_panels * hidden + extra.shape[1]
    halves = ((0, middle), (middle, columns - middle))
    query_width = HEADS * HD
    kv_width = KVH * HD
    ahead = 4

    def dense_region(dp, z, half):
        first, count = halves[half]
        row = pl.multiple_of((dp * 4 + z) * stripe, stripe)
        return dense_ref.at[pl.ds(row, stripe), pl.ds(first, count)]

    def own(half):
        first, count = halves[half]
        return stripe_ref.at[:, pl.ds(first, count)]

    def sequence(ref, z):
        return ref.at[pl.ds(pl.multiple_of(z * length, length), length), :]

    def shard_region(dp, panel):
        return weights_ref.at[panel, pl.ds(pl.multiple_of(dp * rows, rows), rows), :]

    lines = [
        LineGather(links, functools.partial(dense_region, links.dp, half=half), own(half))
        for half in range(2)
    ]
    cotangents = LineGather(links, functools.partial(sequence, cotangents_ref), cotangent_ref)
    tokens = LineGather(links, functools.partial(sequence, tokens_ref), normed_mixer_ref)
    gates = LineGather(links, lambda z: all_gates.at[z], gates_ref)
    planes = [
        [
            PlaneGather(
                links,
                functools.partial(dense_region, z=links.order(index), half=half),
                index % 2,
                own(half) if index == 0 else None,
            )
            for index in range(4)
        ]
        for half in range(2)
    ]

    def shard_copy(kind, panel, source_dp, device):
        block = shard_region(source_dp, panel)
        return links.copy_with(
            block, block, shard_out.at[kind, panel], shard_in.at[kind, panel], device
        )

    dp = links.dp
    dp_core, dp_x, dp_y = flipped(dp, 0), flipped(dp, 1), flipped(dp, 2)
    dp_corner = flipped(dp_x, 2)

    def hop(kind, panel):
        source, device = (
            (dp, links.along_x),
            (dp, links.along_y),
            (dp, links.core),
            None,
            (dp_x, links.core),
            (dp_y, links.core),
            (dp_corner, links.core),
        )[kind]
        return shard_copy(kind, panel, source, device)

    def corner_copy(panel, parity):
        if parity == 0:
            return shard_copy(3, panel, dp_x, links.along_y)
        return shard_copy(3, panel, dp_y, links.along_x)

    def shard_arrived(kind, panel, source_dp):
        shard_copy(kind, panel, source_dp, links.core).wait_recv()

    def shard_start(panel):
        for kind in range(3):
            hop(kind, panel).start()

    def shard_forward(panel):
        shard_arrived(0, panel, dp_x)
        pl.when(panel % 2 == 0)(corner_copy(panel, 0).start)
        hop(4, panel).start()
        shard_arrived(1, panel, dp_y)
        pl.when(panel % 2 == 1)(corner_copy(panel, 1).start)
        hop(5, panel).start()

    def shard_last(panel):
        shard_arrived(3, panel, dp_corner)
        hop(6, panel).start()

    def shard_complete(panel):
        shard_arrived(2, panel, dp_core)
        shard_arrived(4, panel, flipped(dp_core, 1))
        shard_arrived(5, panel, flipped(dp_core, 2))
        shard_arrived(6, panel, flipped(flipped(dp_core, 1), 2))

    def shard_finish(panel):
        for kind in (0, 1, 2, 4, 5, 6):
            hop(kind, panel).wait_send()
        corner_copy(panel, 0).wait_send()

    def exchange(panel):
        shard_forward(panel)
        if panel + ahead < panels:
            shard_start(panel + ahead)
        if panel >= 3:
            shard_last(panel - 3)

    local_copies = [
        pltpu.make_async_copy(source, target, local.at[index])
        for index, (source, target) in enumerate(
            (
                (
                    stripe_ref,
                    dense_ref.at[
                        pl.ds(pl.multiple_of((links.dp * 4 + links.z) * stripe, stripe), stripe), :
                    ],
                ),
                (gates_ref, all_gates.at[links.z]),
                (cotangent_ref, sequence(cotangents_ref, links.z)),
            )
        )
    ]
    token_copy = pltpu.make_async_copy(
        normed_mixer_ref, sequence(tokens_ref, links.z), local.at[3]
    )

    def dense_column(panel):
        return panel * hidden + (0 if panel < first_panels else extra.shape[1])

    loads = [
        pltpu.make_async_copy(
            dense_ref.at[:, pl.ds(dense_column(panel), hidden)],
            matrices.at[panel],
            load_sems.at[panel],
        )
        for panel in range(14)
    ]
    extra_load = pltpu.make_async_copy(
        dense_ref.at[:, pl.ds(first_panels * hidden, extra.shape[1])], extra, load_sems.at[14]
    )

    def half_columns(panel):
        return pl.ds(pl.multiple_of(panel % 2 * hidden, hidden), hidden)

    def master_load(panel):
        return pltpu.make_async_copy(
            masters_ref.at[panel],
            grad_shared_ref.at[pl.ds(0, rows), half_columns(panel)],
            expert_sems.at[0, panel % 2],
        )

    def master_store(panel):
        return pltpu.make_async_copy(
            shared_act_ref.at[pl.ds(0, rows), half_columns(panel)],
            shard_region(dp, panel),
            expert_sems.at[1, panel % 2],
        )

    master_load(0).start()
    links.barrier()
    lines[0].start()
    planes[0][0].start()
    lines[1].start()
    gates.start()
    for copy in local_copies:
        copy.start()

    def round_masters(first, last):
        @pl.loop(first, last)
        def _(panel):
            master_load(panel).wait()

            @pl.when(panel + 1 < panels)
            def _():
                master_load(panel + 1).start()

            @pl.when(panel >= 2)
            def _():
                master_store(panel - 2).wait()

            shared_act_ref[:rows, half_columns(panel)] = grad_shared_ref[
                :rows, half_columns(panel)
            ].astype(jnp.bfloat16)
            master_store(panel).start()

    lines[0].arrive(1)
    planes[0][1].start()
    lines[0].arrive(2)
    planes[0][2].start()
    round_masters(0, panels // 3)
    for panel in range(2):
        shard_start(panel)
    planes[0][0].forward()
    lines[0].relay()
    lines[0].arrive(3)
    planes[0][3].start()
    planes[0][1].forward()
    lines[1].relay()
    round_masters(panels // 3, panels)
    for panel in (panels - 2, panels - 1):
        master_store(panel).wait()
    for panel in range(2, ahead):
        shard_start(panel)
    planes[1][0].start()
    planes[0][2].forward()
    lines[1].arrive(1)
    planes[1][1].start()
    planes[0][3].forward()
    cotangents.start()
    gates.relay()
    lines[1].arrive(2)
    planes[1][2].start()
    for plane in planes[0]:
        plane.last()
    planes[1][0].forward()
    for plane in planes[0]:
        plane.complete()
    local_copies[0].wait()
    extra_load.start()
    for copy in loads[:first_panels]:
        copy.start()

    rows_step = 32

    def norm_rows(source, gain, scale_out, target):
        @pl.loop(0, length // rows_step)
        def _(index):
            part = pl.ds(index * rows_step, rows_step)
            values = source[part, :].astype(jnp.float32)
            scale = lax.rsqrt(jnp.mean(values * values, axis=-1, keepdims=True) + 1e-06)
            if scale_out is not None:
                scale_out[part, :] = scale
            target[part, :] = (values * scale * gains_ref[gain : gain + 1, :]).astype(jnp.bfloat16)

    def project():
        extra_load.wait()
        gains_ref[...] = extra[...].astype(jnp.float32).T[:8, :]
        norm_rows(hidden_ref, 0, None, normed_attend_ref)
        for panel in range(5):
            loads[panel].wait()
            projected_ref[:, panel * hidden : (panel + 1) * hidden] = matmul(
                normed_attend_ref[...], matrices[panel]
            ).astype(jnp.bfloat16)

    def attend(group):
        key_rows = projected_ref[:, query_width + group * HD : query_width + (group + 1) * HD]
        value_first = query_width + kv_width + group * HD
        value_rows = projected_ref[:, value_first : value_first + HD]
        row = lax.broadcasted_iota(jnp.int32, (length, length), 0)
        column = lax.broadcasted_iota(jnp.int32, (length, length), 1)
        per_group = HEADS // KVH
        for head in range(group * per_group, (group + 1) * per_group):
            spot = slice(head * HD, (head + 1) * HD)
            scores = matmul_nt(projected_ref[:, spot], key_rows) * HD ** (-0.5)
            scores = jnp.where(column <= row, scores, -1e30)
            raised = jnp.exp(scores - jnp.max(scores, axis=-1, keepdims=True))
            shares = (raised / jnp.sum(raised, axis=-1, keepdims=True)).astype(jnp.bfloat16)
            attended_ref[:, spot] = matmul(shares, value_rows).astype(jnp.bfloat16)

    def join():
        for part in range(3):
            loads[5 + part].wait()
            update = matmul_nt(
                attended_ref[:, part * hidden : (part + 1) * hidden], matrices[5 + part]
            )
            if part == 0:
                residual_ref[...] = hidden_ref[...].astype(jnp.float32) + update
            else:
                residual_ref[...] += update
        norm_rows(residual_ref, 1, scale_ref, normed_mixer_ref)
        tokens.start()
        token_copy.start()

    def shared(part):
        spot = slice(part * hidden, (part + 1) * hidden)
        for panel in (8, 10, 12):
            loads[panel + part].wait()
        gate = matmul(normed_mixer_ref[...], matrices[8 + part])
        up = matmul(normed_mixer_ref[...], matrices[10 + part])
        sig = jax.nn.sigmoid(gate)
        gate_act = gate * sig
        shared_act_ref[:, spot] = (gate_act * up).astype(jnp.bfloat16)
        grad_act = matmul(cotangent_ref[...], matrices[12 + part])
        grad_shared_pre_ref[:, spot] = (
            grad_act * up * sig * (1.0 + gate * (1.0 - sig))
        ).astype(jnp.bfloat16)
        up_spot = slice((2 + part) * hidden, (3 + part) * hidden)
        grad_shared_pre_ref[:, up_spot] = (grad_act * gate_act).astype(jnp.bfloat16)

    def shared_back(part):
        spot = slice(part * hidden, (part + 1) * hidden)
        up_spot = slice((2 + part) * hidden, (3 + part) * hidden)
        grad = matmul_nt(grad_shared_pre_ref[:, spot], matrices[8 + part]) + matmul_nt(
            grad_shared_pre_ref[:, up_spot], matrices[10 + part]
        )
        out = matmul_nt(shared_act_ref[:, spot], matrices[12 + part])
        if part == 0:
            grad_shared_ref[...] = grad
            base_ref[...] = residual_ref[...] + out
        else:
            grad_shared_ref[...] += grad
            base_ref[...] += out

    kept = [
        pltpu.make_async_copy(source, target, keep_sems.at[index])
        for index, (source, target) in enumerate(
            (
                (normed_attend_ref, normed_attend_out),
                (projected_ref, projected_out),
                (attended_ref, attended_out),
                (residual_ref, residual_out),
                (grad_shared_ref, grad_shared_out),
                (base_ref, base_out),
            )
        )
    ]

    def place_slots():
        local_copies[1].wait()
        before = (
            lax.broadcasted_iota(jnp.int32, (length, length), 0)
            < lax.broadcasted_iota(jnp.int32, (length, length), 1)
        )
        earlier_mask = jnp.where(before, 1.0, 0.0).astype(jnp.bfloat16)
        for source in range(4):
            gate = all_gates[source, links.z]
            hot = gate > 0.0
            earlier = matmul(jnp.where(hot, 1.0, 0.0).astype(jnp.bfloat16), earlier_mask)
            place = jnp.where(hot, earlier, -1.0).astype(jnp.int32)
            for expert in range(experts):
                places[expert, source : source + 1, :] = place[expert : expert + 1, :]
                my_gates[expert, source : source + 1, :] = gate[expert : expert + 1, :]

    core, chip = dp % 2, dp // 2
    chip_x, chip_y = flipped(chip, 0), flipped(chip, 1)
    chip_corner = flipped(chip_x, 1)
    shared_panels = pair_sum.shape[0]
    half = rows // 2
    quarter = width // 4

    ring = matrices.at[13]

    def ring_rows(index, which):
        return pl.ds(pl.multiple_of((2 * index + which) * rows, rows), rows)

    def pair_copy(panel, index):
        return links.copy_with(
            ring.at[ring_rows(index, 1 - core)],
            pair_sum.at[panel, index],
            shared_sems.at[0, 0, panel],
            shared_sems.at[1, 0, panel],
            links.core,
        )

    def shared_copy(kind, panel):
        source, target, device = (
            (pair_sum.at[panel], pair_sum.at[panel], links.core),
            (pair_sum.at[panel, chip_corner, pl.ds(0, half)], corner_x.at[panel], links.along_x),
            (pair_sum.at[panel, chip_corner, pl.ds(half, half)], corner_y.at[panel], links.along_y),
            (pair_sum.at[panel, chip_x], side_x.at[panel], links.along_x),
            (pair_sum.at[panel, chip_y], side_y.at[panel], links.along_y),
        )[kind]
        return links.copy_with(
            source, target, shared_sems.at[0, kind, panel], shared_sems.at[1, kind, panel], device
        )

    def shared_fill(panel):
        left_ref = normed_mixer_ref if panel < 4 else cotangent_ref
        right_ref = grad_shared_pre_ref if panel < 4 else shared_act_ref
        first = (panel if panel < 4 else panel - 4) * hidden
        right = right_ref[:, first : first + hidden]
        for index in range(4):
            part = matmul_tn(left_ref[:, index * quarter : (index + 1) * quarter], right)
            ring[index * quarter : (index + 1) * quarter, :] = part.astype(jnp.bfloat16)
        for index in range(4):
            pair_copy(panel, index).start()

    def shared_pair(panel):
        shared_copy(0, panel).wait()
        for index in range(4):
            pair_sum[panel, index] = (
                pair_sum[panel, index].astype(jnp.float32)
                + ring[ring_rows(index, core), :].astype(jnp.float32)
            ).astype(jnp.bfloat16)

    def shared_corners(panel):
        for kind in (1, 2):
            shared_copy(kind, panel).start()

    def shared_sides(panel):
        for kind in (1, 2):
            shared_copy(kind, panel).wait()
        pair_sum[panel, chip_y, :half] = (
            pair_sum[panel, chip_y, :half].astype(jnp.float32)
            + corner_x[panel].astype(jnp.float32)
        ).astype(jnp.bfloat16)
        pair_sum[panel, chip_x, half:] = (
            pair_sum[panel, chip_x, half:].astype(jnp.float32)
            + corner_y[panel].astype(jnp.float32)
        ).astype(jnp.bfloat16)
        for kind in (3, 4):
            shared_copy(kind, panel).start()

    def shared_total(panel):
        for kind in (3, 4):
            shared_copy(kind, panel).wait()
        value = (
            pair_sum[panel, chip].astype(jnp.float32)
            + side_x[panel].astype(jnp.float32)
            + side_y[panel].astype(jnp.float32)
        )
        matrices[12, pl.ds(panel % 2 * rows, rows), :] = value.astype(jnp.bfloat16)

    def shared_store(panel):
        return pltpu.make_async_copy(
            matrices.at[12, pl.ds(panel % 2 * rows, rows)],
            shared_sum_ref.at[panel],
            local.at[4 + panel % 2],
        )

    project()
    lines[1].arrive(3)
    planes[1][3].start()
    planes[1][1].forward()
    attend(0)
    attend(1)
    planes[1][2].forward()
    attend(2)
    attend(3)
    planes[1][3].forward()
    cotangents.relay()
    join()
    for plane in planes[1]:
        plane.last()
    for index in range(1, 4):
        gates.arrive(index)
    place_slots()
    for plane in planes[1]:
        plane.complete()
    for copy in loads[first_panels:]:
        copy.start()
    exchange(0)
    shared(0)
    exchange(1)
    shared(1)
    exchange(2)
    shared_back(0)
    exchange(3)
    shared_back(1)
    for copy in kept:
        copy.start()
    exchange(4)
    shared_fill(0)
    tokens.relay()
    for panel in range(5, 11):
        exchange(panel)
        shared_pair(panel - 5)
        shared_corners(panel - 5)
        if panel < 10:
            shared_fill(panel - 4)
    for index in range(1, 4):
        cotangents.arrive(index)
        tokens.arrive(index)
    local_copies[2].wait()
    token_copy.wait()
    token_loads = [
        pltpu.make_async_copy(
            source.at[:, pl.ds(part * hidden, hidden)],
            matrices.at[first + part, pl.ds(0, 4 * length)],
            load_sems.at[first + part],
        )
        for first, source in ((6, tokens_ref), (9, cotangents_ref))
        for part in range(3)
    ]
    for copy in token_loads:
        copy.start()
    slot_iota = lax.broadcasted_iota(jnp.int32, (slots, length), 0)

    def slot_gate(expert, source):
        hot = slot_iota == places[expert, pl.ds(source, 1), :]
        return jnp.sum(
            jnp.where(hot, my_gates[expert, pl.ds(source, 1), :], 0.0), axis=1, keepdims=True
        )

    for source in range(4):
        for expert in range(experts):
            hot = slot_iota == places[expert, source : source + 1, :]
            chosen[source, expert * slots : (expert + 1) * slots, :] = jnp.where(
                hot, 1.0, 0.0
            ).astype(jnp.bfloat16)
    exchange(11)
    for copy in token_loads:
        copy.wait()

    @pl.loop(0, 4)
    def _(source):
        part = pl.ds(source * length, length)
        spots = pl.ds(pl.multiple_of(source * slots, slots), slots)
        slot_gates = [slot_gate(expert, source) for expert in range(experts)]
        for block in range(3):
            spot = pl.ds(block * hidden, hidden)
            token_slots = matmul(chosen[source], matrices[6 + block, part, :])
            grad_slots = matmul(chosen[source], matrices[9 + block, part, :])
            for expert in range(experts):
                rows_of = slice(expert * slots, (expert + 1) * slots)
                forward_slots[expert, spots, spot] = token_slots[rows_of].astype(jnp.bfloat16)
                backward_slots[expert, spots, spot] = (
                    grad_slots[rows_of] * slot_gates[expert]
                ).astype(jnp.bfloat16)

    def slot_stores(expert):
        return [
            pltpu.make_async_copy(
                source.at[expert], target.at[expert], expert_sems.at[2 + index, expert]
            )
            for index, (source, target) in enumerate(
                ((forward_slots, received_ref), (backward_slots, grad_returned_ref))
            )
        ]

    def narrow_stores(expert):
        buffer = expert % 2
        return [
            pltpu.make_async_copy(
                narrow.at[buffer, index], target.at[expert], expert_sems.at[4 + buffer, index]
            )
            for index, target in enumerate((act_ref, grad_gate_ref, grad_up_ref))
        ]

    def weight_loads(expert):
        buffer = expert % 2
        return [
            pltpu.make_async_copy(
                weights_ref.at[3 * expert + matrix],
                matrices.at[3 * buffer + matrix],
                expert_sems.at[6 + buffer, matrix],
            )
            for matrix in range(3)
        ]

    def fetch(expert):
        for matrix, copy in enumerate(weight_loads(expert)):
            shard_complete(3 * expert + matrix)
            copy.start()

    for expert in range(experts):
        for copy in slot_stores(expert):
            copy.start()
    fetch(0)

    @pl.loop(0, experts)
    def _(expert):
        buffer = expert % 2
        loaded = weight_loads(expert)

        @pl.when(expert >= 2)
        def _():
            for copy in narrow_stores(expert - 2):
                copy.wait()

        received = forward_slots[expert]
        grad_out = backward_slots[expert]
        loaded[0].wait()
        gate_pre = matmul(received, matrices[3 * buffer])
        loaded[1].wait()
        up_pre = matmul(received, matrices[3 * buffer + 1])
        loaded[2].wait()
        grad_act = matmul(grad_out, matrices[3 * buffer + 2])
        gate_sig = jax.nn.sigmoid(gate_pre)
        gate_act = gate_pre * gate_sig
        act = (gate_act * up_pre).astype(jnp.bfloat16)
        grad_gate = (grad_act * up_pre * gate_sig * (1.0 + gate_pre * (1.0 - gate_sig))).astype(
            jnp.bfloat16
        )
        grad_up = (grad_act * gate_act).astype(jnp.bfloat16)
        narrow[buffer, 0] = act
        narrow[buffer, 1] = grad_gate
        narrow[buffer, 2] = grad_up
        for copy in narrow_stores(expert):
            copy.start()
        for copy in slot_stores(expert):
            copy.wait()
        slot_gates = jnp.concatenate([slot_gate(expert, source) for source in range(4)], 0)
        for block in range(3):
            rows_of = pl.ds(block * hidden, hidden)
            spot = pl.ds(block * hidden, hidden)
            out = matmul_nt(act, matrices[3 * buffer + 2, rows_of, :]).astype(jnp.bfloat16)
            forward_slots[expert, :, spot] = (
                out.astype(jnp.float32) * slot_gates
            ).astype(jnp.bfloat16)
            backward_slots[expert, :, spot] = (
                matmul_nt(grad_gate, matrices[3 * buffer, rows_of, :])
                + matmul_nt(grad_up, matrices[3 * buffer + 1, rows_of, :])
            ).astype(jnp.bfloat16)

        later = (
            (lambda: exchange(12),),
            (lambda: exchange(13),),
            (lambda: exchange(14),),
            (
                lambda: exchange(15),
                lambda: exchange(16),
                lambda: shard_last(14),
                lambda: shared_sides(0),
                lambda: shared_sides(1),
            ),
            (
                lambda: shard_forward(17),
                lambda: shared_sides(2),
                lambda: shared_sides(3),
                lambda: shared_sides(4),
                lambda: shared_sides(5),
                lambda: shard_last(15),
                lambda: shard_last(16),
                lambda: shard_last(17),
            ),
        )
        for done, calls in enumerate(later):

            @pl.when(expert == done)
            def _():
                for call in calls:
                    call()

        @pl.when(expert + 1 < experts)
        def _():
            fetch(expert + 1)

    for expert in (experts - 2, experts - 1):
        for copy in narrow_stores(expert):
            copy.wait()
    out_copies = []
    for first, values, target in ((0, backward_slots, grad_parts_ref), (3, forward_slots, routed_parts_ref)):
        for block in range(3):
            spot = slice(block * hidden, (block + 1) * hidden)
            for source in range(4):
                slots_of = jnp.concatenate(
                    [
                        values[expert, source * slots : (source + 1) * slots, spot]
                        for expert in range(experts)
                    ],
                    0,
                )
                matrices[first + block, source * length : (source + 1) * length, :] = matmul_tn(
                    chosen[source], slots_of
                ).astype(jnp.bfloat16)
            out_copies.append(
                pltpu.make_async_copy(
                    matrices.at[first + block, pl.ds(0, 4 * length)],
                    target.at[:, pl.ds(block * hidden, hidden)],
                    load_sems.at[first + block],
                )
            )
            out_copies[-1].start()
    @pl.loop(0, panels)
    def _(panel):
        shard_finish(panel)

    for panel in range(shared_panels):
        if panel >= 2:
            shared_store(panel - 2).wait()
        shared_total(panel)
        shared_store(panel).start()
    for panel in (shared_panels - 2, shared_panels - 1):
        shared_store(panel).wait()
    for copy in (*kept, *out_copies):
        copy.wait()

    links.finish()


def front(stripe, gates, masters, hidden_in, cotangent, slots):
    length, width = cotangent.shape
    stripe_rows, columns = stripe.shape
    panels, rows, hidden = masters.shape
    experts = panels // 3
    low, full = jnp.bfloat16, jnp.float32
    vmem = pl.BlockSpec(memory_space=pltpu.VMEM)
    query_width = HEADS * HD
    spots = 4 * slots
    return pl.pallas_call(
        front_kernel,
        in_specs=[ANY] * 3 + [vmem] * 2,
        out_specs=[ANY] * 18 + [vmem] * 2,
        out_shape=[
            jax.ShapeDtypeStruct((stripe_rows * 32, columns), low),
            jax.ShapeDtypeStruct((panels, rows * 8, hidden), low),
            *[jax.ShapeDtypeStruct((length * 4, width), low)] * 4,
            *[jax.ShapeDtypeStruct((experts, spots, width), low)] * 2,
            *[jax.ShapeDtypeStruct((experts, spots, hidden), low)] * 3,
            jax.ShapeDtypeStruct((length, width), low),
            jax.ShapeDtypeStruct((length, query_width + 2 * KVH * HD), low),
            jax.ShapeDtypeStruct((length, query_width), low),
            jax.ShapeDtypeStruct((length, width), full),
            jax.ShapeDtypeStruct((length, width), full),
            jax.ShapeDtypeStruct((length, width), full),
            jax.ShapeDtypeStruct((6, rows, hidden), low),
            jax.ShapeDtypeStruct((length, 1), full),
            jax.ShapeDtypeStruct((8, width), full),
        ],
        scratch_shapes=[
            pltpu.VMEM((length, width), low),
            pltpu.VMEM((length, query_width + 2 * KVH * HD), low),
            pltpu.VMEM((length, query_width), low),
            pltpu.VMEM((length, width), full),
            pltpu.VMEM((length, width), full),
            pltpu.VMEM((length, width), full),
            pltpu.VMEM((length, width), low),
            pltpu.VMEM((length, FFS), low),
            pltpu.VMEM((length, 2 * FFS), low),
            pltpu.VMEM((14, width, hidden), low),
            pltpu.VMEM((width, 128), low),
            pltpu.VMEM((4, 4, 8, length), full),
            pltpu.VMEM((experts, 4, length), jnp.int32),
            pltpu.VMEM((experts, 4, length), full),
            pltpu.VMEM((4, experts * slots, length), low),
            pltpu.VMEM((experts, spots, width), low),
            pltpu.VMEM((experts, spots, width), low),
            pltpu.VMEM((2, 3, spots, hidden), low),
            pltpu.VMEM((6, 4, rows, hidden), low),
            pltpu.VMEM((6, rows // 2, hidden), low),
            pltpu.VMEM((6, rows // 2, hidden), low),
            pltpu.VMEM((6, rows, hidden), low),
            pltpu.VMEM((6, rows, hidden), low),
            pltpu.SemaphoreType.DMA((170,)),
            pltpu.SemaphoreType.DMA((7, panels)),
            pltpu.SemaphoreType.DMA((7, panels)),
            pltpu.SemaphoreType.DMA((6,)),
            pltpu.SemaphoreType.DMA((15,)),
            pltpu.SemaphoreType.DMA((8, 6)),
            pltpu.SemaphoreType.DMA((2, 5, 6)),
            pltpu.SemaphoreType.DMA((6,)),
        ],
        compiler_params=pltpu.CompilerParams(
            collective_id=1, has_side_effects=True, vmem_limit_bytes=63 * MIB
        ),
        name="front",
    )(stripe, gates, masters, hidden_in, cotangent)


def scatter_kernel(
    grad_parts_ref,
    received_ref,
    grad_returned_ref,
    act_ref,
    grad_gate_ref,
    grad_up_ref,
    dense_ref,
    shared_sum_ref,
    cotangent_ref,
    normed_attend_ref,
    attended_ref,
    residual_in,
    grad_shared_in,
    projected_in,
    hidden_in,
    scale_ref,
    gains_ref,
    expert_sum_ref,
    stripes_ref,
    grad_input_ref,
    grad_gain_ref,
    residual_ref,
    grad_shared_ref,
    projected_ref,
    hidden_ref,
    ring,
    pair_sum,
    corner_x,
    corner_y,
    side_x,
    side_y,
    staged,
    wide,
    narrow,
    left,
    right,
    out_weights,
    grad_tokens,
    grad_attended,
    grad_pair,
    grad_residual_ref,
    key_weights,
    line_out,
    line_in,
    pair_sems,
    slot_sems,
    line_sems,
    token_sems,
    load_sems,
    free,
):
    dp, z = lax.axis_index("dp"), lax.axis_index("expert")
    core, chip = dp % 2, dp // 2
    chip_x, chip_y = flipped(chip, 0), flipped(chip, 1)
    chip_corner = flipped(chip_x, 1)
    device_core = (flipped(dp, 0), z)
    device_x = (flipped(dp, 1), z)
    device_y = (flipped(dp, 2), z)
    others = [(dp, (z + turn) % 4) for turn in range(1, 4)]
    slots = pair_sum.shape[0]
    experts = received_ref.shape[0]
    expert_panels = 3 * experts
    dense_panels = line_out.shape[0]
    shared_panels = dense_panels - right.shape[0]
    panels = expert_panels + right.shape[0]
    length, width = residual_ref.shape
    share, hidden = staged.shape[1:]
    half = share // 2
    stripe = share // 4
    query_width = HEADS * HD
    kv_width = KVH * HD
    block = width // 4

    def remote(source, target, send, receive, device):
        return pltpu.make_async_remote_copy(
            src_ref=source,
            dst_ref=target,
            send_sem=send,
            recv_sem=receive,
            device_id=device,
            device_id_type=MESH,
        )

    barrier = pltpu.get_barrier_semaphore()
    for device in (device_core, device_x, device_y, *others):
        pl.semaphore_signal(barrier, inc=1, device_id=device, device_id_type=MESH)
    pl.semaphore_wait(barrier, 6)

    grad_copies = [
        remote(
            grad_parts_ref.at[pl.ds(pl.multiple_of(device[1] * length, length), length), :],
            grad_tokens.at[turn],
            token_sems.at[turn],
            token_sems.at[3 + turn],
            device,
        )
        for turn, device in enumerate(others)
    ]
    for copy in grad_copies:
        copy.start()

    def expert_loads(expert):
        buffer = expert % 2
        return [
            pltpu.make_async_copy(source.at[expert], target, load_sems.at[buffer, index])
            for index, (source, target) in enumerate(
                (
                    (received_ref, wide.at[buffer, 0]),
                    (grad_returned_ref, wide.at[buffer, 1]),
                    (grad_gate_ref, narrow.at[buffer, 0]),
                    (grad_up_ref, narrow.at[buffer, 1]),
                    (act_ref, narrow.at[buffer, 2]),
                )
            )
        ]

    for copy in expert_loads(0):
        copy.start()

    def columns(ref, panel):
        return ref.at[:, pl.ds(panel * hidden, hidden)]

    sources = [
        (cotangent_ref, left.at[0]),
        (normed_attend_ref, left.at[2]),
        *[(columns(attended_ref, panel), right.at[panel]) for panel in range(3)],
        (shared_sum_ref, line_out.at[pl.ds(0, shared_panels)]),
        (residual_in, residual_ref),
        (grad_shared_in, grad_shared_ref),
        (projected_in, projected_ref),
        (hidden_in, hidden_ref),
        (dense_ref.at[:, pl.ds(query_width + 2 * kv_width, query_width)], out_weights),
        (dense_ref.at[:, pl.ds(query_width, 2 * kv_width)], key_weights),
        (
            grad_parts_ref.at[pl.ds(pl.multiple_of(z * length, length), length), :],
            grad_tokens.at[3],
        ),
    ]
    dense_loads = [
        pltpu.make_async_copy(source, target, load_sems.at[2 + index // 5, index % 5])
        for index, (source, target) in enumerate(sources)
    ]
    for copy in dense_loads:
        copy.start()
    query_load = pltpu.make_async_copy(
        dense_ref.at[:, pl.ds(0, query_width)], out_weights, pair_sems.at[4]
    )

    def fill(pair, left_ref, right_value):
        for chip_index in range(4):
            part = matmul_tn(left_ref[:, chip_index * block : (chip_index + 1) * block], right_value)
            ring[pair, chip_index] = part.astype(jnp.bfloat16).reshape(2, share, hidden)

    def total(first, *more):
        result = first.astype(jnp.float32)
        for value in more:
            result = result + value.astype(jnp.float32)
        return result

    def pair_copy(panel):
        pair, slot = panel % 2, panel % slots
        return remote(
            ring.at[pair, :, 1 - core],
            pair_sum.at[slot],
            pair_sems.at[pair],
            slot_sems.at[0, slot],
            device_core,
        )

    def corner_copies(panel):
        slot = panel % slots
        return (
            remote(
                pair_sum.at[slot, chip_corner, pl.ds(0, half)],
                corner_x.at[slot],
                slot_sems.at[1, slot],
                slot_sems.at[2, slot],
                device_x,
            ),
            remote(
                pair_sum.at[slot, chip_corner, pl.ds(half, half)],
                corner_y.at[slot],
                slot_sems.at[3, slot],
                slot_sems.at[4, slot],
                device_y,
            ),
        )

    def side_copies(panel):
        slot = panel % slots
        return (
            remote(
                pair_sum.at[slot, chip_x],
                side_x.at[slot],
                slot_sems.at[5, slot],
                slot_sems.at[6, slot],
                device_x,
            ),
            remote(
                pair_sum.at[slot, chip_y],
                side_y.at[slot],
                slot_sems.at[7, slot],
                slot_sems.at[8, slot],
                device_y,
            ),
        )

    def line_copies(panel):
        return [
            remote(
                line_out.at[panel, pl.ds(pl.multiple_of(device[1] * stripe, stripe), stripe)],
                line_in.at[panel, turn],
                line_sems.at[0, panel, turn],
                line_sems.at[1, panel, turn],
                device,
            )
            for turn, device in enumerate(others)
        ]

    def staged_copy(panel):
        return pltpu.make_async_copy(
            staged.at[panel % 2], expert_sum_ref.at[panel], pair_sems.at[2 + panel % 2]
        )

    def post(panel):
        @pl.when(panel >= slots)
        def _():
            pl.semaphore_wait(free.at[0], 1)

        pair_copy(panel).start()

    def sum_pair(panel):
        pair, slot = panel % 2, panel % slots
        pair_copy(panel).wait()
        for chip_index in range(4):
            pair_sum[slot, chip_index] = total(
                pair_sum[slot, chip_index], ring[pair, chip_index, core]
            ).astype(jnp.bfloat16)

        @pl.when(panel >= slots)
        def _():
            pl.semaphore_wait(free.at[1], 1)
            pl.semaphore_wait(free.at[2], 1)

        for copy in corner_copies(panel):
            copy.start()

    def sum_corner(panel):
        slot = panel % slots
        for copy in corner_copies(panel):
            copy.wait_recv()
        pair_sum[slot, chip_y, :half] = total(
            pair_sum[slot, chip_y, :half], corner_x[slot]
        ).astype(jnp.bfloat16)
        pair_sum[slot, chip_x, half:] = total(
            pair_sum[slot, chip_x, half:], corner_y[slot]
        ).astype(jnp.bfloat16)
        for copy in side_copies(panel):
            copy.start()

    def sum_sides(panel):
        slot = panel % slots
        for copy in corner_copies(panel):
            copy.wait_send()
        for copy in side_copies(panel):
            copy.wait()
        value = total(pair_sum[slot, chip], side_x[slot], side_y[slot]).astype(jnp.bfloat16)

        @pl.when(panel < expert_panels)
        def _():
            @pl.when(panel >= 2)
            def _():
                staged_copy(panel - 2).wait()

            staged[panel % 2] = value
            staged_copy(panel).start()

        @pl.when(panel >= expert_panels)
        def _():
            index = panel - expert_panels + shared_panels
            line_out[index] = value
            for copy in line_copies(index):
                copy.start()

        @pl.when(panel < panels - slots)
        def _():
            for index, device in enumerate((device_core, device_x, device_y)):
                pl.semaphore_signal(
                    free.at[index], inc=1, device_id=device, device_id_type=MESH
                )

    def residual_backward(part):
        if part == 0:
            for copy in dense_loads:
                copy.wait()
            for copy in grad_copies:
                copy.wait()
            grad_gain_ref[...] = jnp.zeros_like(grad_gain_ref)
        rows_step = 32
        steps = length // rows_step // 2

        @pl.loop(part * steps, (part + 1) * steps)
        def _(index):
            rows = pl.ds(index * rows_step, rows_step)
            grad_normed = (
                total(
                    grad_tokens[3, rows, :],
                    grad_tokens[0, rows, :],
                    grad_tokens[1, rows, :],
                    grad_tokens[2, rows, :],
                )
                + grad_shared_ref[rows, :]
            )
            residual, scale = residual_ref[rows, :], scale_ref[rows, :]
            grad_scaled = grad_normed * gains_ref[1:2, :]
            mean = jnp.mean(grad_scaled * residual, axis=-1, keepdims=True)
            grad_residual = (
                left[0, rows, :].astype(jnp.float32)
                + scale * grad_scaled
                - residual * (scale * scale * scale) * mean
            )
            grad_residual_ref[rows, :] = grad_residual
            left[1, rows, :] = grad_residual.astype(jnp.bfloat16)
            grad_gain_ref[1:2, :] += jnp.sum(
                grad_normed * residual * scale, axis=0, keepdims=True
            )

    def attended_backward():
        grad_attended[...] = matmul(left[1], out_weights[...]).astype(jnp.bfloat16)
        query_load.start()

    def query_backward():
        query_load.wait()
        for part in range(3):
            update = matmul_nt(right[3 + part], out_weights[:, part * hidden : (part + 1) * hidden])
            if part == 0:
                grad_input_ref[...] = update
            else:
                grad_input_ref[...] += update

    def key_backward():
        for part in range(2):
            grad_input_ref[...] += matmul_nt(
                right[6 + part], key_weights[:, part * hidden : (part + 1) * hidden]
            )

    def input_backward():
        rows_step = 32

        @pl.loop(0, length // rows_step)
        def _(index):
            rows = pl.ds(index * rows_step, rows_step)
            values, grad_normed = hidden_ref[rows, :].astype(jnp.float32), grad_input_ref[rows, :]
            scale = lax.rsqrt(jnp.mean(values * values, axis=-1, keepdims=True) + 1e-06)
            grad_scaled = grad_normed * gains_ref[0:1, :]
            mean = jnp.mean(grad_scaled * values, axis=-1, keepdims=True)
            grad_input_ref[rows, :] = (
                grad_residual_ref[rows, :]
                + scale * grad_scaled
                - values * (scale * scale * scale) * mean
            )
            grad_gain_ref[0:1, :] += jnp.sum(
                grad_normed * values * scale, axis=0, keepdims=True
            )

    def attention_backward(head):
        score_scale = HD ** (-0.5)
        per_group = HEADS // KVH
        heads_wide = hidden // HD
        group = head // per_group
        key_rows = projected_ref[:, query_width + group * HD : query_width + (group + 1) * HD]
        value_first = query_width + kv_width + group * HD
        value_rows = projected_ref[:, value_first : value_first + HD]
        row = lax.broadcasted_iota(jnp.int32, (length, length), 0)
        column = lax.broadcasted_iota(jnp.int32, (length, length), 1)
        spot = slice(head * HD, (head + 1) * HD)
        query, grad_out = projected_ref[:, spot], grad_attended[:, spot]
        scores = jnp.where(column <= row, matmul_nt(query, key_rows) * score_scale, -1e30)
        raised = jnp.exp(scores - jnp.max(scores, axis=-1, keepdims=True))
        weights = raised / jnp.sum(raised, axis=-1, keepdims=True)
        grad_weights = matmul_nt(grad_out, value_rows)
        inner = jnp.sum(weights * grad_weights, axis=-1, keepdims=True)
        grad_scores = (weights * (grad_weights - inner)).astype(jnp.bfloat16)
        grad_query = matmul(grad_scores, key_rows) * score_scale
        place = slice(head % heads_wide * HD, (head % heads_wide + 1) * HD)
        right[3 + head // heads_wide, :, place] = grad_query.astype(jnp.bfloat16)
        grad_key = matmul_tn(grad_scores, query)
        grad_value = matmul_tn(weights.astype(jnp.bfloat16), grad_out)
        if head % per_group > 0:
            grad_key = grad_key + grad_pair[0]
            grad_value = grad_value + grad_pair[1]
        if head % per_group < per_group - 1:
            grad_pair[0] = grad_key
            grad_pair[1] = grad_value
        else:
            place = slice(group * HD, (group + 1) * HD)
            right[6, :, place] = (grad_key * score_scale).astype(jnp.bfloat16)
            right[7, :, place] = grad_value.astype(jnp.bfloat16)

    def two_heads_backward(head):
        attention_backward(head)
        attention_backward(head + 1)

    @pl.loop(0, panels + 5)
    def _(step):
        @pl.when(step < expert_panels)
        def _():
            expert, matrix = step // 3, step % 3

            @pl.when(matrix == 0)
            def _():
                for copy in expert_loads(expert):
                    copy.wait()

                @pl.when(expert + 1 < experts)
                def _():
                    for copy in expert_loads(expert + 1):
                        copy.start()

            fill(step % 2, wide.at[expert % 2, matrix // 2], narrow[expert % 2, matrix])

        backward = [
            *[functools.partial(residual_backward, part) for part in range(2)],
            attended_backward,
            *[functools.partial(two_heads_backward, head) for head in range(0, HEADS, 2)],
            query_backward,
            key_backward,
            input_backward,
        ]
        for index, call in enumerate(backward):
            pl.when(step == GRAD_STEP + index)(call)

        @pl.when((step >= expert_panels) & (step < panels))
        def _():
            panel = step - expert_panels
            fill(step % 2, left.at[jnp.where(panel < 3, 1, 2)], right[panel])

        @pl.when(step == GRAD_STEP + 1)
        def _():
            for panel in range(shared_panels):
                for copy in line_copies(panel):
                    copy.start()

        @pl.when(step < panels)
        def _():
            post(step)

        @pl.when((step >= 1) & (step < panels + 1))
        def _():
            sum_pair(step - 1)

        @pl.when((step >= 3) & (step < panels + 3))
        def _():
            sum_corner(step - 3)

        @pl.when(step >= 5)
        def _():
            sum_sides(step - 5)

    for panel in (expert_panels - 2, expert_panels - 1):
        staged_copy(panel).wait()

    for panel in range(dense_panels):
        for copy in line_copies(panel):
            copy.wait()
        place = panel + 8 if panel < 6 else panel - 1 if panel < 9 else panel - 9
        stripes_ref[place] = total(
            line_out[panel, pl.ds(pl.multiple_of(z * stripe, stripe), stripe), :],
            line_in[panel, 0],
            line_in[panel, 1],
            line_in[panel, 2],
        )


def scatter_grads(
    grad_parts,
    saved,
    dense_all,
    shared_sum,
    cotangent,
    normed_attend,
    attended,
    residual,
    grad_shared,
    projected,
    hidden_in,
    scale,
    gains,
):
    experts, spots, width = saved[0].shape
    hidden = saved[2].shape[-1]
    length = residual.shape[0]
    share = width // 8
    stripe = share // 4
    dense_panels = 14
    low = jnp.bfloat16
    vmem = pl.BlockSpec(memory_space=pltpu.VMEM)
    return pl.pallas_call(
        scatter_kernel,
        in_specs=[ANY] * 15 + [vmem] * 2,
        out_specs=[ANY] + [vmem] * 3,
        out_shape=[
            jax.ShapeDtypeStruct((3 * experts, share, hidden), low),
            jax.ShapeDtypeStruct((dense_panels, stripe, hidden), jnp.float32),
            jax.ShapeDtypeStruct((length, width), jnp.float32),
            jax.ShapeDtypeStruct((2, width), jnp.float32),
        ],
        scratch_shapes=[
            pltpu.VMEM((length, width), jnp.float32),
            pltpu.VMEM((length, width), jnp.float32),
            pltpu.VMEM(projected.shape, low),
            pltpu.VMEM((length, width), low),
            pltpu.VMEM((2, 4, 2, share, hidden), low),
            pltpu.VMEM((SLOTS, 4, share, hidden), low),
            pltpu.VMEM((SLOTS, share // 2, hidden), low),
            pltpu.VMEM((SLOTS, share // 2, hidden), low),
            pltpu.VMEM((SLOTS, share, hidden), low),
            pltpu.VMEM((SLOTS, share, hidden), low),
            pltpu.VMEM((2, share, hidden), low),
            pltpu.VMEM((2, 2, spots, width), low),
            pltpu.VMEM((2, 3, spots, hidden), low),
            pltpu.VMEM((3, length, width), low),
            pltpu.VMEM((8, length, hidden), low),
            pltpu.VMEM((width, HEADS * HD), low),
            pltpu.VMEM((4, length, width), low),
            pltpu.VMEM((length, HEADS * HD), low),
            pltpu.VMEM((2, length, HD), jnp.float32),
            pltpu.VMEM((length, width), jnp.float32),
            pltpu.VMEM((width, 2 * KVH * HD), low),
            pltpu.VMEM((dense_panels, share, hidden), low),
            pltpu.VMEM((dense_panels, 3, stripe, hidden), low),
            pltpu.SemaphoreType.DMA((5,)),
            pltpu.SemaphoreType.DMA((9, SLOTS)),
            pltpu.SemaphoreType.DMA((2, dense_panels, 3)),
            pltpu.SemaphoreType.DMA((6,)),
            pltpu.SemaphoreType.DMA((5, 5)),
            pltpu.SemaphoreType.REGULAR((3,)),
        ],
        compiler_params=pltpu.CompilerParams(
            collective_id=3, has_side_effects=True, vmem_limit_bytes=62 * MIB
        ),
        name="scatter_grads",
    )(
        grad_parts,
        *saved,
        dense_all,
        shared_sum,
        cotangent,
        normed_attend,
        attended,
        residual,
        grad_shared,
        projected,
        hidden_in,
        scale,
        gains,
    )


def muon_kernel(
    expert_ref,
    dense_ref,
    routed_parts_ref,
    expert_out_ref,
    dense_out_ref,
    routed_received_ref,
    dense_back,
    moments,
    units,
    orthogonal,
    current,
    low,
    identity,
    line_sems,
    out_sems,
    in_sems,
    back_out_sems,
    back_in_sems,
    load_sems,
):
    dp, z = lax.axis_index("dp"), lax.axis_index("expert")
    count, share, _ = moments.shape
    first, dense_count = 10, 4
    stripe = dense_ref.shape[1]
    others = [(dp, (z + turn) % 4) for turn in range(1, 4)]
    peers = [((dp + turn) % 8, z) for turn in range(1, 8)]

    def remote(source, target, send, receive, device):
        return pltpu.make_async_remote_copy(
            src_ref=source,
            dst_ref=target,
            send_sem=send,
            recv_sem=receive,
            device_id=device,
            device_id_type=MESH,
        )

    def share_of(index):
        return pl.ds(pl.multiple_of(index * share, share), share)

    def stripe_of(index):
        return pl.ds(pl.multiple_of(index * stripe, stripe), stripe)

    barrier = pltpu.get_barrier_semaphore()
    for device in (*others, *peers):
        pl.semaphore_signal(barrier, inc=1, device_id=device, device_id_type=MESH)
    dense_rows = pl.ds(first, dense_count)
    loads = [
        pltpu.make_async_copy(
            expert_ref.at[pl.ds(0, first)], moments.at[pl.ds(0, first)], load_sems.at[0]
        ),
        pltpu.make_async_copy(
            expert_ref.at[pl.ds(first, count - first - dense_count)],
            moments.at[pl.ds(first + dense_count, count - first - dense_count)],
            load_sems.at[1],
        ),
        pltpu.make_async_copy(
            dense_ref.at[pl.ds(z * dense_count, dense_count)],
            moments.at[dense_rows, stripe_of(z)],
            load_sems.at[2],
        ),
    ]
    for copy in loads:
        copy.start()
    pl.semaphore_wait(barrier, len(others) + len(peers))
    line_copies = [
        remote(
            dense_ref.at[pl.ds(device[1] * dense_count, dense_count)],
            moments.at[dense_rows, stripe_of(z)],
            line_sems.at[0, turn],
            line_sems.at[1, turn],
            device,
        )
        for turn, device in enumerate(others)
    ]
    line_back = [
        remote(
            dense_back.at[:, stripe_of(device[1])],
            dense_out_ref.at[pl.ds(z * dense_count, dense_count)],
            line_sems.at[2, turn],
            line_sems.at[3, turn],
            device,
        )
        for turn, device in enumerate(others)
    ]
    own_back = pltpu.make_async_copy(
        dense_back.at[:, stripe_of(z)],
        dense_out_ref.at[pl.ds(z * dense_count, dense_count)],
        load_sems.at[2],
    )

    def out_copy(slot, turn):
        owner = peers[turn][0]
        return remote(
            moments.at[8 * slot + owner],
            units.at[slot, share_of(dp)],
            out_sems.at[slot, turn],
            in_sems.at[slot],
            peers[turn],
        )

    def own_copy(slot):
        return pltpu.make_async_copy(
            moments.at[8 * slot + dp], units.at[slot, share_of(dp)], load_sems.at[3 + slot]
        )

    def is_dense(slot, owner):
        unit = 8 * slot + owner
        return (unit >= first) & (unit < first + dense_count)

    def expert_place(slot, owner):
        unit = 8 * slot + owner
        return expert_out_ref.at[jnp.where(unit < first, unit, unit - dense_count)]

    def dense_place(slot, owner):
        return dense_back.at[8 * slot + owner - first]

    def back_copy(place, slot, turn):
        return remote(
            orthogonal.at[slot, share_of(peers[turn][0])],
            place(slot, dp),
            back_out_sems.at[slot, turn],
            back_in_sems.at[slot, dp],
            peers[turn],
        )

    def own_back_copy(place, slot):
        return pltpu.make_async_copy(
            orthogonal.at[slot, share_of(dp)], place(slot, dp), load_sems.at[3 + slot]
        )

    def send_back(place, slot):
        for turn in range(7):
            back_copy(place, slot, turn).start()
        own_back_copy(place, slot).start()

    def exists(slot, owner):
        return 8 * slot + owner < count

    def send_slot(slot):
        for turn in range(7):
            pl.when(exists(slot, peers[turn][0]))(out_copy(slot, turn).start)
        pl.when(exists(slot, dp))(own_copy(slot).start)

    length = routed_received_ref.shape[1]
    own_routed = pltpu.make_async_copy(
        routed_parts_ref.at[pl.ds(pl.multiple_of(z * length, length), length), :],
        routed_received_ref.at[3],
        load_sems.at[6],
    )
    own_routed.start()
    routed_copies = [
        remote(
            routed_parts_ref.at[pl.ds(pl.multiple_of(device[1] * length, length), length), :],
            routed_received_ref.at[turn],
            line_sems.at[4, turn],
            line_sems.at[5, turn],
            device,
        )
        for turn, device in enumerate(others)
    ]
    for copy in line_copies:
        copy.start()
    loads[0].wait()
    send_slot(0)
    loads[1].wait()
    loads[2].wait()
    for copy in line_copies:
        copy.wait()
    send_slot(1)
    send_slot(2)
    for copy in routed_copies:
        copy.start()

    @pl.loop(0, 3)
    def _(slot):
        @pl.when(exists(slot, dp))
        def _():
            own_copy(slot).wait()
            arrived = units.at[slot, pl.ds(0, 7 * share)]
            remote(arrived, arrived, in_sems.at[slot], in_sems.at[slot], peers[0]).wait_recv()
            newton_schulz_unit(units.at[slot], orthogonal.at[slot], current, low, identity)

            @pl.when(is_dense(slot, dp))
            def _():
                send_back(dense_place, slot)

            @pl.when(jnp.logical_not(is_dense(slot, dp)))
            def _():
                send_back(expert_place, slot)

    def own_back_wait(slot):
        def wait():
            pltpu.make_async_copy(
                orthogonal.at[slot, share_of(dp)], expert_out_ref.at[0], load_sems.at[3 + slot]
            ).wait()

        return wait

    def wait_back(slot):
        for turn in range(7):
            owner = peers[turn][0]

            @pl.when(exists(slot, owner))
            def _():
                block = expert_out_ref.at[0]
                semaphore = back_in_sems.at[slot, owner]
                remote(block, block, semaphore, semaphore, peers[0]).wait_recv()

        pl.when(exists(slot, dp))(own_back_wait(slot))

    wait_back(1)
    for copy in line_back:
        copy.start()
    own_back.start()
    wait_back(0)
    wait_back(2)
    for slot in range(3):
        for turn in range(7):
            pl.when(exists(slot, peers[turn][0]))(out_copy(slot, turn).wait_send)

        @pl.when(exists(slot, dp))
        def _():
            for turn in range(7):
                back_copy(expert_place, slot, turn).wait_send()

    for copy in line_back:
        copy.wait()
    own_back.wait()
    own_routed.wait()
    for copy in routed_copies:
        copy.wait()


def muon(expert_units, dense_units, routed_parts):
    experts, share, columns = expert_units.shape
    panels, stripe, _ = dense_units.shape
    count = experts + panels // 4
    low = jnp.bfloat16
    return pl.pallas_call(
        muon_kernel,
        in_specs=[ANY] * 3,
        out_specs=[ANY] * 3,
        out_shape=[
            jax.ShapeDtypeStruct(expert_units.shape, low),
            jax.ShapeDtypeStruct(dense_units.shape, low),
            jax.ShapeDtypeStruct((4, routed_parts.shape[0] // 4, routed_parts.shape[1]), low),
        ],
        scratch_shapes=[
            pltpu.VMEM((panels // 4, share, columns), low),
            pltpu.VMEM((count, share, columns), low),
            pltpu.VMEM((3, 8 * share, columns), low),
            pltpu.VMEM((3, 8 * share, columns), low),
            pltpu.VMEM((columns, 8 * share), jnp.float32),
            pltpu.VMEM((columns, 8 * share), low),
            pltpu.VMEM((columns, columns), low),
            pltpu.SemaphoreType.DMA((6, 3)),
            pltpu.SemaphoreType.DMA((3, 7)),
            pltpu.SemaphoreType.DMA((3,)),
            pltpu.SemaphoreType.DMA((3, 7)),
            pltpu.SemaphoreType.DMA((3, 8)),
            pltpu.SemaphoreType.DMA((7,)),
        ],
        compiler_params=pltpu.CompilerParams(
            collective_id=4, has_side_effects=True, vmem_limit_bytes=56 * MIB
        ),
        name="muon",
    )(expert_units, dense_units, routed_parts)


GROUP = 2


def blocks_over(steps, shape, axis):
    def place(index):
        return tuple(
            jnp.minimum(index, steps - 1) if position == axis else 0
            for position in range(len(shape))
        )

    return pl.BlockSpec(shape, place)


def moments_kernel(
    momentum_ref,
    sum_ref,
    dense_momentum_ref,
    dense_sum_ref,
    grad_ref,
    moment_ref,
    units_ref,
    dense_grad_ref,
    dense_moment_ref,
    dense_units_ref,
):
    grad = sum_ref[...].astype(jnp.float32)
    moment = MOMENTUM_DECAY * momentum_ref[...] + grad
    grad_ref[...] = grad
    moment_ref[...] = moment
    units_ref[...] = moment.astype(jnp.bfloat16)
    columns = dense_sum_ref.shape[2]
    real = pl.program_id(0) < pl.num_programs(0) - 2
    for panel in range(GROUP):
        spot = slice(panel * columns, (panel + 1) * columns)
        dense_grad = dense_sum_ref[panel]
        dense_moment = MOMENTUM_DECAY * dense_momentum_ref[:, spot] + dense_grad
        dense_grad_ref[:, spot] = dense_grad
        dense_moment_ref[:, spot] = dense_moment
        dense_units_ref[panel] = jnp.where(real, dense_moment, 0.0).astype(jnp.bfloat16)


def moments(momentum, grad_sum, dense_momentum, dense_sum):
    panels, rows, columns = grad_sum.shape
    dense_panels, stripe, _ = dense_sum.shape
    steps = panels // GROUP
    block = pl.BlockSpec((GROUP, rows, columns), lambda index: (index, 0, 0))
    wide = blocks_over(dense_panels // GROUP, (stripe, GROUP * columns), 1)
    full = jax.ShapeDtypeStruct(grad_sum.shape, jnp.float32)
    dense_full = jax.ShapeDtypeStruct(dense_momentum.shape, jnp.float32)
    grad, moment, *rest = pl.pallas_call(
        moments_kernel,
        grid=(steps,),
        in_specs=[
            block,
            block,
            wide,
            blocks_over(dense_panels // GROUP, (GROUP, stripe, columns), 0),
        ],
        out_specs=[
            block,
            block,
            block,
            wide,
            wide,
            blocks_over(dense_panels // GROUP + 1, (GROUP, stripe, columns), 0),
        ],
        out_shape=[
            full,
            full,
            jax.ShapeDtypeStruct(grad_sum.shape, jnp.bfloat16),
            dense_full,
            dense_full,
            jax.ShapeDtypeStruct((dense_panels + GROUP, stripe, columns), jnp.bfloat16),
        ],
        compiler_params=pltpu.CompilerParams(vmem_limit_bytes=60 * MIB),
        name="moments",
    )(momentum.reshape(grad_sum.shape), grad_sum, dense_momentum, dense_sum)
    return grad.reshape(momentum.shape), moment.reshape(momentum.shape), *rest


def update_kernel(
    weights_ref,
    orthogonal_ref,
    dense_weights_ref,
    dense_orthogonal_ref,
    base_ref,
    routed_ref,
    grad_ref,
    new_ref,
    dense_new_ref,
    out_ref,
    grad_out_ref,
):
    keep_factor = 1.0 - LEARN_RATE * WEIGHT_DECAY
    new_ref[...] = keep_factor * weights_ref[...] - LEARN_RATE * orthogonal_ref[...].astype(
        jnp.float32
    )
    columns = dense_orthogonal_ref.shape[2]
    for panel in range(GROUP):
        spot = slice(panel * columns, (panel + 1) * columns)
        dense_new_ref[:, spot] = keep_factor * dense_weights_ref[:, spot] - LEARN_RATE * (
            dense_orthogonal_ref[panel].astype(jnp.float32)
        )
    total = base_ref[...]
    for source in (3, 0, 1, 2):
        total = total + routed_ref[source].astype(jnp.float32)
    out_ref[...] = total.astype(jnp.bfloat16)
    grad_out_ref[...] = grad_ref[...]


def updated(weights, orthogonal, dense_weights, dense_orthogonal, base, routed, grad):
    panels, rows, columns = orthogonal.shape
    stripe, dense_columns = dense_weights.shape
    length, width = base.shape
    dense_steps = dense_columns // (GROUP * columns)
    row_steps = 8
    block = pl.BlockSpec((GROUP, rows, columns), lambda index: (index, 0, 0))
    wide = blocks_over(dense_steps, (stripe, GROUP * columns), 1)
    part = blocks_over(row_steps, (length // row_steps, width), 0)
    new, *rest = pl.pallas_call(
        update_kernel,
        grid=(panels // GROUP,),
        in_specs=[
            block,
            block,
            wide,
            blocks_over(dense_steps, (GROUP, stripe, columns), 0),
            part,
            blocks_over(row_steps, (4, length // row_steps, width), 1),
            part,
        ],
        out_specs=[block, wide, part, part],
        out_shape=[
            jax.ShapeDtypeStruct(orthogonal.shape, jnp.float32),
            jax.ShapeDtypeStruct(dense_weights.shape, jnp.float32),
            jax.ShapeDtypeStruct(base.shape, jnp.bfloat16),
            jax.ShapeDtypeStruct(base.shape, jnp.float32),
        ],
        compiler_params=pltpu.CompilerParams(vmem_limit_bytes=60 * MIB),
        name="update",
    )(
        weights.reshape(orthogonal.shape),
        orthogonal,
        dense_weights,
        dense_orthogonal,
        base,
        routed,
        grad,
    )
    return new.reshape(weights.shape), *rest


def on_device(
    hidden_in,
    cotangent,
    routes,
    route_weights,
    dense_weights,
    dense_momentum,
    expert_weights,
    expert_momentum,
    norm_gains,
    gain_first,
    gain_second,
):
    length, width = hidden_in.shape
    topk_count = routes.shape[1]
    local_experts = expert_weights.shape[0]
    expert_size = lax.axis_size("expert")
    dp_size = lax.axis_size("dp")
    expert_count = local_experts * expert_size
    capacity = 5 * length * topk_count // (4 * expert_count)
    block_rows = min(512, length)
    query_width = HEADS * HD
    kv_width = KVH * HD
    qkv_end = query_width + 2 * kv_width
    shared_base = 2 * query_width + 2 * kv_width
    gate_table = jnp.sum(
        jnp.where(
            routes.T[None, :, :] == jnp.arange(expert_count, dtype=jnp.int32)[:, None, None],
            route_weights.T[None, :, :],
            0.0,
        ),
        axis=1,
    )
    direct = dp_size == 8 and expert_size == 4
    inputs = hidden_in.astype(jnp.float32)
    scale_attend = norm_scale(inputs)
    if direct:
        stripe_rows = dense_weights.shape[0]
        extra = jnp.zeros((stripe_rows, 128 - norm_gains.shape[0]), jnp.float32)
        plane_gates = gate_table.reshape(expert_size, local_experts, length)
        (
            dense_all,
            _,
            _,
            _,
            routed_parts,
            grad_parts,
            *saved,
            normed_attend,
            projected,
            attended,
            residual,
            grad_shared,
            base_out,
            shared_sum,
            scale_mixer,
            gains_all,
        ) = front(
            jnp.concatenate(
                [
                    dense_weights[:, :shared_base],
                    norm_gains.T,
                    extra,
                    dense_weights[:, shared_base:],
                ],
                1,
            ).astype(jnp.bfloat16),
            jnp.pad(plane_gates, ((0, 0), (0, 8 - local_experts), (0, 0))),
            expert_weights.reshape(-1, *expert_weights.shape[2:]),
            hidden_in,
            cotangent,
            -(-capacity // 16) * 16,
        )
    else:
        gate_tables = lax.all_gather(gate_table, "expert", axis=0, tiled=False)
        cotangents = lax.all_gather(cotangent, "expert", axis=0, tiled=True)
        dense_all, gains_all = (
            lax.all_gather(
                dense_weights.astype(jnp.bfloat16), ("dp", "expert"), axis=0, tiled=True
            ),
            lax.all_gather(norm_gains.astype(jnp.bfloat16), ("dp", "expert"), axis=1, tiled=True),
        )
        gain_attend = gains_all[0].astype(jnp.float32)
        gain_mixer = gains_all[1].astype(jnp.float32)
        normed_attend = (inputs * scale_attend * gain_attend).astype(jnp.bfloat16)
        projected = jnp.dot(
            normed_attend, dense_all[:, :qkv_end], preferred_element_type=jnp.float32
        ).astype(jnp.bfloat16)
        query = projected[:, :query_width]
        key_rows = projected[:, query_width : query_width + kv_width]
        value_rows = projected[:, query_width + kv_width :]
        attended, saved_stats = attend_forward(query, key_rows, value_rows, block_rows)
        residual = inputs + jnp.einsum(
            "sq,dq->sd", attended, dense_all[:, qkv_end:shared_base], preferred_element_type=jnp.float32
        )
        scale_mixer = norm_scale(residual)
        normed_mixer = (residual * scale_mixer * gain_mixer).astype(jnp.bfloat16)
        expert_all = lax.all_gather(expert_weights.astype(jnp.bfloat16), "dp", axis=2, tiled=True)
        tokens = lax.all_gather(normed_mixer, "expert", axis=0, tiled=True)
        shared_pre = jnp.dot(
            normed_mixer,
            dense_all[:, shared_base : shared_base + 2 * FFS],
            preferred_element_type=jnp.float32,
        )
        shared_gate = shared_pre[:, :FFS]
        shared_up = shared_pre[:, FFS:]
        shared_act = (jax.nn.silu(shared_gate) * shared_up).astype(jnp.bfloat16)
        shared_out = jnp.einsum(
            "sf,df->sd",
            shared_act,
            dense_all[:, shared_base + 2 * FFS : shared_base + 3 * FFS],
            preferred_element_type=jnp.float32,
        )
        grad_shared_act = jnp.dot(
            cotangent,
            dense_all[:, shared_base + 2 * FFS : shared_base + 3 * FFS],
            preferred_element_type=jnp.float32,
        )
        shared_sig = jax.nn.sigmoid(shared_gate)
        grad_shared_pre = jnp.concatenate(
            [
                grad_shared_act * shared_up * shared_sig * (1.0 + shared_gate * (1.0 - shared_sig)),
                grad_shared_act * jax.nn.silu(shared_gate),
            ],
            1,
        ).astype(jnp.bfloat16)
        grad_shared = jnp.einsum(
            "sf,df->sd",
            grad_shared_pre,
            dense_all[:, shared_base : shared_base + 2 * FFS],
            preferred_element_type=jnp.float32,
        )
        base_out = residual + shared_out
        my_gates = lax.dynamic_slice_in_dim(
            gate_tables, lax.axis_index("expert") * local_experts, local_experts, 1
        ).transpose(1, 0, 2)
        hot = my_gates > 0.0
        earlier = jnp.einsum(
            "est,ut->esu",
            hot.astype(jnp.bfloat16),
            jnp.tril(jnp.ones((length, length), jnp.bfloat16), -1),
            preferred_element_type=jnp.float32,
        ).astype(jnp.int32)
        place = jnp.where(hot, earlier, -1)
        routed_parts, grad_parts, saved = grouped_experts(
            tokens, cotangents, place, my_gates, expert_all, capacity
        )
    if direct:
        expert_sum, dense_sum, grad_inputs, grad_gains = scatter_grads(
            grad_parts,
            saved,
            dense_all,
            shared_sum,
            cotangent,
            normed_attend,
            attended,
            residual,
            grad_shared,
            projected,
            hidden_in,
            scale_mixer,
            gains_all,
        )
        expert_grad, expert_moment, expert_units, dense_grad, dense_moment, dense_units = moments(
            expert_momentum, expert_sum, dense_momentum, dense_sum
        )
        orth_expert, orth_dense, routed = muon(expert_units, dense_units, routed_parts)
        expert_new, dense_new, block_out, grad_inputs = updated(
            expert_weights,
            orth_expert,
            dense_weights,
            orth_dense,
            base_out,
            routed,
            grad_inputs,
        )
    else:
        routed = lax.psum_scatter(routed_parts, "expert", scatter_dimension=0, tiled=True)
        grad_routed = lax.psum_scatter(grad_parts, "expert", scatter_dimension=0, tiled=True)
        expert_parts = [expert_grads(*kept) for kept in saved]
        expert_grad = lax.psum_scatter(
            sum(part.astype(jnp.float32) for part in expert_parts).astype(jnp.bfloat16),
            "dp",
            scatter_dimension=2,
            tiled=True,
        ).astype(jnp.float32)
        grad_normed = grad_routed.astype(jnp.float32) + grad_shared
        grad_scaled = grad_normed * gain_mixer
        grad_residual = (
            cotangent.astype(jnp.float32)
            + scale_mixer * grad_scaled
            - residual * scale_mixer**3 * jnp.mean(grad_scaled * residual, axis=-1, keepdims=True)
        )
        grad_gain_mixer = jnp.sum(grad_normed * residual * scale_mixer, axis=0)
        grad_attn_low = grad_residual.astype(jnp.bfloat16)
        grad_attended = jnp.dot(
            grad_attn_low, dense_all[:, qkv_end:shared_base], preferred_element_type=jnp.float32
        ).astype(jnp.bfloat16)
        grad_query, grad_key, grad_value = attend_backward(
            query, key_rows, value_rows, grad_attended, saved_stats, block_rows
        )
        grad_projected = jnp.concatenate([grad_query, grad_key, grad_value], 1)
        dense_parts = [
            jnp.einsum("sd,sf->df", left, right, preferred_element_type=jnp.float32)
            for left, right in (
                (normed_attend, grad_projected),
                (grad_attn_low, attended),
                (normed_mixer, grad_shared_pre),
                (cotangent, shared_act),
            )
        ]
        dense_grad = lax.psum_scatter(
            jnp.concatenate([part.astype(jnp.bfloat16) for part in dense_parts], 1),
            ("dp", "expert"),
            scatter_dimension=0,
            tiled=True,
        ).astype(jnp.float32)
        grad_normed_attend = jnp.einsum(
            "sc,dc->sd", grad_projected, dense_all[:, :qkv_end], preferred_element_type=jnp.float32
        )
        grad_scaled_attend = grad_normed_attend * gain_attend
        grad_inputs = (
            grad_residual
            + scale_attend * grad_scaled_attend
            - inputs * scale_attend**3 * jnp.mean(grad_scaled_attend * inputs, axis=-1, keepdims=True)
        )
        grad_gain_attend = jnp.sum(grad_normed_attend * inputs * scale_attend, axis=0)
        block_out = (base_out + routed.astype(jnp.float32)).astype(jnp.bfloat16)
        grad_gains = jnp.stack([grad_gain_attend, grad_gain_mixer], 0)
        dense_moment = MOMENTUM_DECAY * dense_momentum + dense_grad
        expert_moment = MOMENTUM_DECAY * expert_momentum + expert_grad
        stripe, dense_columns = dense_weights.shape
        row_count = stripe * expert_size
        dense_total = dense_columns // FFE
        dense_share = -(-dense_total // expert_size)
        dense_padded = jnp.pad(
            dense_moment.astype(jnp.bfloat16),
            ((0, 0), (0, dense_share * expert_size * FFE - dense_columns)),
        ).reshape(stripe, dense_share * expert_size, FFE).transpose(1, 0, 2)
        expert_units = expert_moment.astype(jnp.bfloat16).reshape(-1, row_count, FFE)
        dense_units = lax.all_to_all(
            dense_padded, "expert", split_axis=0, concat_axis=1, tiled=True
        )
        expert_unit_count = expert_units.shape[0]
        base_count = expert_unit_count + dense_share
        unit_count = -(-base_count // dp_size) * dp_size
        all_units = jnp.concatenate(
            [
                expert_units,
                dense_units,
                jnp.zeros((unit_count - base_count, row_count, FFE), jnp.bfloat16),
            ],
            0,
        )
        owned = lax.all_to_all(all_units, "dp", split_axis=0, concat_axis=1, tiled=True)
        orthogonal = newton_schulz(owned)
        orth_units = lax.all_to_all(orthogonal, "dp", split_axis=1, concat_axis=0, tiled=True)
        orth_expert = orth_units[:expert_unit_count]
        orth_stripe = lax.all_to_all(
            orth_units[expert_unit_count:base_count],
            "expert",
            split_axis=1,
            concat_axis=0,
            tiled=True,
        )
        orth_stripe = (
            orth_stripe[:dense_total]
            .transpose(1, 0, 2)
            .reshape(stripe, dense_columns)
            .astype(jnp.float32)
        )
        keep_factor = 1.0 - LEARN_RATE * WEIGHT_DECAY
        dense_new = keep_factor * dense_weights - LEARN_RATE * orth_stripe
        expert_new = keep_factor * expert_weights - LEARN_RATE * orth_expert.reshape(
            expert_weights.shape
        ).astype(jnp.float32)
    gain_grad = lax.psum_scatter(
        grad_gains, ("dp", "expert"), scatter_dimension=1, tiled=True
    )
    first_new = FIRST_DECAY * gain_first + (1.0 - FIRST_DECAY) * gain_grad
    second_new = SECOND_DECAY * gain_second + (1.0 - SECOND_DECAY) * gain_grad * gain_grad
    step_ratio = (
        first_new
        / (1.0 - FIRST_DECAY**STEP)
        / (jnp.sqrt(second_new / (1.0 - SECOND_DECAY**STEP)) + 1e-08)
    )
    gain_new = norm_gains - GAIN_RATE * step_ratio
    return (
        block_out,
        grad_inputs,
        dense_grad,
        dense_moment,
        dense_new,
        expert_grad,
        expert_moment,
        expert_new,
        gain_grad,
        first_new,
        second_new,
        gain_new,
    )


def solution(mesh):
    in_specs = (
        P(("dp", "expert"), None),
        P(("dp", "expert"), None),
        P(("dp", "expert"), None),
        P(("dp", "expert"), None),
        P(("dp", "expert"), None),
        P(("dp", "expert"), None),
        P("expert", None, "dp", None),
        P("expert", None, "dp", None),
        P(None, ("dp", "expert")),
        P(None, ("dp", "expert")),
        P(None, ("dp", "expert")),
    )
    out_specs = (
        P(("dp", "expert"), None),
        P(("dp", "expert"), None),
        P(("dp", "expert"), None),
        P(("dp", "expert"), None),
        P(("dp", "expert"), None),
        P("expert", None, "dp", None),
        P("expert", None, "dp", None),
        P("expert", None, "dp", None),
        P(None, ("dp", "expert")),
        P(None, ("dp", "expert")),
        P(None, ("dp", "expert")),
        P(None, ("dp", "expert")),
    )
    return jax.shard_map(
        on_device, mesh=mesh, in_specs=in_specs, out_specs=out_specs, check_vma=False
    )
```

```python
import functools

import jax
import jax.numpy as jnp
from jax import lax
from jax.experimental import pallas as pl
from jax.experimental.pallas import tpu as pltpu
from jax.sharding import PartitionSpec as P

HEADS = 12
HD = 128
KVH = 4
FFE = 512
FFS = 1024
NS_STEPS = 5
STEP = 10


POLY_FIRST = 3.4445
POLY_SECOND = -4.775
POLY_THIRD = 2.0315
MOMENTUM_DECAY = 0.95
LEARN_RATE = 0.6
WEIGHT_DECAY = 0.1
GAIN_RATE = 0.8
FIRST_DECAY = 0.9
SECOND_DECAY = 0.95


def norm_scale(values):
    return lax.rsqrt(jnp.mean(values * values, axis=-1, keepdims=True) + 1e-06)


def block_scores(query_block, key_block, first_row, block_rows, last_row):
    score_scale = HD ** (-0.5)
    scores = (
        jnp.einsum("qgrd,kgd->grqk", query_block, key_block, preferred_element_type=jnp.float32)
        * score_scale
    )
    allowed = jnp.arange(last_row)[None, :] <= (first_row + jnp.arange(block_rows))[:, None]
    return jnp.where(allowed, scores, -1e30)


def attend_forward(query, key_rows, value_rows, block_rows):
    length = query.shape[0]
    query_heads = query.reshape(length, KVH, HEADS // KVH, HD)
    key_heads = key_rows.reshape(length, KVH, HD)
    value_heads = value_rows.reshape(length, KVH, HD)
    scores = block_scores(query_heads, key_heads, 0, block_rows, block_rows)
    highest = jnp.max(scores, axis=-1, keepdims=True)
    raised = jnp.exp(scores - highest)
    totals = jnp.sum(raised, axis=-1, keepdims=True)
    weights = (raised / totals).astype(jnp.bfloat16)
    outputs = jnp.einsum("grqk,kgd->qgrd", weights, value_heads, preferred_element_type=jnp.float32)
    saved_stats = [(highest, totals)]
    attended = outputs.reshape(length, HEADS * HD)
    return (attended.astype(jnp.bfloat16), saved_stats)


def attend_backward(query, key_rows, value_rows, grad_attended, saved_stats, block_rows):
    length = query.shape[0]
    score_scale = HD ** (-0.5)
    query_heads = query.reshape(length, KVH, HEADS // KVH, HD)
    grad_heads = grad_attended.reshape(length, KVH, HEADS // KVH, HD)
    key_heads = key_rows.reshape(length, KVH, HD)
    value_heads = value_rows.reshape(length, KVH, HD)
    grad_key = jnp.zeros((length, KVH, HD), jnp.float32)
    grad_value = jnp.zeros((length, KVH, HD), jnp.float32)
    query_parts = []
    for block_index, first_row in enumerate(range(0, length, block_rows)):
        last_row = first_row + block_rows
        scores = block_scores(query_heads, key_heads, first_row, block_rows, last_row)
        highest, totals = saved_stats[block_index]
        weights = jnp.exp(scores - highest) / totals
        grad_weights = jnp.einsum(
            "qgrd,kgd->grqk", grad_heads, value_heads, preferred_element_type=jnp.float32
        )
        inner_sum = jnp.sum(weights * grad_weights, axis=-1, keepdims=True)
        grad_scores = (weights * (grad_weights - inner_sum)).astype(jnp.bfloat16)
        query_parts.append(
            jnp.einsum("grqk,kgd->qgrd", grad_scores, key_heads, preferred_element_type=jnp.float32)
            * score_scale
        )
        grad_key = grad_key.at[:last_row].add(
            jnp.einsum(
                "grqk,qgrd->kgd", grad_scores, query_heads, preferred_element_type=jnp.float32
            )
            * score_scale
        )
        grad_value = grad_value.at[:last_row].add(
            jnp.einsum(
                "grqk,qgrd->kgd",
                weights.astype(jnp.bfloat16),
                grad_heads,
                preferred_element_type=jnp.float32,
            )
        )
    grad_query = query_parts[0].reshape(length, HEADS * HD)
    return (
        grad_query.astype(jnp.bfloat16),
        grad_key.reshape(length, KVH * HD).astype(jnp.bfloat16),
        grad_value.reshape(length, KVH * HD).astype(jnp.bfloat16),
    )


MIB = 2**20
GRAD_STEP = 14
SLOTS = 8
MESH = pl.DeviceIdType.MESH


def matmul(left, right):
    return jnp.dot(left, right, preferred_element_type=jnp.float32)


def matmul_nt(left, right):
    return lax.dot_general(left, right, (((1,), (1,)), ((), ())), preferred_element_type=jnp.float32)


def matmul_tn(left, right):
    return lax.dot_general(left, right, (((0,), (0,)), ((), ())), preferred_element_type=jnp.float32)


def newton_schulz_unit(moment_ref, orthogonal_ref, current, low, identity):
    columns, rows = current.shape
    step = 256
    parts = [pl.ds(index * step, step) for index in range(rows // step)]
    identity[...] = jnp.where(
        lax.broadcasted_iota(jnp.int32, identity.shape, 0)
        == lax.broadcasted_iota(jnp.int32, identity.shape, 1),
        1.0,
        0.0,
    ).astype(jnp.bfloat16)
    squares = jnp.zeros((1, columns), jnp.float32)
    for part in parts:
        values = moment_ref[part, :].astype(jnp.float32)
        squares = squares + jnp.sum(values * values, axis=0, keepdims=True)
    scale = 1.0 / (jnp.sqrt(jnp.sum(squares, axis=1, keepdims=True)) + 1e-07)
    for part in parts:
        scaled = matmul_nt(identity[...], moment_ref[part, :]) * scale
        current[:, part] = scaled
        low[:, part] = scaled.astype(jnp.bfloat16)

    def polynomial():
        gram = matmul_nt(low[...], low[...])
        gram_low = gram.astype(jnp.bfloat16)
        return (POLY_SECOND * gram + POLY_THIRD * matmul(gram_low, gram_low)).astype(jnp.bfloat16)

    @pl.loop(0, NS_STEPS - 1)
    def _(index):
        weights = polynomial()
        for part in parts:
            updated = POLY_FIRST * current[:, part] + matmul(weights, low[:, part])
            current[:, part] = updated
            low[:, part] = updated.astype(jnp.bfloat16)

    weights = polynomial()
    for part in parts:
        updated = POLY_FIRST * current[:, part] + matmul(weights, low[:, part])
        orthogonal_ref[part, :] = updated.T.astype(jnp.bfloat16)


def newton_schulz_kernel(moment_ref, orthogonal_ref, current, low, identity):
    newton_schulz_unit(moment_ref.at[0], orthogonal_ref.at[0], current, low, identity)


def newton_schulz(units):
    count, rows, columns = units.shape
    return pl.pallas_call(
        newton_schulz_kernel,
        grid=(count,),
        in_specs=[pl.BlockSpec((1, rows, columns), lambda unit: (unit, 0, 0))],
        out_specs=pl.BlockSpec((1, rows, columns), lambda unit: (unit, 0, 0)),
        out_shape=jax.ShapeDtypeStruct(units.shape, jnp.bfloat16),
        scratch_shapes=[
            pltpu.VMEM((columns, rows), jnp.float32),
            pltpu.VMEM((columns, rows), jnp.bfloat16),
            pltpu.VMEM((columns, columns), jnp.bfloat16),
        ],
        compiler_params=pltpu.CompilerParams(vmem_limit_bytes=48 * MIB),
        cost_estimate=pl.CostEstimate(
            flops=count * NS_STEPS * 2 * columns * columns * (2 * rows + columns),
            bytes_accessed=count * rows * columns * 4,
            transcendentals=0,
        ),
        name="newton_schulz",
    )(units)


def experts_kernel(
    tokens_ref,
    cotangent_ref,
    place_ref,
    gate_ref,
    weights_ref,
    routed_ref,
    grad_tokens_ref,
    received,
    grad_returned,
    act_ref,
    grad_gate_ref,
    grad_up_ref,
    routed_sum,
    grad_sum,
    chosen,
    weighted,
    grad_received,
):
    expert = pl.program_id(0)
    sequences, slots, length = chosen.shape

    @pl.when(expert == 0)
    def _():
        routed_sum[...] = jnp.zeros_like(routed_sum)
        grad_sum[...] = jnp.zeros_like(grad_sum)

    slot_weights = []
    for sequence in range(sequences):
        rows = pl.ds(sequence * length, length)
        spots = pl.ds(sequence * slots, slots)
        place = place_ref[0, sequence : sequence + 1, :]
        gate = gate_ref[0, sequence : sequence + 1, :]
        hot = lax.broadcasted_iota(jnp.int32, (slots, length), 0) == place
        slot_weight = jnp.sum(jnp.where(hot, gate, 0.0), axis=1, keepdims=True)
        slot_weights.append(slot_weight)
        hot_low = jnp.where(hot, 1.0, 0.0).astype(jnp.bfloat16)
        chosen[sequence] = hot_low
        received[0, spots, :] = matmul(hot_low, tokens_ref[rows, :]).astype(jnp.bfloat16)
        grad_returned[0, spots, :] = (
            matmul(hot_low, cotangent_ref[rows, :]) * slot_weight
        ).astype(jnp.bfloat16)
    tokens = received[0]
    grad_out = grad_returned[0]
    gate_pre = matmul(tokens, weights_ref[0, 0])
    up_pre = matmul(tokens, weights_ref[0, 1])
    gate_sig = jax.nn.sigmoid(gate_pre)
    gate_act = gate_pre * gate_sig
    act = (gate_act * up_pre).astype(jnp.bfloat16)
    act_ref[0] = act
    out = matmul_nt(act, weights_ref[0, 2]).astype(jnp.bfloat16).astype(jnp.float32)
    for sequence in range(sequences):
        spots = slice(sequence * slots, (sequence + 1) * slots)
        weighted[spots, :] = (out[spots] * slot_weights[sequence]).astype(jnp.bfloat16)
    grad_act = matmul(grad_out, weights_ref[0, 2])
    grad_gate = (grad_act * up_pre * gate_sig * (1.0 + gate_pre * (1.0 - gate_sig))).astype(
        jnp.bfloat16
    )
    grad_up = (grad_act * gate_act).astype(jnp.bfloat16)
    grad_gate_ref[0] = grad_gate
    grad_up_ref[0] = grad_up
    grad_received[...] = (
        matmul_nt(grad_gate, weights_ref[0, 0]) + matmul_nt(grad_up, weights_ref[0, 1])
    ).astype(jnp.bfloat16)
    for sequence in range(sequences):
        rows = pl.ds(sequence * length, length)
        spots = pl.ds(sequence * slots, slots)
        routed_sum[rows, :] += matmul_tn(chosen[sequence], weighted[spots, :])
        grad_sum[rows, :] += matmul_tn(chosen[sequence], grad_received[spots, :])

    @pl.when(expert == pl.num_programs(0) - 1)
    def _():
        routed_ref[...] = routed_sum[...].astype(jnp.bfloat16)
        grad_tokens_ref[...] = grad_sum[...].astype(jnp.bfloat16)


def run_experts(tokens, cotangents, place, gates, weights, capacity):
    experts, sequences, length = place.shape
    total, width = tokens.shape
    hidden = weights.shape[-1]
    slots = -(-capacity // 16) * 16
    spots = sequences * slots
    whole = pl.BlockSpec((total, width), lambda expert: (0, 0))
    table = pl.BlockSpec((1, sequences, length), lambda expert: (expert, 0, 0))
    matrices = pl.BlockSpec((1, 3, width, hidden), lambda expert: (expert, 0, 0, 0))
    wide = pl.BlockSpec((1, spots, width), lambda expert: (expert, 0, 0))
    narrow = pl.BlockSpec((1, spots, hidden), lambda expert: (expert, 0, 0))
    return pl.pallas_call(
        experts_kernel,
        grid=(experts,),
        in_specs=[whole, whole, table, table, matrices],
        out_specs=[whole, whole, wide, wide, narrow, narrow, narrow],
        out_shape=[
            *[jax.ShapeDtypeStruct((total, width), jnp.bfloat16)] * 2,
            *[jax.ShapeDtypeStruct((experts, spots, width), jnp.bfloat16)] * 2,
            *[jax.ShapeDtypeStruct((experts, spots, hidden), jnp.bfloat16)] * 3,
        ],
        scratch_shapes=[
            pltpu.VMEM((total, width), jnp.float32),
            pltpu.VMEM((total, width), jnp.float32),
            pltpu.VMEM((sequences, slots, length), jnp.bfloat16),
            pltpu.VMEM((spots, width), jnp.bfloat16),
            pltpu.VMEM((spots, width), jnp.bfloat16),
        ],
        compiler_params=pltpu.CompilerParams(vmem_limit_bytes=63 * MIB),
        cost_estimate=pl.CostEstimate(
            flops=experts * (12 * spots * width * hidden + 8 * spots * length * width),
            bytes_accessed=2 * weights.size + 16 * tokens.size,
            transcendentals=experts * spots * hidden,
        ),
        name="experts",
    )(tokens, cotangents, place, gates, weights)


def expert_grads_kernel(
    received_ref, grad_returned_ref, act_ref, grad_gate_ref, grad_up_ref, grad_weights_ref
):
    received, grad_returned = received_ref[0], grad_returned_ref[0]
    grad_weights_ref[0, 0] = matmul_tn(received, grad_gate_ref[0]).astype(jnp.bfloat16)
    grad_weights_ref[0, 1] = matmul_tn(received, grad_up_ref[0]).astype(jnp.bfloat16)
    grad_weights_ref[0, 2] = matmul_tn(grad_returned, act_ref[0]).astype(jnp.bfloat16)


def expert_grads(received, grad_returned, act, grad_gate, grad_up):
    experts, spots, width = received.shape
    hidden = act.shape[-1]
    wide = pl.BlockSpec((1, spots, width), lambda expert: (expert, 0, 0))
    narrow = pl.BlockSpec((1, spots, hidden), lambda expert: (expert, 0, 0))
    return pl.pallas_call(
        expert_grads_kernel,
        grid=(experts,),
        in_specs=[wide, wide, narrow, narrow, narrow],
        out_specs=pl.BlockSpec((1, 3, width, hidden), lambda expert: (expert, 0, 0, 0)),
        out_shape=jax.ShapeDtypeStruct((experts, 3, width, hidden), jnp.bfloat16),
        compiler_params=pltpu.CompilerParams(vmem_limit_bytes=48 * MIB),
        name="expert_grads",
    )(received, grad_returned, act, grad_gate, grad_up)


def grouped_experts(tokens, cotangents, place, gates, weights, capacity):
    experts, sequences, length = place.shape
    group = min(4, sequences)
    routed, grad_tokens, saved = [], [], []
    for first in range(0, sequences, group):
        rows = slice(first * length, (first + group) * length)
        part = slice(first, first + group)
        routed_part, grad_part, *kept = run_experts(
            tokens[rows], cotangents[rows], place[:, part], gates[:, part], weights, capacity
        )
        routed.append(routed_part)
        grad_tokens.append(grad_part)
        saved.append(kept)

    def joined(parts):
        return parts[0] if len(parts) == 1 else jnp.concatenate(parts, 0)

    return joined(routed), joined(grad_tokens), saved


def flipped(index, bit):
    unit = 2**bit
    return index + unit * (1 - 2 * ((index // unit) % 2))


class Links:
    def __init__(self, semaphores):
        self.semaphores = semaphores
        self.taken = 0
        self.dp = lax.axis_index("dp")
        self.z = lax.axis_index("expert")
        self.upper = self.z // 2
        self.position = self.z * (1 - 2 * self.upper) + 3 * self.upper
        self.step = 1 - 2 * self.upper
        self.core = (flipped(self.dp, 0), self.z)
        self.along_x = (flipped(self.dp, 1), self.z)
        self.along_y = (flipped(self.dp, 2), self.z)
        self.inward = (self.dp, self.z + self.step)
        self.outward = (self.dp, self.z - self.step)
        self.further = (self.dp, self.z + 2 * self.step)
        self.pending = []

    def order(self, index):
        near = (self.position + index) % 2 if index < 2 else index
        return near * self.step + 3 * self.upper

    def take(self, count=1):
        first = self.taken
        self.taken += count
        return first

    def barrier(self):
        barrier = pltpu.get_barrier_semaphore()
        for device in (self.core, self.along_x, self.along_y, self.inward, self.further):
            pl.semaphore_signal(barrier, inc=1, device_id=device, device_id_type=MESH)

        @pl.when(self.position == 1)
        def _():
            pl.semaphore_signal(barrier, inc=1, device_id=self.outward, device_id_type=MESH)

        pl.semaphore_wait(barrier, 5 + self.position)

    def copy_with(self, source, target, send, receive, device):
        return pltpu.make_async_remote_copy(
            src_ref=source,
            dst_ref=target,
            send_sem=send,
            recv_sem=receive,
            device_id=device,
            device_id_type=MESH,
        )

    def copy(self, source, target, send, receive, device):
        return self.copy_with(
            source, target, self.semaphores.at[send], self.semaphores.at[receive], device
        )

    def send(self, source, target, receive, device, position=None):
        copy = self.copy(source, target, self.take(), receive, device)
        if position is None:
            copy.start()
        else:
            pl.when(self.position == position)(copy.start)
        self.pending.append((copy, position))

    def arrived(self, region, receive):
        self.copy(region, region, receive, receive, self.core).wait_recv()

    def finish(self):
        for copy, position in self.pending:
            if position is None:
                copy.wait_send()
            else:
                pl.when(self.position == position)(copy.wait_send)


class LineGather:
    def __init__(self, links, region, own=None):
        self.links, self.region = links, region
        self.receives = links.take(4)
        self.own = region(links.z) if own is None else own

    def start(self):
        links = self.links
        target, receive = self.region(links.z), self.receives + links.z
        links.send(self.own, target, receive, links.further)
        links.send(self.own, target, receive, links.inward)
        links.send(self.own, target, receive, links.outward, 1)

    def relay(self):
        links = self.links
        source = links.order(3)
        block = self.region(source)

        @pl.when(links.position == 1)
        def _():
            links.arrived(block, self.receives + source)

        links.send(block, block, self.receives + source, links.outward, 1)

    def arrive(self, index):
        links = self.links
        source = links.order(index)

        def wait():
            links.arrived(self.region(source), self.receives + source)

        if index < 3:
            wait()
        else:
            pl.when(links.position == 0)(wait)


class PlaneGather:
    def __init__(self, links, region, parity, own=None):
        self.links, self.region, self.parity = links, region, parity
        self.receives = links.take(7)
        self.own = region(links.dp) if own is None else own

    def start(self):
        links, first = self.links, self.receives
        target = self.region(links.dp)
        links.send(self.own, target, first, links.along_x)
        links.send(self.own, target, first + 1, links.along_y)
        links.send(self.own, target, first + 2, links.core)

    def forward(self):
        links, first = self.links, self.receives
        across = self.region(flipped(links.dp, 1))
        links.arrived(across, first)
        if self.parity == 0:
            links.send(across, across, first + 3, links.along_y)
        links.send(across, across, first + 4, links.core)
        along = self.region(flipped(links.dp, 2))
        links.arrived(along, first + 1)
        if self.parity == 1:
            links.send(along, along, first + 3, links.along_x)
        links.send(along, along, first + 5, links.core)

    def last(self):
        links, first = self.links, self.receives
        corner = self.region(flipped(flipped(links.dp, 1), 2))
        links.arrived(corner, first + 3)
        links.send(corner, corner, first + 6, links.core)

    def complete(self):
        links, first = self.links, self.receives
        other = flipped(links.dp, 0)
        links.arrived(self.region(other), first + 2)
        links.arrived(self.region(flipped(other, 1)), first + 4)
        links.arrived(self.region(flipped(other, 2)), first + 5)
        links.arrived(self.region(flipped(flipped(other, 1), 2)), first + 6)


ANY = pl.BlockSpec(memory_space=pl.ANY)


def front_kernel(
    stripe_ref,
    gates_ref,
    masters_ref,
    hidden_ref,
    cotangent_ref,
    dense_ref,
    weights_ref,
    cotangents_ref,
    tokens_ref,
    routed_parts_ref,
    grad_parts_ref,
    received_ref,
    grad_returned_ref,
    act_ref,
    grad_gate_ref,
    grad_up_ref,
    normed_attend_out,
    projected_out,
    attended_out,
    residual_out,
    grad_shared_out,
    base_out,
    shared_sum_ref,
    scale_ref,
    gains_ref,
    normed_attend_ref,
    projected_ref,
    attended_ref,
    residual_ref,
    grad_shared_ref,
    base_ref,
    normed_mixer_ref,
    shared_act_ref,
    grad_shared_pre_ref,
    matrices,
    extra,
    all_gates,
    places,
    my_gates,
    chosen,
    forward_slots,
    backward_slots,
    narrow,
    pair_sum,
    corner_x,
    corner_y,
    side_x,
    side_y,
    semaphores,
    shard_out,
    shard_in,
    local,
    load_sems,
    expert_sems,
    shared_sems,
    keep_sems,
):
    links = Links(semaphores)
    stripe, columns = stripe_ref.shape
    length, width = hidden_ref.shape
    panels, rows, hidden = masters_ref.shape
    experts = panels // 3
    slots = chosen.shape[1] // experts
    first_panels = 8
    middle = first_panels * hidden + extra.shape[1]
    halves = ((0, middle), (middle, columns - middle))
    query_width = HEADS * HD
    kv_width = KVH * HD
    ahead = 4

    def dense_region(dp, z, half):
        first, count = halves[half]
        row = pl.multiple_of((dp * 4 + z) * stripe, stripe)
        return dense_ref.at[pl.ds(row, stripe), pl.ds(first, count)]

    def own(half):
        first, count = halves[half]
        return stripe_ref.at[:, pl.ds(first, count)]

    def sequence(ref, z):
        return ref.at[pl.ds(pl.multiple_of(z * length, length), length), :]

    def shard_region(dp, panel):
        return weights_ref.at[panel, pl.ds(pl.multiple_of(dp * rows, rows), rows), :]

    lines = [
        LineGather(links, functools.partial(dense_region, links.dp, half=half), own(half))
        for half in range(2)
    ]
    cotangents = LineGather(links, functools.partial(sequence, cotangents_ref), cotangent_ref)
    tokens = LineGather(links, functools.partial(sequence, tokens_ref), normed_mixer_ref)
    gates = LineGather(links, lambda z: all_gates.at[z], gates_ref)
    planes = [
        [
            PlaneGather(
                links,
                functools.partial(dense_region, z=links.order(index), half=half),
                index % 2,
                own(half) if index == 0 else None,
            )
            for index in range(4)
        ]
        for half in range(2)
    ]

    def shard_copy(kind, panel, source_dp, device):
        block = shard_region(source_dp, panel)
        return links.copy_with(
            block, block, shard_out.at[kind, panel], shard_in.at[kind, panel], device
        )

    dp = links.dp
    dp_core, dp_x, dp_y = flipped(dp, 0), flipped(dp, 1), flipped(dp, 2)
    dp_corner = flipped(dp_x, 2)

    def hop(kind, panel):
        source, device = (
            (dp, links.along_x),
            (dp, links.along_y),
            (dp, links.core),
            None,
            (dp_x, links.core),
            (dp_y, links.core),
            (dp_corner, links.core),
        )[kind]
        return shard_copy(kind, panel, source, device)

    def corner_copy(panel, parity):
        if parity == 0:
            return shard_copy(3, panel, dp_x, links.along_y)
        return shard_copy(3, panel, dp_y, links.along_x)

    def shard_arrived(kind, panel, source_dp):
        shard_copy(kind, panel, source_dp, links.core).wait_recv()

    def shard_start(panel):
        for kind in range(3):
            hop(kind, panel).start()

    def shard_forward(panel):
        shard_arrived(0, panel, dp_x)
        pl.when(panel % 2 == 0)(corner_copy(panel, 0).start)
        hop(4, panel).start()
        shard_arrived(1, panel, dp_y)
        pl.when(panel % 2 == 1)(corner_copy(panel, 1).start)
        hop(5, panel).start()

    def shard_last(panel):
        shard_arrived(3, panel, dp_corner)
        hop(6, panel).start()

    def shard_complete(panel):
        shard_arrived(2, panel, dp_core)
        shard_arrived(4, panel, flipped(dp_core, 1))
        shard_arrived(5, panel, flipped(dp_core, 2))
        shard_arrived(6, panel, flipped(flipped(dp_core, 1), 2))

    def shard_finish(panel):
        for kind in (0, 1, 2, 4, 5, 6):
            hop(kind, panel).wait_send()
        corner_copy(panel, 0).wait_send()

    def exchange(panel):
        shard_forward(panel)
        if panel + ahead < panels:
            shard_start(panel + ahead)
        if panel >= 3:
            shard_last(panel - 3)

    local_copies = [
        pltpu.make_async_copy(source, target, local.at[index])
        for index, (source, target) in enumerate(
            (
                (
                    stripe_ref,
                    dense_ref.at[
                        pl.ds(pl.multiple_of((links.dp * 4 + links.z) * stripe, stripe), stripe), :
                    ],
                ),
                (gates_ref, all_gates.at[links.z]),
                (cotangent_ref, sequence(cotangents_ref, links.z)),
            )
        )
    ]
    token_copy = pltpu.make_async_copy(
        normed_mixer_ref, sequence(tokens_ref, links.z), local.at[3]
    )

    def dense_column(panel):
        return panel * hidden + (0 if panel < first_panels else extra.shape[1])

    loads = [
        pltpu.make_async_copy(
            dense_ref.at[:, pl.ds(dense_column(panel), hidden)],
            matrices.at[panel],
            load_sems.at[panel],
        )
        for panel in range(14)
    ]
    extra_load = pltpu.make_async_copy(
        dense_ref.at[:, pl.ds(first_panels * hidden, extra.shape[1])], extra, load_sems.at[14]
    )

    def half_columns(panel):
        return pl.ds(pl.multiple_of(panel % 2 * hidden, hidden), hidden)

    def master_load(panel):
        return pltpu.make_async_copy(
            masters_ref.at[panel],
            grad_shared_ref.at[pl.ds(0, rows), half_columns(panel)],
            expert_sems.at[0, panel % 2],
        )

    def master_store(panel):
        return pltpu.make_async_copy(
            shared_act_ref.at[pl.ds(0, rows), half_columns(panel)],
            shard_region(dp, panel),
            expert_sems.at[1, panel % 2],
        )

    master_load(0).start()
    links.barrier()
    lines[0].start()
    planes[0][0].start()
    lines[1].start()
    gates.start()
    for copy in local_copies:
        copy.start()

    def round_masters(first, last):
        @pl.loop(first, last)
        def _(panel):
            master_load(panel).wait()

            @pl.when(panel + 1 < panels)
            def _():
                master_load(panel + 1).start()

            @pl.when(panel >= 2)
            def _():
                master_store(panel - 2).wait()

            shared_act_ref[:rows, half_columns(panel)] = grad_shared_ref[
                :rows, half_columns(panel)
            ].astype(jnp.bfloat16)
            master_store(panel).start()

    lines[0].arrive(1)
    planes[0][1].start()
    lines[0].arrive(2)
    planes[0][2].start()
    round_masters(0, panels // 3)
    for panel in range(2):
        shard_start(panel)
    planes[0][0].forward()
    lines[0].relay()
    lines[0].arrive(3)
    planes[0][3].start()
    planes[0][1].forward()
    lines[1].relay()
    round_masters(panels // 3, panels)
    for panel in (panels - 2, panels - 1):
        master_store(panel).wait()
    for panel in range(2, ahead):
        shard_start(panel)
    planes[1][0].start()
    planes[0][2].forward()
    lines[1].arrive(1)
    planes[1][1].start()
    planes[0][3].forward()
    cotangents.start()
    gates.relay()
    lines[1].arrive(2)
    planes[1][2].start()
    for plane in planes[0]:
        plane.last()
    planes[1][0].forward()
    for plane in planes[0]:
        plane.complete()
    local_copies[0].wait()
    extra_load.start()
    for copy in loads[:first_panels]:
        copy.start()

    rows_step = 32

    def norm_rows(source, gain, scale_out, target):
        @pl.loop(0, length // rows_step)
        def _(index):
            part = pl.ds(index * rows_step, rows_step)
            values = source[part, :].astype(jnp.float32)
            scale = lax.rsqrt(jnp.mean(values * values, axis=-1, keepdims=True) + 1e-06)
            if scale_out is not None:
                scale_out[part, :] = scale
            target[part, :] = (values * scale * gains_ref[gain : gain + 1, :]).astype(jnp.bfloat16)

    def project():
        extra_load.wait()
        gains_ref[...] = extra[...].astype(jnp.float32).T[:8, :]
        norm_rows(hidden_ref, 0, None, normed_attend_ref)
        for panel in range(5):
            loads[panel].wait()
            projected_ref[:, panel * hidden : (panel + 1) * hidden] = matmul(
                normed_attend_ref[...], matrices[panel]
            ).astype(jnp.bfloat16)

    def attend(group):
        key_rows = projected_ref[:, query_width + group * HD : query_width + (group + 1) * HD]
        value_first = query_width + kv_width + group * HD
        value_rows = projected_ref[:, value_first : value_first + HD]
        row = lax.broadcasted_iota(jnp.int32, (length, length), 0)
        column = lax.broadcasted_iota(jnp.int32, (length, length), 1)
        per_group = HEADS // KVH
        for head in range(group * per_group, (group + 1) * per_group):
            spot = slice(head * HD, (head + 1) * HD)
            scores = matmul_nt(projected_ref[:, spot], key_rows) * HD ** (-0.5)
            scores = jnp.where(column <= row, scores, -1e30)
            raised = jnp.exp(scores - jnp.max(scores, axis=-1, keepdims=True))
            shares = (raised / jnp.sum(raised, axis=-1, keepdims=True)).astype(jnp.bfloat16)
            attended_ref[:, spot] = matmul(shares, value_rows).astype(jnp.bfloat16)

    def join():
        for part in range(3):
            loads[5 + part].wait()
            update = matmul_nt(
                attended_ref[:, part * hidden : (part + 1) * hidden], matrices[5 + part]
            )
            if part == 0:
                residual_ref[...] = hidden_ref[...].astype(jnp.float32) + update
            else:
                residual_ref[...] += update
        norm_rows(residual_ref, 1, scale_ref, normed_mixer_ref)
        tokens.start()
        token_copy.start()

    def shared(part):
        spot = slice(part * hidden, (part + 1) * hidden)
        for panel in (8, 10, 12):
            loads[panel + part].wait()
        gate = matmul(normed_mixer_ref[...], matrices[8 + part])
        up = matmul(normed_mixer_ref[...], matrices[10 + part])
        sig = jax.nn.sigmoid(gate)
        gate_act = gate * sig
        shared_act_ref[:, spot] = (gate_act * up).astype(jnp.bfloat16)
        grad_act = matmul(cotangent_ref[...], matrices[12 + part])
        grad_shared_pre_ref[:, spot] = (
            grad_act * up * sig * (1.0 + gate * (1.0 - sig))
        ).astype(jnp.bfloat16)
        up_spot = slice((2 + part) * hidden, (3 + part) * hidden)
        grad_shared_pre_ref[:, up_spot] = (grad_act * gate_act).astype(jnp.bfloat16)

    def shared_back(part):
        spot = slice(part * hidden, (part + 1) * hidden)
        up_spot = slice((2 + part) * hidden, (3 + part) * hidden)
        grad = matmul_nt(grad_shared_pre_ref[:, spot], matrices[8 + part]) + matmul_nt(
            grad_shared_pre_ref[:, up_spot], matrices[10 + part]
        )
        out = matmul_nt(shared_act_ref[:, spot], matrices[12 + part])
        if part == 0:
            grad_shared_ref[...] = grad
            base_ref[...] = residual_ref[...] + out
        else:
            grad_shared_ref[...] += grad
            base_ref[...] += out

    kept = [
        pltpu.make_async_copy(source, target, keep_sems.at[index])
        for index, (source, target) in enumerate(
            (
                (normed_attend_ref, normed_attend_out),
                (projected_ref, projected_out),
                (attended_ref, attended_out),
                (residual_ref, residual_out),
                (grad_shared_ref, grad_shared_out),
                (base_ref, base_out),
            )
        )
    ]

    def place_slots():
        local_copies[1].wait()
        before = (
            lax.broadcasted_iota(jnp.int32, (length, length), 0)
            < lax.broadcasted_iota(jnp.int32, (length, length), 1)
        )
        earlier_mask = jnp.where(before, 1.0, 0.0).astype(jnp.bfloat16)
        for source in range(4):
            gate = all_gates[source, links.z]
            hot = gate > 0.0
            earlier = matmul(jnp.where(hot, 1.0, 0.0).astype(jnp.bfloat16), earlier_mask)
            place = jnp.where(hot, earlier, -1.0).astype(jnp.int32)
            for expert in range(experts):
                places[expert, source : source + 1, :] = place[expert : expert + 1, :]
                my_gates[expert, source : source + 1, :] = gate[expert : expert + 1, :]

    core, chip = dp % 2, dp // 2
    chip_x, chip_y = flipped(chip, 0), flipped(chip, 1)
    chip_corner = flipped(chip_x, 1)
    shared_panels = pair_sum.shape[0]
    half = rows // 2
    quarter = width // 4

    ring = matrices.at[13]

    def ring_rows(index, which):
        return pl.ds(pl.multiple_of((2 * index + which) * rows, rows), rows)

    def pair_copy(panel, index):
        return links.copy_with(
            ring.at[ring_rows(index, 1 - core)],
            pair_sum.at[panel, index],
            shared_sems.at[0, 0, panel],
            shared_sems.at[1, 0, panel],
            links.core,
        )

    def shared_copy(kind, panel):
        source, target, device = (
            (pair_sum.at[panel], pair_sum.at[panel], links.core),
            (pair_sum.at[panel, chip_corner, pl.ds(0, half)], corner_x.at[panel], links.along_x),
            (pair_sum.at[panel, chip_corner, pl.ds(half, half)], corner_y.at[panel], links.along_y),
            (pair_sum.at[panel, chip_x], side_x.at[panel], links.along_x),
            (pair_sum.at[panel, chip_y], side_y.at[panel], links.along_y),
        )[kind]
        return links.copy_with(
            source, target, shared_sems.at[0, kind, panel], shared_sems.at[1, kind, panel], device
        )

    def shared_fill(panel):
        left_ref = normed_mixer_ref if panel < 4 else cotangent_ref
        right_ref = grad_shared_pre_ref if panel < 4 else shared_act_ref
        first = (panel if panel < 4 else panel - 4) * hidden
        right = right_ref[:, first : first + hidden]
        for index in range(4):
            part = matmul_tn(left_ref[:, index * quarter : (index + 1) * quarter], right)
            ring[index * quarter : (index + 1) * quarter, :] = part.astype(jnp.bfloat16)
        for index in range(4):
            pair_copy(panel, index).start()

    def shared_pair(panel):
        shared_copy(0, panel).wait()
        for index in range(4):
            pair_sum[panel, index] = (
                pair_sum[panel, index].astype(jnp.float32)
                + ring[ring_rows(index, core), :].astype(jnp.float32)
            ).astype(jnp.bfloat16)

    def shared_corners(panel):
        for kind in (1, 2):
            shared_copy(kind, panel).start()

    def shared_sides(panel):
        for kind in (1, 2):
            shared_copy(kind, panel).wait()
        pair_sum[panel, chip_y, :half] = (
            pair_sum[panel, chip_y, :half].astype(jnp.float32)
            + corner_x[panel].astype(jnp.float32)
        ).astype(jnp.bfloat16)
        pair_sum[panel, chip_x, half:] = (
            pair_sum[panel, chip_x, half:].astype(jnp.float32)
            + corner_y[panel].astype(jnp.float32)
        ).astype(jnp.bfloat16)
        for kind in (3, 4):
            shared_copy(kind, panel).start()

    def shared_total(panel):
        for kind in (3, 4):
            shared_copy(kind, panel).wait()
        value = (
            pair_sum[panel, chip].astype(jnp.float32)
            + side_x[panel].astype(jnp.float32)
            + side_y[panel].astype(jnp.float32)
        )
        matrices[12, pl.ds(panel % 2 * rows, rows), :] = value.astype(jnp.bfloat16)

    def shared_store(panel):
        return pltpu.make_async_copy(
            matrices.at[12, pl.ds(panel % 2 * rows, rows)],
            shared_sum_ref.at[panel],
            local.at[4 + panel % 2],
        )

    project()
    lines[1].arrive(3)
    planes[1][3].start()
    planes[1][1].forward()
    attend(0)
    attend(1)
    planes[1][2].forward()
    attend(2)
    attend(3)
    planes[1][3].forward()
    cotangents.relay()
    join()
    for plane in planes[1]:
        plane.last()
    for index in range(1, 4):
        gates.arrive(index)
    place_slots()
    for plane in planes[1]:
        plane.complete()
    for copy in loads[first_panels:]:
        copy.start()
    exchange(0)
    shared(0)
    exchange(1)
    shared(1)
    exchange(2)
    shared_back(0)
    exchange(3)
    shared_back(1)
    for copy in kept:
        copy.start()
    exchange(4)
    shared_fill(0)
    tokens.relay()
    for panel in range(5, 11):
        exchange(panel)
        shared_pair(panel - 5)
        shared_corners(panel - 5)
        if panel < 10:
            shared_fill(panel - 4)
    for index in range(1, 4):
        cotangents.arrive(index)
        tokens.arrive(index)
    local_copies[2].wait()
    token_copy.wait()
    token_loads = [
        pltpu.make_async_copy(
            source.at[:, pl.ds(part * hidden, hidden)],
            matrices.at[first + part, pl.ds(0, 4 * length)],
            load_sems.at[first + part],
        )
        for first, source in ((6, tokens_ref), (9, cotangents_ref))
        for part in range(3)
    ]
    for copy in token_loads:
        copy.start()
    slot_iota = lax.broadcasted_iota(jnp.int32, (slots, length), 0)

    def slot_gate(expert, source):
        hot = slot_iota == places[expert, pl.ds(source, 1), :]
        return jnp.sum(
            jnp.where(hot, my_gates[expert, pl.ds(source, 1), :], 0.0), axis=1, keepdims=True
        )

    for source in range(4):
        for expert in range(experts):
            hot = slot_iota == places[expert, source : source + 1, :]
            chosen[source, expert * slots : (expert + 1) * slots, :] = jnp.where(
                hot, 1.0, 0.0
            ).astype(jnp.bfloat16)
    exchange(11)
    for copy in token_loads:
        copy.wait()

    @pl.loop(0, 4)
    def _(source):
        part = pl.ds(source * length, length)
        spots = pl.ds(pl.multiple_of(source * slots, slots), slots)
        slot_gates = [slot_gate(expert, source) for expert in range(experts)]
        for block in range(3):
            spot = pl.ds(block * hidden, hidden)
            token_slots = matmul(chosen[source], matrices[6 + block, part, :])
            grad_slots = matmul(chosen[source], matrices[9 + block, part, :])
            for expert in range(experts):
                rows_of = slice(expert * slots, (expert + 1) * slots)
                forward_slots[expert, spots, spot] = token_slots[rows_of].astype(jnp.bfloat16)
                backward_slots[expert, spots, spot] = (
                    grad_slots[rows_of] * slot_gates[expert]
                ).astype(jnp.bfloat16)

    def slot_stores(expert):
        return [
            pltpu.make_async_copy(
                source.at[expert], target.at[expert], expert_sems.at[2 + index, expert]
            )
            for index, (source, target) in enumerate(
                ((forward_slots, received_ref), (backward_slots, grad_returned_ref))
            )
        ]

    def narrow_stores(expert):
        buffer = expert % 2
        return [
            pltpu.make_async_copy(
                narrow.at[buffer, index], target.at[expert], expert_sems.at[4 + buffer, index]
            )
            for index, target in enumerate((act_ref, grad_gate_ref, grad_up_ref))
        ]

    def weight_loads(expert):
        buffer = expert % 2
        return [
            pltpu.make_async_copy(
                weights_ref.at[3 * expert + matrix],
                matrices.at[3 * buffer + matrix],
                expert_sems.at[6 + buffer, matrix],
            )
            for matrix in range(3)
        ]

    def fetch(expert):
        for matrix, copy in enumerate(weight_loads(expert)):
            shard_complete(3 * expert + matrix)
            copy.start()

    for expert in range(experts):
        for copy in slot_stores(expert):
            copy.start()
    fetch(0)

    @pl.loop(0, experts)
    def _(expert):
        buffer = expert % 2
        loaded = weight_loads(expert)

        @pl.when(expert >= 2)
        def _():
            for copy in narrow_stores(expert - 2):
                copy.wait()

        received = forward_slots[expert]
        grad_out = backward_slots[expert]
        loaded[0].wait()
        gate_pre = matmul(received, matrices[3 * buffer])
        loaded[1].wait()
        up_pre = matmul(received, matrices[3 * buffer + 1])
        loaded[2].wait()
        grad_act = matmul(grad_out, matrices[3 * buffer + 2])
        gate_sig = jax.nn.sigmoid(gate_pre)
        gate_act = gate_pre * gate_sig
        act = (gate_act * up_pre).astype(jnp.bfloat16)
        grad_gate = (grad_act * up_pre * gate_sig * (1.0 + gate_pre * (1.0 - gate_sig))).astype(
            jnp.bfloat16
        )
        grad_up = (grad_act * gate_act).astype(jnp.bfloat16)
        narrow[buffer, 0] = act
        narrow[buffer, 1] = grad_gate
        narrow[buffer, 2] = grad_up
        for copy in narrow_stores(expert):
            copy.start()
        for copy in slot_stores(expert):
            copy.wait()
        slot_gates = jnp.concatenate([slot_gate(expert, source) for source in range(4)], 0)
        for block in range(3):
            rows_of = pl.ds(block * hidden, hidden)
            spot = pl.ds(block * hidden, hidden)
            out = matmul_nt(act, matrices[3 * buffer + 2, rows_of, :]).astype(jnp.bfloat16)
            forward_slots[expert, :, spot] = (
                out.astype(jnp.float32) * slot_gates
            ).astype(jnp.bfloat16)
            backward_slots[expert, :, spot] = (
                matmul_nt(grad_gate, matrices[3 * buffer, rows_of, :])
                + matmul_nt(grad_up, matrices[3 * buffer + 1, rows_of, :])
            ).astype(jnp.bfloat16)

        later = (
            (lambda: exchange(12),),
            (lambda: exchange(13),),
            (lambda: exchange(14),),
            (
                lambda: exchange(15),
                lambda: exchange(16),
                lambda: shard_last(14),
                lambda: shared_sides(0),
                lambda: shared_sides(1),
            ),
            (
                lambda: shard_forward(17),
                lambda: shared_sides(2),
                lambda: shared_sides(3),
                lambda: shared_sides(4),
                lambda: shared_sides(5),
                lambda: shard_last(15),
                lambda: shard_last(16),
                lambda: shard_last(17),
            ),
        )
        for done, calls in enumerate(later):

            @pl.when(expert == done)
            def _():
                for call in calls:
                    call()

        @pl.when(expert + 1 < experts)
        def _():
            fetch(expert + 1)

    for expert in (experts - 2, experts - 1):
        for copy in narrow_stores(expert):
            copy.wait()
    out_copies = []
    for first, values, target in ((0, backward_slots, grad_parts_ref), (3, forward_slots, routed_parts_ref)):
        for block in range(3):
            spot = slice(block * hidden, (block + 1) * hidden)
            for source in range(4):
                slots_of = jnp.concatenate(
                    [
                        values[expert, source * slots : (source + 1) * slots, spot]
                        for expert in range(experts)
                    ],
                    0,
                )
                matrices[first + block, source * length : (source + 1) * length, :] = matmul_tn(
                    chosen[source], slots_of
                ).astype(jnp.bfloat16)
            out_copies.append(
                pltpu.make_async_copy(
                    matrices.at[first + block, pl.ds(0, 4 * length)],
                    target.at[:, pl.ds(block * hidden, hidden)],
                    load_sems.at[first + block],
                )
            )
            out_copies[-1].start()
    @pl.loop(0, panels)
    def _(panel):
        shard_finish(panel)

    for panel in range(shared_panels):
        if panel >= 2:
            shared_store(panel - 2).wait()
        shared_total(panel)
        shared_store(panel).start()
    for panel in (shared_panels - 2, shared_panels - 1):
        shared_store(panel).wait()
    for copy in (*kept, *out_copies):
        copy.wait()

    links.finish()


def front(stripe, gates, masters, hidden_in, cotangent, slots):
    length, width = cotangent.shape
    stripe_rows, columns = stripe.shape
    panels, rows, hidden = masters.shape
    experts = panels // 3
    low, full = jnp.bfloat16, jnp.float32
    vmem = pl.BlockSpec(memory_space=pltpu.VMEM)
    query_width = HEADS * HD
    spots = 4 * slots
    return pl.pallas_call(
        front_kernel,
        in_specs=[ANY] * 3 + [vmem] * 2,
        out_specs=[ANY] * 18 + [vmem] * 2,
        out_shape=[
            jax.ShapeDtypeStruct((stripe_rows * 32, columns), low),
            jax.ShapeDtypeStruct((panels, rows * 8, hidden), low),
            *[jax.ShapeDtypeStruct((length * 4, width), low)] * 4,
            *[jax.ShapeDtypeStruct((experts, spots, width), low)] * 2,
            *[jax.ShapeDtypeStruct((experts, spots, hidden), low)] * 3,
            jax.ShapeDtypeStruct((length, width), low),
            jax.ShapeDtypeStruct((length, query_width + 2 * KVH * HD), low),
            jax.ShapeDtypeStruct((length, query_width), low),
            jax.ShapeDtypeStruct((length, width), full),
            jax.ShapeDtypeStruct((length, width), full),
            jax.ShapeDtypeStruct((length, width), full),
            jax.ShapeDtypeStruct((6, rows, hidden), low),
            jax.ShapeDtypeStruct((length, 1), full),
            jax.ShapeDtypeStruct((8, width), full),
        ],
        scratch_shapes=[
            pltpu.VMEM((length, width), low),
            pltpu.VMEM((length, query_width + 2 * KVH * HD), low),
            pltpu.VMEM((length, query_width), low),
            pltpu.VMEM((length, width), full),
            pltpu.VMEM((length, width), full),
            pltpu.VMEM((length, width), full),
            pltpu.VMEM((length, width), low),
            pltpu.VMEM((length, FFS), low),
            pltpu.VMEM((length, 2 * FFS), low),
            pltpu.VMEM((14, width, hidden), low),
            pltpu.VMEM((width, 128), low),
            pltpu.VMEM((4, 4, 8, length), full),
            pltpu.VMEM((experts, 4, length), jnp.int32),
            pltpu.VMEM((experts, 4, length), full),
            pltpu.VMEM((4, experts * slots, length), low),
            pltpu.VMEM((experts, spots, width), low),
            pltpu.VMEM((experts, spots, width), low),
            pltpu.VMEM((2, 3, spots, hidden), low),
            pltpu.VMEM((6, 4, rows, hidden), low),
            pltpu.VMEM((6, rows // 2, hidden), low),
            pltpu.VMEM((6, rows // 2, hidden), low),
            pltpu.VMEM((6, rows, hidden), low),
            pltpu.VMEM((6, rows, hidden), low),
            pltpu.SemaphoreType.DMA((170,)),
            pltpu.SemaphoreType.DMA((7, panels)),
            pltpu.SemaphoreType.DMA((7, panels)),
            pltpu.SemaphoreType.DMA((6,)),
            pltpu.SemaphoreType.DMA((15,)),
            pltpu.SemaphoreType.DMA((8, 6)),
            pltpu.SemaphoreType.DMA((2, 5, 6)),
            pltpu.SemaphoreType.DMA((6,)),
        ],
        compiler_params=pltpu.CompilerParams(
            collective_id=1, has_side_effects=True, vmem_limit_bytes=63 * MIB
        ),
        name="front",
    )(stripe, gates, masters, hidden_in, cotangent)


def scatter_kernel(
    grad_parts_ref,
    received_ref,
    grad_returned_ref,
    act_ref,
    grad_gate_ref,
    grad_up_ref,
    dense_ref,
    shared_sum_ref,
    cotangent_ref,
    normed_attend_ref,
    attended_ref,
    residual_in,
    grad_shared_in,
    projected_in,
    hidden_in,
    scale_ref,
    gains_ref,
    expert_sum_ref,
    stripes_ref,
    grad_input_ref,
    grad_gain_ref,
    residual_ref,
    grad_shared_ref,
    projected_ref,
    hidden_ref,
    ring,
    pair_sum,
    corner_x,
    corner_y,
    side_x,
    side_y,
    staged,
    wide,
    narrow,
    left,
    right,
    out_weights,
    grad_tokens,
    grad_attended,
    grad_pair,
    grad_residual_ref,
    key_weights,
    line_out,
    line_in,
    pair_sems,
    slot_sems,
    line_sems,
    token_sems,
    load_sems,
    free,
):
    dp, z = lax.axis_index("dp"), lax.axis_index("expert")
    core, chip = dp % 2, dp // 2
    chip_x, chip_y = flipped(chip, 0), flipped(chip, 1)
    chip_corner = flipped(chip_x, 1)
    device_core = (flipped(dp, 0), z)
    device_x = (flipped(dp, 1), z)
    device_y = (flipped(dp, 2), z)
    others = [(dp, (z + turn) % 4) for turn in range(1, 4)]
    slots = pair_sum.shape[0]
    experts = received_ref.shape[0]
    expert_panels = 3 * experts
    dense_panels = line_out.shape[0]
    shared_panels = dense_panels - right.shape[0]
    panels = expert_panels + right.shape[0]
    length, width = residual_ref.shape
    share, hidden = staged.shape[1:]
    half = share // 2
    stripe = share // 4
    query_width = HEADS * HD
    kv_width = KVH * HD
    block = width // 4

    def remote(source, target, send, receive, device):
        return pltpu.make_async_remote_copy(
            src_ref=source,
            dst_ref=target,
            send_sem=send,
            recv_sem=receive,
            device_id=device,
            device_id_type=MESH,
        )

    barrier = pltpu.get_barrier_semaphore()
    for device in (device_core, device_x, device_y, *others):
        pl.semaphore_signal(barrier, inc=1, device_id=device, device_id_type=MESH)
    pl.semaphore_wait(barrier, 6)

    grad_copies = [
        remote(
            grad_parts_ref.at[pl.ds(pl.multiple_of(device[1] * length, length), length), :],
            grad_tokens.at[turn],
            token_sems.at[turn],
            token_sems.at[3 + turn],
            device,
        )
        for turn, device in enumerate(others)
    ]
    for copy in grad_copies:
        copy.start()

    def expert_loads(expert):
        buffer = expert % 2
        return [
            pltpu.make_async_copy(source.at[expert], target, load_sems.at[buffer, index])
            for index, (source, target) in enumerate(
                (
                    (received_ref, wide.at[buffer, 0]),
                    (grad_returned_ref, wide.at[buffer, 1]),
                    (grad_gate_ref, narrow.at[buffer, 0]),
                    (grad_up_ref, narrow.at[buffer, 1]),
                    (act_ref, narrow.at[buffer, 2]),
                )
            )
        ]

    for copy in expert_loads(0):
        copy.start()

    def columns(ref, panel):
        return ref.at[:, pl.ds(panel * hidden, hidden)]

    sources = [
        (cotangent_ref, left.at[0]),
        (normed_attend_ref, left.at[2]),
        *[(columns(attended_ref, panel), right.at[panel]) for panel in range(3)],
        (shared_sum_ref, line_out.at[pl.ds(0, shared_panels)]),
        (residual_in, residual_ref),
        (grad_shared_in, grad_shared_ref),
        (projected_in, projected_ref),
        (hidden_in, hidden_ref),
        (dense_ref.at[:, pl.ds(query_width + 2 * kv_width, query_width)], out_weights),
        (dense_ref.at[:, pl.ds(query_width, 2 * kv_width)], key_weights),
        (
            grad_parts_ref.at[pl.ds(pl.multiple_of(z * length, length), length), :],
            grad_tokens.at[3],
        ),
    ]
    dense_loads = [
        pltpu.make_async_copy(source, target, load_sems.at[2 + index // 5, index % 5])
        for index, (source, target) in enumerate(sources)
    ]
    for copy in dense_loads:
        copy.start()
    query_load = pltpu.make_async_copy(
        dense_ref.at[:, pl.ds(0, query_width)], out_weights, pair_sems.at[4]
    )

    def fill(pair, left_ref, right_value):
        for chip_index in range(4):
            part = matmul_tn(left_ref[:, chip_index * block : (chip_index + 1) * block], right_value)
            ring[pair, chip_index] = part.astype(jnp.bfloat16).reshape(2, share, hidden)

    def total(first, *more):
        result = first.astype(jnp.float32)
        for value in more:
            result = result + value.astype(jnp.float32)
        return result

    def pair_copy(panel):
        pair, slot = panel % 2, panel % slots
        return remote(
            ring.at[pair, :, 1 - core],
            pair_sum.at[slot],
            pair_sems.at[pair],
            slot_sems.at[0, slot],
            device_core,
        )

    def corner_copies(panel):
        slot = panel % slots
        return (
            remote(
                pair_sum.at[slot, chip_corner, pl.ds(0, half)],
                corner_x.at[slot],
                slot_sems.at[1, slot],
                slot_sems.at[2, slot],
                device_x,
            ),
            remote(
                pair_sum.at[slot, chip_corner, pl.ds(half, half)],
                corner_y.at[slot],
                slot_sems.at[3, slot],
                slot_sems.at[4, slot],
                device_y,
            ),
        )

    def side_copies(panel):
        slot = panel % slots
        return (
            remote(
                pair_sum.at[slot, chip_x],
                side_x.at[slot],
                slot_sems.at[5, slot],
                slot_sems.at[6, slot],
                device_x,
            ),
            remote(
                pair_sum.at[slot, chip_y],
                side_y.at[slot],
                slot_sems.at[7, slot],
                slot_sems.at[8, slot],
                device_y,
            ),
        )

    def line_copies(panel):
        return [
            remote(
                line_out.at[panel, pl.ds(pl.multiple_of(device[1] * stripe, stripe), stripe)],
                line_in.at[panel, turn],
                line_sems.at[0, panel, turn],
                line_sems.at[1, panel, turn],
                device,
            )
            for turn, device in enumerate(others)
        ]

    def staged_copy(panel):
        return pltpu.make_async_copy(
            staged.at[panel % 2], expert_sum_ref.at[panel], pair_sems.at[2 + panel % 2]
        )

    def post(panel):
        @pl.when(panel >= slots)
        def _():
            pl.semaphore_wait(free.at[0], 1)

        pair_copy(panel).start()

    def sum_pair(panel):
        pair, slot = panel % 2, panel % slots
        pair_copy(panel).wait()
        for chip_index in range(4):
            pair_sum[slot, chip_index] = total(
                pair_sum[slot, chip_index], ring[pair, chip_index, core]
            ).astype(jnp.bfloat16)

        @pl.when(panel >= slots)
        def _():
            pl.semaphore_wait(free.at[1], 1)
            pl.semaphore_wait(free.at[2], 1)

        for copy in corner_copies(panel):
            copy.start()

    def sum_corner(panel):
        slot = panel % slots
        for copy in corner_copies(panel):
            copy.wait_recv()
        pair_sum[slot, chip_y, :half] = total(
            pair_sum[slot, chip_y, :half], corner_x[slot]
        ).astype(jnp.bfloat16)
        pair_sum[slot, chip_x, half:] = total(
            pair_sum[slot, chip_x, half:], corner_y[slot]
        ).astype(jnp.bfloat16)
        for copy in side_copies(panel):
            copy.start()

    def sum_sides(panel):
        slot = panel % slots
        for copy in corner_copies(panel):
            copy.wait_send()
        for copy in side_copies(panel):
            copy.wait()
        value = total(pair_sum[slot, chip], side_x[slot], side_y[slot]).astype(jnp.bfloat16)

        @pl.when(panel < expert_panels)
        def _():
            @pl.when(panel >= 2)
            def _():
                staged_copy(panel - 2).wait()

            staged[panel % 2] = value
            staged_copy(panel).start()

        @pl.when(panel >= expert_panels)
        def _():
            index = panel - expert_panels + shared_panels
            line_out[index] = value
            for copy in line_copies(index):
                copy.start()

        @pl.when(panel < panels - slots)
        def _():
            for index, device in enumerate((device_core, device_x, device_y)):
                pl.semaphore_signal(
                    free.at[index], inc=1, device_id=device, device_id_type=MESH
                )

    def residual_backward(part):
        if part == 0:
            for copy in dense_loads:
                copy.wait()
            for copy in grad_copies:
                copy.wait()
            grad_gain_ref[...] = jnp.zeros_like(grad_gain_ref)
        rows_step = 32
        steps = length // rows_step // 2

        @pl.loop(part * steps, (part + 1) * steps)
        def _(index):
            rows = pl.ds(index * rows_step, rows_step)
            grad_normed = (
                total(
                    grad_tokens[3, rows, :],
                    grad_tokens[0, rows, :],
                    grad_tokens[1, rows, :],
                    grad_tokens[2, rows, :],
                )
                + grad_shared_ref[rows, :]
            )
            residual, scale = residual_ref[rows, :], scale_ref[rows, :]
            grad_scaled = grad_normed * gains_ref[1:2, :]
            mean = jnp.mean(grad_scaled * residual, axis=-1, keepdims=True)
            grad_residual = (
                left[0, rows, :].astype(jnp.float32)
                + scale * grad_scaled
                - residual * (scale * scale * scale) * mean
            )
            grad_residual_ref[rows, :] = grad_residual
            left[1, rows, :] = grad_residual.astype(jnp.bfloat16)
            grad_gain_ref[1:2, :] += jnp.sum(
                grad_normed * residual * scale, axis=0, keepdims=True
            )

    def attended_backward():
        grad_attended[...] = matmul(left[1], out_weights[...]).astype(jnp.bfloat16)
        query_load.start()

    def query_backward():
        query_load.wait()
        for part in range(3):
            update = matmul_nt(right[3 + part], out_weights[:, part * hidden : (part + 1) * hidden])
            if part == 0:
                grad_input_ref[...] = update
            else:
                grad_input_ref[...] += update

    def key_backward():
        for part in range(2):
            grad_input_ref[...] += matmul_nt(
                right[6 + part], key_weights[:, part * hidden : (part + 1) * hidden]
            )

    def input_backward():
        rows_step = 32

        @pl.loop(0, length // rows_step)
        def _(index):
            rows = pl.ds(index * rows_step, rows_step)
            values, grad_normed = hidden_ref[rows, :].astype(jnp.float32), grad_input_ref[rows, :]
            scale = lax.rsqrt(jnp.mean(values * values, axis=-1, keepdims=True) + 1e-06)
            grad_scaled = grad_normed * gains_ref[0:1, :]
            mean = jnp.mean(grad_scaled * values, axis=-1, keepdims=True)
            grad_input_ref[rows, :] = (
                grad_residual_ref[rows, :]
                + scale * grad_scaled
                - values * (scale * scale * scale) * mean
            )
            grad_gain_ref[0:1, :] += jnp.sum(
                grad_normed * values * scale, axis=0, keepdims=True
            )

    def attention_backward(head):
        score_scale = HD ** (-0.5)
        per_group = HEADS // KVH
        heads_wide = hidden // HD
        group = head // per_group
        key_rows = projected_ref[:, query_width + group * HD : query_width + (group + 1) * HD]
        value_first = query_width + kv_width + group * HD
        value_rows = projected_ref[:, value_first : value_first + HD]
        row = lax.broadcasted_iota(jnp.int32, (length, length), 0)
        column = lax.broadcasted_iota(jnp.int32, (length, length), 1)
        spot = slice(head * HD, (head + 1) * HD)
        query, grad_out = projected_ref[:, spot], grad_attended[:, spot]
        scores = jnp.where(column <= row, matmul_nt(query, key_rows) * score_scale, -1e30)
        raised = jnp.exp(scores - jnp.max(scores, axis=-1, keepdims=True))
        weights = raised / jnp.sum(raised, axis=-1, keepdims=True)
        grad_weights = matmul_nt(grad_out, value_rows)
        inner = jnp.sum(weights * grad_weights, axis=-1, keepdims=True)
        grad_scores = (weights * (grad_weights - inner)).astype(jnp.bfloat16)
        grad_query = matmul(grad_scores, key_rows) * score_scale
        place = slice(head % heads_wide * HD, (head % heads_wide + 1) * HD)
        right[3 + head // heads_wide, :, place] = grad_query.astype(jnp.bfloat16)
        grad_key = matmul_tn(grad_scores, query)
        grad_value = matmul_tn(weights.astype(jnp.bfloat16), grad_out)
        if head % per_group > 0:
            grad_key = grad_key + grad_pair[0]
            grad_value = grad_value + grad_pair[1]
        if head % per_group < per_group - 1:
            grad_pair[0] = grad_key
            grad_pair[1] = grad_value
        else:
            place = slice(group * HD, (group + 1) * HD)
            right[6, :, place] = (grad_key * score_scale).astype(jnp.bfloat16)
            right[7, :, place] = grad_value.astype(jnp.bfloat16)

    def two_heads_backward(head):
        attention_backward(head)
        attention_backward(head + 1)

    @pl.loop(0, panels + 5)
    def _(step):
        @pl.when(step < expert_panels)
        def _():
            expert, matrix = step // 3, step % 3

            @pl.when(matrix == 0)
            def _():
                for copy in expert_loads(expert):
                    copy.wait()

                @pl.when(expert + 1 < experts)
                def _():
                    for copy in expert_loads(expert + 1):
                        copy.start()

            fill(step % 2, wide.at[expert % 2, matrix // 2], narrow[expert % 2, matrix])

        backward = [
            *[functools.partial(residual_backward, part) for part in range(2)],
            attended_backward,
            *[functools.partial(two_heads_backward, head) for head in range(0, HEADS, 2)],
            query_backward,
            key_backward,
            input_backward,
        ]
        for index, call in enumerate(backward):
            pl.when(step == GRAD_STEP + index)(call)

        @pl.when((step >= expert_panels) & (step < panels))
        def _():
            panel = step - expert_panels
            fill(step % 2, left.at[jnp.where(panel < 3, 1, 2)], right[panel])

        @pl.when(step == GRAD_STEP + 1)
        def _():
            for panel in range(shared_panels):
                for copy in line_copies(panel):
                    copy.start()

        @pl.when(step < panels)
        def _():
            post(step)

        @pl.when((step >= 1) & (step < panels + 1))
        def _():
            sum_pair(step - 1)

        @pl.when((step >= 3) & (step < panels + 3))
        def _():
            sum_corner(step - 3)

        @pl.when(step >= 5)
        def _():
            sum_sides(step - 5)

    for panel in (expert_panels - 2, expert_panels - 1):
        staged_copy(panel).wait()

    for panel in range(dense_panels):
        for copy in line_copies(panel):
            copy.wait()
        place = panel + 8 if panel < 6 else panel - 1 if panel < 9 else panel - 9
        stripes_ref[place] = total(
            line_out[panel, pl.ds(pl.multiple_of(z * stripe, stripe), stripe), :],
            line_in[panel, 0],
            line_in[panel, 1],
            line_in[panel, 2],
        )


def scatter_grads(
    grad_parts,
    saved,
    dense_all,
    shared_sum,
    cotangent,
    normed_attend,
    attended,
    residual,
    grad_shared,
    projected,
    hidden_in,
    scale,
    gains,
):
    experts, spots, width = saved[0].shape
    hidden = saved[2].shape[-1]
    length = residual.shape[0]
    share = width // 8
    stripe = share // 4
    dense_panels = 14
    low = jnp.bfloat16
    vmem = pl.BlockSpec(memory_space=pltpu.VMEM)
    return pl.pallas_call(
        scatter_kernel,
        in_specs=[ANY] * 15 + [vmem] * 2,
        out_specs=[ANY] + [vmem] * 3,
        out_shape=[
            jax.ShapeDtypeStruct((3 * experts, share, hidden), low),
            jax.ShapeDtypeStruct((dense_panels, stripe, hidden), jnp.float32),
            jax.ShapeDtypeStruct((length, width), jnp.float32),
            jax.ShapeDtypeStruct((2, width), jnp.float32),
        ],
        scratch_shapes=[
            pltpu.VMEM((length, width), jnp.float32),
            pltpu.VMEM((length, width), jnp.float32),
            pltpu.VMEM(projected.shape, low),
            pltpu.VMEM((length, width), low),
            pltpu.VMEM((2, 4, 2, share, hidden), low),
            pltpu.VMEM((SLOTS, 4, share, hidden), low),
            pltpu.VMEM((SLOTS, share // 2, hidden), low),
            pltpu.VMEM((SLOTS, share // 2, hidden), low),
            pltpu.VMEM((SLOTS, share, hidden), low),
            pltpu.VMEM((SLOTS, share, hidden), low),
            pltpu.VMEM((2, share, hidden), low),
            pltpu.VMEM((2, 2, spots, width), low),
            pltpu.VMEM((2, 3, spots, hidden), low),
            pltpu.VMEM((3, length, width), low),
            pltpu.VMEM((8, length, hidden), low),
            pltpu.VMEM((width, HEADS * HD), low),
            pltpu.VMEM((4, length, width), low),
            pltpu.VMEM((length, HEADS * HD), low),
            pltpu.VMEM((2, length, HD), jnp.float32),
            pltpu.VMEM((length, width), jnp.float32),
            pltpu.VMEM((width, 2 * KVH * HD), low),
            pltpu.VMEM((dense_panels, share, hidden), low),
            pltpu.VMEM((dense_panels, 3, stripe, hidden), low),
            pltpu.SemaphoreType.DMA((5,)),
            pltpu.SemaphoreType.DMA((9, SLOTS)),
            pltpu.SemaphoreType.DMA((2, dense_panels, 3)),
            pltpu.SemaphoreType.DMA((6,)),
            pltpu.SemaphoreType.DMA((5, 5)),
            pltpu.SemaphoreType.REGULAR((3,)),
        ],
        compiler_params=pltpu.CompilerParams(
            collective_id=3, has_side_effects=True, vmem_limit_bytes=62 * MIB
        ),
        name="scatter_grads",
    )(
        grad_parts,
        *saved,
        dense_all,
        shared_sum,
        cotangent,
        normed_attend,
        attended,
        residual,
        grad_shared,
        projected,
        hidden_in,
        scale,
        gains,
    )


def muon_kernel(
    expert_ref,
    dense_ref,
    routed_parts_ref,
    expert_out_ref,
    dense_out_ref,
    routed_received_ref,
    dense_back,
    moments,
    units,
    orthogonal,
    current,
    low,
    identity,
    line_sems,
    out_sems,
    in_sems,
    back_out_sems,
    back_in_sems,
    load_sems,
):
    dp, z = lax.axis_index("dp"), lax.axis_index("expert")
    count, share, _ = moments.shape
    first, dense_count = 10, 4
    stripe = dense_ref.shape[1]
    others = [(dp, (z + turn) % 4) for turn in range(1, 4)]
    peers = [((dp + turn) % 8, z) for turn in range(1, 8)]

    def remote(source, target, send, receive, device):
        return pltpu.make_async_remote_copy(
            src_ref=source,
            dst_ref=target,
            send_sem=send,
            recv_sem=receive,
            device_id=device,
            device_id_type=MESH,
        )

    def share_of(index):
        return pl.ds(pl.multiple_of(index * share, share), share)

    def stripe_of(index):
        return pl.ds(pl.multiple_of(index * stripe, stripe), stripe)

    barrier = pltpu.get_barrier_semaphore()
    for device in (*others, *peers):
        pl.semaphore_signal(barrier, inc=1, device_id=device, device_id_type=MESH)
    dense_rows = pl.ds(first, dense_count)
    loads = [
        pltpu.make_async_copy(
            expert_ref.at[pl.ds(0, first)], moments.at[pl.ds(0, first)], load_sems.at[0]
        ),
        pltpu.make_async_copy(
            expert_ref.at[pl.ds(first, count - first - dense_count)],
            moments.at[pl.ds(first + dense_count, count - first - dense_count)],
            load_sems.at[1],
        ),
        pltpu.make_async_copy(
            dense_ref.at[pl.ds(z * dense_count, dense_count)],
            moments.at[dense_rows, stripe_of(z)],
            load_sems.at[2],
        ),
    ]
    for copy in loads:
        copy.start()
    pl.semaphore_wait(barrier, len(others) + len(peers))
    line_copies = [
        remote(
            dense_ref.at[pl.ds(device[1] * dense_count, dense_count)],
            moments.at[dense_rows, stripe_of(z)],
            line_sems.at[0, turn],
            line_sems.at[1, turn],
            device,
        )
        for turn, device in enumerate(others)
    ]
    line_back = [
        remote(
            dense_back.at[:, stripe_of(device[1])],
            dense_out_ref.at[pl.ds(z * dense_count, dense_count)],
            line_sems.at[2, turn],
            line_sems.at[3, turn],
            device,
        )
        for turn, device in enumerate(others)
    ]
    own_back = pltpu.make_async_copy(
        dense_back.at[:, stripe_of(z)],
        dense_out_ref.at[pl.ds(z * dense_count, dense_count)],
        load_sems.at[2],
    )

    def out_copy(slot, turn):
        owner = peers[turn][0]
        return remote(
            moments.at[8 * slot + owner],
            units.at[slot, share_of(dp)],
            out_sems.at[slot, turn],
            in_sems.at[slot],
            peers[turn],
        )

    def own_copy(slot):
        return pltpu.make_async_copy(
            moments.at[8 * slot + dp], units.at[slot, share_of(dp)], load_sems.at[3 + slot]
        )

    def is_dense(slot, owner):
        unit = 8 * slot + owner
        return (unit >= first) & (unit < first + dense_count)

    def expert_place(slot, owner):
        unit = 8 * slot + owner
        return expert_out_ref.at[jnp.where(unit < first, unit, unit - dense_count)]

    def dense_place(slot, owner):
        return dense_back.at[8 * slot + owner - first]

    def back_copy(place, slot, turn):
        return remote(
            orthogonal.at[slot, share_of(peers[turn][0])],
            place(slot, dp),
            back_out_sems.at[slot, turn],
            back_in_sems.at[slot, dp],
            peers[turn],
        )

    def own_back_copy(place, slot):
        return pltpu.make_async_copy(
            orthogonal.at[slot, share_of(dp)], place(slot, dp), load_sems.at[3 + slot]
        )

    def send_back(place, slot):
        for turn in range(7):
            back_copy(place, slot, turn).start()
        own_back_copy(place, slot).start()

    def exists(slot, owner):
        return 8 * slot + owner < count

    def send_slot(slot):
        for turn in range(7):
            pl.when(exists(slot, peers[turn][0]))(out_copy(slot, turn).start)
        pl.when(exists(slot, dp))(own_copy(slot).start)

    length = routed_received_ref.shape[1]
    own_routed = pltpu.make_async_copy(
        routed_parts_ref.at[pl.ds(pl.multiple_of(z * length, length), length), :],
        routed_received_ref.at[3],
        load_sems.at[6],
    )
    own_routed.start()
    routed_copies = [
        remote(
            routed_parts_ref.at[pl.ds(pl.multiple_of(device[1] * length, length), length), :],
            routed_received_ref.at[turn],
            line_sems.at[4, turn],
            line_sems.at[5, turn],
            device,
        )
        for turn, device in enumerate(others)
    ]
    for copy in line_copies:
        copy.start()
    loads[0].wait()
    send_slot(0)
    loads[1].wait()
    loads[2].wait()
    for copy in line_copies:
        copy.wait()
    send_slot(1)
    send_slot(2)
    for copy in routed_copies:
        copy.start()

    @pl.loop(0, 3)
    def _(slot):
        @pl.when(exists(slot, dp))
        def _():
            own_copy(slot).wait()
            arrived = units.at[slot, pl.ds(0, 7 * share)]
            remote(arrived, arrived, in_sems.at[slot], in_sems.at[slot], peers[0]).wait_recv()
            newton_schulz_unit(units.at[slot], orthogonal.at[slot], current, low, identity)

            @pl.when(is_dense(slot, dp))
            def _():
                send_back(dense_place, slot)

            @pl.when(jnp.logical_not(is_dense(slot, dp)))
            def _():
                send_back(expert_place, slot)

    def own_back_wait(slot):
        def wait():
            pltpu.make_async_copy(
                orthogonal.at[slot, share_of(dp)], expert_out_ref.at[0], load_sems.at[3 + slot]
            ).wait()

        return wait

    def wait_back(slot):
        for turn in range(7):
            owner = peers[turn][0]

            @pl.when(exists(slot, owner))
            def _():
                block = expert_out_ref.at[0]
                semaphore = back_in_sems.at[slot, owner]
                remote(block, block, semaphore, semaphore, peers[0]).wait_recv()

        pl.when(exists(slot, dp))(own_back_wait(slot))

    wait_back(1)
    for copy in line_back:
        copy.start()
    own_back.start()
    wait_back(0)
    wait_back(2)
    for slot in range(3):
        for turn in range(7):
            pl.when(exists(slot, peers[turn][0]))(out_copy(slot, turn).wait_send)

        @pl.when(exists(slot, dp))
        def _():
            for turn in range(7):
                back_copy(expert_place, slot, turn).wait_send()

    for copy in line_back:
        copy.wait()
    own_back.wait()
    own_routed.wait()
    for copy in routed_copies:
        copy.wait()


def muon(expert_units, dense_units, routed_parts):
    experts, share, columns = expert_units.shape
    panels, stripe, _ = dense_units.shape
    count = experts + panels // 4
    low = jnp.bfloat16
    return pl.pallas_call(
        muon_kernel,
        in_specs=[ANY] * 3,
        out_specs=[ANY] * 3,
        out_shape=[
            jax.ShapeDtypeStruct(expert_units.shape, low),
            jax.ShapeDtypeStruct(dense_units.shape, low),
            jax.ShapeDtypeStruct((4, routed_parts.shape[0] // 4, routed_parts.shape[1]), low),
        ],
        scratch_shapes=[
            pltpu.VMEM((panels // 4, share, columns), low),
            pltpu.VMEM((count, share, columns), low),
            pltpu.VMEM((3, 8 * share, columns), low),
            pltpu.VMEM((3, 8 * share, columns), low),
            pltpu.VMEM((columns, 8 * share), jnp.float32),
            pltpu.VMEM((columns, 8 * share), low),
            pltpu.VMEM((columns, columns), low),
            pltpu.SemaphoreType.DMA((6, 3)),
            pltpu.SemaphoreType.DMA((3, 7)),
            pltpu.SemaphoreType.DMA((3,)),
            pltpu.SemaphoreType.DMA((3, 7)),
            pltpu.SemaphoreType.DMA((3, 8)),
            pltpu.SemaphoreType.DMA((7,)),
        ],
        compiler_params=pltpu.CompilerParams(
            collective_id=4, has_side_effects=True, vmem_limit_bytes=56 * MIB
        ),
        name="muon",
    )(expert_units, dense_units, routed_parts)


GROUP = 3


def blocks_over(steps, shape, axis):
    def place(index):
        return tuple(
            jnp.minimum(index, steps - 1) if position == axis else 0
            for position in range(len(shape))
        )

    return pl.BlockSpec(shape, place)


def moments_kernel(
    dense_panels,
    momentum_ref,
    sum_ref,
    dense_momentum_ref,
    dense_sum_ref,
    grad_ref,
    moment_ref,
    units_ref,
    dense_grad_ref,
    dense_moment_ref,
    dense_units_ref,
):
    grad = sum_ref[...].astype(jnp.float32)
    moment = MOMENTUM_DECAY * momentum_ref[...] + grad
    grad_ref[...] = grad
    moment_ref[...] = moment
    units_ref[...] = moment.astype(jnp.bfloat16)
    columns = dense_sum_ref.shape[2]
    for panel in range(GROUP):
        spot = slice(panel * columns, (panel + 1) * columns)
        dense_grad = dense_sum_ref[panel]
        dense_moment = MOMENTUM_DECAY * dense_momentum_ref[:, spot] + dense_grad
        dense_grad_ref[:, spot] = dense_grad
        dense_moment_ref[:, spot] = dense_moment
        real = pl.program_id(0) * GROUP + panel < dense_panels
        dense_units_ref[panel] = jnp.where(real, dense_moment, 0.0).astype(jnp.bfloat16)


def moments(momentum, grad_sum, dense_momentum, dense_sum):
    panels, rows, columns = grad_sum.shape
    dense_panels, stripe, _ = dense_sum.shape
    steps = panels // GROUP
    dense_steps = -(-dense_panels // GROUP)
    block = pl.BlockSpec((GROUP, rows, columns), lambda index: (index, 0, 0))
    wide = blocks_over(dense_steps, (stripe, GROUP * columns), 1)
    full = jax.ShapeDtypeStruct(grad_sum.shape, jnp.float32)
    dense_full = jax.ShapeDtypeStruct(dense_momentum.shape, jnp.float32)
    grad, moment, *rest = pl.pallas_call(
        functools.partial(moments_kernel, dense_panels),
        grid=(steps,),
        in_specs=[
            block,
            block,
            wide,
            blocks_over(dense_steps, (GROUP, stripe, columns), 0),
        ],
        out_specs=[
            block,
            block,
            block,
            wide,
            wide,
            blocks_over(dense_steps + 1, (GROUP, stripe, columns), 0),
        ],
        out_shape=[
            full,
            full,
            jax.ShapeDtypeStruct(grad_sum.shape, jnp.bfloat16),
            dense_full,
            dense_full,
            jax.ShapeDtypeStruct((dense_panels + 2, stripe, columns), jnp.bfloat16),
        ],
        compiler_params=pltpu.CompilerParams(vmem_limit_bytes=60 * MIB),
        name="moments",
    )(momentum.reshape(grad_sum.shape), grad_sum, dense_momentum, dense_sum)
    return grad.reshape(momentum.shape), moment.reshape(momentum.shape), *rest


def update_kernel(
    weights_ref,
    orthogonal_ref,
    dense_weights_ref,
    dense_orthogonal_ref,
    base_ref,
    routed_ref,
    grad_ref,
    new_ref,
    dense_new_ref,
    out_ref,
    grad_out_ref,
):
    keep_factor = 1.0 - LEARN_RATE * WEIGHT_DECAY
    new_ref[...] = keep_factor * weights_ref[...] - LEARN_RATE * orthogonal_ref[...].astype(
        jnp.float32
    )
    columns = dense_orthogonal_ref.shape[2]
    for panel in range(GROUP):
        spot = slice(panel * columns, (panel + 1) * columns)
        dense_new_ref[:, spot] = keep_factor * dense_weights_ref[:, spot] - LEARN_RATE * (
            dense_orthogonal_ref[panel].astype(jnp.float32)
        )
    total = base_ref[...]
    for source in (3, 0, 1, 2):
        total = total + routed_ref[source].astype(jnp.float32)
    out_ref[...] = total.astype(jnp.bfloat16)
    grad_out_ref[...] = grad_ref[...]


def updated(weights, orthogonal, dense_weights, dense_orthogonal, base, routed, grad):
    panels, rows, columns = orthogonal.shape
    stripe, dense_columns = dense_weights.shape
    length, width = base.shape
    dense_steps = -(-dense_columns // (GROUP * columns))
    row_steps = 4
    block = pl.BlockSpec((GROUP, rows, columns), lambda index: (index, 0, 0))
    wide = blocks_over(dense_steps, (stripe, GROUP * columns), 1)
    part = blocks_over(row_steps, (length // row_steps, width), 0)
    new, *rest = pl.pallas_call(
        update_kernel,
        grid=(panels // GROUP,),
        in_specs=[
            block,
            block,
            wide,
            blocks_over(dense_steps, (GROUP, stripe, columns), 0),
            part,
            blocks_over(row_steps, (4, length // row_steps, width), 1),
            part,
        ],
        out_specs=[block, wide, part, part],
        out_shape=[
            jax.ShapeDtypeStruct(orthogonal.shape, jnp.float32),
            jax.ShapeDtypeStruct(dense_weights.shape, jnp.float32),
            jax.ShapeDtypeStruct(base.shape, jnp.bfloat16),
            jax.ShapeDtypeStruct(base.shape, jnp.float32),
        ],
        compiler_params=pltpu.CompilerParams(vmem_limit_bytes=60 * MIB),
        name="update",
    )(
        weights.reshape(orthogonal.shape),
        orthogonal,
        dense_weights,
        dense_orthogonal,
        base,
        routed,
        grad,
    )
    return new.reshape(weights.shape), *rest


def on_device(
    hidden_in,
    cotangent,
    routes,
    route_weights,
    dense_weights,
    dense_momentum,
    expert_weights,
    expert_momentum,
    norm_gains,
    gain_first,
    gain_second,
):
    length, width = hidden_in.shape
    topk_count = routes.shape[1]
    local_experts = expert_weights.shape[0]
    expert_size = lax.axis_size("expert")
    dp_size = lax.axis_size("dp")
    expert_count = local_experts * expert_size
    capacity = 5 * length * topk_count // (4 * expert_count)
    block_rows = min(512, length)
    query_width = HEADS * HD
    kv_width = KVH * HD
    qkv_end = query_width + 2 * kv_width
    shared_base = 2 * query_width + 2 * kv_width
    gate_table = jnp.sum(
        jnp.where(
            routes.T[None, :, :] == jnp.arange(expert_count, dtype=jnp.int32)[:, None, None],
            route_weights.T[None, :, :],
            0.0,
        ),
        axis=1,
    )
    direct = dp_size == 8 and expert_size == 4
    inputs = hidden_in.astype(jnp.float32)
    scale_attend = norm_scale(inputs)
    if direct:
        stripe_rows = dense_weights.shape[0]
        extra = jnp.zeros((stripe_rows, 128 - norm_gains.shape[0]), jnp.float32)
        plane_gates = gate_table.reshape(expert_size, local_experts, length)
        (
            dense_all,
            _,
            _,
            _,
            routed_parts,
            grad_parts,
            *saved,
            normed_attend,
            projected,
            attended,
            residual,
            grad_shared,
            base_out,
            shared_sum,
            scale_mixer,
            gains_all,
        ) = front(
            jnp.concatenate(
                [
                    dense_weights[:, :shared_base],
                    norm_gains.T,
                    extra,
                    dense_weights[:, shared_base:],
                ],
                1,
            ).astype(jnp.bfloat16),
            jnp.pad(plane_gates, ((0, 0), (0, 8 - local_experts), (0, 0))),
            expert_weights.reshape(-1, *expert_weights.shape[2:]),
            hidden_in,
            cotangent,
            -(-capacity // 16) * 16,
        )
    else:
        gate_tables = lax.all_gather(gate_table, "expert", axis=0, tiled=False)
        cotangents = lax.all_gather(cotangent, "expert", axis=0, tiled=True)
        dense_all, gains_all = (
            lax.all_gather(
                dense_weights.astype(jnp.bfloat16), ("dp", "expert"), axis=0, tiled=True
            ),
            lax.all_gather(norm_gains.astype(jnp.bfloat16), ("dp", "expert"), axis=1, tiled=True),
        )
        gain_attend = gains_all[0].astype(jnp.float32)
        gain_mixer = gains_all[1].astype(jnp.float32)
        normed_attend = (inputs * scale_attend * gain_attend).astype(jnp.bfloat16)
        projected = jnp.dot(
            normed_attend, dense_all[:, :qkv_end], preferred_element_type=jnp.float32
        ).astype(jnp.bfloat16)
        query = projected[:, :query_width]
        key_rows = projected[:, query_width : query_width + kv_width]
        value_rows = projected[:, query_width + kv_width :]
        attended, saved_stats = attend_forward(query, key_rows, value_rows, block_rows)
        residual = inputs + jnp.einsum(
            "sq,dq->sd", attended, dense_all[:, qkv_end:shared_base], preferred_element_type=jnp.float32
        )
        scale_mixer = norm_scale(residual)
        normed_mixer = (residual * scale_mixer * gain_mixer).astype(jnp.bfloat16)
        expert_all = lax.all_gather(expert_weights.astype(jnp.bfloat16), "dp", axis=2, tiled=True)
        tokens = lax.all_gather(normed_mixer, "expert", axis=0, tiled=True)
        shared_pre = jnp.dot(
            normed_mixer,
            dense_all[:, shared_base : shared_base + 2 * FFS],
            preferred_element_type=jnp.float32,
        )
        shared_gate = shared_pre[:, :FFS]
        shared_up = shared_pre[:, FFS:]
        shared_act = (jax.nn.silu(shared_gate) * shared_up).astype(jnp.bfloat16)
        shared_out = jnp.einsum(
            "sf,df->sd",
            shared_act,
            dense_all[:, shared_base + 2 * FFS : shared_base + 3 * FFS],
            preferred_element_type=jnp.float32,
        )
        grad_shared_act = jnp.dot(
            cotangent,
            dense_all[:, shared_base + 2 * FFS : shared_base + 3 * FFS],
            preferred_element_type=jnp.float32,
        )
        shared_sig = jax.nn.sigmoid(shared_gate)
        grad_shared_pre = jnp.concatenate(
            [
                grad_shared_act * shared_up * shared_sig * (1.0 + shared_gate * (1.0 - shared_sig)),
                grad_shared_act * jax.nn.silu(shared_gate),
            ],
            1,
        ).astype(jnp.bfloat16)
        grad_shared = jnp.einsum(
            "sf,df->sd",
            grad_shared_pre,
            dense_all[:, shared_base : shared_base + 2 * FFS],
            preferred_element_type=jnp.float32,
        )
        base_out = residual + shared_out
        my_gates = lax.dynamic_slice_in_dim(
            gate_tables, lax.axis_index("expert") * local_experts, local_experts, 1
        ).transpose(1, 0, 2)
        hot = my_gates > 0.0
        earlier = jnp.einsum(
            "est,ut->esu",
            hot.astype(jnp.bfloat16),
            jnp.tril(jnp.ones((length, length), jnp.bfloat16), -1),
            preferred_element_type=jnp.float32,
        ).astype(jnp.int32)
        place = jnp.where(hot, earlier, -1)
        routed_parts, grad_parts, saved = grouped_experts(
            tokens, cotangents, place, my_gates, expert_all, capacity
        )
    if direct:
        expert_sum, dense_sum, grad_inputs, grad_gains = scatter_grads(
            grad_parts,
            saved,
            dense_all,
            shared_sum,
            cotangent,
            normed_attend,
            attended,
            residual,
            grad_shared,
            projected,
            hidden_in,
            scale_mixer,
            gains_all,
        )
        expert_grad, expert_moment, expert_units, dense_grad, dense_moment, dense_units = moments(
            expert_momentum, expert_sum, dense_momentum, dense_sum
        )
        orth_expert, orth_dense, routed = muon(expert_units, dense_units, routed_parts)
        expert_new, dense_new, block_out, grad_inputs = updated(
            expert_weights,
            orth_expert,
            dense_weights,
            orth_dense,
            base_out,
            routed,
            grad_inputs,
        )
    else:
        routed = lax.psum_scatter(routed_parts, "expert", scatter_dimension=0, tiled=True)
        grad_routed = lax.psum_scatter(grad_parts, "expert", scatter_dimension=0, tiled=True)
        expert_parts = [expert_grads(*kept) for kept in saved]
        expert_grad = lax.psum_scatter(
            sum(part.astype(jnp.float32) for part in expert_parts).astype(jnp.bfloat16),
            "dp",
            scatter_dimension=2,
            tiled=True,
        ).astype(jnp.float32)
        grad_normed = grad_routed.astype(jnp.float32) + grad_shared
        grad_scaled = grad_normed * gain_mixer
        grad_residual = (
            cotangent.astype(jnp.float32)
            + scale_mixer * grad_scaled
            - residual * scale_mixer**3 * jnp.mean(grad_scaled * residual, axis=-1, keepdims=True)
        )
        grad_gain_mixer = jnp.sum(grad_normed * residual * scale_mixer, axis=0)
        grad_attn_low = grad_residual.astype(jnp.bfloat16)
        grad_attended = jnp.dot(
            grad_attn_low, dense_all[:, qkv_end:shared_base], preferred_element_type=jnp.float32
        ).astype(jnp.bfloat16)
        grad_query, grad_key, grad_value = attend_backward(
            query, key_rows, value_rows, grad_attended, saved_stats, block_rows
        )
        grad_projected = jnp.concatenate([grad_query, grad_key, grad_value], 1)
        dense_parts = [
            jnp.einsum("sd,sf->df", left, right, preferred_element_type=jnp.float32)
            for left, right in (
                (normed_attend, grad_projected),
                (grad_attn_low, attended),
                (normed_mixer, grad_shared_pre),
                (cotangent, shared_act),
            )
        ]
        dense_grad = lax.psum_scatter(
            jnp.concatenate([part.astype(jnp.bfloat16) for part in dense_parts], 1),
            ("dp", "expert"),
            scatter_dimension=0,
            tiled=True,
        ).astype(jnp.float32)
        grad_normed_attend = jnp.einsum(
            "sc,dc->sd", grad_projected, dense_all[:, :qkv_end], preferred_element_type=jnp.float32
        )
        grad_scaled_attend = grad_normed_attend * gain_attend
        grad_inputs = (
            grad_residual
            + scale_attend * grad_scaled_attend
            - inputs * scale_attend**3 * jnp.mean(grad_scaled_attend * inputs, axis=-1, keepdims=True)
        )
        grad_gain_attend = jnp.sum(grad_normed_attend * inputs * scale_attend, axis=0)
        block_out = (base_out + routed.astype(jnp.float32)).astype(jnp.bfloat16)
        grad_gains = jnp.stack([grad_gain_attend, grad_gain_mixer], 0)
        dense_moment = MOMENTUM_DECAY * dense_momentum + dense_grad
        expert_moment = MOMENTUM_DECAY * expert_momentum + expert_grad
        stripe, dense_columns = dense_weights.shape
        row_count = stripe * expert_size
        dense_total = dense_columns // FFE
        dense_share = -(-dense_total // expert_size)
        dense_padded = jnp.pad(
            dense_moment.astype(jnp.bfloat16),
            ((0, 0), (0, dense_share * expert_size * FFE - dense_columns)),
        ).reshape(stripe, dense_share * expert_size, FFE).transpose(1, 0, 2)
        expert_units = expert_moment.astype(jnp.bfloat16).reshape(-1, row_count, FFE)
        dense_units = lax.all_to_all(
            dense_padded, "expert", split_axis=0, concat_axis=1, tiled=True
        )
        expert_unit_count = expert_units.shape[0]
        base_count = expert_unit_count + dense_share
        unit_count = -(-base_count // dp_size) * dp_size
        all_units = jnp.concatenate(
            [
                expert_units,
                dense_units,
                jnp.zeros((unit_count - base_count, row_count, FFE), jnp.bfloat16),
            ],
            0,
        )
        owned = lax.all_to_all(all_units, "dp", split_axis=0, concat_axis=1, tiled=True)
        orthogonal = newton_schulz(owned)
        orth_units = lax.all_to_all(orthogonal, "dp", split_axis=1, concat_axis=0, tiled=True)
        orth_expert = orth_units[:expert_unit_count]
        orth_stripe = lax.all_to_all(
            orth_units[expert_unit_count:base_count],
            "expert",
            split_axis=1,
            concat_axis=0,
            tiled=True,
        )
        orth_stripe = (
            orth_stripe[:dense_total]
            .transpose(1, 0, 2)
            .reshape(stripe, dense_columns)
            .astype(jnp.float32)
        )
        keep_factor = 1.0 - LEARN_RATE * WEIGHT_DECAY
        dense_new = keep_factor * dense_weights - LEARN_RATE * orth_stripe
        expert_new = keep_factor * expert_weights - LEARN_RATE * orth_expert.reshape(
            expert_weights.shape
        ).astype(jnp.float32)
    gain_grad = lax.psum_scatter(
        grad_gains, ("dp", "expert"), scatter_dimension=1, tiled=True
    )
    first_new = FIRST_DECAY * gain_first + (1.0 - FIRST_DECAY) * gain_grad
    second_new = SECOND_DECAY * gain_second + (1.0 - SECOND_DECAY) * gain_grad * gain_grad
    step_ratio = (
        first_new
        / (1.0 - FIRST_DECAY**STEP)
        / (jnp.sqrt(second_new / (1.0 - SECOND_DECAY**STEP)) + 1e-08)
    )
    gain_new = norm_gains - GAIN_RATE * step_ratio
    return (
        block_out,
        grad_inputs,
        dense_grad,
        dense_moment,
        dense_new,
        expert_grad,
        expert_moment,
        expert_new,
        gain_grad,
        first_new,
        second_new,
        gain_new,
    )


def solution(mesh):
    in_specs = (
        P(("dp", "expert"), None),
        P(("dp", "expert"), None),
        P(("dp", "expert"), None),
        P(("dp", "expert"), None),
        P(("dp", "expert"), None),
        P(("dp", "expert"), None),
        P("expert", None, "dp", None),
        P("expert", None, "dp", None),
        P(None, ("dp", "expert")),
        P(None, ("dp", "expert")),
        P(None, ("dp", "expert")),
    )
    out_specs = (
        P(("dp", "expert"), None),
        P(("dp", "expert"), None),
        P(("dp", "expert"), None),
        P(("dp", "expert"), None),
        P(("dp", "expert"), None),
        P("expert", None, "dp", None),
        P("expert", None, "dp", None),
        P("expert", None, "dp", None),
        P(None, ("dp", "expert")),
        P(None, ("dp", "expert")),
        P(None, ("dp", "expert")),
        P(None, ("dp", "expert")),
    )
    return jax.shard_map(
        on_device, mesh=mesh, in_specs=in_specs, out_specs=out_specs, check_vma=False
    )
```
